32 devices in a mesh: row: 4 (over z), col: 8 (over y, x, core).
Axes of the slice: x: 2, y: 2, z: 4, core: 2. Of those that a mesh axis runs over, the one named last changes fastest.
Arguments:
- field: bfloat16 [64, 256, 512], P('row', 'col'), may hold values from -6 to 6
- cotangent: bfloat16 [64, 256, 512], P('row', 'col'), may hold values from -6 to 6
- gains: float32 [2, 512], replicated, may hold values from 0.1 to 1.9
- weights: bfloat16 [2, 4, 512, 512], replicated, as said below
Outputs:
- output: bfloat16 [64, 256, 512], P('row', 'col')
- field_grad: bfloat16 [64, 256, 512], P('row', 'col')
- weight_grad: float32 [8, 512, 512], P(None, ('row', 'col'))
The draws below stay inside these ranges and needn't reach their ends.
Inputs may be any that keep to these rules, and one draw needn't show every extreme that they name: `weights`: finite projection matrices, one per block and role.
All inputs are finite; a program needn't handle non-finite values.
Results may differ from the reference program's by a relative error of at most 0.014.
Values may be sent and summed in bfloat16 or wider, within the bound.
No kernel may reach another device: no remote copies, remote signals or barrier semaphores. Data moves between devices by JAX's collectives and lax.ppermute only.
A program may use at most 128 MiB of HBM per device.

```python
import jax
import jax.numpy as jnp
from jax import lax

C = 512
HEADS = 8
GRID_H = 64
GRID_W = 256


def draw_weights(key, part):
    key = jax.random.fold_in(key, 7)
    keys = jax.random.split(key, 1)
    base = jax.random.normal(keys[0], (2, 4, C, C), jnp.float32) * C ** (-0.5)
    return base.astype(jnp.bfloat16)


def steps_of(rng, dims, pieces, low, largest):
    factor_of, own = 1.0, jax.random.fold_in(rng, 6)
    for axis_at, parts in pieces:
        steps = jnp.exp(jax.random.uniform(jax.random.fold_in(own, axis_at), (parts,), jnp.float32, low / len(pieces), largest / len(pieces)))
        factor_of = factor_of * jnp.repeat(steps, dims[axis_at] // parts).reshape([-1 if axis == axis_at else 1 for axis in range(len(dims))])
    return factor_of


def gaussian(rng, dims, scale, most, cuts=(), held_as=jnp.bfloat16):
    level = steps_of(rng, dims, cuts, -0.22, 0.18) if cuts else 1.0
    entries = jax.random.normal(rng, dims, jnp.float32) * scale * level
    return jnp.minimum(jnp.maximum(entries, -most), most).astype(held_as)


def setup_inputs(seed: int = 0) -> dict:
    key_of = jax.random.split(jax.random.key(seed), 5)
    return {
        "field": gaussian(key_of[0], (GRID_H, GRID_W, C), 1.0, 6.0, ((0, 4), (1, 8))),
        "cotangent": gaussian(key_of[1], (GRID_H, GRID_W, C), 1.0, 6.0, ((0, 4), (1, 8))),
        "gains": jnp.clip(1.0 + 0.18 * jax.random.normal(key_of[2], (2, C), jnp.float32), 0.1, 1.9),
        "weights": draw_weights(jax.random.fold_in(key_of[4], 71), 0),
    }


eps = 1e-05

def normalize(values, gain):
    average = lax.optimization_barrier(jnp.mean(values, axis=-1, keepdims=True))
    centred = values - average
    spread = lax.optimization_barrier(jnp.mean(centred * centred, axis=-1, keepdims=True))
    return centred * lax.rsqrt(spread + eps) * gain

def project(left, weight):
    return jnp.dot(left, weight, preferred_element_type=jnp.float32)

def contract(left, right):
    width = left.shape[-1]
    return jnp.dot(left.reshape(-1, width).T, right.reshape(-1, width), preferred_element_type=jnp.float32)

def mix(form, left, right):
    return jnp.einsum(form, left.astype(jnp.float32), right.astype(jnp.float32), precision=lax.Precision.HIGHEST)

def split_heads(tensor):
    return tensor.reshape(tensor.shape[:-1] + (HEADS, tensor.shape[-1] // HEADS))

def forms(layout):
    if layout == 'r':
        return ('bqhd', 'bkhd')
    return ('qbhd', 'kbhd')

def probabilities(query, key, layout):
    form_q, form_k = forms(layout)
    query4 = split_heads(query)
    scale = query4.shape[-1] ** (-0.5)
    scores = mix(form_q + ',' + form_k + '->bhqk', query4, split_heads(key)) * scale
    top = lax.optimization_barrier(jnp.max(scores, axis=-1, keepdims=True))
    expo = jnp.exp(scores - top)
    return (expo / lax.optimization_barrier(jnp.sum(expo, axis=-1, keepdims=True))).astype(jnp.bfloat16)

def attend(query, key, value, layout):
    form_q, form_k = forms(layout)
    probs = probabilities(query, key, layout)
    result = mix('bhqk,' + form_k + '->' + form_q, probs, split_heads(value))
    return result.reshape(query.shape).astype(jnp.bfloat16)

def attend_back(query, key, value, d_out, layout):
    form_q, form_k = forms(layout)
    probs = probabilities(query, key, layout)
    query4, key4 = (split_heads(query), split_heads(key))
    value4, d_out4 = (split_heads(value), split_heads(d_out))
    scale = query4.shape[-1] ** (-0.5)
    d_probs = mix(form_q + ',' + form_k + '->bhqk', d_out4, value4)
    probs32 = probs.astype(jnp.float32)
    total = lax.optimization_barrier(jnp.sum(probs32 * d_probs, axis=-1, keepdims=True))
    d_scores = (probs32 * (d_probs - total) * scale).astype(jnp.bfloat16)
    d_query = mix('bhqk,' + form_k + '->' + form_q, d_scores, key4).reshape(query.shape).astype(jnp.bfloat16)
    d_key = mix('bhqk,' + form_q + '->' + form_k, d_scores, query4).reshape(key.shape).astype(jnp.bfloat16)
    d_value = mix('bhqk,' + form_q + '->' + form_k, probs, d_out4).reshape(value.shape).astype(jnp.bfloat16)
    return (d_query, d_key, d_value)

def rows_map(func, arrays):
    shaped = tuple((item.reshape((item.shape[0], 1) + item.shape[1:]) for item in arrays))
    result = lax.map(lambda items: func(*items), shaped)
    return jax.tree.map(lambda piece: piece.reshape(piece.shape[0], piece.shape[2], piece.shape[3]), result)

def cols_map(func, arrays):

    def fold(item):
        return item.reshape(item.shape[0], item.shape[1] // 8, 8, item.shape[2]).transpose(1, 0, 2, 3)
    result = lax.map(lambda items: func(*items), tuple((fold(item) for item in arrays)))
    return jax.tree.map(lambda piece: piece.transpose(1, 0, 2, 3).reshape(piece.shape[1], piece.shape[0] * 8, piece.shape[3]), result)

def forward_block(inputs, gain, matrices, mapper, layout):
    normed = normalize(inputs.astype(jnp.float32), gain).astype(jnp.bfloat16)
    query = project(normed, matrices[0]).astype(jnp.bfloat16)
    key = project(normed, matrices[1]).astype(jnp.bfloat16)
    value = project(normed, matrices[2]).astype(jnp.bfloat16)
    attended = mapper(lambda a, b, c: attend(a, b, c, layout), (query, key, value))
    result = (inputs.astype(jnp.float32) + project(attended, matrices[3])).astype(jnp.bfloat16)
    return (result, (normed, query, key, value, attended))

def backward_block(d_top, inputs, gain, matrices, saved, mapper, layout):
    normed, query, key, value, attended = saved
    grad_out = contract(attended, d_top)
    d_attended = project(d_top, matrices[3].T).astype(jnp.bfloat16)
    d_query, d_key, d_value = mapper(lambda a, b, c, d: attend_back(a, b, c, d, layout), (query, key, value, d_attended))
    grads = (contract(normed, d_query), contract(normed, d_key), contract(normed, d_value), grad_out)
    d_normed = (project(d_query, matrices[0].T) + project(d_key, matrices[1].T) + project(d_value, matrices[2].T)).astype(jnp.bfloat16)
    back_fn = jax.vjp(lambda u: normalize(u, gain), inputs.astype(jnp.float32))[1]
    d_inputs = d_top.astype(jnp.float32) + back_fn(d_normed.astype(jnp.float32))[0]
    return (grads, d_inputs.astype(jnp.bfloat16))

def reference(field, cotangent, gains, weights):
    middle, saved_a = forward_block(field, gains[0], weights[0], rows_map, 'r')
    output, saved_b = forward_block(middle, gains[1], weights[1], cols_map, 'c')
    grads_b, d_middle = backward_block(cotangent, middle, gains[1], weights[1], saved_b, cols_map, 'c')
    grads_a, field_grad = backward_block(d_middle, field, gains[0], weights[0], saved_a, rows_map, 'r')
    weight_grad = jnp.stack(grads_a + grads_b)
    return (output, field_grad, weight_grad)
```

```python
import functools

import jax
import jax.numpy as jnp
from jax import lax
from jax.experimental import pallas as pl
from jax.experimental.pallas import tpu as pltpu
from jax.sharding import PartitionSpec as P

HEADS = 8
eps = 1e-05
F32 = jnp.float32
BF16 = jnp.bfloat16


def log2(n):
    assert n & (n - 1) == 0
    return n.bit_length() - 1


def dot(left, right):
    return jnp.dot(left, right, preferred_element_type=F32)


def dot_nt(left, right):
    return lax.dot_general(left, right, (((1,), (1,)), ((), ())), preferred_element_type=F32)


def dot_tn(left, right):
    return lax.dot_general(left, right, (((0,), (0,)), ((), ())), preferred_element_type=F32)


def digits(index, sizes):
    out = []
    for size in reversed(sizes):
        out.append(index & (size - 1))
        index = index >> log2(size)
    return out[::-1]


def reorder(sizes, order, transposed=False):
    total = 1
    for size in sizes:
        total *= size
    out_axis, in_axis = (1, 0) if transposed else (0, 1)
    index = lax.broadcasted_iota(jnp.int32, (total, total), out_axis)
    found = digits(index, [sizes[axis] for axis in order])
    source = jnp.zeros_like(index)
    for axis, size in enumerate(sizes):
        source = source * size + found[order.index(axis)]
    hit = source == lax.broadcasted_iota(jnp.int32, (total, total), in_axis)
    return jnp.where(hit, 1.0, 0.0).astype(BF16)


def statistics(values):
    average = jnp.mean(values, axis=-1, keepdims=True)
    centred = values - average
    spread = jnp.mean(centred * centred, axis=-1, keepdims=True)
    return centred, lax.rsqrt(spread + eps)


def norm_back(values, gain, d_normed):
    centred, inverse = statistics(values)
    unit = centred * inverse
    scaled = d_normed * gain
    return inverse * (
        scaled
        - jnp.mean(scaled, axis=-1, keepdims=True)
        - unit * jnp.mean(scaled * unit, axis=-1, keepdims=True)
    )


def head_lanes(count, width):
    return lax.broadcasted_iota(jnp.int32, (count, 2 * width), 1) < width


def attention_forward(q_ref, k_ref, v_ref, att_ref, p_ref, groups, count, width, span):
    first = head_lanes(count, width)
    pairs = HEADS // 2

    def step(index, carry):
        group, pair = index // pairs, index % pairs
        rows = pl.ds(pl.multiple_of(group * count, count), count)
        lanes = pl.ds(pl.multiple_of(pair * 2 * width, 2 * width), 2 * width)
        query, key, value = q_ref[rows, lanes], k_ref[rows, lanes], v_ref[rows, lanes]
        total = jnp.zeros((count, 2 * width), F32)
        for half in range(2):
            mine = first if half == 0 else jnp.logical_not(first)
            scores = dot_nt(jnp.where(mine, query, jnp.zeros_like(query)), key)
            scores = scores * (width ** (-0.5))
            if span < count:
                shift = log2(span)
                same = (lax.broadcasted_iota(jnp.int32, (count, count), 0) >> shift) == (
                    lax.broadcasted_iota(jnp.int32, (count, count), 1) >> shift
                )
                scores = jnp.where(same, scores, -jnp.inf)
            expo = jnp.exp(scores - jnp.max(scores, axis=-1, keepdims=True))
            probs = (expo * (1.0 / jnp.sum(expo, axis=-1, keepdims=True))).astype(BF16)
            p_ref[index * 2 + half] = probs
            total += dot(probs, jnp.where(mine, value, jnp.zeros_like(value)))
        att_ref[rows, lanes] = total.astype(BF16)
        return carry

    lax.fori_loop(0, groups * pairs, step, 0)


def attention_back(q_ref, k_ref, v_ref, p_ref, da_ref, dqkv_ref, groups, count, width):
    first = head_lanes(count, width)
    pairs = HEADS // 2
    channels = HEADS * width

    def step(index, carry):
        group, pair = index // pairs, index % pairs
        rows = pl.ds(pl.multiple_of(group * count, count), count)
        lanes = pl.ds(pl.multiple_of(pair * 2 * width, 2 * width), 2 * width)
        query, key, value = q_ref[rows, lanes], k_ref[rows, lanes], v_ref[rows, lanes]
        d_out = da_ref[rows, lanes]
        zero = jnp.zeros_like(query)
        d_query = jnp.zeros((count, 2 * width), F32)
        d_key, d_value = d_query, d_query
        for half in range(2):
            mine = first if half == 0 else jnp.logical_not(first)
            probs = p_ref[index * 2 + half]
            d_mine = jnp.where(mine, d_out, zero)
            d_probs = dot_nt(d_mine, value)
            probs32 = probs.astype(F32)
            weighted = probs32 * d_probs
            total = jnp.sum(weighted, axis=-1, keepdims=True)
            d_scores = ((weighted - probs32 * total) * (width ** (-0.5))).astype(BF16)
            d_query += dot(d_scores, jnp.where(mine, key, zero))
            d_key += dot_tn(d_scores, jnp.where(mine, query, zero))
            d_value += dot_tn(probs, d_mine)
        for part, item in enumerate((d_query, d_key, d_value)):
            at = pl.ds(pl.multiple_of(part * channels + pair * 2 * width, 2 * width), 2 * width)
            dqkv_ref[rows, at] = item.astype(BF16)
        return carry

    lax.fori_loop(0, groups * pairs, step, 0)


def weight_grads(normed, attended, dqkv_ref, d_top, grads_ref, shards):
    channels = normed.shape[-1]
    row_parts, plane, core, piece = shards
    turn = reorder((row_parts, plane, core, piece), (2, 1, 0, 3), transposed=True)
    normed = dot(normed, turn).astype(BF16)
    attended = dot(attended, turn).astype(BF16)
    size = row_parts * piece
    for part in range(4):
        if part < 3:
            whole = dot_tn(normed, dqkv_ref[:, part * channels : (part + 1) * channels])
        else:
            whole = dot_tn(attended, d_top)
        whole = whole.astype(BF16)
        for group in range(plane * core):
            grads_ref[group, part] = whole[group * size : (group + 1) * size]


def input_back(dqkv_ref, w_ref):
    channels = w_ref.shape[-1]
    total = dot_nt(dqkv_ref[:, :channels], w_ref[0, 0])
    total += dot_nt(dqkv_ref[:, channels : 2 * channels], w_ref[0, 1])
    total += dot_nt(dqkv_ref[:, 2 * channels :], w_ref[0, 2])
    return total.astype(BF16).astype(F32)


def project_in(values, gain, w_ref, n_ref, q_ref, k_ref, v_ref):
    centred, inverse = statistics(values)
    normed = (centred * inverse * gain).astype(BF16)
    n_ref[...] = normed
    q_ref[...] = dot(normed, w_ref[0, 0]).astype(BF16)
    k_ref[...] = dot(normed, w_ref[0, 1]).astype(BF16)
    v_ref[...] = dot(normed, w_ref[0, 2]).astype(BF16)


def row_forward(sizes, x_ref, g_ref, w_ref, mid_ref, n_ref, q_ref, k_ref, v_ref, att_ref, p_ref):
    rows, col_parts, row_parts, cols, width = sizes
    channels = x_ref.shape[-1]
    length = col_parts * row_parts * cols
    field = jnp.concatenate([x_ref[:, i].reshape(length, channels) for i in range(rows)], axis=0)
    field = field.astype(F32)
    project_in(field, g_ref[0:1], w_ref, n_ref, q_ref, k_ref, v_ref)
    attention_forward(q_ref, k_ref, v_ref, att_ref, p_ref, rows, length, width, length)
    middle = (field + dot(att_ref[...], w_ref[0, 3])).astype(BF16)
    turn = reorder((rows, col_parts, row_parts, cols), (2, 1, 0, 3))
    mid_ref[...] = dot(turn, middle).astype(BF16)


def row_back(sizes, shards, d_ref, x_ref, g_ref, w_ref, n_ref, q_ref, k_ref, v_ref, att_ref, p_ref,
             fg_ref, grads_ref, da_ref, dqkv_ref):
    rows, col_parts, row_parts, cols, width = sizes
    channels = x_ref.shape[-1]
    length = col_parts * row_parts * cols
    turn = reorder((row_parts, col_parts, rows, cols), (2, 1, 0, 3))
    d_middle = dot(turn, d_ref[...]).astype(BF16)
    da_ref[...] = dot_nt(d_middle, w_ref[0, 3]).astype(BF16)
    attention_back(q_ref, k_ref, v_ref, p_ref, da_ref, dqkv_ref, rows, length, width)
    weight_grads(n_ref[...], att_ref[...], dqkv_ref, d_middle, grads_ref, shards)
    d_normed = input_back(dqkv_ref, w_ref)
    field = jnp.concatenate([x_ref[:, i].reshape(length, channels) for i in range(rows)], axis=0)
    result = d_middle.astype(F32) + norm_back(field.astype(F32), g_ref[0:1], d_normed)
    result = result.astype(BF16)
    for i in range(rows):
        piece = result[i * length : (i + 1) * length]
        fg_ref[:, i] = piece.reshape(col_parts, row_parts * cols, channels)


def column_both(sizes, shards, m_ref, c_ref, g_ref, w_ref, out_ref, dm_ref, grads_ref,
                n_ref, q_ref, k_ref, v_ref, att_ref, p_ref, da_ref, dqkv_ref):
    height, cols, width, together = sizes
    turn = reorder((height, cols), (1, 0))
    turn_back = reorder((height, cols), (1, 0), transposed=True)
    middle = dot(turn, m_ref[...])
    cotangent = dot(turn, c_ref[...]).astype(BF16)
    project_in(middle, g_ref[1:2], w_ref, n_ref, q_ref, k_ref, v_ref)
    count = together * height
    groups = cols // together
    attention_forward(q_ref, k_ref, v_ref, att_ref, p_ref, groups, count, width, height)
    output = (middle + dot(att_ref[...], w_ref[0, 3])).astype(BF16)
    out_ref[...] = dot(turn_back, output).astype(BF16)
    da_ref[...] = dot_nt(cotangent, w_ref[0, 3]).astype(BF16)
    attention_back(q_ref, k_ref, v_ref, p_ref, da_ref, dqkv_ref, groups, count, width)
    weight_grads(n_ref[...], att_ref[...], dqkv_ref, cotangent, grads_ref, shards)
    d_normed = input_back(dqkv_ref, w_ref)
    d_middle = cotangent.astype(F32) + norm_back(middle, g_ref[1:2], d_normed)
    dm_ref[...] = dot(turn_back, d_middle.astype(BF16)).astype(BF16)


def call(kernel, outs, scratch, args, block, flops):
    def whole(shape):
        return pl.BlockSpec(shape, lambda i: (0,) * len(shape))

    specs = []
    for arg in args:
        if arg.ndim == 4 and arg.shape[0] == 2 and arg.shape[1] == 4 and arg.shape[2] == arg.shape[3]:
            specs.append(pl.BlockSpec((1,) + arg.shape[1:], lambda i: (block, 0, 0, 0)))
        else:
            specs.append(whole(arg.shape))
    moved = sum(item.size * item.dtype.itemsize for item in list(args) + list(outs))
    return pl.pallas_call(
        kernel,
        grid=(1,),
        in_specs=specs,
        out_specs=[whole(item.shape) for item in outs],
        out_shape=outs,
        scratch_shapes=scratch,
        compiler_params=pltpu.CompilerParams(
            dimension_semantics=("arbitrary",), vmem_limit_bytes=40 * 1024 * 1024
        ),
        cost_estimate=pl.CostEstimate(flops=flops, bytes_accessed=moved, transcendentals=0),
    )(*args)


def reduce_grads(grads, row_parts, plane, core):
    groups, parts, size, channels = grads.shape
    total = plane * core
    pairs = [[p * core + c for c in range(core)] for p in range(plane)]
    planes = [[p * core + c for p in range(plane)] for c in range(core)]
    got = lax.all_to_all(
        grads.reshape(core, plane, parts, size, channels), "col", 0, 0, axis_index_groups=pairs, tiled=True
    )
    held = jnp.sum(got.astype(F32), axis=0).astype(BF16)
    got = lax.all_to_all(held, "col", 0, 0, axis_index_groups=planes, tiled=True)
    held = jnp.sum(got.astype(F32), axis=0).astype(BF16)
    held = held.reshape(parts, row_parts, size // row_parts, channels).transpose(1, 0, 2, 3)
    got = lax.all_to_all(held, "row", 0, 0, tiled=True)
    return jnp.sum(got.astype(F32), axis=0)


def body(row_parts, col_parts, field, cotangent, gains, weights):
    high, wide, channels = field.shape
    core = 2
    plane = col_parts // core
    rows = high // col_parts
    cols = wide // row_parts
    tokens = high * wide
    height = high * row_parts
    length = wide * col_parts
    width = channels // HEADS
    together = min(cols, max(1, 256 // height))
    devices = row_parts * col_parts
    shards = (row_parts, plane, core, channels // devices)

    def like(*shape, dtype=BF16):
        return jax.ShapeDtypeStruct(shape, dtype)

    flat = like(tokens, channels)
    x = lax.all_to_all(field.reshape(col_parts, rows, wide, channels), "col", 0, 0, tiled=True)
    cot = cotangent.reshape(high, row_parts, cols, channels).transpose(1, 0, 2, 3)
    cot = lax.all_to_all(cot, "row", 0, 0, tiled=True).reshape(tokens, channels)

    sizes = (rows, col_parts, row_parts, cols, width)
    probs = like(rows * HEADS, length, length)
    unit = 2 * tokens * channels * channels
    mid, *saved = call(
        functools.partial(row_forward, sizes),
        [flat, flat, flat, flat, flat, flat, probs], [], (x, gains, weights), 0, 5 * unit,
    )
    mid = lax.all_to_all(
        mid.reshape(devices, rows * cols, channels), ("row", "col"), 0, 0, tiled=True
    ).reshape(tokens, channels)

    count = together * height
    scratch = [pltpu.VMEM((tokens, channels), BF16) for _ in range(5)]
    scratch += [
        pltpu.VMEM((cols // together * HEADS, count, count), BF16),
        pltpu.VMEM((tokens, channels), BF16),
        pltpu.VMEM((tokens, 3 * channels), BF16),
    ]
    packed = like(col_parts, 4, channels // col_parts, channels)
    out, d_mid, grads_b = call(
        functools.partial(column_both, (height, cols, width, together), shards),
        [flat, flat, packed], scratch, (mid, cot, gains, weights), 1, 18 * unit,
    )
    d_mid = lax.all_to_all(
        d_mid.reshape(devices, rows * cols, channels), ("row", "col"), 0, 0, tiled=True
    ).reshape(tokens, channels)
    out = lax.all_to_all(out.reshape(row_parts, high, cols, channels), "row", 0, 0, tiled=True)
    output = out.transpose(1, 0, 2, 3).reshape(high, wide, channels)

    scratch = [pltpu.VMEM((tokens, channels), BF16), pltpu.VMEM((tokens, 3 * channels), BF16)]
    field_grad, grads_a = call(
        functools.partial(row_back, sizes, shards),
        [like(col_parts, rows, wide, channels), packed], scratch,
        (d_mid, x, gains, weights, *saved), 0, 12 * unit,
    )
    field_grad = lax.all_to_all(field_grad, "col", 0, 0, tiled=True).reshape(high, wide, channels)
    weight_grad = jnp.concatenate(
        [reduce_grads(grads_a, row_parts, plane, core), reduce_grads(grads_b, row_parts, plane, core)], axis=0
    )
    return output, field_grad, weight_grad


def solution(mesh):
    return jax.shard_map(
        functools.partial(body, mesh.shape["row"], mesh.shape["col"]),
        mesh=mesh,
        in_specs=(P("row", "col", None), P("row", "col", None), P(), P()),
        out_specs=(P("row", "col", None), P("row", "col", None), P(None, ("row", "col"), None)),
        check_vma=False,
    )
```

```python
import functools
import math

import jax
import jax.numpy as jnp
import numpy as np
from jax import lax
from jax.experimental import pallas as pl
from jax.experimental.pallas import tpu as pltpu
from jax.sharding import PartitionSpec as P

HEADS = 8
eps = 1e-05
F32 = jnp.float32
BF16 = jnp.bfloat16


def log2(n):
    assert n & (n - 1) == 0
    return n.bit_length() - 1


def dot(left, right):
    return jnp.dot(left, right, preferred_element_type=F32)


def dot_nt(left, right):
    return lax.dot_general(left, right, (((1,), (1,)), ((), ())), preferred_element_type=F32)


def dot_tn(left, right):
    return lax.dot_general(left, right, (((0,), (0,)), ((), ())), preferred_element_type=F32)


def one_hot(sizes, order, me=None, lead=0):
    total = math.prod(sizes)
    index = np.arange(total)
    found = {}
    for axis in reversed(order):
        found[axis] = index % sizes[axis]
        index = index // sizes[axis]
    source = 0
    for axis, size in enumerate(sizes):
        digit = found[axis].astype(np.int32)
        if me and axis in me:
            digit = digit ^ me[axis]
        source = source * size + digit
    source = jnp.expand_dims(source, 1 - lead)
    return (source == lax.broadcasted_iota(jnp.int32, (total, total), 1 - lead)).astype(BF16)


def statistics(values):
    average = jnp.mean(values, axis=-1, keepdims=True)
    centred = values - average
    spread = jnp.mean(centred * centred, axis=-1, keepdims=True)
    return centred, lax.rsqrt(spread + eps)


def norm_back(values, gain, d_normed):
    centred, inverse = statistics(values)
    unit = centred * inverse
    scaled = d_normed * gain
    return inverse * (
        scaled
        - jnp.mean(scaled, axis=-1, keepdims=True)
        - unit * jnp.mean(scaled * unit, axis=-1, keepdims=True)
    )


def head_lanes(count, width):
    return lax.broadcasted_iota(jnp.int32, (count, 2 * width), 1) < width


def attention_forward(q_ref, k_ref, v_ref, att_ref, p_ref, groups, count, width, span):
    first = head_lanes(count, width)
    pairs = HEADS // 2

    def step(index, carry):
        group, pair = index // pairs, index % pairs
        rows = pl.ds(pl.multiple_of(group * count, count), count)
        lanes = pl.ds(pl.multiple_of(pair * 2 * width, 2 * width), 2 * width)
        query, key, value = q_ref[rows, lanes], k_ref[rows, lanes], v_ref[rows, lanes]
        total = jnp.zeros((count, 2 * width), F32)
        for half in range(2):
            mine = first if half == 0 else jnp.logical_not(first)
            scores = dot_nt(jnp.where(mine, query, jnp.zeros_like(query)), key)
            scores = scores * (width ** (-0.5))
            if span < count:
                shift = log2(span)
                same = (lax.broadcasted_iota(jnp.int32, (count, count), 0) >> shift) == (
                    lax.broadcasted_iota(jnp.int32, (count, count), 1) >> shift
                )
                scores = jnp.where(same, scores, -jnp.inf)
            expo = jnp.exp(scores - jnp.max(scores, axis=-1, keepdims=True))
            probs = (expo * (1.0 / jnp.sum(expo, axis=-1, keepdims=True))).astype(BF16)
            p_ref[index * 2 + half] = probs
            total += dot(probs, jnp.where(mine, value, jnp.zeros_like(value)))
        att_ref[rows, lanes] = total.astype(BF16)
        return carry

    lax.fori_loop(0, groups * pairs, step, 0)


def attention_back(q_ref, k_ref, v_ref, p_ref, da_ref, dqkv_ref, groups, count, width):
    first = head_lanes(count, width)
    pairs = HEADS // 2
    channels = HEADS * width

    def step(index, carry):
        group, pair = index // pairs, index % pairs
        rows = pl.ds(pl.multiple_of(group * count, count), count)
        lanes = pl.ds(pl.multiple_of(pair * 2 * width, 2 * width), 2 * width)
        query, key, value = q_ref[rows, lanes], k_ref[rows, lanes], v_ref[rows, lanes]
        d_out = da_ref[rows, lanes]
        zero = jnp.zeros_like(query)
        d_query = jnp.zeros((count, 2 * width), F32)
        d_key, d_value = d_query, d_query
        for half in range(2):
            mine = first if half == 0 else jnp.logical_not(first)
            probs = p_ref[index * 2 + half]
            d_mine = jnp.where(mine, d_out, zero)
            d_probs = dot_nt(d_mine, value)
            probs32 = probs.astype(F32)
            weighted = probs32 * d_probs
            total = jnp.sum(weighted, axis=-1, keepdims=True)
            d_scores = ((weighted - probs32 * total) * (width ** (-0.5))).astype(BF16)
            d_query += dot(d_scores, jnp.where(mine, key, zero))
            d_key += dot_tn(d_scores, jnp.where(mine, query, zero))
            d_value += dot_tn(probs, d_mine)
        for part, item in enumerate((d_query, d_key, d_value)):
            at = pl.ds(pl.multiple_of(part * channels + pair * 2 * width, 2 * width), 2 * width)
            dqkv_ref[rows, at] = item.astype(BF16)
        return carry

    lax.fori_loop(0, groups * pairs, step, 0)


def start(source, target, sem):
    copy = pltpu.make_async_copy(source, target, sem)
    copy.start()
    return copy


def start_all(pairs, sems, first=0):
    return [start(source, target, sems.at[first + at]) for at, (source, target) in enumerate(pairs)]


def weight_grads(normed, attended, dqkv_ref, d_top, turn, keep_ref, send_ref):
    channels = normed.shape[-1]
    plane, _, size, _ = keep_ref.shape
    normed = dot(normed, turn).astype(BF16)
    attended = dot(attended, turn).astype(BF16)
    for part in range(4):
        if part < 3:
            whole = dot_tn(normed, dqkv_ref[:, part * channels : (part + 1) * channels])
        else:
            whole = dot_tn(attended, d_top)
        whole = whole.astype(BF16)
        for group in range(plane):
            keep_ref[group, part] = whole[group * size : (group + 1) * size]
            at = plane + group
            send_ref[group, part] = whole[at * size : (at + 1) * size]


def input_back(dqkv_ref, w_ref):
    channels = w_ref.shape[-1]
    total = dot_nt(dqkv_ref[:, :channels], w_ref[0])
    total += dot_nt(dqkv_ref[:, channels : 2 * channels], w_ref[1])
    total += dot_nt(dqkv_ref[:, 2 * channels :], w_ref[2])
    return total.astype(BF16).astype(F32)


def row_forward(sizes, x_ref, g_ref, w_hbm, turn_hbm, mid_ref, n_hbm, q_hbm, k_hbm, v_hbm, att_hbm, p_hbm,
                w_ref, turn_ref, n_ref, q_ref, k_ref, v_ref, att_ref, p_ref, in_sem, out_sem):
    rows, length, width = sizes
    channels = x_ref.shape[-1]
    coming = start_all([(w_hbm.at[0, part], w_ref.at[part]) for part in range(4)], in_sem)
    coming.append(start(turn_hbm, turn_ref, in_sem.at[4]))
    field = jnp.concatenate([x_ref[:, i].reshape(length, channels) for i in range(rows)], axis=0)
    field = field.astype(F32)
    centred, inverse = statistics(field)
    normed = (centred * inverse * g_ref[0:1]).astype(BF16)
    n_ref[...] = normed
    going = [start(n_ref, n_hbm, out_sem.at[0])]
    for part, (ref, hbm) in enumerate(((q_ref, q_hbm), (k_ref, k_hbm), (v_ref, v_hbm))):
        coming[part].wait()
        ref[...] = dot(normed, w_ref[part]).astype(BF16)
        going.append(start(ref, hbm, out_sem.at[1 + part]))
    attention_forward(q_ref, k_ref, v_ref, att_ref, p_ref, rows, length, width, length)
    going.append(start(att_ref, att_hbm, out_sem.at[4]))
    going.append(start(p_ref, p_hbm, out_sem.at[5]))
    coming[3].wait()
    middle = (field + dot(att_ref[...], w_ref[3])).astype(BF16)
    coming[4].wait()
    mid_ref[...] = dot(turn_ref[...], middle).astype(BF16)
    for copy in going:
        copy.wait()


def row_back(sizes, d_ref, x_ref, g_ref, w_hbm, turn_hbm, tg_hbm, n_hbm, q_hbm, k_hbm, v_hbm, att_hbm, p_hbm,
             fg_ref, keep_ref, send_ref,
             w_ref, turn_ref, tg_ref, n_ref, q_ref, k_ref, v_ref, att_ref, p_ref, da_ref, dqkv_ref, in_sem):
    rows, length, width = sizes
    channels = x_ref.shape[-1]
    coming = start_all(
        [(turn_hbm, turn_ref), (w_hbm.at[0, 3], w_ref.at[3]), (p_hbm, p_ref), (v_hbm, v_ref), (k_hbm, k_ref),
         (q_hbm, q_ref), (tg_hbm, tg_ref), (n_hbm, n_ref), (att_hbm, att_ref),
         (w_hbm.at[0, 0:3], w_ref.at[0:3])],
        in_sem,
    )
    coming[0].wait()
    d_middle = dot(turn_ref[...], d_ref[...]).astype(BF16)
    coming[1].wait()
    da_ref[...] = dot_nt(d_middle, w_ref[3]).astype(BF16)
    for copy in coming[2:6]:
        copy.wait()
    attention_back(q_ref, k_ref, v_ref, p_ref, da_ref, dqkv_ref, rows, length, width)
    for copy in coming[6:10]:
        copy.wait()
    weight_grads(n_ref[...], att_ref[...], dqkv_ref, d_middle, tg_ref[...], keep_ref, send_ref)
    d_normed = input_back(dqkv_ref, w_ref)
    field = jnp.concatenate([x_ref[:, i].reshape(length, channels) for i in range(rows)], axis=0)
    result = d_middle.astype(F32) + norm_back(field.astype(F32), g_ref[0:1], d_normed)
    result = result.astype(BF16)
    for i in range(rows):
        piece = result[i * length : (i + 1) * length]
        fg_ref[:, i] = piece.reshape(fg_ref.shape[0], fg_ref.shape[2], channels)


def column_both(sizes, parts, m_ref, *refs):
    height, cols, width, together = sizes
    c_refs, refs = refs[:parts], refs[parts:]
    g_ref, w_hbm, tm_hbm, tc_hbm, to_hbm, td_hbm, tg_hbm = refs[:7]
    out_refs, refs = refs[7 : 7 + parts], refs[7 + parts :]
    dm_ref, keep_ref, send_ref = refs[:3]
    w_ref, t_ref, n_ref, q_ref, k_ref, v_ref, att_ref, p_ref, da_ref, dqkv_ref, in_sem = refs[3:]
    coming = start_all([(tm_hbm, t_ref.at[0])], in_sem)
    coming += start_all([(w_hbm.at[1, part], w_ref.at[part]) for part in range(4)], in_sem, 1)
    coming += start_all(
        [(hbm, t_ref.at[1 + at]) for at, hbm in enumerate((tc_hbm, to_hbm, td_hbm, tg_hbm))], in_sem, 5
    )
    coming[0].wait()
    middle = dot(t_ref[0], m_ref[...])
    centred, inverse = statistics(middle)
    normed = (centred * inverse * g_ref[1:2]).astype(BF16)
    n_ref[...] = normed
    for part, ref in enumerate((q_ref, k_ref, v_ref)):
        coming[1 + part].wait()
        ref[...] = dot(normed, w_ref[part]).astype(BF16)
    count = together * height
    groups = cols // together
    attention_forward(q_ref, k_ref, v_ref, att_ref, p_ref, groups, count, width, height)
    for copy in coming[4:]:
        copy.wait()
    output = (middle + dot(att_ref[...], w_ref[3])).astype(BF16)
    output = dot(t_ref[2], output).astype(BF16)
    size = output.shape[0] // parts
    for part in range(parts):
        out_refs[part][...] = output[part * size : (part + 1) * size]
    cotangent = jnp.concatenate([ref[...] for ref in c_refs], axis=0)
    cotangent = dot(t_ref[1], cotangent).astype(BF16)
    da_ref[...] = dot_nt(cotangent, w_ref[3]).astype(BF16)
    attention_back(q_ref, k_ref, v_ref, p_ref, da_ref, dqkv_ref, groups, count, width)
    weight_grads(n_ref[...], att_ref[...], dqkv_ref, cotangent, t_ref[4], keep_ref, send_ref)
    d_normed = input_back(dqkv_ref, w_ref)
    d_middle = cotangent.astype(F32) + norm_back(middle, g_ref[1:2], d_normed)
    dm_ref[...] = dot(t_ref[3], d_middle.astype(BF16)).astype(BF16)


VMEM = pl.BlockSpec(memory_space=pltpu.VMEM)
HBM = pl.BlockSpec(memory_space=pltpu.HBM)


def call(kernel, ins, outs, scratch, flops):
    moved = sum(item.size * item.dtype.itemsize for item, _ in list(ins) + list(outs))
    return pl.pallas_call(
        kernel,
        in_specs=[spec for _, spec in ins],
        out_specs=[spec for _, spec in outs],
        out_shape=[shape for shape, _ in outs],
        scratch_shapes=scratch,
        compiler_params=pltpu.CompilerParams(vmem_limit_bytes=40 * 1024 * 1024),
        cost_estimate=pl.CostEstimate(flops=flops, bytes_accessed=moved, transcendentals=0),
    )(*[item for item, _ in ins])


def swap(item, axis, count, step):
    return lax.ppermute(item, axis, [(at, at ^ step) for at in range(count)])


def reduce_grads(keep, send, row_parts, plane, core):
    _, parts, size, channels = keep.shape
    got = swap(send, "col", plane * core, 1)
    total = (keep.astype(F32) + got.astype(F32)).astype(BF16)
    held = total[0].astype(F32)
    for step in range(1, plane):
        held = held + swap(total[step], "col", plane * core, step * core).astype(F32)
    held = held.astype(BF16).reshape(parts, row_parts, size // row_parts, channels)
    result = held[:, 0].astype(F32)
    for step in range(1, row_parts):
        result = result + swap(held[:, step], "row", row_parts, step).astype(F32)
    return result


def body(row_parts, col_parts, field, cotangent, gains, weights):
    high, wide, channels = field.shape
    core = 2
    plane = col_parts // core
    rows = high // col_parts
    cols = wide // row_parts
    tokens = high * wide
    height = high * row_parts
    length = wide * col_parts
    width = channels // HEADS
    together = min(cols, max(1, 256 // height))
    devices = row_parts * col_parts
    my_row, my_col = lax.axis_index("row"), lax.axis_index("col")

    def like(*shape):
        return jax.ShapeDtypeStruct(shape, BF16)

    flat = like(tokens, channels)
    square = pltpu.VMEM((channels, channels), BF16)
    plain = pltpu.VMEM((tokens, channels), BF16)
    copies = pltpu.SemaphoreType.DMA
    packed = (like(plane, 4, channels // col_parts, channels), VMEM)
    turn_rows = one_hot((rows, col_parts, row_parts, cols), (2, 1, 0, 3))
    turn_rows_back = one_hot((row_parts, col_parts, rows, cols), (2, 1, 0, 3))
    turn_in = one_hot((height, cols), (1, 0))
    turn_out = one_hot((cols, height), (1, 0))
    turn_cot = one_hot((row_parts, high, cols), (2, 0, 1), {0: my_row})
    turn_output = one_hot((cols, row_parts, high), (1, 2, 0), {1: my_row})
    turn_grads = one_hot(
        (row_parts, plane, core, channels // devices), (2, 1, 0, 3),
        {0: my_row, 1: my_col // core, 2: my_col % core}, lead=1,
    )

    x = lax.all_to_all(field.reshape(col_parts, rows, wide, channels), "col", 0, 0, tiled=True)
    cots = []
    for step in range(row_parts):
        piece = lax.dynamic_slice_in_dim(cotangent, (my_row ^ step) * cols, cols, axis=1)
        piece = piece if step == 0 else swap(piece, "row", row_parts, step)
        cots.append(piece.reshape(high * cols, channels))

    sizes = (rows, length, width)
    probs = like(rows * HEADS, length, length)
    probs_ref = pltpu.VMEM(probs.shape, BF16)
    unit = 2 * tokens * channels * channels
    mid, *saved = call(
        functools.partial(row_forward, sizes),
        [(x, VMEM), (gains, VMEM), (weights, HBM), (turn_rows, HBM)],
        [(flat, VMEM)] + [(flat, HBM)] * 5 + [(probs, HBM)],
        [pltpu.VMEM((4, channels, channels), BF16), plain, plain, plain, plain, plain, plain, probs_ref,
         copies((5,)), copies((6,))],
        5 * unit,
    )
    mid = lax.all_to_all(
        mid.reshape(devices, rows * cols, channels), ("row", "col"), 0, 0, tiled=True
    ).reshape(tokens, channels)

    count = together * height
    results = call(
        functools.partial(column_both, (height, cols, width, together), row_parts),
        [(mid, VMEM)] + [(item, VMEM) for item in cots] + [(gains, VMEM), (weights, HBM)]
        + [(turn, HBM) for turn in (turn_in, turn_cot, turn_output, turn_out, turn_grads)],
        [(like(high * cols, channels), VMEM)] * row_parts + [(flat, VMEM), packed, packed],
        [pltpu.VMEM((4, channels, channels), BF16), pltpu.VMEM((5, tokens, channels), BF16),
         plain, plain, plain, plain, plain, pltpu.VMEM((cols // together * HEADS, count, count), BF16),
         plain, pltpu.VMEM((tokens, 3 * channels), BF16), copies((9,))],
        18 * unit,
    )
    outs, (d_mid, keep_b, send_b) = results[:row_parts], results[row_parts:]
    d_mid = lax.all_to_all(
        d_mid.reshape(devices, rows * cols, channels), ("row", "col"), 0, 0, tiled=True
    ).reshape(tokens, channels)
    output = jnp.zeros((high, wide, channels), BF16)
    for step in range(row_parts):
        piece = outs[step].reshape(high, cols, channels)
        piece = piece if step == 0 else swap(piece, "row", row_parts, step)
        output = lax.dynamic_update_slice_in_dim(output, piece, (my_row ^ step) * cols, axis=1)
    grads_b = reduce_grads(keep_b, send_b, row_parts, plane, core)

    field_grad, keep_a, send_a = call(
        functools.partial(row_back, sizes),
        [(d_mid, VMEM), (x, VMEM), (gains, VMEM), (weights, HBM), (turn_rows_back, HBM), (turn_grads, HBM)]
        + [(item, HBM) for item in saved],
        [(like(col_parts, rows, wide, channels), VMEM), packed, packed],
        [pltpu.VMEM((4, channels, channels), BF16), plain, square, plain, plain, plain, plain, plain, probs_ref,
         plain, pltpu.VMEM((tokens, 3 * channels), BF16), copies((10,))],
        12 * unit,
    )
    field_grad = lax.all_to_all(field_grad, "col", 0, 0, tiled=True).reshape(high, wide, channels)
    grads_a = reduce_grads(keep_a, send_a, row_parts, plane, core)
    return output, field_grad, jnp.concatenate([grads_a, grads_b], axis=0)


def solution(mesh):
    return jax.shard_map(
        functools.partial(body, mesh.shape["row"], mesh.shape["col"]),
        mesh=mesh,
        in_specs=(P("row", "col", None), P("row", "col", None), P(), P()),
        out_specs=(P("row", "col", None), P("row", "col", None), P(None, ("row", "col"), None)),
        check_vma=False,
    )
```

```python
import functools
import math

import jax
import jax.numpy as jnp
import numpy as np
from jax import lax
from jax.experimental import pallas as pl
from jax.experimental.pallas import tpu as pltpu
from jax.sharding import PartitionSpec as P

HEADS = 8
eps = 1e-05
F32 = jnp.float32
BF16 = jnp.bfloat16


def log2(n):
    assert n & (n - 1) == 0
    return n.bit_length() - 1


def dot(left, right):
    return jnp.dot(left, right, preferred_element_type=F32)


def dot_nt(left, right):
    return lax.dot_general(left, right, (((1,), (1,)), ((), ())), preferred_element_type=F32)


def dot_tn(left, right):
    return lax.dot_general(left, right, (((0,), (0,)), ((), ())), preferred_element_type=F32)


def one_hot(sizes, order, me=None, lead=0):
    total = math.prod(sizes)
    index = np.arange(total)
    found = {}
    for axis in reversed(order):
        found[axis] = index % sizes[axis]
        index = index // sizes[axis]
    source = 0
    for axis, size in enumerate(sizes):
        digit = found[axis].astype(np.int32)
        if me and axis in me:
            digit = digit ^ me[axis]
        source = source * size + digit
    source = jnp.expand_dims(source, 1 - lead)
    return (source == lax.broadcasted_iota(jnp.int32, (total, total), 1 - lead)).astype(BF16)


def statistics(values):
    average = jnp.mean(values, axis=-1, keepdims=True)
    centred = values - average
    spread = jnp.mean(centred * centred, axis=-1, keepdims=True)
    return centred, lax.rsqrt(spread + eps)


def norm_back(values, gain, d_normed):
    centred, inverse = statistics(values)
    unit = centred * inverse
    scaled = d_normed * gain
    return inverse * (
        scaled
        - jnp.mean(scaled, axis=-1, keepdims=True)
        - unit * jnp.mean(scaled * unit, axis=-1, keepdims=True)
    )


def head_lanes(count, width):
    return lax.broadcasted_iota(jnp.int32, (count, 2 * width), 1) < width


def attention_forward(q_ref, k_ref, v_ref, att_ref, p_ref, groups, count, width, span):
    first = head_lanes(count, width)
    pairs = HEADS // 2
    scale = width ** (-0.5)

    def step(index, carry):
        group, pair = index // pairs, index % pairs
        rows = pl.ds(pl.multiple_of(group * count, count), count)
        lanes = pl.ds(pl.multiple_of(pair * 2 * width, 2 * width), 2 * width)
        query, key, value = q_ref[rows, lanes] * scale, k_ref[rows, lanes], v_ref[rows, lanes]
        zero = jnp.zeros_like(query)
        total = jnp.zeros((count, 2 * width), F32)
        for half in range(2):
            mine = first if half == 0 else jnp.logical_not(first)
            scores = dot_nt(key, jnp.where(mine, query, zero))
            if span < count:
                shift = log2(span)
                same = (lax.broadcasted_iota(jnp.int32, (count, count), 0) >> shift) == (
                    lax.broadcasted_iota(jnp.int32, (count, count), 1) >> shift
                )
                scores = jnp.where(same, scores, -jnp.inf)
            expo = jnp.exp(scores - jnp.max(scores, axis=0, keepdims=True))
            probs = (expo * (1.0 / jnp.sum(expo, axis=0, keepdims=True))).astype(BF16)
            p_ref[index * 2 + half] = probs
            total += dot_tn(probs, jnp.where(mine, value, zero))
        att_ref[rows, lanes] = total.astype(BF16)
        return carry

    lax.fori_loop(0, groups * pairs, step, 0, unroll=2)


def attention_back(q_ref, k_ref, v_ref, p_ref, da_ref, dqkv_ref, groups, count, width):
    first = head_lanes(count, width)
    pairs = HEADS // 2
    channels = HEADS * width
    scale = width ** (-0.5)

    def step(index, carry):
        group, pair = index // pairs, index % pairs
        rows = pl.ds(pl.multiple_of(group * count, count), count)
        lanes = pl.ds(pl.multiple_of(pair * 2 * width, 2 * width), 2 * width)
        query, key, value = q_ref[rows, lanes] * scale, k_ref[rows, lanes], v_ref[rows, lanes]
        d_out = da_ref[rows, lanes]
        zero = jnp.zeros_like(query)
        d_query = jnp.zeros((count, 2 * width), F32)
        d_key, d_value = d_query, d_query
        for half in range(2):
            mine = first if half == 0 else jnp.logical_not(first)
            probs = p_ref[index * 2 + half]
            d_mine = jnp.where(mine, d_out, zero)
            d_probs = dot_nt(value, d_mine)
            probs32 = probs.astype(F32)
            weighted = probs32 * d_probs
            total = jnp.sum(weighted, axis=0, keepdims=True)
            d_scores = (weighted - probs32 * total).astype(BF16)
            d_query += dot_tn(d_scores, jnp.where(mine, key, zero))
            d_key += dot(d_scores, jnp.where(mine, query, zero))
            d_value += dot(probs, d_mine)
        for part, item in enumerate((d_query * scale, d_key, d_value)):
            at = pl.ds(pl.multiple_of(part * channels + pair * 2 * width, 2 * width), 2 * width)
            dqkv_ref[rows, at] = item.astype(BF16)
        return carry

    lax.fori_loop(0, groups * pairs, step, 0, unroll=2)


def start(source, target, sem):
    copy = pltpu.make_async_copy(source, target, sem)
    copy.start()
    return copy


def start_all(pairs, sems, first=0):
    return [start(source, target, sems.at[first + at]) for at, (source, target) in enumerate(pairs)]


def weight_grads(normed, attended, dqkv_ref, d_top, turn, keep_ref, send_ref):
    channels = normed.shape[-1]
    plane, _, size, _ = keep_ref.shape
    normed = dot(normed, turn).astype(BF16)
    attended = dot(attended, turn).astype(BF16)
    for part in range(4):
        if part < 3:
            whole = dot_tn(normed, dqkv_ref[:, part * channels : (part + 1) * channels])
        else:
            whole = dot_tn(attended, d_top)
        whole = whole.astype(BF16)
        for group in range(plane):
            keep_ref[group, part] = whole[group * size : (group + 1) * size]
            at = plane + group
            send_ref[group, part] = whole[at * size : (at + 1) * size]


def input_back(dqkv_ref, w_ref):
    channels = w_ref.shape[-1]
    total = dot_nt(dqkv_ref[:, :channels], w_ref[0])
    total += dot_nt(dqkv_ref[:, channels : 2 * channels], w_ref[1])
    total += dot_nt(dqkv_ref[:, 2 * channels :], w_ref[2])
    return total.astype(BF16).astype(F32)


def row_forward(sizes, x_ref, g_ref, w_hbm, turn_hbm, mid_ref, n_hbm, q_hbm, k_hbm, v_hbm, att_hbm, p_hbm,
                w_ref, turn_ref, n_ref, q_ref, k_ref, v_ref, att_ref, p_ref, in_sem, out_sem):
    rows, length, width = sizes
    channels = x_ref.shape[-1]
    coming = start_all([(w_hbm.at[0, part], w_ref.at[part]) for part in range(4)], in_sem)
    coming.append(start(turn_hbm, turn_ref, in_sem.at[4]))
    field = jnp.concatenate([x_ref[:, i].reshape(length, channels) for i in range(rows)], axis=0)
    field = field.astype(F32)
    centred, inverse = statistics(field)
    normed = (centred * inverse * g_ref[0:1]).astype(BF16)
    n_ref[...] = normed
    going = [start(n_ref, n_hbm, out_sem.at[0])]
    for part, (ref, hbm) in enumerate(((q_ref, q_hbm), (k_ref, k_hbm), (v_ref, v_hbm))):
        coming[part].wait()
        ref[...] = dot(normed, w_ref[part]).astype(BF16)
        going.append(start(ref, hbm, out_sem.at[1 + part]))
    attention_forward(q_ref, k_ref, v_ref, att_ref, p_ref, rows, length, width, length)
    going.append(start(att_ref, att_hbm, out_sem.at[4]))
    going.append(start(p_ref, p_hbm, out_sem.at[5]))
    coming[3].wait()
    middle = (field + dot(att_ref[...], w_ref[3])).astype(BF16)
    coming[4].wait()
    mid_ref[...] = dot(turn_ref[...], middle).astype(BF16)
    for copy in going:
        copy.wait()


def row_back(sizes, d_ref, w_hbm, turn_hbm, tg_hbm, n_hbm, q_hbm, k_hbm, v_hbm, att_hbm, p_hbm,
             dm_ref, dqkv_ref, keep_ref, send_ref,
             w_ref, turn_ref, tg_ref, n_ref, q_ref, k_ref, v_ref, att_ref, p_ref, da_ref, in_sem):
    rows, length, width = sizes
    coming = start_all(
        [(turn_hbm, turn_ref), (w_hbm.at[0, 3], w_ref), (p_hbm, p_ref), (v_hbm, v_ref), (k_hbm, k_ref),
         (q_hbm, q_ref), (tg_hbm, tg_ref), (n_hbm, n_ref), (att_hbm, att_ref)],
        in_sem,
    )
    coming[0].wait()
    d_middle = dot(turn_ref[...], d_ref[...]).astype(BF16)
    dm_ref[...] = d_middle
    coming[1].wait()
    da_ref[...] = dot_nt(d_middle, w_ref[...]).astype(BF16)
    for copy in coming[2:6]:
        copy.wait()
    attention_back(q_ref, k_ref, v_ref, p_ref, da_ref, dqkv_ref, rows, length, width)
    for copy in coming[6:9]:
        copy.wait()
    weight_grads(n_ref[...], att_ref[...], dqkv_ref, d_middle, tg_ref[...], keep_ref, send_ref)


def field_back(rows, x_ref, dm_ref, dqkv_ref, g_ref, w_hbm, fg_ref, w_ref, in_sem):
    channels = x_ref.shape[-1]
    copy = start(w_hbm.at[0, 0:3], w_ref, in_sem)
    length = dm_ref.shape[0] // rows
    field = jnp.concatenate([x_ref[:, i].reshape(length, channels) for i in range(rows)], axis=0)
    copy.wait()
    d_normed = input_back(dqkv_ref, w_ref)
    result = dm_ref[...].astype(F32) + norm_back(field.astype(F32), g_ref[0:1], d_normed)
    result = result.astype(BF16)
    for i in range(rows):
        piece = result[i * length : (i + 1) * length]
        fg_ref[:, i] = piece.reshape(fg_ref.shape[0], fg_ref.shape[2], channels)


def column_first(parts, *refs):
    c_refs, (w_hbm, tc_hbm, cot_ref, da_ref, w_ref, t_ref, in_sem) = refs[:parts], refs[parts:]
    coming = start_all([(tc_hbm, t_ref), (w_hbm.at[1, 3], w_ref)], in_sem)
    cotangent = jnp.concatenate([ref[...] for ref in c_refs], axis=0)
    coming[0].wait()
    cotangent = dot(t_ref[...], cotangent).astype(BF16)
    cot_ref[...] = cotangent
    coming[1].wait()
    da_ref[...] = dot_nt(cotangent, w_ref[...]).astype(BF16)


def column_main(sizes, m_ref, cot_ref, da_ref, g_ref, w_hbm, tm_hbm, td_hbm,
                dm_ref, mid_ref, n_ref, att_ref, dqkv_ref,
                w_ref, t_ref, q_ref, k_ref, v_ref, p_ref, in_sem):
    height, cols, width, together = sizes
    coming = start_all([(tm_hbm, t_ref.at[0])], in_sem)
    coming += start_all([(w_hbm.at[1, part], w_ref.at[part]) for part in range(3)], in_sem, 1)
    coming += start_all([(td_hbm, t_ref.at[1])], in_sem, 4)
    coming[0].wait()
    middle = dot(t_ref[0], m_ref[...])
    mid_ref[...] = middle.astype(BF16)
    centred, inverse = statistics(middle)
    normed = (centred * inverse * g_ref[1:2]).astype(BF16)
    n_ref[...] = normed
    for part, ref in enumerate((q_ref, k_ref, v_ref)):
        coming[1 + part].wait()
        ref[...] = dot(normed, w_ref[part]).astype(BF16)
    count = together * height
    groups = cols // together
    attention_forward(q_ref, k_ref, v_ref, att_ref, p_ref, groups, count, width, height)
    attention_back(q_ref, k_ref, v_ref, p_ref, da_ref, dqkv_ref, groups, count, width)
    d_normed = input_back(dqkv_ref, w_ref)
    middle = mid_ref[...].astype(F32)
    d_middle = cot_ref[...].astype(F32) + norm_back(middle, g_ref[1:2], d_normed)
    coming[4].wait()
    dm_ref[...] = dot(t_ref[1], d_middle.astype(BF16)).astype(BF16)


def column_last(parts, cot_ref, mid_ref, n_ref, att_ref, dqkv_ref, w_hbm, to_hbm, tg_hbm, *refs):
    out_refs, (keep_ref, send_ref, w_ref, to_ref, tg_ref, in_sem) = refs[:parts], refs[parts:]
    coming = start_all([(tg_hbm, tg_ref), (w_hbm.at[1, 3], w_ref), (to_hbm, to_ref)], in_sem)
    coming[0].wait()
    weight_grads(n_ref[...], att_ref[...], dqkv_ref, cot_ref[...], tg_ref[...], keep_ref, send_ref)
    coming[1].wait()
    output = (mid_ref[...].astype(F32) + dot(att_ref[...], w_ref[...])).astype(BF16)
    coming[2].wait()
    output = dot(to_ref[...], output).astype(BF16)
    size = output.shape[0] // parts
    for part in range(parts):
        out_refs[part][...] = output[part * size : (part + 1) * size]


VMEM = pl.BlockSpec(memory_space=pltpu.VMEM)
HBM = pl.BlockSpec(memory_space=pltpu.HBM)


def call(kernel, ins, outs, scratch, flops):
    moved = sum(item.size * item.dtype.itemsize for item, _ in list(ins) + list(outs))
    return pl.pallas_call(
        kernel,
        in_specs=[spec for _, spec in ins],
        out_specs=[spec for _, spec in outs],
        out_shape=[shape for shape, _ in outs],
        scratch_shapes=scratch,
        compiler_params=pltpu.CompilerParams(vmem_limit_bytes=61 * 1024 * 1024),
        cost_estimate=pl.CostEstimate(flops=flops, bytes_accessed=moved, transcendentals=0),
    )(*[item for item, _ in ins])


def swap(item, axis, count, step):
    return lax.ppermute(item, axis, [(at, at ^ step) for at in range(count)])


def add_pair(keep, send, plane, core):
    got = swap(send, "col", plane * core, 1)
    return (keep.astype(F32) + got.astype(F32)).astype(BF16)


def reduce_grads(total, row_parts, plane, core):
    _, parts, size, channels = total.shape
    held = total[0].astype(F32)
    for step in range(1, plane):
        held = held + swap(total[step], "col", plane * core, step * core).astype(F32)
    held = held.astype(BF16).reshape(parts, row_parts, size // row_parts, channels)
    result = held[:, 0].astype(F32)
    for step in range(1, row_parts):
        result = result + swap(held[:, step], "row", row_parts, step).astype(F32)
    return result


def body(row_parts, col_parts, field, cotangent, gains, weights):
    high, wide, channels = field.shape
    core = 2
    plane = col_parts // core
    rows = high // col_parts
    cols = wide // row_parts
    tokens = high * wide
    height = high * row_parts
    length = wide * col_parts
    width = channels // HEADS
    together = min(cols, max(1, 256 // height))
    devices = row_parts * col_parts
    my_row, my_col = lax.axis_index("row"), lax.axis_index("col")

    def like(*shape):
        return jax.ShapeDtypeStruct(shape, BF16)

    flat = like(tokens, channels)
    square = pltpu.VMEM((channels, channels), BF16)
    plain = pltpu.VMEM((tokens, channels), BF16)
    copies = pltpu.SemaphoreType.DMA
    packed = (like(plane, 4, channels // col_parts, channels), VMEM)
    turn_rows = one_hot((rows, col_parts, row_parts, cols), (2, 1, 0, 3))
    turn_rows_back = one_hot((row_parts, col_parts, rows, cols), (2, 1, 0, 3))
    turn_in = one_hot((height, cols), (1, 0))
    turn_out = one_hot((cols, height), (1, 0))
    turn_cot = one_hot((row_parts, high, cols), (2, 0, 1), {0: my_row})
    turn_output = one_hot((cols, row_parts, high), (1, 2, 0), {1: my_row})
    turn_grads = one_hot(
        (row_parts, plane, core, channels // devices), (2, 1, 0, 3),
        {0: my_row, 1: my_col // core, 2: my_col % core}, lead=1,
    )

    x = lax.all_to_all(field.reshape(col_parts, rows, wide, channels), "col", 0, 0, tiled=True)
    cots = []
    for step in range(row_parts):
        piece = lax.dynamic_slice_in_dim(cotangent, (my_row ^ step) * cols, cols, axis=1)
        piece = piece if step == 0 else swap(piece, "row", row_parts, step)
        cots.append(piece.reshape(high * cols, channels))

    sizes = (rows, length, width)
    probs = like(rows * HEADS, length, length)
    probs_ref = pltpu.VMEM(probs.shape, BF16)
    unit = 2 * tokens * channels * channels
    mid, *saved = call(
        functools.partial(row_forward, sizes),
        [(x, VMEM), (gains, VMEM), (weights, HBM), (turn_rows, HBM)],
        [(flat, VMEM)] + [(flat, HBM)] * 5 + [(probs, HBM)],
        [pltpu.VMEM((4, channels, channels), BF16), plain, plain, plain, plain, plain, plain, probs_ref,
         copies((5,)), copies((6,))],
        5 * unit,
    )
    sent = mid
    mid = lax.all_to_all(
        mid.reshape(devices, rows * cols, channels), ("row", "col"), 0, 0, tiled=True
    ).reshape(tokens, channels)

    cots[0], _ = lax.optimization_barrier((cots[0], sent))
    cot, d_att = call(
        functools.partial(column_first, row_parts),
        [(item, VMEM) for item in cots] + [(weights, HBM), (turn_cot, HBM)],
        [(flat, VMEM), (flat, VMEM)], [square, plain, copies((2,))], 2 * unit,
    )
    count = together * height
    wide_flat = like(tokens, 3 * channels)
    d_mid, mid_kept, normed_b, att_b, dqkv_b = call(
        functools.partial(column_main, (height, cols, width, together)),
        [(mid, VMEM), (cot, VMEM), (d_att, VMEM), (gains, VMEM), (weights, HBM), (turn_in, HBM), (turn_out, HBM)],
        [(flat, VMEM)] * 4 + [(wide_flat, VMEM)],
        [pltpu.VMEM((3, channels, channels), BF16), pltpu.VMEM((2, tokens, channels), BF16),
         plain, plain, plain, pltpu.VMEM((cols // together * HEADS, count, count), BF16), copies((5,))],
        13 * unit,
    )
    d_mid = lax.all_to_all(
        d_mid.reshape(devices, rows * cols, channels), ("row", "col"), 0, 0, tiled=True
    ).reshape(tokens, channels)
    *outs, keep_b, send_b = call(
        functools.partial(column_last, row_parts),
        [(item, VMEM) for item in (cot, mid_kept, normed_b, att_b, dqkv_b)]
        + [(item, HBM) for item in (weights, turn_output, turn_grads)],
        [(like(high * cols, channels), VMEM)] * row_parts + [packed, packed],
        [square, plain, square, copies((3,))], 8 * unit,
    )
    sum_b = add_pair(keep_b, send_b, plane, core)
    d_mid, sum_b = lax.optimization_barrier((d_mid, sum_b))
    output = jnp.zeros((high, wide, channels), BF16)
    for step in range(row_parts):
        piece = outs[step].reshape(high, cols, channels)
        piece = piece if step == 0 else swap(piece, "row", row_parts, step)
        output = lax.dynamic_update_slice_in_dim(output, piece, (my_row ^ step) * cols, axis=1)

    d_mid, dqkv_a, keep_a, send_a = call(
        functools.partial(row_back, sizes),
        [(d_mid, VMEM), (weights, HBM), (turn_rows_back, HBM), (turn_grads, HBM)] + [(item, HBM) for item in saved],
        [(flat, VMEM), (wide_flat, VMEM), packed, packed],
        [square, plain, square, plain, plain, plain, plain, plain, probs_ref, plain, copies((9,))],
        10 * unit,
    )
    field_grad, = call(
        functools.partial(field_back, rows),
        [(x, VMEM), (d_mid, VMEM), (dqkv_a, VMEM), (gains, VMEM), (weights, HBM)],
        [(like(col_parts, rows, wide, channels), VMEM)],
        [pltpu.VMEM((3, channels, channels), BF16), copies], 3 * unit,
    )
    field_grad = lax.all_to_all(field_grad, "col", 0, 0, tiled=True).reshape(high, wide, channels)
    grads_b = reduce_grads(sum_b, row_parts, plane, core)
    grads_a = reduce_grads(add_pair(keep_a, send_a, plane, core), row_parts, plane, core)
    return output, field_grad, jnp.concatenate([grads_a, grads_b], axis=0)


def solution(mesh):
    return jax.shard_map(
        functools.partial(body, mesh.shape["row"], mesh.shape["col"]),
        mesh=mesh,
        in_specs=(P("row", "col", None), P("row", "col", None), P(), P()),
        out_specs=(P("row", "col", None), P("row", "col", None), P(None, ("row", "col"), None)),
        check_vma=False,
    )
```

```python
import functools
import math

import jax
import jax.numpy as jnp
from jax import lax
from jax.experimental import pallas as pl
from jax.experimental.pallas import tpu as pltpu
from jax.sharding import PartitionSpec as P

HEADS = 8
eps = 1e-05
F32 = jnp.float32
BF16 = jnp.bfloat16


def log2(n):
    assert n & (n - 1) == 0
    return n.bit_length() - 1


def dot(left, right):
    return jnp.dot(left, right, preferred_element_type=F32)


def dot_nt(left, right):
    return lax.dot_general(left, right, (((1,), (1,)), ((), ())), preferred_element_type=F32)


def dot_tn(left, right):
    return lax.dot_general(left, right, (((0,), (0,)), ((), ())), preferred_element_type=F32)


def one_hot(sizes, order, me=None, lead=0):
    total = math.prod(sizes)
    index = lax.broadcasted_iota(jnp.int32, (total, total), lead)
    found = {}
    for axis in reversed(order):
        found[axis] = index & (sizes[axis] - 1)
        index = index >> log2(sizes[axis])
    source, shift = None, 0
    for axis in reversed(range(len(sizes))):
        digit = found[axis] << shift
        source = digit if source is None else source | digit
        shift += log2(sizes[axis])
    if me:
        place, shift = 0, 0
        for axis in reversed(range(len(sizes))):
            if axis in me:
                place = place | (me[axis] << shift)
            shift += log2(sizes[axis])
        source = source ^ place
    hit = source == lax.broadcasted_iota(jnp.int32, (total, total), 1 - lead)
    return jnp.where(hit, 1.0, 0.0).astype(BF16)


def statistics(values):
    average = jnp.mean(values, axis=-1, keepdims=True)
    centred = values - average
    spread = jnp.mean(centred * centred, axis=-1, keepdims=True)
    return centred, lax.rsqrt(spread + eps)


def norm_back(values, gain, d_normed):
    centred, inverse = statistics(values)
    unit = centred * inverse
    scaled = d_normed * gain
    return inverse * (
        scaled
        - jnp.mean(scaled, axis=-1, keepdims=True)
        - unit * jnp.mean(scaled * unit, axis=-1, keepdims=True)
    )


def head_lanes(count, width):
    return lax.broadcasted_iota(jnp.int32, (count, 2 * width), 1) < width


def attention_forward(q_ref, k_ref, v_ref, att_ref, p_ref, groups, count, width, span):
    first = head_lanes(count, width)
    pairs = HEADS // 2
    scale = width ** (-0.5)

    def step(index, carry):
        group, pair = index // pairs, index % pairs
        rows = pl.ds(pl.multiple_of(group * count, count), count)
        lanes = pl.ds(pl.multiple_of(pair * 2 * width, 2 * width), 2 * width)
        query, key, value = q_ref[rows, lanes] * scale, k_ref[rows, lanes], v_ref[rows, lanes]
        zero = jnp.zeros_like(query)
        total = jnp.zeros((count, 2 * width), F32)
        for half in range(2):
            mine = first if half == 0 else jnp.logical_not(first)
            scores = dot_nt(key, jnp.where(mine, query, zero))
            if span < count:
                shift = log2(span)
                same = (lax.broadcasted_iota(jnp.int32, (count, count), 0) >> shift) == (
                    lax.broadcasted_iota(jnp.int32, (count, count), 1) >> shift
                )
                scores = jnp.where(same, scores, -jnp.inf)
            expo = jnp.exp(scores - jnp.max(scores, axis=0, keepdims=True))
            probs = (expo * (1.0 / jnp.sum(expo, axis=0, keepdims=True))).astype(BF16)
            p_ref[index * 2 + half] = probs
            total += dot_tn(probs, jnp.where(mine, value, zero))
        att_ref[rows, lanes] = total.astype(BF16)
        return carry

    lax.fori_loop(0, groups * pairs, step, 0, unroll=2)


def attention_back(q_ref, k_ref, v_ref, p_ref, da_ref, dqkv_ref, groups, count, width):
    first = head_lanes(count, width)
    pairs = HEADS // 2
    channels = HEADS * width
    scale = width ** (-0.5)

    def step(index, carry):
        group, pair = index // pairs, index % pairs
        rows = pl.ds(pl.multiple_of(group * count, count), count)
        lanes = pl.ds(pl.multiple_of(pair * 2 * width, 2 * width), 2 * width)
        query, key, value = q_ref[rows, lanes] * scale, k_ref[rows, lanes], v_ref[rows, lanes]
        d_out = da_ref[rows, lanes]
        zero = jnp.zeros_like(query)
        d_query = jnp.zeros((count, 2 * width), F32)
        d_key, d_value = d_query, d_query
        for half in range(2):
            mine = first if half == 0 else jnp.logical_not(first)
            probs = p_ref[index * 2 + half]
            d_mine = jnp.where(mine, d_out, zero)
            d_probs = dot_nt(value, d_mine)
            probs32 = probs.astype(F32)
            weighted = probs32 * d_probs
            total = jnp.sum(weighted, axis=0, keepdims=True)
            d_scores = (weighted - probs32 * total).astype(BF16)
            d_query += dot_tn(d_scores, jnp.where(mine, key, zero))
            d_key += dot(d_scores, jnp.where(mine, query, zero))
            d_value += dot(probs, d_mine)
        for part, item in enumerate((d_query * scale, d_key, d_value)):
            at = pl.ds(pl.multiple_of(part * channels + pair * 2 * width, 2 * width), 2 * width)
            dqkv_ref[rows, at] = item.astype(BF16)
        return carry

    lax.fori_loop(0, groups * pairs, step, 0, unroll=2)


def start(source, target, sem):
    copy = pltpu.make_async_copy(source, target, sem)
    copy.start()
    return copy


def finish(copies):
    for copy in copies:
        copy.wait()


def set_up(turns, w_hbm, w_ref, turn_ref, sem):
    copy = start(w_hbm, w_ref, sem)
    my_row, my_col = lax.axis_index("row"), lax.axis_index("col")
    for at, (sizes, order, me, lead) in enumerate(turns):
        places = {"row": my_row, "plane": my_col >> 1, "core": my_col & 1}
        turn_ref[at] = one_hot(sizes, order, {axis: places[name] for axis, name in me.items()}, lead)
    copy.wait()


def weight_grads(normed, attended, dqkv_ref, d_top, turn, keep_ref, send_ref, send_hbm, sems):
    channels = normed.shape[-1]
    plane, _, size, _ = keep_ref.shape
    normed = dot(normed, turn).astype(BF16)
    attended = dot(attended, turn).astype(BF16)
    going = []
    for part in (3, 0, 1, 2):
        if part < 3:
            whole = dot_tn(normed, dqkv_ref[:, part * channels : (part + 1) * channels])
        else:
            whole = dot_tn(attended, d_top)
        whole = whole.astype(BF16)
        for group in range(plane):
            at = plane + group
            send_ref[group, part] = whole[at * size : (at + 1) * size]
            keep_ref[group, part] = whole[group * size : (group + 1) * size]
        going.append(start(send_ref.at[:, part], send_hbm.at[:, part], sems.at[part]))
    return going


def send_turned(turn_ref, values, stage_ref, targets, sems):
    size = values.shape[0] // len(targets)
    going = []
    for at, target in enumerate(targets):
        piece = pl.ds(at * size, size)
        stage_ref[piece] = dot(turn_ref[piece], values).astype(BF16)
        going.append(start(stage_ref.at[piece], target, sems.at[at]))
    return going


def quarters(ref):
    size = ref.shape[0] // 4
    return [ref.at[pl.ds(at * size, size)] for at in range(4)]


def input_back(dqkv_ref, w_ref):
    channels = w_ref.shape[-1]
    total = dot_nt(dqkv_ref[:, :channels], w_ref[0])
    total += dot_nt(dqkv_ref[:, channels : 2 * channels], w_ref[1])
    total += dot_nt(dqkv_ref[:, 2 * channels :], w_ref[2])
    return total.astype(BF16).astype(F32)


def row_forward(sizes, x_ref, g_ref, w_ref, turn_ref, mid_hbm, n_ref, q_ref, k_ref, v_ref, att_ref, p_ref,
                mid_ref, sems):
    rows, length, width = sizes
    channels = x_ref.shape[-1]
    field = jnp.concatenate([x_ref[:, i].reshape(length, channels) for i in range(rows)], axis=0)
    field = field.astype(F32)
    centred, inverse = statistics(field)
    normed = (centred * inverse * g_ref[0:1]).astype(BF16)
    n_ref[...] = normed
    for part, ref in enumerate((q_ref, k_ref, v_ref)):
        ref[...] = dot(normed, w_ref[0, part]).astype(BF16)
    attention_forward(q_ref, k_ref, v_ref, att_ref, p_ref, rows, length, width, length)
    field = jnp.concatenate([x_ref[:, i].reshape(length, channels) for i in range(rows)], axis=0)
    middle = (field.astype(F32) + dot(att_ref[...], w_ref[0, 3])).astype(BF16)
    finish(send_turned(turn_ref.at[0], middle, mid_ref, quarters(mid_hbm), sems))


def row_back(sizes, d_ref, w_ref, turn_ref, n_ref, q_ref, k_ref, v_ref, att_ref, p_ref,
             dm_ref, dqkv_ref, keep_ref, send_hbm, da_ref, send_ref, sems):
    rows, length, width = sizes
    d_middle = dot(turn_ref[1], d_ref[...]).astype(BF16)
    dm_ref[...] = d_middle
    da_ref[...] = dot_nt(d_middle, w_ref[0, 3]).astype(BF16)
    attention_back(q_ref, k_ref, v_ref, p_ref, da_ref, dqkv_ref, rows, length, width)
    finish(weight_grads(
        n_ref[...], att_ref[...], dqkv_ref, d_middle, turn_ref[6], keep_ref, send_ref, send_hbm, sems
    ))


def field_back(rows, x_ref, dm_ref, dqkv_ref, g_ref, w_ref, fg_hbm, fg_ref, sem):
    channels = x_ref.shape[-1]
    length = dm_ref.shape[0] // rows
    field = jnp.concatenate([x_ref[:, i].reshape(length, channels) for i in range(rows)], axis=0)
    d_normed = input_back(dqkv_ref, w_ref.at[0])
    result = dm_ref[...].astype(F32) + norm_back(field.astype(F32), g_ref[0:1], d_normed)
    result = result.astype(BF16)
    for i in range(rows):
        piece = result[i * length : (i + 1) * length]
        fg_ref[:, i] = piece.reshape(fg_ref.shape[0], fg_ref.shape[2], channels)
    start(fg_ref, fg_hbm, sem).wait()


def column_first(parts, *refs):
    c_refs, (w_ref, turn_ref, cot_ref, da_ref) = refs[:parts], refs[parts:]
    cotangent = jnp.concatenate([ref[...] for ref in c_refs], axis=0)
    cotangent = dot(turn_ref[4], cotangent).astype(BF16)
    cot_ref[...] = cotangent
    da_ref[...] = dot_nt(cotangent, w_ref[1, 3]).astype(BF16)


def column_main(sizes, m_ref, cot_ref, da_ref, g_ref, w_ref, turn_ref,
                dm_hbm, mid_ref, n_ref, att_ref, dqkv_ref, dm_ref, q_ref, k_ref, v_ref, p_ref, sems):
    height, cols, width, together = sizes
    middle = dot(turn_ref[2], m_ref[...])
    mid_ref[...] = middle.astype(BF16)
    centred, inverse = statistics(middle)
    normed = (centred * inverse * g_ref[1:2]).astype(BF16)
    n_ref[...] = normed
    for part, ref in enumerate((q_ref, k_ref, v_ref)):
        ref[...] = dot(normed, w_ref[1, part]).astype(BF16)
    count = together * height
    groups = cols // together
    attention_forward(q_ref, k_ref, v_ref, att_ref, p_ref, groups, count, width, height)
    attention_back(q_ref, k_ref, v_ref, p_ref, da_ref, dqkv_ref, groups, count, width)
    d_normed = input_back(dqkv_ref, w_ref.at[1])
    middle = mid_ref[...].astype(F32)
    d_middle = cot_ref[...].astype(F32) + norm_back(middle, g_ref[1:2], d_normed)
    finish(send_turned(turn_ref.at[3], d_middle.astype(BF16), dm_ref, quarters(dm_hbm), sems))


def column_last(parts, cot_ref, mid_ref, n_ref, att_ref, dqkv_ref, w_ref, turn_ref, *refs):
    out_hbms, (keep_ref, send_hbm, out_ref, send_ref, sems, out_sems) = refs[:parts], refs[parts:]
    going = weight_grads(
        n_ref[...], att_ref[...], dqkv_ref, cot_ref[...], turn_ref[6], keep_ref, send_ref, send_hbm, sems
    )
    output = (mid_ref[...].astype(F32) + dot(att_ref[...], w_ref[1, 3])).astype(BF16)
    going += send_turned(turn_ref.at[5], output, out_ref, out_hbms, out_sems)
    finish(going)


def call(kernel, ins, outs, scratch, micros):
    def spec(far):
        return pl.BlockSpec(memory_space=pltpu.HBM if far else pltpu.VMEM)

    def place(item, far):
        return pltpu.with_memory_space_constraint(item, pltpu.HBM if far else pltpu.VMEM)

    return pl.pallas_call(
        kernel,
        in_specs=[spec(far) for _, far in ins],
        out_specs=[spec(far) for _, far in outs],
        out_shape=[(pltpu.HBM if far else pltpu.VMEM)(shape, BF16) for shape, far in outs],
        scratch_shapes=scratch,
        compiler_params=pltpu.CompilerParams(vmem_limit_bytes=20 * 1024 * 1024),
        cost_estimate=pl.CostEstimate(flops=int(micros * 1.1e9), bytes_accessed=1 << 20, transcendentals=0),
    )(*[place(item, far) for item, far in ins])


def swap(item, axis, count, step):
    return lax.ppermute(item, axis, [(at, at ^ step) for at in range(count)])


def add_pair(keep, send, plane, core):
    got = swap(send, "col", plane * core, 1)
    return (keep.astype(F32) + got.astype(F32)).astype(BF16)


def plane_pieces(total, plane, core):
    return [total[0]] + [swap(total[step], "col", plane * core, step * core) for step in range(1, plane)]


def last_sums(pieces, row_parts):
    parts, size, channels = pieces[0].shape
    held = sum(piece.astype(F32) for piece in pieces).astype(BF16)
    held = held.reshape(parts, row_parts, size // row_parts, channels)
    result = held[:, 0].astype(F32)
    for step in range(1, row_parts):
        result = result + swap(held[:, step], "row", row_parts, step).astype(F32)
    return result


def body(row_parts, col_parts, field, cotangent, gains, weights):
    high, wide, channels = field.shape
    core = 2
    plane = col_parts // core
    rows = high // col_parts
    cols = wide // row_parts
    tokens = high * wide
    height = high * row_parts
    length = wide * col_parts
    width = channels // HEADS
    together = min(cols, max(1, 256 // height))
    devices = row_parts * col_parts
    my_row = lax.axis_index("row")

    flat, triple = ((tokens, channels), False), ((tokens, 3 * channels), False)
    leaving = ((tokens, channels), True)
    packed = (plane, 4, channels // col_parts, channels)
    square = pltpu.VMEM((tokens, channels), BF16)
    copies = pltpu.SemaphoreType.DMA
    assert channels == tokens
    turns = [
        ((rows, col_parts, row_parts, cols), (2, 1, 0, 3), {}, 0),
        ((row_parts, col_parts, rows, cols), (2, 1, 0, 3), {}, 0),
        ((height, cols), (1, 0), {}, 0),
        ((cols, height), (1, 0), {}, 0),
        ((row_parts, high, cols), (2, 0, 1), {0: "row"}, 0),
        ((cols, row_parts, high), (1, 2, 0), {1: "row"}, 0),
        ((row_parts, plane, core, channels // devices), (2, 1, 0, 3), {0: "row", 1: "plane", 2: "core"}, 1),
    ]

    def all_to_all(item):
        item = item.reshape(devices, rows * cols, channels)
        return lax.all_to_all(item, ("row", "col"), 0, 0, tiled=True).reshape(tokens, channels)

    x = lax.all_to_all(field.reshape(col_parts, rows, wide, channels), "col", 0, 0, tiled=True)
    cots = []
    for step in range(row_parts):
        piece = lax.dynamic_slice_in_dim(cotangent, (my_row ^ step) * cols, cols, axis=1)
        piece = piece if step == 0 else swap(piece, "row", row_parts, step)
        cots.append(piece.reshape(high * cols, channels))
    weights, turn = call(
        functools.partial(set_up, turns), [(weights, True)],
        [(weights.shape, False), ((len(turns), tokens, channels), False)], [copies], 5,
    )

    sizes = (rows, length, width)
    probs = ((rows * HEADS, length, length), False)
    mid, *saved = call(
        functools.partial(row_forward, sizes),
        [(x, False), (gains, False), (weights, False), (turn, False)],
        [leaving] + [flat] * 5 + [probs], [square, copies((4,))], 6,
    )
    cots[0], _ = lax.optimization_barrier((cots[0], mid))
    cot, d_att = call(
        functools.partial(column_first, row_parts),
        [(item, False) for item in cots] + [(weights, False), (turn, False)], [flat, flat], [], 2,
    )
    mid = all_to_all(mid)

    count = together * height
    d_mid, *kept = call(
        functools.partial(column_main, (height, cols, width, together)),
        [(item, False) for item in (mid, cot, d_att, gains, weights, turn)],
        [leaving] + [flat] * 3 + [triple],
        [square] * 4 + [pltpu.VMEM((cols // together * HEADS, count, count), BF16), copies((4,))], 14,
    )
    d_mid = all_to_all(d_mid)
    *outs, keep_b, send_b = call(
        functools.partial(column_last, row_parts),
        [(item, False) for item in (cot, *kept, weights, turn)],
        [((high * cols, channels), True)] * row_parts + [(packed, False), (packed, True)],
        [square, pltpu.VMEM(packed, BF16), copies((4,)), copies((row_parts,))], 5,
    )
    sum_b = add_pair(keep_b, send_b, plane, core)
    d_mid, sum_b, outs = lax.optimization_barrier((d_mid, sum_b, outs))
    pieces_b = plane_pieces(sum_b, plane, core)
    pieces_out = [piece if step == 0 else swap(piece, "row", row_parts, step) for step, piece in enumerate(outs)]

    d_mid, dqkv_a, keep_a, send_a = call(
        functools.partial(row_back, sizes),
        [(item, False) for item in (d_mid, weights, turn, *saved)],
        [flat, triple, (packed, False), (packed, True)],
        [square, pltpu.VMEM(packed, BF16), copies((4,))], 10,
    )
    field_grad, = call(
        functools.partial(field_back, rows),
        [(item, False) for item in (x, d_mid, dqkv_a, gains, weights)],
        [((col_parts, rows, wide, channels), True)],
        [pltpu.VMEM((col_parts, rows, wide, channels), BF16), copies], 4,
    )
    keep_a, field_grad = lax.optimization_barrier((keep_a, field_grad))
    sum_a = add_pair(keep_a, send_a, plane, core)
    sum_a, field_grad, pieces_b, pieces_out = lax.optimization_barrier((sum_a, field_grad, pieces_b, pieces_out))
    pieces_a = plane_pieces(sum_a, plane, core)
    field_grad = lax.all_to_all(field_grad, "col", 0, 0, tiled=True).reshape(high, wide, channels)
    grads_b = last_sums(pieces_b, row_parts)
    grads_a = last_sums(pieces_a, row_parts)
    output = jnp.zeros((high, wide, channels), BF16)
    for step, piece in enumerate(pieces_out):
        piece = piece.reshape(high, cols, channels)
        output = lax.dynamic_update_slice_in_dim(output, piece, (my_row ^ step) * cols, axis=1)
    return output, field_grad, jnp.concatenate([grads_a, grads_b], axis=0)


def solution(mesh):
    return jax.shard_map(
        functools.partial(body, mesh.shape["row"], mesh.shape["col"]),
        mesh=mesh,
        in_specs=(P("row", "col", None), P("row", "col", None), P(), P()),
        out_specs=(P("row", "col", None), P("row", "col", None), P(None, ("row", "col"), None)),
        check_vma=False,
    )
```

```python
import functools
import math

import jax
import jax.numpy as jnp
from jax import lax
from jax.experimental import pallas as pl
from jax.experimental.pallas import tpu as pltpu
from jax.sharding import PartitionSpec as P

HEADS = 8
eps = 1e-05
F32 = jnp.float32
BF16 = jnp.bfloat16


def log2(n):
    assert n & (n - 1) == 0
    return n.bit_length() - 1


def dot(left, right):
    return jnp.dot(left, right, preferred_element_type=F32)


def dot_nt(left, right):
    return lax.dot_general(left, right, (((1,), (1,)), ((), ())), preferred_element_type=F32)


def dot_tn(left, right):
    return lax.dot_general(left, right, (((0,), (0,)), ((), ())), preferred_element_type=F32)


def one_hot(sizes, order, me=None, lead=0):
    total = math.prod(sizes)
    index = lax.broadcasted_iota(jnp.int32, (total, total), lead)
    found = {}
    for axis in reversed(order):
        found[axis] = index & (sizes[axis] - 1)
        index = index >> log2(sizes[axis])
    source, shift = None, 0
    for axis in reversed(range(len(sizes))):
        digit = found[axis] << shift
        source = digit if source is None else source | digit
        shift += log2(sizes[axis])
    if me:
        place, shift = 0, 0
        for axis in reversed(range(len(sizes))):
            if axis in me:
                place = place | (me[axis] << shift)
            shift += log2(sizes[axis])
        source = source ^ place
    hit = source == lax.broadcasted_iota(jnp.int32, (total, total), 1 - lead)
    return jnp.where(hit, 1.0, 0.0).astype(BF16)


def statistics(values):
    average = jnp.mean(values, axis=-1, keepdims=True)
    centred = values - average
    spread = jnp.mean(centred * centred, axis=-1, keepdims=True)
    return centred, lax.rsqrt(spread + eps)


def norm_back(values, gain, d_normed):
    centred, inverse = statistics(values)
    unit = centred * inverse
    scaled = d_normed * gain
    return inverse * (
        scaled
        - jnp.mean(scaled, axis=-1, keepdims=True)
        - unit * jnp.mean(scaled * unit, axis=-1, keepdims=True)
    )


def head_lanes(count, width):
    return lax.broadcasted_iota(jnp.int32, (count, 2 * width), 1) < width


def attention_forward(q_ref, k_ref, v_ref, att_ref, p_ref, groups, count, width, span):
    first = head_lanes(count, width)
    pairs = HEADS // 2
    scale = width ** (-0.5)

    def step(index, carry):
        group, pair = index // pairs, index % pairs
        rows = pl.ds(pl.multiple_of(group * count, count), count)
        lanes = pl.ds(pl.multiple_of(pair * 2 * width, 2 * width), 2 * width)
        query, key, value = q_ref[rows, lanes] * scale, k_ref[rows, lanes], v_ref[rows, lanes]
        zero = jnp.zeros_like(query)
        total = jnp.zeros((count, 2 * width), F32)
        for half in range(2):
            mine = first if half == 0 else jnp.logical_not(first)
            scores = dot_nt(key, jnp.where(mine, query, zero))
            if span < count:
                shift = log2(span)
                same = (lax.broadcasted_iota(jnp.int32, (count, count), 0) >> shift) == (
                    lax.broadcasted_iota(jnp.int32, (count, count), 1) >> shift
                )
                scores = jnp.where(same, scores, -jnp.inf)
            expo = jnp.exp(scores - jnp.max(scores, axis=0, keepdims=True))
            probs = (expo * (1.0 / jnp.sum(expo, axis=0, keepdims=True))).astype(BF16)
            p_ref[index * 2 + half] = probs
            total += dot_tn(probs, jnp.where(mine, value, zero))
        att_ref[rows, lanes] = total.astype(BF16)
        return carry

    lax.fori_loop(0, groups * pairs, step, 0, unroll=2)


def attention_back(q_ref, k_ref, v_ref, p_ref, da_ref, dqkv_ref, groups, count, width):
    first = head_lanes(count, width)
    pairs = HEADS // 2
    channels = HEADS * width
    scale = width ** (-0.5)

    def step(index, carry):
        group, pair = index // pairs, index % pairs
        rows = pl.ds(pl.multiple_of(group * count, count), count)
        lanes = pl.ds(pl.multiple_of(pair * 2 * width, 2 * width), 2 * width)
        query, key, value = q_ref[rows, lanes] * scale, k_ref[rows, lanes], v_ref[rows, lanes]
        d_out = da_ref[rows, lanes]
        zero = jnp.zeros_like(query)
        d_query = jnp.zeros((count, 2 * width), F32)
        d_key, d_value = d_query, d_query
        for half in range(2):
            mine = first if half == 0 else jnp.logical_not(first)
            probs = p_ref[index * 2 + half]
            d_mine = jnp.where(mine, d_out, zero)
            d_probs = dot_nt(value, d_mine)
            probs32 = probs.astype(F32)
            weighted = probs32 * d_probs
            total = jnp.sum(weighted, axis=0, keepdims=True)
            d_scores = (weighted - probs32 * total).astype(BF16)
            d_query += dot_tn(d_scores, jnp.where(mine, key, zero))
            d_key += dot(d_scores, jnp.where(mine, query, zero))
            d_value += dot(probs, d_mine)
        for part, item in enumerate((d_query * scale, d_key, d_value)):
            at = pl.ds(pl.multiple_of(part * channels + pair * 2 * width, 2 * width), 2 * width)
            dqkv_ref[rows, at] = item.astype(BF16)
        return carry

    lax.fori_loop(0, groups * pairs, step, 0, unroll=2)


def start(source, target, sem):
    copy = pltpu.make_async_copy(source, target, sem)
    copy.start()
    return copy


def finish(copies):
    for copy in copies:
        copy.wait()


def set_up(turns, turn_hbm, turn_ref, sems):
    my_row, my_col = lax.axis_index("row"), lax.axis_index("col")
    places = {"row": my_row, "plane": my_col >> 1, "core": my_col & 1}
    going = []
    for at, (sizes, order, me, lead) in enumerate(turns):
        turn_ref[at] = one_hot(sizes, order, {axis: places[name] for axis, name in me.items()}, lead)
        going.append(start(turn_ref.at[at], turn_hbm.at[at], sems.at[at]))
    finish(going)


def weight_grad(at, left, right, keep_ref, send_ref, keep_hbm, send_hbm, keep_sem, send_sem):
    plane, _, size, _ = keep_ref.shape
    whole = dot_tn(left, right).astype(BF16)
    for group in range(plane):
        send_ref[group, at] = whole[(plane + group) * size : (plane + group + 1) * size]
        keep_ref[group, at] = whole[group * size : (group + 1) * size]
    return [
        start(send_ref.at[:, at], send_hbm.at[:, at], send_sem),
        start(keep_ref.at[:, at], keep_hbm.at[:, at], keep_sem),
    ]


def third(ref, part):
    channels = ref.shape[-1] // 3
    return ref[:, part * channels : (part + 1) * channels]


def send_turned(turn_ref, values, stage_ref, targets, sems):
    size = values.shape[0] // len(targets)
    going = []
    for at, target in enumerate(targets):
        piece = pl.ds(at * size, size)
        stage_ref[piece] = dot(turn_ref[piece], values).astype(BF16)
        going.append(start(stage_ref.at[piece], target, sems.at[at]))
    return going


def quarters(ref):
    size = ref.shape[0] // 4
    return [ref.at[pl.ds(at * size, size)] for at in range(4)]


def input_back(dqkv_ref, w_refs):
    total = dot_nt(third(dqkv_ref, 0), w_refs[0][...])
    total += dot_nt(third(dqkv_ref, 1), w_refs[1][...])
    total += dot_nt(third(dqkv_ref, 2), w_refs[2][...])
    return total.astype(BF16).astype(F32)


def rows_of(x_ref):
    _, rows, _, channels = x_ref.shape
    length = x_ref.shape[0] * x_ref.shape[2]
    pieces = [x_ref[:, i].reshape(length, channels) for i in range(rows)]
    return jnp.concatenate(pieces, axis=0).astype(F32)


def row_forward(sizes, x_ref, g_ref, w_hbm, turn_hbm, mid_hbm, n_hbm, q_hbm, k_hbm, v_hbm, att_hbm, p_hbm,
                w_ref, turn_ref, mid_ref, n_ref, q_ref, k_ref, v_ref, att_ref, p_ref, in_sems, out_sems, sems):
    rows, length, width = sizes
    coming = [start(w_hbm.at[0, part], w_ref.at[part], in_sems.at[part]) for part in range(4)]
    coming.append(start(turn_hbm.at[0], turn_ref, in_sems.at[4]))
    centred, inverse = statistics(rows_of(x_ref))
    normed = (centred * inverse * g_ref[0:1]).astype(BF16)
    n_ref[...] = normed
    going = [start(n_ref, n_hbm, out_sems.at[0])]
    for part, (ref, hbm) in enumerate(((q_ref, q_hbm), (k_ref, k_hbm), (v_ref, v_hbm))):
        coming[part].wait()
        ref[...] = dot(normed, w_ref[part]).astype(BF16)
        going.append(start(ref, hbm, out_sems.at[1 + part]))
    attention_forward(q_ref, k_ref, v_ref, att_ref, p_ref, rows, length, width, length)
    going.append(start(p_ref, p_hbm, out_sems.at[5]))
    going.append(start(att_ref, att_hbm, out_sems.at[4]))
    coming[3].wait()
    middle = (rows_of(x_ref) + dot(att_ref[...], w_ref[3])).astype(BF16)
    coming[4].wait()
    finish(going + send_turned(turn_ref, middle, mid_ref, quarters(mid_hbm), sems))


def row_back_first(d_ref, w_hbm, turn_hbm, att_hbm, dm_ref, da_ref, keep_hbm, send_hbm,
                   w_ref, turn_ref, att_ref, keep_ref, send_ref, sems):
    coming = [
        start(turn_hbm.at[1], turn_ref.at[0], sems.at[0]),
        start(att_hbm, att_ref, sems.at[1]),
        start(turn_hbm.at[6], turn_ref.at[1], sems.at[2]),
        start(w_hbm.at[0, 3], w_ref, sems.at[3]),
    ]
    coming[0].wait()
    d_middle = dot(turn_ref[0], d_ref[...]).astype(BF16)
    dm_ref[...] = d_middle
    finish(coming[1:3])
    attended = dot(att_ref[...], turn_ref[1]).astype(BF16)
    going = weight_grad(
        0, attended, d_middle, keep_ref, send_ref, keep_hbm, send_hbm, sems.at[4], sems.at[5]
    )
    coming[3].wait()
    da_ref[...] = dot_nt(d_middle, w_ref[...]).astype(BF16)
    finish(going)


def row_back(sizes, da_ref, turn_hbm, n_hbm, q_hbm, k_hbm, v_hbm, p_hbm, dqkv_hbm, keep_hbm, send_hbm,
             turn_ref, n_ref, q_ref, k_ref, v_ref, p_ref, dqkv_ref, keep_ref, send_ref, sems):
    rows, length, width = sizes
    half = p_ref.shape[0] // 2
    coming = [
        start(v_hbm, v_ref, sems.at[0]), start(k_hbm, k_ref, sems.at[1]), start(q_hbm, q_ref, sems.at[2]),
        start(p_hbm.at[pl.ds(0, half)], p_ref.at[pl.ds(0, half)], sems.at[3]),
        start(p_hbm.at[pl.ds(half, half)], p_ref.at[pl.ds(half, half)], sems.at[4]),
        start(turn_hbm.at[6], turn_ref, sems.at[5]), start(n_hbm, n_ref, sems.at[6]),
    ]
    finish(coming[:5])
    attention_back(q_ref, k_ref, v_ref, p_ref, da_ref, dqkv_ref, rows, length, width)
    going = [start(dqkv_ref, dqkv_hbm, sems.at[7])]
    finish(coming[5:])
    normed = dot(n_ref[...], turn_ref[...]).astype(BF16)
    for part in range(3):
        going += weight_grad(
            part, normed, third(dqkv_ref, part), keep_ref, send_ref, keep_hbm, send_hbm,
            sems.at[8 + part], sems.at[11 + part],
        )
    finish(going)


def field_back(x_ref, dm_ref, g_ref, dqkv_hbm, w_hbm, fg_hbm, dqkv_ref, w_ref, fg_ref, sems):
    coming = [start(dqkv_hbm, dqkv_ref, sems.at[0]), start(w_hbm.at[0, 0:3], w_ref, sems.at[1])]
    _, rows, _, channels = x_ref.shape
    length = x_ref.shape[0] * x_ref.shape[2]
    finish(coming)
    d_normed = input_back(dqkv_ref, [w_ref.at[part] for part in range(3)])
    result = dm_ref[...].astype(F32) + norm_back(rows_of(x_ref), g_ref[0:1], d_normed)
    result = result.astype(BF16)
    for i in range(rows):
        piece = result[i * length : (i + 1) * length]
        fg_ref[:, i] = piece.reshape(fg_ref.shape[0], fg_ref.shape[2], channels)
    start(fg_ref, fg_hbm, sems.at[2]).wait()


def column_first(parts, *refs):
    c_refs, (w_hbm, turn_hbm, cot_ref, da_ref, early_ref, w_ref, turn_ref, sems) = refs[:parts], refs[parts:]
    coming = [
        start(turn_hbm.at[4], turn_ref, sems.at[0]), start(w_hbm.at[1, 3], w_ref, sems.at[1]),
        start(turn_hbm.at[2], early_ref.at[0], sems.at[2]), start(w_hbm.at[1, 0], early_ref.at[1], sems.at[3]),
    ]
    cotangent = jnp.concatenate([ref[...] for ref in c_refs], axis=0)
    coming[0].wait()
    cotangent = dot(turn_ref[...], cotangent).astype(BF16)
    cot_ref[...] = cotangent
    coming[1].wait()
    da_ref[...] = dot_nt(cotangent, w_ref[...]).astype(BF16)
    finish(coming[2:])


def column_main(sizes, m_ref, cot_ref, da_ref, early_ref, g_ref, w_hbm, turn_hbm,
                dm_hbm, mid_hbm, n_hbm, att_hbm, dqkv_hbm,
                w_ref, turn_ref, dm_ref, mid_ref, n_ref, att_ref, dqkv_ref, q_ref, k_ref, v_ref, p_ref, sems):
    height, cols, width, together = sizes
    coming = [
        start(w_hbm.at[1, 1], w_ref.at[0], sems.at[0]), start(w_hbm.at[1, 2], w_ref.at[1], sems.at[1]),
        start(turn_hbm.at[3], turn_ref, sems.at[2]),
    ]
    middle = dot(early_ref[0], m_ref[...])
    mid_ref[...] = middle.astype(BF16)
    going = [start(mid_ref, mid_hbm, sems.at[3])]
    centred, inverse = statistics(middle)
    normed = (centred * inverse * g_ref[1:2]).astype(BF16)
    n_ref[...] = normed
    going.append(start(n_ref, n_hbm, sems.at[4]))
    q_ref[...] = dot(normed, early_ref[1]).astype(BF16)
    coming[0].wait()
    k_ref[...] = dot(normed, w_ref[0]).astype(BF16)
    coming[1].wait()
    v_ref[...] = dot(normed, w_ref[1]).astype(BF16)
    count = together * height
    groups = cols // together
    attention_forward(q_ref, k_ref, v_ref, att_ref, p_ref, groups, count, width, height)
    going.append(start(att_ref, att_hbm, sems.at[5]))
    attention_back(q_ref, k_ref, v_ref, p_ref, da_ref, dqkv_ref, groups, count, width)
    going.append(start(dqkv_ref, dqkv_hbm, sems.at[6]))
    d_normed = input_back(dqkv_ref, [early_ref.at[1], w_ref.at[0], w_ref.at[1]])
    middle = mid_ref[...].astype(F32)
    d_middle = cot_ref[...].astype(F32) + norm_back(middle, g_ref[1:2], d_normed)
    coming[2].wait()
    finish(going + send_turned(turn_ref, d_middle.astype(BF16), dm_ref, quarters(dm_hbm), sems.at[pl.ds(7, 4)]))


def column_last(parts, cot_hbm, mid_hbm, n_hbm, att_hbm, dqkv_hbm, w_hbm, turn_hbm, *refs):
    out_hbms, refs = refs[:parts], refs[parts:]
    keep_hbm, send_hbm, out_ref, keep_ref, send_ref, w_ref, turn_ref, flat_ref, dqkv_ref, sems = refs
    coming = [
        start(turn_hbm.at[6], turn_ref.at[0], sems.at[0]), start(n_hbm, flat_ref.at[0], sems.at[1]),
        start(dqkv_hbm, dqkv_ref, sems.at[2]), start(att_hbm, flat_ref.at[1], sems.at[3]),
        start(cot_hbm, flat_ref.at[2], sems.at[4]), start(mid_hbm, flat_ref.at[3], sems.at[5]),
        start(w_hbm.at[1, 3], w_ref, sems.at[6]), start(turn_hbm.at[5], turn_ref.at[1], sems.at[7]),
    ]
    finish(coming[:3])
    going = []
    normed = dot(flat_ref[0], turn_ref[0]).astype(BF16)
    for part in range(3):
        going += weight_grad(
            part, normed, third(dqkv_ref, part), keep_ref, send_ref, keep_hbm, send_hbm,
            sems.at[8 + part], sems.at[12 + part],
        )
    finish(coming[3:])
    attended = dot(flat_ref[1], turn_ref[0]).astype(BF16)
    going += weight_grad(
        3, attended, flat_ref[2], keep_ref, send_ref, keep_hbm, send_hbm, sems.at[11], sems.at[15]
    )
    output = (flat_ref[3].astype(F32) + dot(flat_ref[1], w_ref[...])).astype(BF16)
    finish(going + send_turned(turn_ref.at[1], output, out_ref, out_hbms, sems.at[pl.ds(16, parts)]))


NEAR, FAR, ANY = pltpu.VMEM, pltpu.HBM, None


def call(kernel, ins, outs, scratch):
    def spec(where):
        return pl.BlockSpec(memory_space=pltpu.HBM if where is FAR else pltpu.VMEM)

    def place(item, where):
        return item if where is ANY else pltpu.with_memory_space_constraint(item, where)

    return pl.pallas_call(
        kernel,
        in_specs=[spec(where) for _, where in ins],
        out_specs=[spec(where) for _, where in outs],
        out_shape=[jax.ShapeDtypeStruct(shape, BF16) if where is ANY else where(shape, BF16) for shape, where in outs],
        scratch_shapes=scratch,
        compiler_params=pltpu.CompilerParams(vmem_limit_bytes=48 * 1024 * 1024),
        cost_estimate=pl.CostEstimate(flops=1 << 20, bytes_accessed=1 << 10, transcendentals=0),
    )(*[place(item, where) for item, where in ins])


def swap(item, axis, count, step):
    return lax.ppermute(item, axis, [(at, at ^ step) for at in range(count)])


def add_pair(keep, send, plane, core):
    got = swap(send, "col", plane * core, 1)
    return (keep.astype(F32) + got.astype(F32)).astype(BF16)


def plane_pieces(total, plane, core):
    return [total[0]] + [swap(total[step], "col", plane * core, step * core) for step in range(1, plane)]


def last_sums(pieces, row_parts):
    parts, size, channels = pieces[0].shape
    held = sum(piece.astype(F32) for piece in pieces).astype(BF16)
    held = held.reshape(parts, row_parts, size // row_parts, channels)
    result = held[:, 0].astype(F32)
    for step in range(1, row_parts):
        result = result + swap(held[:, step], "row", row_parts, step).astype(F32)
    return result


def body(row_parts, col_parts, field, cotangent, gains, weights):
    high, wide, channels = field.shape
    core = 2
    plane = col_parts // core
    rows = high // col_parts
    cols = wide // row_parts
    tokens = high * wide
    height = high * row_parts
    length = wide * col_parts
    width = channels // HEADS
    together = min(cols, max(1, 256 // height))
    devices = row_parts * col_parts
    my_row = lax.axis_index("row")

    flat, triple = (tokens, channels), (tokens, 3 * channels)
    probs = (rows * HEADS, length, length)
    size = channels // col_parts

    def packed(parts):
        return (plane, parts, size, channels)

    def scratch(*shape):
        return pltpu.VMEM(shape, BF16)

    def at(where, *items):
        return [(item, where) for item in items]

    square = scratch(*flat)
    copies = pltpu.SemaphoreType.DMA
    assert channels == tokens
    turns = [
        ((rows, col_parts, row_parts, cols), (2, 1, 0, 3), {}, 0),
        ((row_parts, col_parts, rows, cols), (2, 1, 0, 3), {}, 0),
        ((height, cols), (1, 0), {}, 0),
        ((cols, height), (1, 0), {}, 0),
        ((row_parts, high, cols), (2, 0, 1), {0: "row"}, 0),
        ((cols, row_parts, high), (1, 2, 0), {1: "row"}, 0),
        ((row_parts, plane, core, channels // devices), (2, 1, 0, 3), {0: "row", 1: "plane", 2: "core"}, 1),
    ]

    def all_to_all(item):
        item = item.reshape(devices, rows * cols, channels)
        return lax.all_to_all(item, ("row", "col"), 0, 0, tiled=True).reshape(tokens, channels)

    x = lax.all_to_all(field.reshape(col_parts, rows, wide, channels), "col", 0, 0, tiled=True)
    cots = []
    for step in range(row_parts):
        piece = lax.dynamic_slice_in_dim(cotangent, (my_row ^ step) * cols, cols, axis=1)
        piece = piece if step == 0 else swap(piece, "row", row_parts, step)
        cots.append(piece.reshape(high * cols, channels))
    turn, = call(
        functools.partial(set_up, turns), [], at(FAR, (len(turns), *flat)),
        [scratch(len(turns), *flat), copies((len(turns),))],
    )

    sizes = (rows, length, width)
    mid, normed, query, key, value, attended, prob = call(
        functools.partial(row_forward, sizes),
        at(ANY, x, gains) + at(FAR, weights, turn), at(FAR, *[flat] * 6, probs),
        [scratch(4, *flat)] + [square] * 7 + [scratch(*probs), copies((5,)), copies((6,)), copies((4,))],
    )
    cots[0], _ = lax.optimization_barrier((cots[0], mid))
    cot, d_att, early = call(
        functools.partial(column_first, row_parts),
        at(ANY, *cots) + at(FAR, weights, turn), at(NEAR, flat, flat, (2, *flat)), [square, square, copies((4,))],
    )
    mid = all_to_all(mid)

    count = together * height
    d_mid, *kept = call(
        functools.partial(column_main, (height, cols, width, together)),
        at(ANY, mid) + at(NEAR, cot, d_att, early) + at(ANY, gains) + at(FAR, weights, turn),
        at(FAR, flat, flat, flat, flat, triple),
        [scratch(2, *flat)] + [square] * 5 + [scratch(*triple)] + [square] * 3
        + [scratch(cols // together * HEADS, count, count), copies((11,))],
    )
    d_mid = all_to_all(d_mid)
    *outs, keep_b, send_b = call(
        functools.partial(column_last, row_parts),
        at(FAR, cot, *kept, weights, turn), at(FAR, *[(high * cols, channels)] * row_parts, packed(4), packed(4)),
        [square, scratch(*packed(4)), scratch(*packed(4)), square, scratch(2, *flat), scratch(4, *flat),
         scratch(*triple), copies((16 + row_parts,))],
    )
    d_mid, outs, keep_b, send_b = lax.optimization_barrier((d_mid, outs, keep_b, send_b))
    sum_b = add_pair(keep_b, send_b, plane, core)
    d_mid, d_att, keep_o, send_o = call(
        row_back_first,
        at(ANY, d_mid) + at(FAR, weights, turn, attended), at(ANY, flat, flat) + at(FAR, packed(1), packed(1)),
        [square, scratch(2, *flat), square, scratch(*packed(1)), scratch(*packed(1)), copies((6,))],
    )
    sum_o = add_pair(keep_o, send_o, plane, core)
    d_att, sum_b, sum_o, outs = lax.optimization_barrier((d_att, sum_b, sum_o, outs))
    pieces_b = plane_pieces(jnp.concatenate([sum_o, sum_b], axis=1), plane, core)
    pieces_out = [piece if step == 0 else swap(piece, "row", row_parts, step) for step, piece in enumerate(outs)]

    dqkv, keep_a, send_a = call(
        functools.partial(row_back, sizes),
        at(ANY, d_att) + at(FAR, turn, normed, query, key, value, prob), at(FAR, triple, packed(3), packed(3)),
        [square] * 5 + [scratch(*probs), scratch(*triple), scratch(*packed(3)), scratch(*packed(3)), copies((14,))],
    )
    field_grad, = call(
        field_back, at(ANY, x, d_mid, gains) + at(FAR, dqkv, weights), at(FAR, x.shape),
        [scratch(*triple), scratch(3, *flat), scratch(*x.shape), copies((3,))],
    )
    keep_a, field_grad, pieces_b, pieces_out = lax.optimization_barrier((keep_a, field_grad, pieces_b, pieces_out))
    sum_a = add_pair(keep_a, send_a, plane, core)
    pieces_a = plane_pieces(sum_a, plane, core)
    field_grad = lax.all_to_all(field_grad, "col", 0, 0, tiled=True).reshape(high, wide, channels)
    grads_b = last_sums(pieces_b, row_parts)
    grads_a = last_sums(pieces_a, row_parts)
    output = jnp.zeros((high, wide, channels), BF16)
    for step, piece in enumerate(pieces_out):
        piece = piece.reshape(high, cols, channels)
        output = lax.dynamic_update_slice_in_dim(output, piece, (my_row ^ step) * cols, axis=1)
    return output, field_grad, jnp.concatenate([grads_a, grads_b], axis=0)


def solution(mesh):
    return jax.shard_map(
        functools.partial(body, mesh.shape["row"], mesh.shape["col"]),
        mesh=mesh,
        in_specs=(P("row", "col", None), P("row", "col", None), P(), P()),
        out_specs=(P("row", "col", None), P("row", "col", None), P(None, ("row", "col"), None)),
        check_vma=False,
    )
```

```python
import functools
import math

import jax
import jax.numpy as jnp
from jax import lax
from jax.experimental import pallas as pl
from jax.experimental.pallas import tpu as pltpu
from jax.sharding import PartitionSpec as P

HEADS = 8
eps = 1e-05
F32 = jnp.float32
BF16 = jnp.bfloat16


def log2(n):
    assert n & (n - 1) == 0
    return n.bit_length() - 1


def dot(left, right):
    return jnp.dot(left, right, preferred_element_type=F32)


def dot_nt(left, right):
    return lax.dot_general(left, right, (((1,), (1,)), ((), ())), preferred_element_type=F32)


def dot_tn(left, right):
    return lax.dot_general(left, right, (((0,), (0,)), ((), ())), preferred_element_type=F32)


def one_hot(sizes, order, me=None, lead=0):
    total = math.prod(sizes)
    index = lax.broadcasted_iota(jnp.int32, (total, total), lead)
    found = {}
    for axis in reversed(order):
        found[axis] = index & (sizes[axis] - 1)
        index = index >> log2(sizes[axis])
    source, shift = None, 0
    for axis in reversed(range(len(sizes))):
        digit = found[axis] << shift
        source = digit if source is None else source | digit
        shift += log2(sizes[axis])
    if me:
        place, shift = 0, 0
        for axis in reversed(range(len(sizes))):
            if axis in me:
                place = place | (me[axis] << shift)
            shift += log2(sizes[axis])
        source = source ^ place
    hit = source == lax.broadcasted_iota(jnp.int32, (total, total), 1 - lead)
    return jnp.where(hit, 1.0, 0.0).astype(BF16)


def statistics(values):
    average = jnp.mean(values, axis=-1, keepdims=True)
    centred = values - average
    spread = jnp.mean(centred * centred, axis=-1, keepdims=True)
    return centred, lax.rsqrt(spread + eps)


def norm_back(values, gain, d_normed):
    centred, inverse = statistics(values)
    unit = centred * inverse
    scaled = d_normed * gain
    return inverse * (
        scaled
        - jnp.mean(scaled, axis=-1, keepdims=True)
        - unit * jnp.mean(scaled * unit, axis=-1, keepdims=True)
    )


def head_lanes(count, width):
    return lax.broadcasted_iota(jnp.int32, (count, 2 * width), 1) < width


def attention_forward(q_ref, k_ref, v_ref, att_ref, p_ref, groups, count, width, span):
    first = head_lanes(count, width)
    pairs = HEADS // 2
    scale = width ** (-0.5)

    def step(index, carry):
        group, pair = index // pairs, index % pairs
        rows = pl.ds(pl.multiple_of(group * count, count), count)
        lanes = pl.ds(pl.multiple_of(pair * 2 * width, 2 * width), 2 * width)
        query, key, value = q_ref[rows, lanes] * scale, k_ref[rows, lanes], v_ref[rows, lanes]
        zero = jnp.zeros_like(query)
        total = jnp.zeros((count, 2 * width), F32)
        for half in range(2):
            mine = first if half == 0 else jnp.logical_not(first)
            scores = dot_nt(key, jnp.where(mine, query, zero))
            if span < count:
                shift = log2(span)
                same = (lax.broadcasted_iota(jnp.int32, (count, count), 0) >> shift) == (
                    lax.broadcasted_iota(jnp.int32, (count, count), 1) >> shift
                )
                scores = jnp.where(same, scores, -jnp.inf)
            expo = jnp.exp(scores - jnp.max(scores, axis=0, keepdims=True))
            probs = (expo * (1.0 / jnp.sum(expo, axis=0, keepdims=True))).astype(BF16)
            p_ref[index * 2 + half] = probs
            total += dot_tn(probs, jnp.where(mine, value, zero))
        att_ref[rows, lanes] = total.astype(BF16)
        return carry

    lax.fori_loop(0, groups * pairs, step, 0, unroll=2)


def attention_back(q_ref, k_ref, v_ref, p_ref, da_ref, dqkv_ref, groups, count, width):
    first = head_lanes(count, width)
    pairs = HEADS // 2
    channels = HEADS * width
    scale = width ** (-0.5)

    def step(index, carry):
        group, pair = index // pairs, index % pairs
        rows = pl.ds(pl.multiple_of(group * count, count), count)
        lanes = pl.ds(pl.multiple_of(pair * 2 * width, 2 * width), 2 * width)
        query, key, value = q_ref[rows, lanes] * scale, k_ref[rows, lanes], v_ref[rows, lanes]
        d_out = da_ref[rows, lanes]
        zero = jnp.zeros_like(query)
        d_query = jnp.zeros((count, 2 * width), F32)
        d_key, d_value = d_query, d_query
        for half in range(2):
            mine = first if half == 0 else jnp.logical_not(first)
            probs = p_ref[index * 2 + half]
            d_mine = jnp.where(mine, d_out, zero)
            d_probs = dot_nt(value, d_mine)
            probs32 = probs.astype(F32)
            weighted = probs32 * d_probs
            total = jnp.sum(weighted, axis=0, keepdims=True)
            d_scores = (weighted - probs32 * total).astype(BF16)
            d_query += dot_tn(d_scores, jnp.where(mine, key, zero))
            d_key += dot(d_scores, jnp.where(mine, query, zero))
            d_value += dot(probs, d_mine)
        for part, item in enumerate((d_query * scale, d_key, d_value)):
            at = pl.ds(pl.multiple_of(part * channels + pair * 2 * width, 2 * width), 2 * width)
            dqkv_ref[rows, at] = item.astype(BF16)
        return carry

    lax.fori_loop(0, groups * pairs, step, 0, unroll=2)


def start(source, target, sem):
    copy = pltpu.make_async_copy(source, target, sem)
    copy.start()
    return copy


def finish(copies):
    for copy in copies:
        copy.wait()


def set_up(turns, turn_hbm, turn_ref, sems):
    my_row, my_col = lax.axis_index("row"), lax.axis_index("col")
    places = {"row": my_row, "plane": my_col >> 1, "core": my_col & 1}
    going = []
    for at, (sizes, order, me, lead) in enumerate(turns):
        turn_ref[at] = one_hot(sizes, order, {axis: places[name] for axis, name in me.items()}, lead)
        going.append(start(turn_ref.at[at], turn_hbm.at[at], sems.at[at]))
    finish(going)


def weight_grad(at, left, right, keep_ref, send_ref, keep_hbm, send_hbm, keep_sem, send_sem):
    plane, _, size, _ = keep_ref.shape
    whole = dot_tn(left, right).astype(BF16)
    for group in range(plane):
        send_ref[group, at] = whole[(plane + group) * size : (plane + group + 1) * size]
        keep_ref[group, at] = whole[group * size : (group + 1) * size]
    return [
        start(send_ref.at[:, at], send_hbm.at[:, at], send_sem),
        start(keep_ref.at[:, at], keep_hbm.at[:, at], keep_sem),
    ]


def third(ref, part):
    channels = ref.shape[-1] // 3
    return ref[:, part * channels : (part + 1) * channels]


def send_turned(turn_ref, values, stage_ref, targets, sems):
    size = values.shape[0] // len(targets)
    going = []
    for at, target in enumerate(targets):
        piece = pl.ds(at * size, size)
        stage_ref[piece] = dot(turn_ref[piece], values).astype(BF16)
        going.append(start(stage_ref.at[piece], target, sems.at[at]))
    return going


def quarters(ref):
    size = ref.shape[0] // 4
    return [ref.at[pl.ds(at * size, size)] for at in range(4)]


def input_back(dqkv_ref, w_refs):
    total = dot_nt(third(dqkv_ref, 0), w_refs[0][...])
    total += dot_nt(third(dqkv_ref, 1), w_refs[1][...])
    total += dot_nt(third(dqkv_ref, 2), w_refs[2][...])
    return total.astype(BF16).astype(F32)


def rows_of(x_ref):
    _, rows, _, channels = x_ref.shape
    length = x_ref.shape[0] * x_ref.shape[2]
    pieces = [x_ref[:, i].reshape(length, channels) for i in range(rows)]
    return jnp.concatenate(pieces, axis=0).astype(F32)


def row_forward(sizes, x_ref, g_ref, w_hbm, turn_hbm, mid_hbm, n_hbm, q_hbm, k_hbm, v_hbm, att_hbm, p_hbm,
                w_ref, turn_ref, mid_ref, n_ref, q_ref, k_ref, v_ref, att_ref, p_ref, in_sems, out_sems, sems):
    rows, length, width = sizes
    coming = [start(w_hbm.at[0, part], w_ref.at[part], in_sems.at[part]) for part in range(4)]
    coming.append(start(turn_hbm.at[0], turn_ref, in_sems.at[4]))
    centred, inverse = statistics(rows_of(x_ref))
    normed = (centred * inverse * g_ref[0:1]).astype(BF16)
    n_ref[...] = normed
    going = [start(n_ref, n_hbm, out_sems.at[0])]
    for part, (ref, hbm) in enumerate(((q_ref, q_hbm), (k_ref, k_hbm), (v_ref, v_hbm))):
        coming[part].wait()
        ref[...] = dot(normed, w_ref[part]).astype(BF16)
        going.append(start(ref, hbm, out_sems.at[1 + part]))
    attention_forward(q_ref, k_ref, v_ref, att_ref, p_ref, rows, length, width, length)
    going.append(start(p_ref, p_hbm, out_sems.at[5]))
    going.append(start(att_ref, att_hbm, out_sems.at[4]))
    coming[3].wait()
    middle = (rows_of(x_ref) + dot(att_ref[...], w_ref[3])).astype(BF16)
    coming[4].wait()
    finish(going + send_turned(turn_ref, middle, mid_ref, quarters(mid_hbm), sems))


def row_back_first(d_ref, w_hbm, turn_hbm, att_hbm, dm_ref, da_ref, keep_hbm, send_hbm,
                   w_ref, turn_ref, att_ref, keep_ref, send_ref, sems):
    coming = [
        start(turn_hbm.at[1], turn_ref.at[0], sems.at[0]),
        start(att_hbm, att_ref, sems.at[1]),
        start(turn_hbm.at[6], turn_ref.at[1], sems.at[2]),
        start(w_hbm.at[0, 3], w_ref, sems.at[3]),
    ]
    coming[0].wait()
    d_middle = dot(turn_ref[0], d_ref[...]).astype(BF16)
    dm_ref[...] = d_middle
    finish(coming[1:3])
    attended = dot(att_ref[...], turn_ref[1]).astype(BF16)
    going = weight_grad(
        0, attended, d_middle, keep_ref, send_ref, keep_hbm, send_hbm, sems.at[4], sems.at[5]
    )
    coming[3].wait()
    da_ref[...] = dot_nt(d_middle, w_ref[...]).astype(BF16)
    finish(going)


def row_back(sizes, da_ref, turn_hbm, n_hbm, q_hbm, k_hbm, v_hbm, p_hbm, dqkv_hbm, keep_hbm, send_hbm,
             turn_ref, n_ref, q_ref, k_ref, v_ref, p_ref, dqkv_ref, keep_ref, send_ref, sems):
    rows, length, width = sizes
    half = p_ref.shape[0] // 2
    coming = [
        start(v_hbm, v_ref, sems.at[0]), start(k_hbm, k_ref, sems.at[1]), start(q_hbm, q_ref, sems.at[2]),
        start(p_hbm.at[pl.ds(0, half)], p_ref.at[pl.ds(0, half)], sems.at[3]),
        start(p_hbm.at[pl.ds(half, half)], p_ref.at[pl.ds(half, half)], sems.at[4]),
        start(turn_hbm.at[6], turn_ref, sems.at[5]), start(n_hbm, n_ref, sems.at[6]),
    ]
    finish(coming[:5])
    attention_back(q_ref, k_ref, v_ref, p_ref, da_ref, dqkv_ref, rows, length, width)
    going = [start(dqkv_ref, dqkv_hbm, sems.at[7])]
    finish(coming[5:])
    normed = dot(n_ref[...], turn_ref[...]).astype(BF16)
    for part in range(3):
        going += weight_grad(
            part, normed, third(dqkv_ref, part), keep_ref, send_ref, keep_hbm, send_hbm,
            sems.at[8 + part], sems.at[11 + part],
        )
    finish(going)


def field_back(x_ref, dm_ref, g_ref, dqkv_hbm, w_hbm, fg_hbm, dqkv_ref, w_ref, fg_ref, sems):
    coming = [start(dqkv_hbm, dqkv_ref, sems.at[0]), start(w_hbm.at[0, 0:3], w_ref, sems.at[1])]
    _, rows, _, channels = x_ref.shape
    length = x_ref.shape[0] * x_ref.shape[2]
    finish(coming)
    d_normed = input_back(dqkv_ref, [w_ref.at[part] for part in range(3)])
    result = dm_ref[...].astype(F32) + norm_back(rows_of(x_ref), g_ref[0:1], d_normed)
    result = result.astype(BF16)
    for i in range(rows):
        piece = result[i * length : (i + 1) * length]
        fg_ref[:, i] = piece.reshape(fg_ref.shape[0], fg_ref.shape[2], channels)
    start(fg_ref, fg_hbm, sems.at[2]).wait()


def column_first(parts, *refs):
    c_refs, (w_hbm, turn_hbm, cot_ref, da_ref, early_ref, w_ref, turn_ref, sems) = refs[:parts], refs[parts:]
    coming = [
        start(turn_hbm.at[4], turn_ref, sems.at[0]), start(w_hbm.at[1, 3], w_ref, sems.at[1]),
        start(turn_hbm.at[2], early_ref.at[0], sems.at[2]), start(w_hbm.at[1, 0], early_ref.at[1], sems.at[3]),
    ]
    cotangent = jnp.concatenate([ref[...] for ref in c_refs], axis=0)
    coming[0].wait()
    cotangent = dot(turn_ref[...], cotangent).astype(BF16)
    cot_ref[...] = cotangent
    coming[1].wait()
    da_ref[...] = dot_nt(cotangent, w_ref[...]).astype(BF16)
    finish(coming[2:])


def column_main(sizes, m_ref, cot_ref, da_ref, early_ref, g_ref, w_hbm, turn_hbm,
                dm_hbm, mid_hbm, n_hbm, att_hbm, dqkv_hbm,
                w_ref, turn_ref, dm_ref, mid_ref, n_ref, att_ref, dqkv_ref, q_ref, k_ref, v_ref, p_ref, sems):
    height, cols, width, together = sizes
    coming = [
        start(w_hbm.at[1, 1], w_ref.at[0], sems.at[0]), start(w_hbm.at[1, 2], w_ref.at[1], sems.at[1]),
        start(turn_hbm.at[3], turn_ref, sems.at[2]),
    ]
    middle = dot(early_ref[0], m_ref[...])
    mid_ref[...] = middle.astype(BF16)
    going = [start(mid_ref, mid_hbm, sems.at[3])]
    centred, inverse = statistics(middle)
    normed = (centred * inverse * g_ref[1:2]).astype(BF16)
    n_ref[...] = normed
    going.append(start(n_ref, n_hbm, sems.at[4]))
    q_ref[...] = dot(normed, early_ref[1]).astype(BF16)
    coming[0].wait()
    k_ref[...] = dot(normed, w_ref[0]).astype(BF16)
    coming[1].wait()
    v_ref[...] = dot(normed, w_ref[1]).astype(BF16)
    count = together * height
    groups = cols // together
    attention_forward(q_ref, k_ref, v_ref, att_ref, p_ref, groups, count, width, height)
    going.append(start(att_ref, att_hbm, sems.at[5]))
    attention_back(q_ref, k_ref, v_ref, p_ref, da_ref, dqkv_ref, groups, count, width)
    going.append(start(dqkv_ref, dqkv_hbm, sems.at[6]))
    d_normed = input_back(dqkv_ref, [early_ref.at[1], w_ref.at[0], w_ref.at[1]])
    middle = mid_ref[...].astype(F32)
    d_middle = cot_ref[...].astype(F32) + norm_back(middle, g_ref[1:2], d_normed)
    coming[2].wait()
    finish(going + send_turned(turn_ref, d_middle.astype(BF16), dm_ref, quarters(dm_hbm), sems.at[pl.ds(7, 4)]))


def column_last(parts, cot_hbm, mid_hbm, n_hbm, att_hbm, dqkv_hbm, w_hbm, turn_hbm, *refs):
    out_hbms, refs = refs[:parts], refs[parts:]
    keep_hbm, send_hbm, out_ref, keep_ref, send_ref, w_ref, turn_ref, flat_ref, dqkv_ref, sems = refs
    coming = [
        start(turn_hbm.at[6], turn_ref.at[0], sems.at[0]), start(n_hbm, flat_ref.at[0], sems.at[1]),
        start(dqkv_hbm, dqkv_ref, sems.at[2]), start(att_hbm, flat_ref.at[1], sems.at[3]),
        start(cot_hbm, flat_ref.at[2], sems.at[4]), start(mid_hbm, flat_ref.at[3], sems.at[5]),
        start(w_hbm.at[1, 3], w_ref, sems.at[6]), start(turn_hbm.at[5], turn_ref.at[1], sems.at[7]),
    ]
    finish(coming[:3])
    going = []
    normed = dot(flat_ref[0], turn_ref[0]).astype(BF16)
    for part in range(3):
        going += weight_grad(
            part, normed, third(dqkv_ref, part), keep_ref, send_ref, keep_hbm, send_hbm,
            sems.at[8 + part], sems.at[12 + part],
        )
    finish(coming[3:])
    attended = dot(flat_ref[1], turn_ref[0]).astype(BF16)
    going += weight_grad(
        3, attended, flat_ref[2], keep_ref, send_ref, keep_hbm, send_hbm, sems.at[11], sems.at[15]
    )
    output = (flat_ref[3].astype(F32) + dot(flat_ref[1], w_ref[...])).astype(BF16)
    finish(going + send_turned(turn_ref.at[1], output, out_ref, out_hbms, sems.at[pl.ds(16, parts)]))


NEAR, FAR, ANY = pltpu.VMEM, pltpu.HBM, None


def call(kernel, ins, outs, scratch):
    def spec(where):
        return pl.BlockSpec(memory_space=pltpu.HBM if where is FAR else pltpu.VMEM)

    def place(item, where):
        return item if where is ANY else pltpu.with_memory_space_constraint(item, where)

    return pl.pallas_call(
        kernel,
        in_specs=[spec(where) for _, where in ins],
        out_specs=[spec(where) for _, where in outs],
        out_shape=[jax.ShapeDtypeStruct(shape, BF16) if where is ANY else where(shape, BF16) for shape, where in outs],
        scratch_shapes=scratch,
        compiler_params=pltpu.CompilerParams(vmem_limit_bytes=48 * 1024 * 1024),
        cost_estimate=pl.CostEstimate(flops=1 << 20, bytes_accessed=1 << 10, transcendentals=0),
    )(*[place(item, where) for item, where in ins])


def swap(item, axis, count, step):
    return lax.ppermute(item, axis, [(at, at ^ step) for at in range(count)])


def add(left, right):
    return (left.astype(F32) + right.astype(F32)).astype(BF16)


def plane_pieces(total, plane, core):
    return [total[0]] + [swap(total[step], "col", plane * core, step * core) for step in range(1, plane)]


def last_sums(pieces, row_parts):
    parts, size, channels = pieces[0].shape
    held = sum(piece.astype(F32) for piece in pieces).astype(BF16)
    held = held.reshape(parts, row_parts, size // row_parts, channels)
    result = held[:, 0].astype(F32)
    for step in range(1, row_parts):
        result = result + swap(held[:, step], "row", row_parts, step).astype(F32)
    return result


def body(row_parts, col_parts, field, cotangent, gains, weights):
    high, wide, channels = field.shape
    core = 2
    plane = col_parts // core
    rows = high // col_parts
    cols = wide // row_parts
    tokens = high * wide
    height = high * row_parts
    length = wide * col_parts
    width = channels // HEADS
    together = min(cols, max(1, 256 // height))
    devices = row_parts * col_parts
    my_row = lax.axis_index("row")

    flat, triple = (tokens, channels), (tokens, 3 * channels)
    probs = (rows * HEADS, length, length)
    size = channels // col_parts

    def packed(parts):
        return (plane, parts, size, channels)

    def scratch(*shape):
        return pltpu.VMEM(shape, BF16)

    def at(where, *items):
        return [(item, where) for item in items]

    square = scratch(*flat)
    copies = pltpu.SemaphoreType.DMA
    assert channels == tokens
    turns = [
        ((rows, col_parts, row_parts, cols), (2, 1, 0, 3), {}, 0),
        ((row_parts, col_parts, rows, cols), (2, 1, 0, 3), {}, 0),
        ((height, cols), (1, 0), {}, 0),
        ((cols, height), (1, 0), {}, 0),
        ((row_parts, high, cols), (2, 0, 1), {0: "row"}, 0),
        ((cols, row_parts, high), (1, 2, 0), {1: "row"}, 0),
        ((row_parts, plane, core, channels // devices), (2, 1, 0, 3), {0: "row", 1: "plane", 2: "core"}, 1),
    ]

    def all_to_all(item):
        item = item.reshape(devices, rows * cols, channels)
        return lax.all_to_all(item, ("row", "col"), 0, 0, tiled=True).reshape(tokens, channels)

    x = lax.all_to_all(field.reshape(col_parts, rows, wide, channels), "col", 0, 0, tiled=True)
    cots = []
    for step in range(row_parts):
        piece = lax.dynamic_slice_in_dim(cotangent, (my_row ^ step) * cols, cols, axis=1)
        piece = piece if step == 0 else swap(piece, "row", row_parts, step)
        cots.append(piece.reshape(high * cols, channels))
    turn, = call(
        functools.partial(set_up, turns), [], at(FAR, (len(turns), *flat)),
        [scratch(len(turns), *flat), copies((len(turns),))],
    )

    sizes = (rows, length, width)
    mid, normed, query, key, value, attended, prob = call(
        functools.partial(row_forward, sizes),
        at(ANY, x, gains) + at(FAR, weights, turn), at(FAR, *[flat] * 6, probs),
        [scratch(4, *flat)] + [square] * 7 + [scratch(*probs), copies((5,)), copies((6,)), copies((4,))],
    )
    mid, cots = lax.optimization_barrier((mid, cots))
    cot, d_att, early = call(
        functools.partial(column_first, row_parts),
        at(ANY, *cots) + at(FAR, weights, turn), at(NEAR, flat, flat, (2, *flat)), [square, square, copies((4,))],
    )
    mid = all_to_all(mid)

    count = together * height
    d_mid, *kept = call(
        functools.partial(column_main, (height, cols, width, together)),
        at(ANY, mid) + at(NEAR, cot, d_att, early) + at(ANY, gains) + at(FAR, weights, turn),
        at(FAR, flat, flat, flat, flat, triple),
        [scratch(2, *flat)] + [square] * 5 + [scratch(*triple)] + [square] * 3
        + [scratch(cols // together * HEADS, count, count), copies((11,))],
    )
    d_mid = all_to_all(d_mid)
    *outs, keep_b, send_b = call(
        functools.partial(column_last, row_parts),
        at(FAR, cot, *kept, weights, turn), at(FAR, *[(high * cols, channels)] * row_parts, packed(4), packed(4)),
        [square, scratch(*packed(4)), scratch(*packed(4)), square, scratch(2, *flat), scratch(4, *flat),
         scratch(*triple), copies((16 + row_parts,))],
    )
    d_mid, outs, keep_b, send_b = lax.optimization_barrier((d_mid, outs, keep_b, send_b))
    sum_b = add(keep_b, swap(send_b, "col", col_parts, 1))
    d_mid, d_att, keep_o, send_o = call(
        row_back_first,
        at(ANY, d_mid) + at(FAR, weights, turn, attended), at(ANY, flat, flat) + at(FAR, packed(1), packed(1)),
        [square, scratch(2, *flat), square, scratch(*packed(1)), scratch(*packed(1)), copies((6,))],
    )
    sum_o = add(keep_o, swap(send_o, "col", col_parts, 1))
    outs[1] = swap(outs[1], "row", row_parts, 1)
    d_att, sum_b, sum_o, outs = lax.optimization_barrier((d_att, sum_b, sum_o, outs))
    pieces_b = plane_pieces(jnp.concatenate([sum_o, sum_b], axis=1), plane, core)
    pieces_out = [piece if step < 2 else swap(piece, "row", row_parts, step) for step, piece in enumerate(outs)]

    dqkv, keep_a, send_a = call(
        functools.partial(row_back, sizes),
        at(ANY, d_att) + at(FAR, turn, normed, query, key, value, prob), at(FAR, triple, packed(3), packed(3)),
        [square] * 5 + [scratch(*probs), scratch(*triple), scratch(*packed(3)), scratch(*packed(3)), copies((14,))],
    )
    field_grad, = call(
        field_back, at(ANY, x, d_mid, gains) + at(FAR, dqkv, weights), at(FAR, x.shape),
        [scratch(*triple), scratch(3, *flat), scratch(*x.shape), copies((3,))],
    )
    got_a = swap(send_a, "col", col_parts, 1)
    keep_a, got_a, field_grad, pieces_b, pieces_out = lax.optimization_barrier(
        (keep_a, got_a, field_grad, pieces_b, pieces_out)
    )
    sum_a = add(keep_a, got_a)
    sum_a, field_grad, pieces_b, pieces_out = lax.optimization_barrier((sum_a, field_grad, pieces_b, pieces_out))
    pieces_a = plane_pieces(sum_a, plane, core)
    field_grad = lax.all_to_all(field_grad, "col", 0, 0, tiled=True).reshape(high, wide, channels)
    grads_b = last_sums(pieces_b, row_parts)
    grads_a = last_sums(pieces_a, row_parts)
    output = jnp.zeros((high, wide, channels), BF16)
    for step, piece in enumerate(pieces_out):
        piece = piece.reshape(high, cols, channels)
        output = lax.dynamic_update_slice_in_dim(output, piece, (my_row ^ step) * cols, axis=1)
    return output, field_grad, jnp.concatenate([grads_a, grads_b], axis=0)


def solution(mesh):
    return jax.shard_map(
        functools.partial(body, mesh.shape["row"], mesh.shape["col"]),
        mesh=mesh,
        in_specs=(P("row", "col", None), P("row", "col", None), P(), P()),
        out_specs=(P("row", "col", None), P("row", "col", None), P(None, ("row", "col"), None)),
        check_vma=False,
    )
```

```python
import functools
import math

import jax
import jax.numpy as jnp
from jax import lax
from jax.experimental import pallas as pl
from jax.experimental.pallas import tpu as pltpu
from jax.sharding import PartitionSpec as P

HEADS = 8
eps = 1e-05
F32 = jnp.float32
BF16 = jnp.bfloat16


def log2(n):
    assert n & (n - 1) == 0
    return n.bit_length() - 1


def dot(left, right):
    return jnp.dot(left, right, preferred_element_type=F32)


def dot_nt(left, right):
    return lax.dot_general(left, right, (((1,), (1,)), ((), ())), preferred_element_type=F32)


def dot_tn(left, right):
    return lax.dot_general(left, right, (((0,), (0,)), ((), ())), preferred_element_type=F32)


def one_hot(sizes, order, me=None, lead=0):
    total = math.prod(sizes)
    index = lax.broadcasted_iota(jnp.int32, (total, total), lead)
    found = {}
    for axis in reversed(order):
        found[axis] = index & (sizes[axis] - 1)
        index = index >> log2(sizes[axis])
    source, shift = None, 0
    for axis in reversed(range(len(sizes))):
        digit = found[axis] << shift
        source = digit if source is None else source | digit
        shift += log2(sizes[axis])
    if me:
        place, shift = 0, 0
        for axis in reversed(range(len(sizes))):
            if axis in me:
                place = place | (me[axis] << shift)
            shift += log2(sizes[axis])
        source = source ^ place
    hit = source == lax.broadcasted_iota(jnp.int32, (total, total), 1 - lead)
    return jnp.where(hit, 1.0, 0.0).astype(BF16)


def statistics(values):
    average = jnp.mean(values, axis=-1, keepdims=True)
    centred = values - average
    spread = jnp.mean(centred * centred, axis=-1, keepdims=True)
    return centred, lax.rsqrt(spread + eps)


def norm_back(values, gain, d_normed):
    centred, inverse = statistics(values)
    unit = centred * inverse
    scaled = d_normed * gain
    return inverse * (
        scaled
        - jnp.mean(scaled, axis=-1, keepdims=True)
        - unit * jnp.mean(scaled * unit, axis=-1, keepdims=True)
    )


def head_lanes(count, width):
    return lax.broadcasted_iota(jnp.int32, (count, 2 * width), 1) < width


def attention_forward(q_ref, k_ref, v_ref, att_ref, p_ref, groups, count, width, span):
    first = head_lanes(count, width)
    pairs = HEADS // 2
    scale = width ** (-0.5)

    def step(index, carry):
        group, pair = index // pairs, index % pairs
        rows = pl.ds(pl.multiple_of(group * count, count), count)
        lanes = pl.ds(pl.multiple_of(pair * 2 * width, 2 * width), 2 * width)
        query, key, value = q_ref[rows, lanes] * scale, k_ref[rows, lanes], v_ref[rows, lanes]
        zero = jnp.zeros_like(query)
        total = jnp.zeros((count, 2 * width), F32)
        for half in range(2):
            mine = first if half == 0 else jnp.logical_not(first)
            scores = dot_nt(key, jnp.where(mine, query, zero))
            if span < count:
                shift = log2(span)
                same = (lax.broadcasted_iota(jnp.int32, (count, count), 0) >> shift) == (
                    lax.broadcasted_iota(jnp.int32, (count, count), 1) >> shift
                )
                scores = jnp.where(same, scores, -jnp.inf)
            expo = jnp.exp(scores - jnp.max(scores, axis=0, keepdims=True))
            probs = (expo * (1.0 / jnp.sum(expo, axis=0, keepdims=True))).astype(BF16)
            p_ref[index * 2 + half] = probs
            total += dot_tn(probs, jnp.where(mine, value, zero))
        att_ref[rows, lanes] = total.astype(BF16)
        return carry

    lax.fori_loop(0, groups * pairs, step, 0, unroll=2)


def attention_back(q_ref, k_ref, v_ref, p_ref, da_ref, dqkv_ref, groups, count, width):
    first = head_lanes(count, width)
    pairs = HEADS // 2
    channels = HEADS * width
    scale = width ** (-0.5)

    def step(index, carry):
        group, pair = index // pairs, index % pairs
        rows = pl.ds(pl.multiple_of(group * count, count), count)
        lanes = pl.ds(pl.multiple_of(pair * 2 * width, 2 * width), 2 * width)
        query, key, value = q_ref[rows, lanes] * scale, k_ref[rows, lanes], v_ref[rows, lanes]
        d_out = da_ref[rows, lanes]
        zero = jnp.zeros_like(query)
        d_query = jnp.zeros((count, 2 * width), F32)
        d_key, d_value = d_query, d_query
        for half in range(2):
            mine = first if half == 0 else jnp.logical_not(first)
            probs = p_ref[index * 2 + half]
            d_mine = jnp.where(mine, d_out, zero)
            d_probs = dot_nt(value, d_mine)
            probs32 = probs.astype(F32)
            weighted = probs32 * d_probs
            total = jnp.sum(weighted, axis=0, keepdims=True)
            d_scores = (weighted - probs32 * total).astype(BF16)
            d_query += dot_tn(d_scores, jnp.where(mine, key, zero))
            d_key += dot(d_scores, jnp.where(mine, query, zero))
            d_value += dot(probs, d_mine)
        for part, item in enumerate((d_query * scale, d_key, d_value)):
            at = pl.ds(pl.multiple_of(part * channels + pair * 2 * width, 2 * width), 2 * width)
            dqkv_ref[rows, at] = item.astype(BF16)
        return carry

    lax.fori_loop(0, groups * pairs, step, 0, unroll=2)


def start(source, target, sem):
    copy = pltpu.make_async_copy(source, target, sem)
    copy.start()
    return copy


def finish(copies):
    for copy in copies:
        copy.wait()


def set_up(turns, turn_hbm, turn_ref, sems):
    my_row, my_col = lax.axis_index("row"), lax.axis_index("col")
    places = {"row": my_row, "plane": my_col >> 1, "core": my_col & 1}
    going = []
    for at, (sizes, order, me, lead) in enumerate(turns):
        turn_ref[at] = one_hot(sizes, order, {axis: places[name] for axis, name in me.items()}, lead)
        going.append(start(turn_ref.at[at], turn_hbm.at[at], sems.at[at]))
    finish(going)


def weight_grad(part, left, right, keep_ref, send_ref):
    plane, _, size, _ = keep_ref.shape
    whole = dot_tn(left, right).astype(BF16)
    for group in range(plane):
        send_ref[group, part] = whole[(plane + group) * size : (plane + group + 1) * size]
        keep_ref[group, part] = whole[group * size : (group + 1) * size]


def send_grads(keep_ref, send_ref, keep_hbms, send_hbms, sems):
    plane = keep_ref.shape[0]
    going = [start(send_ref.at[at], send_hbms[at], sems.at[at]) for at in range(plane)]
    return going + [start(keep_ref.at[at], keep_hbms[at], sems.at[plane + at]) for at in range(plane)]


def third(ref, part):
    channels = ref.shape[-1] // 3
    return ref[:, part * channels : (part + 1) * channels]


def send_turned(turn_ref, values, stage_ref, targets, sems):
    size = values.shape[0] // len(targets)
    going = []
    for at, target in enumerate(targets):
        piece = pl.ds(at * size, size)
        stage_ref[piece] = dot(turn_ref[piece], values).astype(BF16)
        going.append(start(stage_ref.at[piece], target, sems.at[at]))
    return going


def quarters(ref):
    size = ref.shape[0] // 4
    return [ref.at[pl.ds(at * size, size)] for at in range(4)]


def input_back(dqkv_ref, w_refs):
    total = dot_nt(third(dqkv_ref, 0), w_refs[0][...])
    total += dot_nt(third(dqkv_ref, 1), w_refs[1][...])
    total += dot_nt(third(dqkv_ref, 2), w_refs[2][...])
    return total.astype(BF16).astype(F32)


def rows_of(x_ref):
    _, rows, _, channels = x_ref.shape
    length = x_ref.shape[0] * x_ref.shape[2]
    pieces = [x_ref[:, i].reshape(length, channels) for i in range(rows)]
    return jnp.concatenate(pieces, axis=0).astype(F32)


def row_forward(sizes, x_ref, g_ref, w_hbm, turn_hbm, mid_hbm, n_hbm, q_hbm, k_hbm, v_hbm, att_hbm, p_hbm,
                w_ref, turn_ref, mid_ref, n_ref, q_ref, k_ref, v_ref, att_ref, p_ref, in_sems, out_sems, sems):
    rows, length, width = sizes
    coming = [start(w_hbm.at[0, part], w_ref.at[part], in_sems.at[part]) for part in range(4)]
    coming.append(start(turn_hbm.at[0], turn_ref, in_sems.at[4]))
    centred, inverse = statistics(rows_of(x_ref))
    normed = (centred * inverse * g_ref[0:1]).astype(BF16)
    n_ref[...] = normed
    going = [start(n_ref, n_hbm, out_sems.at[0])]
    for part, (ref, hbm) in enumerate(((q_ref, q_hbm), (k_ref, k_hbm), (v_ref, v_hbm))):
        coming[part].wait()
        ref[...] = dot(normed, w_ref[part]).astype(BF16)
        going.append(start(ref, hbm, out_sems.at[1 + part]))
    attention_forward(q_ref, k_ref, v_ref, att_ref, p_ref, rows, length, width, length)
    going.append(start(p_ref, p_hbm, out_sems.at[5]))
    going.append(start(att_ref, att_hbm, out_sems.at[4]))
    coming[3].wait()
    middle = (rows_of(x_ref) + dot(att_ref[...], w_ref[3])).astype(BF16)
    coming[4].wait()
    finish(going + send_turned(turn_ref, middle, mid_ref, quarters(mid_hbm), sems))


def row_back(sizes, d_ref, w_hbm, turn_hbm, n_hbm, q_hbm, k_hbm, v_hbm, att_hbm, p_hbm, *refs):
    rows, length, width, plane = sizes
    dm_ref, dqkv_hbm, keep_hbms, send_hbms = refs[0], refs[1], refs[2 : 2 + plane], refs[2 + plane : 2 + 2 * plane]
    w_ref, turn_ref, n_ref, q_ref, k_ref, v_ref, att_ref, p_ref, da_ref, dqkv_ref = refs[2 + 2 * plane : -4]
    keep_ref, send_ref, sems, out_sems = refs[-4:]
    half = p_ref.shape[0] // 2
    coming = [
        start(turn_hbm.at[1], turn_ref.at[0], sems.at[0]), start(w_hbm.at[0, 3], w_ref, sems.at[1]),
        start(v_hbm, v_ref, sems.at[2]), start(k_hbm, k_ref, sems.at[3]), start(q_hbm, q_ref, sems.at[4]),
        start(p_hbm.at[pl.ds(0, half)], p_ref.at[pl.ds(0, half)], sems.at[5]),
        start(p_hbm.at[pl.ds(half, half)], p_ref.at[pl.ds(half, half)], sems.at[6]),
        start(turn_hbm.at[6], turn_ref.at[1], sems.at[7]), start(att_hbm, att_ref, sems.at[8]),
        start(n_hbm, n_ref, sems.at[9]),
    ]
    coming[0].wait()
    d_middle = dot(turn_ref[0], d_ref[...]).astype(BF16)
    dm_ref[...] = d_middle
    coming[1].wait()
    da_ref[...] = dot_nt(d_middle, w_ref[...]).astype(BF16)
    finish(coming[2:7])
    attention_back(q_ref, k_ref, v_ref, p_ref, da_ref, dqkv_ref, rows, length, width)
    going = [start(dqkv_ref, dqkv_hbm, sems.at[10])]
    finish(coming[7:])
    normed = dot(n_ref[...], turn_ref[1]).astype(BF16)
    for part in range(3):
        weight_grad(part, normed, third(dqkv_ref, part), keep_ref, send_ref)
    attended = dot(att_ref[...], turn_ref[1]).astype(BF16)
    weight_grad(3, attended, dm_ref[...], keep_ref, send_ref)
    finish(going + send_grads(keep_ref, send_ref, keep_hbms, send_hbms, out_sems))


def field_back(x_ref, dm_ref, g_ref, dqkv_hbm, w_hbm, fg_hbm, dqkv_ref, w_ref, fg_ref, sems):
    coming = [start(dqkv_hbm, dqkv_ref, sems.at[0]), start(w_hbm.at[0, 0:3], w_ref, sems.at[1])]
    _, rows, _, channels = x_ref.shape
    length = x_ref.shape[0] * x_ref.shape[2]
    finish(coming)
    d_normed = input_back(dqkv_ref, [w_ref.at[part] for part in range(3)])
    result = dm_ref[...].astype(F32) + norm_back(rows_of(x_ref), g_ref[0:1], d_normed)
    result = result.astype(BF16)
    for i in range(rows):
        piece = result[i * length : (i + 1) * length]
        fg_ref[:, i] = piece.reshape(fg_ref.shape[0], fg_ref.shape[2], channels)
    start(fg_ref, fg_hbm, sems.at[2]).wait()


def column_first(parts, *refs):
    c_refs, (w_hbm, turn_hbm, cot_ref, da_ref, early_ref, w_ref, turn_ref, sems) = refs[:parts], refs[parts:]
    coming = [
        start(turn_hbm.at[4], turn_ref, sems.at[0]), start(w_hbm.at[1, 3], w_ref, sems.at[1]),
        start(turn_hbm.at[2], early_ref.at[0], sems.at[2]), start(w_hbm.at[1, 0], early_ref.at[1], sems.at[3]),
    ]
    cotangent = jnp.concatenate([ref[...] for ref in c_refs], axis=0)
    coming[0].wait()
    cotangent = dot(turn_ref[...], cotangent).astype(BF16)
    cot_ref[...] = cotangent
    coming[1].wait()
    da_ref[...] = dot_nt(cotangent, w_ref[...]).astype(BF16)
    finish(coming[2:])


def column_main(sizes, m_ref, cot_ref, da_ref, early_ref, g_ref, w_hbm, turn_hbm,
                dm_hbm, mid_hbm, n_hbm, att_hbm, dqkv_hbm,
                w_ref, turn_ref, dm_ref, mid_ref, n_ref, att_ref, dqkv_ref, q_ref, k_ref, v_ref, p_ref, sems):
    height, cols, width, together = sizes
    coming = [
        start(w_hbm.at[1, 1], w_ref.at[0], sems.at[0]), start(w_hbm.at[1, 2], w_ref.at[1], sems.at[1]),
        start(turn_hbm.at[3], turn_ref, sems.at[2]),
    ]
    middle = dot(early_ref[0], m_ref[...])
    mid_ref[...] = middle.astype(BF16)
    going = [start(mid_ref, mid_hbm, sems.at[3])]
    centred, inverse = statistics(middle)
    normed = (centred * inverse * g_ref[1:2]).astype(BF16)
    n_ref[...] = normed
    going.append(start(n_ref, n_hbm, sems.at[4]))
    q_ref[...] = dot(normed, early_ref[1]).astype(BF16)
    coming[0].wait()
    k_ref[...] = dot(normed, w_ref[0]).astype(BF16)
    coming[1].wait()
    v_ref[...] = dot(normed, w_ref[1]).astype(BF16)
    count = together * height
    groups = cols // together
    attention_forward(q_ref, k_ref, v_ref, att_ref, p_ref, groups, count, width, height)
    going.append(start(att_ref, att_hbm, sems.at[5]))
    attention_back(q_ref, k_ref, v_ref, p_ref, da_ref, dqkv_ref, groups, count, width)
    going.append(start(dqkv_ref, dqkv_hbm, sems.at[6]))
    d_normed = input_back(dqkv_ref, [early_ref.at[1], w_ref.at[0], w_ref.at[1]])
    middle = mid_ref[...].astype(F32)
    d_middle = cot_ref[...].astype(F32) + norm_back(middle, g_ref[1:2], d_normed)
    coming[2].wait()
    finish(going + send_turned(turn_ref, d_middle.astype(BF16), dm_ref, quarters(dm_hbm), sems.at[pl.ds(7, 4)]))


def column_last(plane, cot_hbm, mid_hbm, n_hbm, att_hbm, dqkv_hbm, w_hbm, turn_hbm, out_hbm, *refs):
    keep_hbms, send_hbms, refs = refs[:plane], refs[plane : 2 * plane], refs[2 * plane :]
    out_ref, keep_ref, send_ref, w_ref, turn_ref, flat_ref, dqkv_ref, sems, out_sems = refs
    coming = [
        start(turn_hbm.at[6], turn_ref.at[0], sems.at[0]), start(n_hbm, flat_ref.at[0], sems.at[1]),
        start(dqkv_hbm, dqkv_ref, sems.at[2]), start(att_hbm, flat_ref.at[1], sems.at[3]),
        start(cot_hbm, flat_ref.at[2], sems.at[4]), start(mid_hbm, flat_ref.at[3], sems.at[5]),
        start(w_hbm.at[1, 3], w_ref, sems.at[6]), start(turn_hbm.at[5], turn_ref.at[1], sems.at[7]),
    ]
    finish(coming[:3])
    normed = dot(flat_ref[0], turn_ref[0]).astype(BF16)
    for part in range(3):
        weight_grad(part, normed, third(dqkv_ref, part), keep_ref, send_ref)
    finish(coming[3:])
    attended = dot(flat_ref[1], turn_ref[0]).astype(BF16)
    weight_grad(3, attended, flat_ref[2], keep_ref, send_ref)
    going = send_grads(keep_ref, send_ref, keep_hbms, send_hbms, out_sems)
    output = (flat_ref[3].astype(F32) + dot(flat_ref[1], w_ref[...])).astype(BF16)
    finish(going + send_turned(turn_ref.at[1], output, out_ref, [out_hbm], sems.at[pl.ds(8, 1)]))


NEAR, FAR, ANY = pltpu.VMEM, pltpu.HBM, None


def call(kernel, ins, outs, scratch):
    def spec(where):
        return pl.BlockSpec(memory_space=pltpu.HBM if where is FAR else pltpu.VMEM)

    def place(item, where):
        return item if where is ANY else pltpu.with_memory_space_constraint(item, where)

    return pl.pallas_call(
        kernel,
        in_specs=[spec(where) for _, where in ins],
        out_specs=[spec(where) for _, where in outs],
        out_shape=[jax.ShapeDtypeStruct(shape, BF16) if where is ANY else where(shape, BF16) for shape, where in outs],
        scratch_shapes=scratch,
        compiler_params=pltpu.CompilerParams(vmem_limit_bytes=48 * 1024 * 1024),
        cost_estimate=pl.CostEstimate(flops=1 << 20, bytes_accessed=1 << 10, transcendentals=0),
    )(*[place(item, where) for item, where in ins])


def swap(item, axis, count, step):
    return lax.ppermute(item, axis, [(at, at ^ step) for at in range(count)])


def add(left, right):
    return (left.astype(F32) + right.astype(F32)).astype(BF16)


def plane_pieces(sums, plane, core):
    return [item if step == 0 else swap(item, "col", plane * core, step * core) for step, item in enumerate(sums)]


def last_sums(pieces, row_parts):
    parts, size, channels = pieces[0].shape
    held = sum(piece.astype(F32) for piece in pieces).astype(BF16)
    held = held.reshape(parts, row_parts, size // row_parts, channels)
    result = held[:, 0].astype(F32)
    for step in range(1, row_parts):
        result = result + swap(held[:, step], "row", row_parts, step).astype(F32)
    return result


def body(row_parts, col_parts, field, cotangent, gains, weights):
    high, wide, channels = field.shape
    core = 2
    plane = col_parts // core
    rows = high // col_parts
    cols = wide // row_parts
    tokens = high * wide
    height = high * row_parts
    length = wide * col_parts
    width = channels // HEADS
    together = min(cols, max(1, 256 // height))
    devices = row_parts * col_parts
    my_row = lax.axis_index("row")

    flat, triple = (tokens, channels), (tokens, 3 * channels)
    probs = (rows * HEADS, length, length)
    packed = (4, channels // col_parts, channels)

    def scratch(*shape):
        return pltpu.VMEM(shape, BF16)

    def at(where, *items):
        return [(item, where) for item in items]

    square = scratch(*flat)
    copies = pltpu.SemaphoreType.DMA
    assert channels == tokens
    turns = [
        ((rows, col_parts, row_parts, cols), (2, 1, 0, 3), {}, 0),
        ((row_parts, col_parts, rows, cols), (2, 1, 0, 3), {}, 0),
        ((height, cols), (1, 0), {}, 0),
        ((cols, height), (1, 0), {}, 0),
        ((row_parts, high, cols), (2, 0, 1), {0: "row"}, 0),
        ((cols, row_parts, high), (1, 2, 0), {}, 0),
        ((row_parts, plane, core, channels // devices), (2, 1, 0, 3), {0: "row", 1: "plane", 2: "core"}, 1),
    ]

    def all_to_all(item):
        item = item.reshape(devices, rows * cols, channels)
        return lax.all_to_all(item, ("row", "col"), 0, 0, tiled=True).reshape(tokens, channels)

    x = lax.all_to_all(field.reshape(col_parts, rows, wide, channels), "col", 0, 0, tiled=True)
    cots = []
    for step in range(row_parts):
        piece = lax.dynamic_slice_in_dim(cotangent, (my_row ^ step) * cols, cols, axis=1)
        piece = piece if step == 0 else swap(piece, "row", row_parts, step)
        cots.append(piece.reshape(high * cols, channels))
    turn, = call(
        functools.partial(set_up, turns), [], at(FAR, (len(turns), *flat)),
        [scratch(len(turns), *flat), copies((len(turns),))],
    )

    sizes = (rows, length, width)
    mid, normed, query, key, value, attended, prob = call(
        functools.partial(row_forward, sizes),
        at(ANY, x, gains) + at(FAR, weights, turn), at(FAR, *[flat] * 6, probs),
        [scratch(4, *flat)] + [square] * 7 + [scratch(*probs), copies((5,)), copies((6,)), copies((4,))],
    )
    mid, cots = lax.optimization_barrier((mid, cots))
    cot, d_att, early = call(
        functools.partial(column_first, row_parts),
        at(ANY, *cots) + at(FAR, weights, turn), at(NEAR, flat, flat, (2, *flat)), [square, square, copies((4,))],
    )
    mid = all_to_all(mid)

    count = together * height
    d_mid, *kept = call(
        functools.partial(column_main, (height, cols, width, together)),
        at(ANY, mid) + at(NEAR, cot, d_att, early) + at(ANY, gains) + at(FAR, weights, turn),
        at(FAR, flat, flat, flat, flat, triple),
        [scratch(2, *flat)] + [square] * 5 + [scratch(*triple)] + [square] * 3
        + [scratch(cols // together * HEADS, count, count), copies((11,))],
    )
    d_mid = all_to_all(d_mid)
    out, *grads = call(
        functools.partial(column_last, plane),
        at(FAR, cot, *kept, weights, turn), at(FAR, flat, *[packed] * (2 * plane)),
        [square, scratch(plane, *packed), scratch(plane, *packed), square, scratch(2, *flat), scratch(4, *flat),
         scratch(*triple), copies((9,)), copies((2 * plane,))],
    )
    sums_b = [add(keep, swap(send, "col", col_parts, 1)) for keep, send in zip(grads[:plane], grads[plane:])]
    pieces_b = plane_pieces(sums_b, plane, core)
    d_mid, sums_b, out = lax.optimization_barrier((d_mid, sums_b, out))
    out = lax.all_to_all(out.reshape(row_parts, high, cols, channels), "row", 0, 0, tiled=True)
    d_mid, dqkv, *grads = call(
        functools.partial(row_back, (rows, length, width, plane)),
        at(ANY, d_mid) + at(FAR, weights, turn, normed, query, key, value, attended, prob),
        at(ANY, flat) + at(FAR, triple, *[packed] * (2 * plane)),
        [square, scratch(2, *flat)] + [square] * 5 + [scratch(*probs), square, scratch(*triple)]
        + [scratch(plane, *packed), scratch(plane, *packed), copies((11,)), copies((2 * plane,))],
    )
    keeps, got = grads[:plane], [swap(send, "col", col_parts, 1) for send in grads[plane:]]
    dqkv, pieces_b = lax.optimization_barrier((dqkv, pieces_b))
    field_grad, = call(
        field_back, at(ANY, x, d_mid, gains) + at(FAR, dqkv, weights), at(FAR, x.shape),
        [scratch(*triple), scratch(3, *flat), scratch(*x.shape), copies((3,))],
    )
    field_grad, keeps, got, pieces_b = lax.optimization_barrier((field_grad, keeps, got, pieces_b))
    sums_a = [add(keep, other) for keep, other in zip(keeps, got)]
    field_grad, sums_a, pieces_b = lax.optimization_barrier((field_grad, sums_a, pieces_b))
    pieces_a = plane_pieces(sums_a, plane, core)
    grads_b = last_sums(pieces_b, row_parts)
    field_grad = lax.all_to_all(field_grad, "col", 0, 0, tiled=True).reshape(high, wide, channels)
    grads_a = last_sums(pieces_a, row_parts)
    output = out.transpose(1, 0, 2, 3).reshape(high, wide, channels)
    return output, field_grad, jnp.concatenate([grads_a, grads_b], axis=0)


def solution(mesh):
    return jax.shard_map(
        functools.partial(body, mesh.shape["row"], mesh.shape["col"]),
        mesh=mesh,
        in_specs=(P("row", "col", None), P("row", "col", None), P(), P()),
        out_specs=(P("row", "col", None), P("row", "col", None), P(None, ("row", "col"), None)),
        check_vma=False,
    )
```

```python
import functools
import math

import jax
import jax.numpy as jnp
from jax import lax
from jax.experimental import pallas as pl
from jax.experimental.pallas import tpu as pltpu
from jax.sharding import PartitionSpec as P

HEADS = 8
eps = 1e-05
F32 = jnp.float32
BF16 = jnp.bfloat16


def log2(n):
    assert n & (n - 1) == 0
    return n.bit_length() - 1


def dot(left, right):
    return jnp.dot(left, right, preferred_element_type=F32)


def dot_nt(left, right):
    return lax.dot_general(left, right, (((1,), (1,)), ((), ())), preferred_element_type=F32)


def dot_tn(left, right):
    return lax.dot_general(left, right, (((0,), (0,)), ((), ())), preferred_element_type=F32)


def one_hot(sizes, order, me=None, lead=0):
    total = math.prod(sizes)
    index = lax.broadcasted_iota(jnp.int32, (total, total), lead)
    found = {}
    for axis in reversed(order):
        found[axis] = index & (sizes[axis] - 1)
        index = index >> log2(sizes[axis])
    source, shift = None, 0
    for axis in reversed(range(len(sizes))):
        digit = found[axis] << shift
        source = digit if source is None else source | digit
        shift += log2(sizes[axis])
    if me:
        place, shift = 0, 0
        for axis in reversed(range(len(sizes))):
            if axis in me:
                place = place | (me[axis] << shift)
            shift += log2(sizes[axis])
        source = source ^ place
    hit = source == lax.broadcasted_iota(jnp.int32, (total, total), 1 - lead)
    return jnp.where(hit, 1.0, 0.0).astype(BF16)


def statistics(values):
    average = jnp.mean(values, axis=-1, keepdims=True)
    centred = values - average
    spread = jnp.mean(centred * centred, axis=-1, keepdims=True)
    return centred, lax.rsqrt(spread + eps)


def norm_back(values, gain, d_normed):
    centred, inverse = statistics(values)
    unit = centred * inverse
    scaled = d_normed * gain
    return inverse * (
        scaled
        - jnp.mean(scaled, axis=-1, keepdims=True)
        - unit * jnp.mean(scaled * unit, axis=-1, keepdims=True)
    )


def head_lanes(count, width):
    return lax.broadcasted_iota(jnp.int32, (count, 2 * width), 1) < width


def attention_forward(q_ref, k_ref, v_ref, att_ref, p_ref, groups, count, width, span):
    first = head_lanes(count, width)
    pairs = HEADS // 2
    scale = width ** (-0.5)

    def step(index, carry):
        group, pair = index // pairs, index % pairs
        rows = pl.ds(pl.multiple_of(group * count, count), count)
        lanes = pl.ds(pl.multiple_of(pair * 2 * width, 2 * width), 2 * width)
        query, key, value = q_ref[rows, lanes] * scale, k_ref[rows, lanes], v_ref[rows, lanes]
        zero = jnp.zeros_like(query)
        total = jnp.zeros((count, 2 * width), F32)
        for half in range(2):
            mine = first if half == 0 else jnp.logical_not(first)
            scores = dot_nt(key, jnp.where(mine, query, zero))
            if span < count:
                shift = log2(span)
                same = (lax.broadcasted_iota(jnp.int32, (count, count), 0) >> shift) == (
                    lax.broadcasted_iota(jnp.int32, (count, count), 1) >> shift
                )
                scores = jnp.where(same, scores, -jnp.inf)
            expo = jnp.exp(scores - jnp.max(scores, axis=0, keepdims=True))
            probs = (expo * (1.0 / jnp.sum(expo, axis=0, keepdims=True))).astype(BF16)
            p_ref[index * 2 + half] = probs
            total += dot_tn(probs, jnp.where(mine, value, zero))
        att_ref[rows, lanes] = total.astype(BF16)
        return carry

    lax.fori_loop(0, groups * pairs, step, 0, unroll=2)


def attention_back(q_ref, k_ref, v_ref, p_ref, da_ref, dqkv_ref, groups, count, width):
    first = head_lanes(count, width)
    pairs = HEADS // 2
    channels = HEADS * width
    scale = width ** (-0.5)

    def step(index, carry):
        group, pair = index // pairs, index % pairs
        rows = pl.ds(pl.multiple_of(group * count, count), count)
        lanes = pl.ds(pl.multiple_of(pair * 2 * width, 2 * width), 2 * width)
        query, key, value = q_ref[rows, lanes] * scale, k_ref[rows, lanes], v_ref[rows, lanes]
        d_out = da_ref[rows, lanes]
        zero = jnp.zeros_like(query)
        d_query = jnp.zeros((count, 2 * width), F32)
        d_key, d_value = d_query, d_query
        for half in range(2):
            mine = first if half == 0 else jnp.logical_not(first)
            probs = p_ref[index * 2 + half]
            d_mine = jnp.where(mine, d_out, zero)
            d_probs = dot_nt(value, d_mine)
            probs32 = probs.astype(F32)
            weighted = probs32 * d_probs
            total = jnp.sum(weighted, axis=0, keepdims=True)
            d_scores = (weighted - probs32 * total).astype(BF16)
            d_query += dot_tn(d_scores, jnp.where(mine, key, zero))
            d_key += dot(d_scores, jnp.where(mine, query, zero))
            d_value += dot(probs, d_mine)
        for part, item in enumerate((d_query * scale, d_key, d_value)):
            at = pl.ds(pl.multiple_of(part * channels + pair * 2 * width, 2 * width), 2 * width)
            dqkv_ref[rows, at] = item.astype(BF16)
        return carry

    lax.fori_loop(0, groups * pairs, step, 0, unroll=2)


def start(source, target, sem):
    copy = pltpu.make_async_copy(source, target, sem)
    copy.start()
    return copy


def finish(copies):
    for copy in copies:
        copy.wait()


def set_up(turns, turn_hbm, turn_ref, sems):
    my_row, my_col = lax.axis_index("row"), lax.axis_index("col")
    places = {"row": my_row, "plane": my_col >> 1, "core": my_col & 1}
    going = []
    for at, (sizes, order, me, lead) in enumerate(turns):
        turn_ref[at] = one_hot(sizes, order, {axis: places[name] for axis, name in me.items()}, lead)
        going.append(start(turn_ref.at[at], turn_hbm.at[at], sems.at[at]))
    finish(going)


def weight_grad(part, left, right, keep_ref, send_ref):
    plane, _, size, _ = keep_ref.shape
    whole = dot_tn(left, right).astype(BF16)
    for group in range(plane):
        send_ref[group, part] = whole[(plane + group) * size : (plane + group + 1) * size]
        keep_ref[group, part] = whole[group * size : (group + 1) * size]


def send_grads(keep_ref, send_ref, keep_hbms, send_hbms, sems):
    plane = keep_ref.shape[0]
    going = [start(send_ref.at[at], send_hbms[at], sems.at[at]) for at in range(plane)]
    return going + [start(keep_ref.at[at], keep_hbms[at], sems.at[plane + at]) for at in range(plane)]


def third(ref, part):
    channels = ref.shape[-1] // 3
    return ref[:, part * channels : (part + 1) * channels]


def send_turned(turn_ref, values, stage_ref, targets, sems):
    size = values.shape[0] // len(targets)
    going = []
    for at, target in enumerate(targets):
        piece = pl.ds(at * size, size)
        stage_ref[piece] = dot(turn_ref[piece], values).astype(BF16)
        going.append(start(stage_ref.at[piece], target, sems.at[at]))
    return going


def quarters(ref):
    size = ref.shape[0] // 4
    return [ref.at[pl.ds(at * size, size)] for at in range(4)]


def input_back(dqkv_ref, w_refs):
    total = dot_nt(third(dqkv_ref, 0), w_refs[0][...])
    total += dot_nt(third(dqkv_ref, 1), w_refs[1][...])
    total += dot_nt(third(dqkv_ref, 2), w_refs[2][...])
    return total.astype(BF16).astype(F32)


def rows_of(x_ref):
    _, rows, _, channels = x_ref.shape
    length = x_ref.shape[0] * x_ref.shape[2]
    pieces = [x_ref[:, i].reshape(length, channels) for i in range(rows)]
    return jnp.concatenate(pieces, axis=0).astype(F32)


def row_forward(sizes, x_ref, g_ref, w_hbm, turn_hbm, mid_hbm, n_hbm, q_hbm, k_hbm, v_hbm, att_hbm, p_hbm,
                w_ref, turn_ref, mid_ref, n_ref, q_ref, k_ref, v_ref, att_ref, p_ref, in_sems, out_sems, sems):
    rows, length, width = sizes
    coming = [start(w_hbm.at[0, part], w_ref.at[part], in_sems.at[part]) for part in range(4)]
    coming.append(start(turn_hbm.at[0], turn_ref, in_sems.at[4]))
    centred, inverse = statistics(rows_of(x_ref))
    normed = (centred * inverse * g_ref[0:1]).astype(BF16)
    n_ref[...] = normed
    going = [start(n_ref, n_hbm, out_sems.at[0])]
    for part, (ref, hbm) in enumerate(((q_ref, q_hbm), (k_ref, k_hbm), (v_ref, v_hbm))):
        coming[part].wait()
        ref[...] = dot(normed, w_ref[part]).astype(BF16)
        going.append(start(ref, hbm, out_sems.at[1 + part]))
    attention_forward(q_ref, k_ref, v_ref, att_ref, p_ref, rows, length, width, length)
    going.append(start(p_ref, p_hbm, out_sems.at[5]))
    going.append(start(att_ref, att_hbm, out_sems.at[4]))
    coming[3].wait()
    middle = (rows_of(x_ref) + dot(att_ref[...], w_ref[3])).astype(BF16)
    coming[4].wait()
    finish(going + send_turned(turn_ref, middle, mid_ref, quarters(mid_hbm), sems))


def row_back(sizes, d_ref, w_hbm, turn_hbm, n_hbm, q_hbm, k_hbm, v_hbm, att_hbm, p_hbm, *refs):
    rows, length, width, plane = sizes
    dm_ref, dqkv_hbm, keep_hbms, send_hbms = refs[0], refs[1], refs[2 : 2 + plane], refs[2 + plane : 2 + 2 * plane]
    w_ref, turn_ref, n_ref, q_ref, k_ref, v_ref, att_ref, p_ref, da_ref, dqkv_ref = refs[2 + 2 * plane : -4]
    keep_ref, send_ref, sems, out_sems = refs[-4:]
    half = p_ref.shape[0] // 2
    coming = [
        start(turn_hbm.at[1], turn_ref.at[0], sems.at[0]), start(w_hbm.at[0, 3], w_ref, sems.at[1]),
        start(v_hbm, v_ref, sems.at[2]), start(k_hbm, k_ref, sems.at[3]), start(q_hbm, q_ref, sems.at[4]),
        start(p_hbm.at[pl.ds(0, half)], p_ref.at[pl.ds(0, half)], sems.at[5]),
        start(p_hbm.at[pl.ds(half, half)], p_ref.at[pl.ds(half, half)], sems.at[6]),
        start(turn_hbm.at[6], turn_ref.at[1], sems.at[7]), start(att_hbm, att_ref, sems.at[8]),
        start(n_hbm, n_ref, sems.at[9]),
    ]
    coming[0].wait()
    d_middle = dot(turn_ref[0], d_ref[...]).astype(BF16)
    dm_ref[...] = d_middle
    coming[1].wait()
    da_ref[...] = dot_nt(d_middle, w_ref[...]).astype(BF16)
    finish(coming[2:7])
    attention_back(q_ref, k_ref, v_ref, p_ref, da_ref, dqkv_ref, rows, length, width)
    going = [start(dqkv_ref, dqkv_hbm, sems.at[10])]
    finish(coming[7:])
    normed = dot(n_ref[...], turn_ref[1]).astype(BF16)
    for part in range(3):
        weight_grad(part, normed, third(dqkv_ref, part), keep_ref, send_ref)
    attended = dot(att_ref[...], turn_ref[1]).astype(BF16)
    weight_grad(3, attended, dm_ref[...], keep_ref, send_ref)
    finish(going + send_grads(keep_ref, send_ref, keep_hbms, send_hbms, out_sems))


def field_back(x_ref, dm_ref, g_ref, dqkv_hbm, w_hbm, fg_hbm, dqkv_ref, w_ref, fg_ref, sems):
    coming = [start(dqkv_hbm, dqkv_ref, sems.at[0]), start(w_hbm.at[0, 0:3], w_ref, sems.at[1])]
    _, rows, _, channels = x_ref.shape
    length = x_ref.shape[0] * x_ref.shape[2]
    finish(coming)
    d_normed = input_back(dqkv_ref, [w_ref.at[part] for part in range(3)])
    result = dm_ref[...].astype(F32) + norm_back(rows_of(x_ref), g_ref[0:1], d_normed)
    result = result.astype(BF16)
    for i in range(rows):
        piece = result[i * length : (i + 1) * length]
        fg_ref[:, i] = piece.reshape(fg_ref.shape[0], fg_ref.shape[2], channels)
    start(fg_ref, fg_hbm, sems.at[2]).wait()


def column_first(parts, *refs):
    c_refs, (w_hbm, turn_hbm, cot_ref, da_ref, early_ref, w_ref, turn_ref, sems) = refs[:parts], refs[parts:]
    coming = [
        start(turn_hbm.at[4], turn_ref, sems.at[0]), start(w_hbm.at[1, 3], w_ref, sems.at[1]),
        start(turn_hbm.at[2], early_ref.at[0], sems.at[2]), start(w_hbm.at[1, 0], early_ref.at[1], sems.at[3]),
    ]
    cotangent = jnp.concatenate([ref[...] for ref in c_refs], axis=0)
    coming[0].wait()
    cotangent = dot(turn_ref[...], cotangent).astype(BF16)
    cot_ref[...] = cotangent
    coming[1].wait()
    da_ref[...] = dot_nt(cotangent, w_ref[...]).astype(BF16)
    finish(coming[2:])


def column_main(sizes, m_ref, cot_ref, da_ref, early_ref, g_ref, w_hbm, turn_hbm,
                dm_hbm, mid_hbm, n_hbm, att_hbm, dqkv_hbm,
                w_ref, turn_ref, dm_ref, mid_ref, n_ref, att_ref, dqkv_ref, q_ref, k_ref, v_ref, p_ref, sems):
    height, cols, width, together = sizes
    coming = [
        start(w_hbm.at[1, 1], w_ref.at[0], sems.at[0]), start(w_hbm.at[1, 2], w_ref.at[1], sems.at[1]),
        start(turn_hbm.at[3], turn_ref, sems.at[2]),
    ]
    middle = dot(early_ref[0], m_ref[...])
    mid_ref[...] = middle.astype(BF16)
    going = [start(mid_ref, mid_hbm, sems.at[3])]
    centred, inverse = statistics(middle)
    normed = (centred * inverse * g_ref[1:2]).astype(BF16)
    n_ref[...] = normed
    going.append(start(n_ref, n_hbm, sems.at[4]))
    q_ref[...] = dot(normed, early_ref[1]).astype(BF16)
    coming[0].wait()
    k_ref[...] = dot(normed, w_ref[0]).astype(BF16)
    coming[1].wait()
    v_ref[...] = dot(normed, w_ref[1]).astype(BF16)
    count = together * height
    groups = cols // together
    attention_forward(q_ref, k_ref, v_ref, att_ref, p_ref, groups, count, width, height)
    going.append(start(att_ref, att_hbm, sems.at[5]))
    attention_back(q_ref, k_ref, v_ref, p_ref, da_ref, dqkv_ref, groups, count, width)
    going.append(start(dqkv_ref, dqkv_hbm, sems.at[6]))
    d_normed = input_back(dqkv_ref, [early_ref.at[1], w_ref.at[0], w_ref.at[1]])
    middle = mid_ref[...].astype(F32)
    d_middle = cot_ref[...].astype(F32) + norm_back(middle, g_ref[1:2], d_normed)
    coming[2].wait()
    finish(going + send_turned(turn_ref, d_middle.astype(BF16), dm_ref, quarters(dm_hbm), sems.at[pl.ds(7, 4)]))


def column_last(plane, cot_hbm, mid_hbm, n_hbm, att_hbm, dqkv_hbm, w_hbm, turn_hbm, out_hbm, *refs):
    keep_hbms, send_hbms, refs = refs[:plane], refs[plane : 2 * plane], refs[2 * plane :]
    out_ref, keep_ref, send_ref, w_ref, turn_ref, flat_ref, dqkv_ref, sems, out_sems = refs
    coming = [
        start(turn_hbm.at[6], turn_ref.at[0], sems.at[0]), start(n_hbm, flat_ref.at[0], sems.at[1]),
        start(dqkv_hbm, dqkv_ref, sems.at[2]), start(att_hbm, flat_ref.at[1], sems.at[3]),
        start(cot_hbm, flat_ref.at[2], sems.at[4]), start(mid_hbm, flat_ref.at[3], sems.at[5]),
        start(w_hbm.at[1, 3], w_ref, sems.at[6]), start(turn_hbm.at[5], turn_ref.at[1], sems.at[7]),
    ]
    finish(coming[:3])
    normed = dot(flat_ref[0], turn_ref[0]).astype(BF16)
    for part in range(3):
        weight_grad(part, normed, third(dqkv_ref, part), keep_ref, send_ref)
    finish(coming[3:])
    attended = dot(flat_ref[1], turn_ref[0]).astype(BF16)
    weight_grad(3, attended, flat_ref[2], keep_ref, send_ref)
    going = send_grads(keep_ref, send_ref, keep_hbms, send_hbms, out_sems)
    output = (flat_ref[3].astype(F32) + dot(flat_ref[1], w_ref[...])).astype(BF16)
    finish(going + send_turned(turn_ref.at[1], output, out_ref, [out_hbm], sems.at[pl.ds(8, 1)]))


def add_pairs(*refs):
    count = len(refs) // 3
    for left, right, target in zip(refs[:count], refs[count : 2 * count], refs[2 * count :]):
        target[...] = (left[...].astype(F32) + right[...].astype(F32)).astype(BF16)


NEAR, FAR, ANY = pltpu.VMEM, pltpu.HBM, None


def call(kernel, ins, outs, scratch):
    def spec(where):
        return pl.BlockSpec(memory_space=pltpu.HBM if where is FAR else pltpu.VMEM)

    def place(item, where):
        return item if where is ANY else pltpu.with_memory_space_constraint(item, where)

    return pl.pallas_call(
        kernel,
        in_specs=[spec(where) for _, where in ins],
        out_specs=[spec(where) for _, where in outs],
        out_shape=[jax.ShapeDtypeStruct(shape, BF16) if where is ANY else where(shape, BF16) for shape, where in outs],
        scratch_shapes=scratch,
        compiler_params=pltpu.CompilerParams(vmem_limit_bytes=48 * 1024 * 1024),
        cost_estimate=pl.CostEstimate(flops=1 << 20, bytes_accessed=1 << 10, transcendentals=0),
    )(*[place(item, where) for item, where in ins])


def swap(item, axis, count, step):
    return lax.ppermute(item, axis, [(at, at ^ step) for at in range(count)])


def chip_sums(keeps, sends, col_parts):
    got = [swap(send, "col", col_parts, 1) for send in sends]
    return call(add_pairs, [(item, ANY) for item in keeps + got], [(item.shape, ANY) for item in keeps], [])


def plane_pieces(sums, plane, core):
    return [item if step == 0 else swap(item, "col", plane * core, step * core) for step, item in enumerate(sums)]


def last_sums(pieces, row_parts):
    parts, size, channels = pieces[0].shape
    held = sum(piece.astype(F32) for piece in pieces).astype(BF16)
    held = held.reshape(parts, row_parts, size // row_parts, channels)
    result = held[:, 0].astype(F32)
    for step in range(1, row_parts):
        result = result + swap(held[:, step], "row", row_parts, step).astype(F32)
    return result


def body(row_parts, col_parts, field, cotangent, gains, weights):
    high, wide, channels = field.shape
    core = 2
    plane = col_parts // core
    rows = high // col_parts
    cols = wide // row_parts
    tokens = high * wide
    height = high * row_parts
    length = wide * col_parts
    width = channels // HEADS
    together = min(cols, max(1, 256 // height))
    devices = row_parts * col_parts
    my_row = lax.axis_index("row")

    flat, triple = (tokens, channels), (tokens, 3 * channels)
    probs = (rows * HEADS, length, length)
    packed = (4, channels // col_parts, channels)

    def scratch(*shape):
        return pltpu.VMEM(shape, BF16)

    def at(where, *items):
        return [(item, where) for item in items]

    square = scratch(*flat)
    copies = pltpu.SemaphoreType.DMA
    assert channels == tokens
    turns = [
        ((rows, col_parts, row_parts, cols), (2, 1, 0, 3), {}, 0),
        ((row_parts, col_parts, rows, cols), (2, 1, 0, 3), {}, 0),
        ((height, cols), (1, 0), {}, 0),
        ((cols, height), (1, 0), {}, 0),
        ((row_parts, high, cols), (2, 0, 1), {0: "row"}, 0),
        ((cols, row_parts, high), (1, 2, 0), {}, 0),
        ((row_parts, plane, core, channels // devices), (2, 1, 0, 3), {0: "row", 1: "plane", 2: "core"}, 1),
    ]

    def all_to_all(item):
        item = item.reshape(devices, rows * cols, channels)
        return lax.all_to_all(item, ("row", "col"), 0, 0, tiled=True).reshape(tokens, channels)

    x = lax.all_to_all(field.reshape(col_parts, rows, wide, channels), "col", 0, 0, tiled=True)
    cots = []
    for step in range(row_parts):
        piece = lax.dynamic_slice_in_dim(cotangent, (my_row ^ step) * cols, cols, axis=1)
        piece = piece if step == 0 else swap(piece, "row", row_parts, step)
        cots.append(piece.reshape(high * cols, channels))
    turn, = call(
        functools.partial(set_up, turns), [], at(FAR, (len(turns), *flat)),
        [scratch(len(turns), *flat), copies((len(turns),))],
    )

    sizes = (rows, length, width)
    mid, normed, query, key, value, attended, prob = call(
        functools.partial(row_forward, sizes),
        at(ANY, x, gains) + at(FAR, weights, turn), at(FAR, *[flat] * 6, probs),
        [scratch(4, *flat)] + [square] * 7 + [scratch(*probs), copies((5,)), copies((6,)), copies((4,))],
    )
    mid, cots = lax.optimization_barrier((mid, cots))
    cot, d_att, early = call(
        functools.partial(column_first, row_parts),
        at(ANY, *cots) + at(FAR, weights, turn), at(NEAR, flat, flat, (2, *flat)), [square, square, copies((4,))],
    )
    mid = all_to_all(mid)

    count = together * height
    d_mid, *kept = call(
        functools.partial(column_main, (height, cols, width, together)),
        at(ANY, mid) + at(NEAR, cot, d_att, early) + at(ANY, gains) + at(FAR, weights, turn),
        at(FAR, flat, flat, flat, flat, triple),
        [scratch(2, *flat)] + [square] * 5 + [scratch(*triple)] + [square] * 3
        + [scratch(cols // together * HEADS, count, count), copies((11,))],
    )
    d_mid = all_to_all(d_mid)
    out, *grads = call(
        functools.partial(column_last, plane),
        at(FAR, cot, *kept, weights, turn), at(FAR, flat, *[packed] * (2 * plane)),
        [square, scratch(plane, *packed), scratch(plane, *packed), square, scratch(2, *flat), scratch(4, *flat),
         scratch(*triple), copies((9,)), copies((2 * plane,))],
    )
    pieces_b = plane_pieces(chip_sums(grads[:plane], grads[plane:], col_parts), plane, core)
    d_mid, out = lax.optimization_barrier((d_mid, out))
    d_mid, dqkv, *grads = call(
        functools.partial(row_back, (rows, length, width, plane)),
        at(ANY, d_mid) + at(FAR, weights, turn, normed, query, key, value, attended, prob),
        at(ANY, flat) + at(FAR, triple, *[packed] * (2 * plane)),
        [square, scratch(2, *flat)] + [square] * 5 + [scratch(*probs), square, scratch(*triple)]
        + [scratch(plane, *packed), scratch(plane, *packed), copies((11,)), copies((2 * plane,))],
    )
    out, d_mid = lax.optimization_barrier((out, d_mid))
    out = lax.all_to_all(out.reshape(row_parts, high, cols, channels), "row", 0, 0, tiled=True)
    pieces_a = plane_pieces(chip_sums(grads[:plane], grads[plane:], col_parts), plane, core)
    dqkv, pieces_b, out = lax.optimization_barrier((dqkv, pieces_b, out))
    grads_b = last_sums(pieces_b, row_parts)
    field_grad, = call(
        field_back, at(ANY, x, d_mid, gains) + at(FAR, dqkv, weights), at(FAR, x.shape),
        [scratch(*triple), scratch(3, *flat), scratch(*x.shape), copies((3,))],
    )
    field_grad, pieces_a = lax.optimization_barrier((field_grad, pieces_a))
    field_grad = lax.all_to_all(field_grad, "col", 0, 0, tiled=True).reshape(high, wide, channels)
    grads_a = last_sums(pieces_a, row_parts)
    output = out.transpose(1, 0, 2, 3).reshape(high, wide, channels)
    return output, field_grad, jnp.concatenate([grads_a, grads_b], axis=0)


def solution(mesh):
    return jax.shard_map(
        functools.partial(body, mesh.shape["row"], mesh.shape["col"]),
        mesh=mesh,
        in_specs=(P("row", "col", None), P("row", "col", None), P(), P()),
        out_specs=(P("row", "col", None), P("row", "col", None), P(None, ("row", "col"), None)),
        check_vma=False,
    )
```

```python
import functools
import math

import jax
import jax.numpy as jnp
from jax import lax
from jax.experimental import pallas as pl
from jax.experimental.pallas import tpu as pltpu
from jax.sharding import PartitionSpec as P

HEADS = 8
eps = 1e-05
F32 = jnp.float32
BF16 = jnp.bfloat16


def log2(n):
    assert n & (n - 1) == 0
    return n.bit_length() - 1


def dot(left, right):
    return jnp.dot(left, right, preferred_element_type=F32)


def dot_nt(left, right):
    return lax.dot_general(left, right, (((1,), (1,)), ((), ())), preferred_element_type=F32)


def dot_tn(left, right):
    return lax.dot_general(left, right, (((0,), (0,)), ((), ())), preferred_element_type=F32)


def one_hot(sizes, order, me=None, lead=0):
    total = math.prod(sizes)
    index = lax.broadcasted_iota(jnp.int32, (total, total), lead)
    found = {}
    for axis in reversed(order):
        found[axis] = index & (sizes[axis] - 1)
        index = index >> log2(sizes[axis])
    source, shift = None, 0
    for axis in reversed(range(len(sizes))):
        digit = found[axis] << shift
        source = digit if source is None else source | digit
        shift += log2(sizes[axis])
    if me:
        place, shift = 0, 0
        for axis in reversed(range(len(sizes))):
            if axis in me:
                place = place | (me[axis] << shift)
            shift += log2(sizes[axis])
        source = source ^ place
    hit = source == lax.broadcasted_iota(jnp.int32, (total, total), 1 - lead)
    return jnp.where(hit, 1.0, 0.0).astype(BF16)


def statistics(values):
    average = jnp.mean(values, axis=-1, keepdims=True)
    centred = values - average
    spread = jnp.mean(centred * centred, axis=-1, keepdims=True)
    return centred, lax.rsqrt(spread + eps)


def norm_back(values, gain, d_normed):
    centred, inverse = statistics(values)
    unit = centred * inverse
    scaled = d_normed * gain
    return inverse * (
        scaled
        - jnp.mean(scaled, axis=-1, keepdims=True)
        - unit * jnp.mean(scaled * unit, axis=-1, keepdims=True)
    )


def head_lanes(count, width):
    return lax.broadcasted_iota(jnp.int32, (count, 2 * width), 1) < width


def attention_forward(q_ref, k_ref, v_ref, att_ref, p_ref, groups, count, width, span):
    first = head_lanes(count, width)
    pairs = HEADS // 2
    scale = width ** (-0.5)

    def step(index, carry):
        group, pair = index // pairs, index % pairs
        rows = pl.ds(pl.multiple_of(group * count, count), count)
        lanes = pl.ds(pl.multiple_of(pair * 2 * width, 2 * width), 2 * width)
        query, key, value = q_ref[rows, lanes] * scale, k_ref[rows, lanes], v_ref[rows, lanes]
        zero = jnp.zeros_like(query)
        total = jnp.zeros((count, 2 * width), F32)
        for half in range(2):
            mine = first if half == 0 else jnp.logical_not(first)
            scores = dot_nt(key, jnp.where(mine, query, zero))
            if span < count:
                shift = log2(span)
                same = (lax.broadcasted_iota(jnp.int32, (count, count), 0) >> shift) == (
                    lax.broadcasted_iota(jnp.int32, (count, count), 1) >> shift
                )
                scores = jnp.where(same, scores, -jnp.inf)
            expo = jnp.exp(scores - jnp.max(scores, axis=0, keepdims=True))
            probs = (expo * (1.0 / jnp.sum(expo, axis=0, keepdims=True))).astype(BF16)
            p_ref[index * 2 + half] = probs
            total += dot_tn(probs, jnp.where(mine, value, zero))
        att_ref[rows, lanes] = total.astype(BF16)
        return carry

    lax.fori_loop(0, groups * pairs, step, 0, unroll=2)


def attention_back(q_ref, k_ref, v_ref, p_ref, da_ref, dqkv_ref, groups, count, width):
    first = head_lanes(count, width)
    pairs = HEADS // 2
    channels = HEADS * width
    scale = width ** (-0.5)

    def step(index, carry):
        group, pair = index // pairs, index % pairs
        rows = pl.ds(pl.multiple_of(group * count, count), count)
        lanes = pl.ds(pl.multiple_of(pair * 2 * width, 2 * width), 2 * width)
        query, key, value = q_ref[rows, lanes] * scale, k_ref[rows, lanes], v_ref[rows, lanes]
        d_out = da_ref[rows, lanes]
        zero = jnp.zeros_like(query)
        d_query = jnp.zeros((count, 2 * width), F32)
        d_key, d_value = d_query, d_query
        for half in range(2):
            mine = first if half == 0 else jnp.logical_not(first)
            probs = p_ref[index * 2 + half]
            d_mine = jnp.where(mine, d_out, zero)
            d_probs = dot_nt(value, d_mine)
            probs32 = probs.astype(F32)
            weighted = probs32 * d_probs
            total = jnp.sum(weighted, axis=0, keepdims=True)
            d_scores = (weighted - probs32 * total).astype(BF16)
            d_query += dot_tn(d_scores, jnp.where(mine, key, zero))
            d_key += dot(d_scores, jnp.where(mine, query, zero))
            d_value += dot(probs, d_mine)
        for part, item in enumerate((d_query * scale, d_key, d_value)):
            at = pl.ds(pl.multiple_of(part * channels + pair * 2 * width, 2 * width), 2 * width)
            dqkv_ref[rows, at] = item.astype(BF16)
        return carry

    lax.fori_loop(0, groups * pairs, step, 0, unroll=2)


def start(source, target, sem):
    copy = pltpu.make_async_copy(source, target, sem)
    copy.start()
    return copy


def finish(copies):
    for copy in copies:
        copy.wait()


def set_up(turns, turn_hbm, turn_ref, sems):
    my_row, my_col = lax.axis_index("row"), lax.axis_index("col")
    places = {"row": my_row, "plane": my_col >> 1, "core": my_col & 1}
    going = []
    for at, (sizes, order, me, lead) in enumerate(turns):
        turn_ref[at] = one_hot(sizes, order, {axis: places[name] for axis, name in me.items()}, lead)
        going.append(start(turn_ref.at[at], turn_hbm.at[at], sems.at[at]))
    finish(going)


def weight_grad(part, left, right, keep_ref, send_ref):
    plane, _, size, _ = keep_ref.shape
    whole = dot_tn(left, right).astype(BF16)
    for group in range(plane):
        send_ref[group, part] = whole[(plane + group) * size : (plane + group + 1) * size]
        keep_ref[group, part] = whole[group * size : (group + 1) * size]


def send_grads(keep_ref, send_ref, keep_hbms, send_hbms, sems):
    plane = keep_ref.shape[0]
    going = [start(send_ref.at[at], send_hbms[at], sems.at[at]) for at in range(plane)]
    return going + [start(keep_ref.at[at], keep_hbms[at], sems.at[plane + at]) for at in range(plane)]


def third(ref, part):
    channels = ref.shape[-1] // 3
    return ref[:, part * channels : (part + 1) * channels]


def send_turned(turn_ref, values, stage_ref, targets, sems):
    size = values.shape[0] // len(targets)
    going = []
    for at, target in enumerate(targets):
        piece = pl.ds(at * size, size)
        stage_ref[piece] = dot(turn_ref[piece], values).astype(BF16)
        going.append(start(stage_ref.at[piece], target, sems.at[at]))
    return going


def quarters(ref):
    size = ref.shape[0] // 4
    return [ref.at[pl.ds(at * size, size)] for at in range(4)]


def input_back(dqkv_ref, w_refs):
    total = dot_nt(third(dqkv_ref, 0), w_refs[0][...])
    total += dot_nt(third(dqkv_ref, 1), w_refs[1][...])
    total += dot_nt(third(dqkv_ref, 2), w_refs[2][...])
    return total.astype(BF16).astype(F32)


def rows_of(x_ref):
    _, rows, _, channels = x_ref.shape
    length = x_ref.shape[0] * x_ref.shape[2]
    pieces = [x_ref[:, i].reshape(length, channels) for i in range(rows)]
    return jnp.concatenate(pieces, axis=0).astype(F32)


def row_forward(sizes, x_ref, g_ref, w_hbm, turn_hbm, mid_hbm, n_hbm, q_hbm, k_hbm, v_hbm, att_hbm, p_hbm,
                w_ref, turn_ref, mid_ref, n_ref, q_ref, k_ref, v_ref, att_ref, p_ref, in_sems, out_sems, sems):
    rows, length, width = sizes
    coming = [start(w_hbm.at[0, part], w_ref.at[part], in_sems.at[part]) for part in range(4)]
    coming.append(start(turn_hbm.at[0], turn_ref, in_sems.at[4]))
    centred, inverse = statistics(rows_of(x_ref))
    normed = (centred * inverse * g_ref[0:1]).astype(BF16)
    n_ref[...] = normed
    going = [start(n_ref, n_hbm, out_sems.at[0])]
    for part, (ref, hbm) in enumerate(((q_ref, q_hbm), (k_ref, k_hbm), (v_ref, v_hbm))):
        coming[part].wait()
        ref[...] = dot(normed, w_ref[part]).astype(BF16)
        going.append(start(ref, hbm, out_sems.at[1 + part]))
    attention_forward(q_ref, k_ref, v_ref, att_ref, p_ref, rows, length, width, length)
    going.append(start(p_ref, p_hbm, out_sems.at[5]))
    going.append(start(att_ref, att_hbm, out_sems.at[4]))
    coming[3].wait()
    middle = (rows_of(x_ref) + dot(att_ref[...], w_ref[3])).astype(BF16)
    coming[4].wait()
    finish(going + send_turned(turn_ref, middle, mid_ref, quarters(mid_hbm), sems))


def row_back(sizes, d_ref, w_hbm, turn_hbm, n_hbm, q_hbm, k_hbm, v_hbm, att_hbm, p_hbm, *refs):
    rows, length, width, plane = sizes
    dm_ref, dqkv_hbm, keep_hbms, send_hbms = refs[0], refs[1], refs[2 : 2 + plane], refs[2 + plane : 2 + 2 * plane]
    w_ref, turn_ref, n_ref, q_ref, k_ref, v_ref, att_ref, p_ref, da_ref, dqkv_ref = refs[2 + 2 * plane : -4]
    keep_ref, send_ref, sems, out_sems = refs[-4:]
    half = p_ref.shape[0] // 2
    coming = [
        start(turn_hbm.at[1], turn_ref.at[0], sems.at[0]), start(w_hbm.at[0, 3], w_ref, sems.at[1]),
        start(v_hbm, v_ref, sems.at[2]), start(k_hbm, k_ref, sems.at[3]), start(q_hbm, q_ref, sems.at[4]),
        start(p_hbm.at[pl.ds(0, half)], p_ref.at[pl.ds(0, half)], sems.at[5]),
        start(p_hbm.at[pl.ds(half, half)], p_ref.at[pl.ds(half, half)], sems.at[6]),
        start(turn_hbm.at[6], turn_ref.at[1], sems.at[7]), start(att_hbm, att_ref, sems.at[8]),
        start(n_hbm, n_ref, sems.at[9]),
    ]
    coming[0].wait()
    d_middle = dot(turn_ref[0], d_ref[...]).astype(BF16)
    dm_ref[...] = d_middle
    coming[1].wait()
    da_ref[...] = dot_nt(d_middle, w_ref[...]).astype(BF16)
    finish(coming[2:7])
    attention_back(q_ref, k_ref, v_ref, p_ref, da_ref, dqkv_ref, rows, length, width)
    going = [start(dqkv_ref, dqkv_hbm, sems.at[10])]
    finish(coming[7:])
    normed = dot(n_ref[...], turn_ref[1]).astype(BF16)
    for part in range(3):
        weight_grad(part, normed, third(dqkv_ref, part), keep_ref, send_ref)
    attended = dot(att_ref[...], turn_ref[1]).astype(BF16)
    weight_grad(3, attended, dm_ref[...], keep_ref, send_ref)
    finish(going + send_grads(keep_ref, send_ref, keep_hbms, send_hbms, out_sems))


def field_back(x_ref, dm_ref, g_ref, dqkv_hbm, w_hbm, fg_hbm, dqkv_ref, w_ref, fg_ref, sems):
    coming = [start(dqkv_hbm, dqkv_ref, sems.at[0]), start(w_hbm.at[0, 0:3], w_ref, sems.at[1])]
    _, rows, _, channels = x_ref.shape
    length = x_ref.shape[0] * x_ref.shape[2]
    finish(coming)
    d_normed = input_back(dqkv_ref, [w_ref.at[part] for part in range(3)])
    result = dm_ref[...].astype(F32) + norm_back(rows_of(x_ref), g_ref[0:1], d_normed)
    result = result.astype(BF16)
    for i in range(rows):
        piece = result[i * length : (i + 1) * length]
        fg_ref[:, i] = piece.reshape(fg_ref.shape[0], fg_ref.shape[2], channels)
    start(fg_ref, fg_hbm, sems.at[2]).wait()


def column_first(parts, *refs):
    c_refs, (w_hbm, turn_hbm, cot_ref, da_ref, early_ref, w_ref, turn_ref, sems) = refs[:parts], refs[parts:]
    coming = [
        start(turn_hbm.at[4], turn_ref, sems.at[0]), start(w_hbm.at[1, 3], w_ref, sems.at[1]),
        start(turn_hbm.at[2], early_ref.at[0], sems.at[2]), start(w_hbm.at[1, 0], early_ref.at[1], sems.at[3]),
    ]
    cotangent = jnp.concatenate([ref[...] for ref in c_refs], axis=0)
    coming[0].wait()
    cotangent = dot(turn_ref[...], cotangent).astype(BF16)
    cot_ref[...] = cotangent
    coming[1].wait()
    da_ref[...] = dot_nt(cotangent, w_ref[...]).astype(BF16)
    finish(coming[2:])


def column_main(sizes, m_ref, cot_ref, da_ref, early_ref, g_ref, w_hbm, turn_hbm,
                dm_hbm, mid_hbm, n_hbm, att_hbm, dqkv_hbm,
                w_ref, turn_ref, dm_ref, mid_ref, n_ref, att_ref, dqkv_ref, q_ref, k_ref, v_ref, p_ref, sems):
    height, cols, width, together = sizes
    coming = [
        start(w_hbm.at[1, 1], w_ref.at[0], sems.at[0]), start(w_hbm.at[1, 2], w_ref.at[1], sems.at[1]),
        start(turn_hbm.at[3], turn_ref, sems.at[2]),
    ]
    middle = dot(early_ref[0], m_ref[...])
    mid_ref[...] = middle.astype(BF16)
    going = [start(mid_ref, mid_hbm, sems.at[3])]
    centred, inverse = statistics(middle)
    normed = (centred * inverse * g_ref[1:2]).astype(BF16)
    n_ref[...] = normed
    going.append(start(n_ref, n_hbm, sems.at[4]))
    q_ref[...] = dot(normed, early_ref[1]).astype(BF16)
    coming[0].wait()
    k_ref[...] = dot(normed, w_ref[0]).astype(BF16)
    coming[1].wait()
    v_ref[...] = dot(normed, w_ref[1]).astype(BF16)
    count = together * height
    groups = cols // together
    attention_forward(q_ref, k_ref, v_ref, att_ref, p_ref, groups, count, width, height)
    going.append(start(att_ref, att_hbm, sems.at[5]))
    attention_back(q_ref, k_ref, v_ref, p_ref, da_ref, dqkv_ref, groups, count, width)
    going.append(start(dqkv_ref, dqkv_hbm, sems.at[6]))
    d_normed = input_back(dqkv_ref, [early_ref.at[1], w_ref.at[0], w_ref.at[1]])
    middle = mid_ref[...].astype(F32)
    d_middle = cot_ref[...].astype(F32) + norm_back(middle, g_ref[1:2], d_normed)
    coming[2].wait()
    finish(going + send_turned(turn_ref, d_middle.astype(BF16), dm_ref, quarters(dm_hbm), sems.at[pl.ds(7, 4)]))


def column_last(parts, plane, cot_hbm, mid_hbm, n_hbm, att_hbm, dqkv_hbm, w_hbm, turn_hbm, *refs):
    out_hbms, refs = refs[:parts], refs[parts:]
    keep_hbms, send_hbms, refs = refs[:plane], refs[plane : 2 * plane], refs[2 * plane :]
    out_ref, keep_ref, send_ref, w_ref, turn_ref, flat_ref, dqkv_ref, sems, out_sems = refs
    coming = [
        start(turn_hbm.at[6], turn_ref.at[0], sems.at[0]), start(n_hbm, flat_ref.at[0], sems.at[1]),
        start(dqkv_hbm, dqkv_ref, sems.at[2]), start(att_hbm, flat_ref.at[1], sems.at[3]),
        start(cot_hbm, flat_ref.at[2], sems.at[4]), start(mid_hbm, flat_ref.at[3], sems.at[5]),
        start(w_hbm.at[1, 3], w_ref, sems.at[6]), start(turn_hbm.at[5], turn_ref.at[1], sems.at[7]),
    ]
    finish(coming[:3])
    normed = dot(flat_ref[0], turn_ref[0]).astype(BF16)
    for part in range(3):
        weight_grad(part, normed, third(dqkv_ref, part), keep_ref, send_ref)
    finish(coming[3:])
    attended = dot(flat_ref[1], turn_ref[0]).astype(BF16)
    weight_grad(3, attended, flat_ref[2], keep_ref, send_ref)
    going = send_grads(keep_ref, send_ref, keep_hbms, send_hbms, out_sems)
    output = (flat_ref[3].astype(F32) + dot(flat_ref[1], w_ref[...])).astype(BF16)
    finish(going + send_turned(turn_ref.at[1], output, out_ref, out_hbms, sems.at[pl.ds(8, parts)]))


def add_pairs(*refs):
    count = len(refs) // 3
    for left, right, target in zip(refs[:count], refs[count : 2 * count], refs[2 * count :]):
        target[...] = (left[...].astype(F32) + right[...].astype(F32)).astype(BF16)


NEAR, FAR, ANY = pltpu.VMEM, pltpu.HBM, None


def call(kernel, ins, outs, scratch):
    def spec(where):
        return pl.BlockSpec(memory_space=pltpu.HBM if where is FAR else pltpu.VMEM)

    def place(item, where):
        return item if where is ANY else pltpu.with_memory_space_constraint(item, where)

    return pl.pallas_call(
        kernel,
        in_specs=[spec(where) for _, where in ins],
        out_specs=[spec(where) for _, where in outs],
        out_shape=[jax.ShapeDtypeStruct(shape, BF16) if where is ANY else where(shape, BF16) for shape, where in outs],
        scratch_shapes=scratch,
        compiler_params=pltpu.CompilerParams(vmem_limit_bytes=48 * 1024 * 1024),
        cost_estimate=pl.CostEstimate(flops=1 << 20, bytes_accessed=1 << 10, transcendentals=0),
    )(*[place(item, where) for item, where in ins])


def swap(item, axis, count, step):
    return lax.ppermute(item, axis, [(at, at ^ step) for at in range(count)])


def chip_sums(keeps, sends, col_parts):
    got = [swap(send, "col", col_parts, 1) for send in sends]
    return call(add_pairs, [(item, ANY) for item in (*keeps, *got)], [(item.shape, ANY) for item in keeps], [])


def plane_pieces(sums, plane, core):
    return [item if step == 0 else swap(item, "col", plane * core, step * core) for step, item in enumerate(sums)]


def last_sums(pieces, row_parts):
    parts, size, channels = pieces[0].shape
    held = sum(piece.astype(F32) for piece in pieces).astype(BF16)
    held = held.reshape(parts, row_parts, size // row_parts, channels)
    result = held[:, 0].astype(F32)
    for step in range(1, row_parts):
        result = result + swap(held[:, step], "row", row_parts, step).astype(F32)
    return result


def body(row_parts, col_parts, field, cotangent, gains, weights):
    high, wide, channels = field.shape
    core = 2
    plane = col_parts // core
    rows = high // col_parts
    cols = wide // row_parts
    tokens = high * wide
    height = high * row_parts
    length = wide * col_parts
    width = channels // HEADS
    together = min(cols, max(1, 256 // height))
    devices = row_parts * col_parts
    my_row = lax.axis_index("row")

    flat, triple = (tokens, channels), (tokens, 3 * channels)
    probs = (rows * HEADS, length, length)
    packed = (4, channels // col_parts, channels)

    def scratch(*shape):
        return pltpu.VMEM(shape, BF16)

    def at(where, *items):
        return [(item, where) for item in items]

    square = scratch(*flat)
    copies = pltpu.SemaphoreType.DMA
    assert channels == tokens
    turns = [
        ((rows, col_parts, row_parts, cols), (2, 1, 0, 3), {}, 0),
        ((row_parts, col_parts, rows, cols), (2, 1, 0, 3), {}, 0),
        ((height, cols), (1, 0), {}, 0),
        ((cols, height), (1, 0), {}, 0),
        ((row_parts, high, cols), (2, 0, 1), {0: "row"}, 0),
        ((cols, row_parts, high), (1, 2, 0), {1: "row"}, 0),
        ((row_parts, plane, core, channels // devices), (2, 1, 0, 3), {0: "row", 1: "plane", 2: "core"}, 1),
    ]

    def all_to_all(item):
        item = item.reshape(devices, rows * cols, channels)
        return lax.all_to_all(item, ("row", "col"), 0, 0, tiled=True).reshape(tokens, channels)

    x = lax.all_to_all(field.reshape(col_parts, rows, wide, channels), "col", 0, 0, tiled=True)
    cots = []
    for step in range(row_parts):
        piece = lax.dynamic_slice_in_dim(cotangent, (my_row ^ step) * cols, cols, axis=1)
        piece = piece if step == 0 else swap(piece, "row", row_parts, step)
        cots.append(piece.reshape(high * cols, channels))
    turn, = call(
        functools.partial(set_up, turns), [], at(FAR, (len(turns), *flat)),
        [scratch(len(turns), *flat), copies((len(turns),))],
    )

    sizes = (rows, length, width)
    mid, normed, query, key, value, attended, prob = call(
        functools.partial(row_forward, sizes),
        at(ANY, x, gains) + at(FAR, weights, turn), at(FAR, *[flat] * 6, probs),
        [scratch(4, *flat)] + [square] * 7 + [scratch(*probs), copies((5,)), copies((6,)), copies((4,))],
    )
    mid, cots = lax.optimization_barrier((mid, cots))
    cot, d_att, early = call(
        functools.partial(column_first, row_parts),
        at(ANY, *cots) + at(FAR, weights, turn), at(NEAR, flat, flat, (2, *flat)), [square, square, copies((4,))],
    )
    mid = all_to_all(mid)

    count = together * height
    d_mid, *kept = call(
        functools.partial(column_main, (height, cols, width, together)),
        at(ANY, mid) + at(NEAR, cot, d_att, early) + at(ANY, gains) + at(FAR, weights, turn),
        at(FAR, flat, flat, flat, flat, triple),
        [scratch(2, *flat)] + [square] * 5 + [scratch(*triple)] + [square] * 3
        + [scratch(cols // together * HEADS, count, count), copies((11,))],
    )
    d_mid = all_to_all(d_mid)
    results = call(
        functools.partial(column_last, row_parts, plane),
        at(FAR, cot, *kept, weights, turn), at(FAR, *[(high * cols, channels)] * row_parts, *[packed] * (2 * plane)),
        [square, scratch(plane, *packed), scratch(plane, *packed), square, scratch(2, *flat), scratch(4, *flat),
         scratch(*triple), copies((8 + row_parts,)), copies((2 * plane,))],
    )
    outs, grads = results[:row_parts], results[row_parts:]
    sums_b = chip_sums(grads[:plane], grads[plane:], col_parts)
    pieces_b = plane_pieces(sums_b, plane, core)
    d_mid, outs, _ = lax.optimization_barrier((d_mid, outs, sums_b))
    early = [item if step == 0 else swap(item, "row", row_parts, step) for step, item in enumerate(outs[:3])]
    results = call(
        functools.partial(row_back, (rows, length, width, plane)),
        at(ANY, d_mid) + at(FAR, weights, turn, normed, query, key, value, attended, prob),
        at(ANY, flat) + at(FAR, triple, *[packed] * (2 * plane)),
        [square, scratch(2, *flat)] + [square] * 5 + [scratch(*probs), square, scratch(*triple)]
        + [scratch(plane, *packed), scratch(plane, *packed), copies((11,)), copies((2 * plane,))],
    )
    (d_mid, dqkv, *grads), pieces_b, early, late = lax.optimization_barrier((results, pieces_b, early, outs[3:]))
    pieces_a = plane_pieces(chip_sums(grads[:plane], grads[plane:], col_parts), plane, core)
    pieces_out = [*early] + [swap(item, "row", row_parts, 3 + step) for step, item in enumerate(late)]
    grads_b = last_sums(pieces_b, row_parts)
    field_grad, = call(
        field_back, at(ANY, x, d_mid, gains) + at(FAR, dqkv, weights), at(FAR, x.shape),
        [scratch(*triple), scratch(3, *flat), scratch(*x.shape), copies((3,))],
    )
    field_grad, pieces_a, grads_b, pieces_out = lax.optimization_barrier((field_grad, pieces_a, grads_b, pieces_out))
    field_grad = lax.all_to_all(field_grad, "col", 0, 0, tiled=True).reshape(high, wide, channels)
    output = jnp.zeros((high, wide, channels), BF16)
    for step, piece in enumerate(pieces_out):
        piece = piece.reshape(high, cols, channels)
        output = lax.dynamic_update_slice_in_dim(output, piece, (my_row ^ step) * cols, axis=1)
    grads_a = last_sums(pieces_a, row_parts)
    return output, field_grad, jnp.concatenate([grads_a, grads_b], axis=0)


def solution(mesh):
    return jax.shard_map(
        functools.partial(body, mesh.shape["row"], mesh.shape["col"]),
        mesh=mesh,
        in_specs=(P("row", "col", None), P("row", "col", None), P(), P()),
        out_specs=(P("row", "col", None), P("row", "col", None), P(None, ("row", "col"), None)),
        check_vma=False,
    )
```

```python
import functools
import math

import jax
import jax.numpy as jnp
from jax import lax
from jax.experimental import pallas as pl
from jax.experimental.pallas import tpu as pltpu
from jax.sharding import PartitionSpec as P

HEADS = 8
eps = 1e-05
F32 = jnp.float32
BF16 = jnp.bfloat16


def log2(n):
    assert n & (n - 1) == 0
    return n.bit_length() - 1


def dot(left, right):
    return jnp.dot(left, right, preferred_element_type=F32)


def dot_nt(left, right):
    return lax.dot_general(left, right, (((1,), (1,)), ((), ())), preferred_element_type=F32)


def dot_tn(left, right):
    return lax.dot_general(left, right, (((0,), (0,)), ((), ())), preferred_element_type=F32)


def one_hot(sizes, order, me=None, lead=0):
    total = math.prod(sizes)
    index = lax.broadcasted_iota(jnp.int32, (total, total), lead)
    found = {}
    for axis in reversed(order):
        found[axis] = index & (sizes[axis] - 1)
        index = index >> log2(sizes[axis])
    source, shift = None, 0
    for axis in reversed(range(len(sizes))):
        digit = found[axis] << shift
        source = digit if source is None else source | digit
        shift += log2(sizes[axis])
    if me:
        place, shift = 0, 0
        for axis in reversed(range(len(sizes))):
            if axis in me:
                place = place | (me[axis] << shift)
            shift += log2(sizes[axis])
        source = source ^ place
    hit = source == lax.broadcasted_iota(jnp.int32, (total, total), 1 - lead)
    return jnp.where(hit, 1.0, 0.0).astype(BF16)


def statistics(values):
    average = jnp.mean(values, axis=-1, keepdims=True)
    centred = values - average
    spread = jnp.mean(centred * centred, axis=-1, keepdims=True)
    return centred, lax.rsqrt(spread + eps)


def norm_back(values, gain, d_normed):
    centred, inverse = statistics(values)
    unit = centred * inverse
    scaled = d_normed * gain
    return inverse * (
        scaled
        - jnp.mean(scaled, axis=-1, keepdims=True)
        - unit * jnp.mean(scaled * unit, axis=-1, keepdims=True)
    )


def head_lanes(count, width):
    return lax.broadcasted_iota(jnp.int32, (count, 2 * width), 1) < width


def attention_forward(q_ref, k_ref, v_ref, att_ref, p_ref, groups, count, width, span):
    first = head_lanes(count, width)
    pairs = HEADS // 2
    scale = width ** (-0.5)

    def step(index, carry):
        group, pair = index // pairs, index % pairs
        rows = pl.ds(pl.multiple_of(group * count, count), count)
        lanes = pl.ds(pl.multiple_of(pair * 2 * width, 2 * width), 2 * width)
        query, key, value = q_ref[rows, lanes] * scale, k_ref[rows, lanes], v_ref[rows, lanes]
        zero = jnp.zeros_like(query)
        total = jnp.zeros((count, 2 * width), F32)
        for half in range(2):
            mine = first if half == 0 else jnp.logical_not(first)
            scores = dot_nt(key, jnp.where(mine, query, zero))
            if span < count:
                shift = log2(span)
                same = (lax.broadcasted_iota(jnp.int32, (count, count), 0) >> shift) == (
                    lax.broadcasted_iota(jnp.int32, (count, count), 1) >> shift
                )
                scores = jnp.where(same, scores, -jnp.inf)
            expo = jnp.exp(scores - jnp.max(scores, axis=0, keepdims=True))
            probs = (expo * (1.0 / jnp.sum(expo, axis=0, keepdims=True))).astype(BF16)
            p_ref[index * 2 + half] = probs
            total += dot_tn(probs, jnp.where(mine, value, zero))
        att_ref[rows, lanes] = total.astype(BF16)
        return carry

    lax.fori_loop(0, groups * pairs, step, 0, unroll=2)


def attention_back(q_ref, k_ref, v_ref, p_ref, da_ref, dqkv_ref, groups, count, width):
    first = head_lanes(count, width)
    pairs = HEADS // 2
    channels = HEADS * width
    scale = width ** (-0.5)

    def step(index, carry):
        group, pair = index // pairs, index % pairs
        rows = pl.ds(pl.multiple_of(group * count, count), count)
        lanes = pl.ds(pl.multiple_of(pair * 2 * width, 2 * width), 2 * width)
        query, key, value = q_ref[rows, lanes] * scale, k_ref[rows, lanes], v_ref[rows, lanes]
        d_out = da_ref[rows, lanes]
        zero = jnp.zeros_like(query)
        d_query = jnp.zeros((count, 2 * width), F32)
        d_key, d_value = d_query, d_query
        for half in range(2):
            mine = first if half == 0 else jnp.logical_not(first)
            probs = p_ref[index * 2 + half]
            d_mine = jnp.where(mine, d_out, zero)
            d_probs = dot_nt(value, d_mine)
            probs32 = probs.astype(F32)
            weighted = probs32 * d_probs
            total = jnp.sum(weighted, axis=0, keepdims=True)
            d_scores = (weighted - probs32 * total).astype(BF16)
            d_query += dot_tn(d_scores, jnp.where(mine, key, zero))
            d_key += dot(d_scores, jnp.where(mine, query, zero))
            d_value += dot(probs, d_mine)
        for part, item in enumerate((d_query * scale, d_key, d_value)):
            at = pl.ds(pl.multiple_of(part * channels + pair * 2 * width, 2 * width), 2 * width)
            dqkv_ref[rows, at] = item.astype(BF16)
        return carry

    lax.fori_loop(0, groups * pairs, step, 0, unroll=2)


def start(source, target, sem):
    copy = pltpu.make_async_copy(source, target, sem)
    copy.start()
    return copy


def finish(copies):
    for copy in copies:
        copy.wait()


def set_up(turns, turn_hbm, turn_ref, sems):
    my_row, my_col = lax.axis_index("row"), lax.axis_index("col")
    places = {"row": my_row, "plane": my_col >> 1, "core": my_col & 1}
    going = []
    for at, (sizes, order, me, lead) in enumerate(turns):
        turn_ref[at] = one_hot(sizes, order, {axis: places[name] for axis, name in me.items()}, lead)
        going.append(start(turn_ref.at[at], turn_hbm.at[at], sems.at[at]))
    finish(going)


def weight_grad(part, left, right, keep_ref, send_ref):
    plane, _, size, _ = keep_ref.shape
    whole = dot_tn(left, right).astype(BF16)
    for group in range(plane):
        send_ref[group, part] = whole[(plane + group) * size : (plane + group + 1) * size]
        keep_ref[group, part] = whole[group * size : (group + 1) * size]


def send_grads(keep_ref, send_ref, keep_hbms, send_hbms, sems):
    plane = keep_ref.shape[0]
    going = [start(send_ref.at[at], send_hbms[at], sems.at[at]) for at in range(plane)]
    return going + [start(keep_ref.at[at], keep_hbms[at], sems.at[plane + at]) for at in range(plane)]


def third(ref, part):
    channels = ref.shape[-1] // 3
    return ref[:, part * channels : (part + 1) * channels]


def send_turned(turn_ref, values, stage_ref, targets, sems):
    size = values.shape[0] // len(targets)
    going = []
    for at, target in enumerate(targets):
        piece = pl.ds(at * size, size)
        stage_ref[piece] = dot(turn_ref[piece], values).astype(BF16)
        going.append(start(stage_ref.at[piece], target, sems.at[at]))
    return going


def quarters(ref):
    size = ref.shape[0] // 4
    return [ref.at[pl.ds(at * size, size)] for at in range(4)]


def input_back(dqkv_ref, w_refs):
    total = dot_nt(third(dqkv_ref, 0), w_refs[0][...])
    total += dot_nt(third(dqkv_ref, 1), w_refs[1][...])
    total += dot_nt(third(dqkv_ref, 2), w_refs[2][...])
    return total.astype(BF16).astype(F32)


def rows_of(x_ref):
    _, rows, _, channels = x_ref.shape
    length = x_ref.shape[0] * x_ref.shape[2]
    pieces = [x_ref[:, i].reshape(length, channels) for i in range(rows)]
    return jnp.concatenate(pieces, axis=0).astype(F32)


def row_forward(sizes, x_ref, g_ref, w_hbm, turn_hbm, mid_hbm, n_hbm, q_hbm, k_hbm, v_hbm, att_hbm, p_hbm,
                w_ref, turn_ref, mid_ref, n_ref, q_ref, k_ref, v_ref, att_ref, p_ref, in_sems, out_sems, sems):
    rows, length, width = sizes
    coming = [start(w_hbm.at[0, part], w_ref.at[part], in_sems.at[part]) for part in range(4)]
    coming.append(start(turn_hbm.at[0], turn_ref, in_sems.at[4]))
    centred, inverse = statistics(rows_of(x_ref))
    normed = (centred * inverse * g_ref[0:1]).astype(BF16)
    n_ref[...] = normed
    going = [start(n_ref, n_hbm, out_sems.at[0])]
    for part, (ref, hbm) in enumerate(((q_ref, q_hbm), (k_ref, k_hbm), (v_ref, v_hbm))):
        coming[part].wait()
        ref[...] = dot(normed, w_ref[part]).astype(BF16)
        going.append(start(ref, hbm, out_sems.at[1 + part]))
    attention_forward(q_ref, k_ref, v_ref, att_ref, p_ref, rows, length, width, length)
    going.append(start(p_ref, p_hbm, out_sems.at[5]))
    going.append(start(att_ref, att_hbm, out_sems.at[4]))
    coming[3].wait()
    middle = (rows_of(x_ref) + dot(att_ref[...], w_ref[3])).astype(BF16)
    coming[4].wait()
    finish(going + send_turned(turn_ref, middle, mid_ref, quarters(mid_hbm), sems))


def row_back(sizes, d_ref, w_hbm, turn_hbm, n_hbm, q_hbm, k_hbm, v_hbm, att_hbm, p_hbm, *refs):
    rows, length, width, plane = sizes
    dm_ref, dqkv_hbm, keep_hbms, send_hbms = refs[0], refs[1], refs[2 : 2 + plane], refs[2 + plane : 2 + 2 * plane]
    w_ref, turn_ref, n_ref, q_ref, k_ref, v_ref, att_ref, p_ref, da_ref, dqkv_ref = refs[2 + 2 * plane : -4]
    keep_ref, send_ref, sems, out_sems = refs[-4:]
    half = p_ref.shape[0] // 2
    coming = [
        start(turn_hbm.at[1], turn_ref.at[0], sems.at[0]), start(w_hbm.at[0, 3], w_ref, sems.at[1]),
        start(v_hbm, v_ref, sems.at[2]), start(k_hbm, k_ref, sems.at[3]), start(q_hbm, q_ref, sems.at[4]),
        start(p_hbm.at[pl.ds(0, half)], p_ref.at[pl.ds(0, half)], sems.at[5]),
        start(p_hbm.at[pl.ds(half, half)], p_ref.at[pl.ds(half, half)], sems.at[6]),
        start(turn_hbm.at[6], turn_ref.at[1], sems.at[7]), start(att_hbm, att_ref, sems.at[8]),
        start(n_hbm, n_ref, sems.at[9]),
    ]
    coming[0].wait()
    d_middle = dot(turn_ref[0], d_ref[...]).astype(BF16)
    dm_ref[...] = d_middle
    coming[1].wait()
    da_ref[...] = dot_nt(d_middle, w_ref[...]).astype(BF16)
    finish(coming[2:7])
    attention_back(q_ref, k_ref, v_ref, p_ref, da_ref, dqkv_ref, rows, length, width)
    going = [start(dqkv_ref, dqkv_hbm, sems.at[10])]
    finish(coming[7:])
    normed = dot(n_ref[...], turn_ref[1]).astype(BF16)
    for part in range(3):
        weight_grad(part, normed, third(dqkv_ref, part), keep_ref, send_ref)
    attended = dot(att_ref[...], turn_ref[1]).astype(BF16)
    weight_grad(3, attended, dm_ref[...], keep_ref, send_ref)
    finish(going + send_grads(keep_ref, send_ref, keep_hbms, send_hbms, out_sems))


def field_back(x_ref, dm_ref, g_ref, dqkv_hbm, w_hbm, fg_hbm, dqkv_ref, w_ref, fg_ref, sems):
    coming = [start(dqkv_hbm, dqkv_ref, sems.at[0]), start(w_hbm.at[0, 0:3], w_ref, sems.at[1])]
    _, rows, _, channels = x_ref.shape
    length = x_ref.shape[0] * x_ref.shape[2]
    finish(coming)
    d_normed = input_back(dqkv_ref, [w_ref.at[part] for part in range(3)])
    result = dm_ref[...].astype(F32) + norm_back(rows_of(x_ref), g_ref[0:1], d_normed)
    result = result.astype(BF16)
    for i in range(rows):
        piece = result[i * length : (i + 1) * length]
        fg_ref[:, i] = piece.reshape(fg_ref.shape[0], fg_ref.shape[2], channels)
    start(fg_ref, fg_hbm, sems.at[2]).wait()


def column_first(parts, *refs):
    c_refs, (w_hbm, turn_hbm, cot_ref, da_ref, early_ref, w_ref, turn_ref, sems) = refs[:parts], refs[parts:]
    coming = [
        start(turn_hbm.at[4], turn_ref, sems.at[0]), start(w_hbm.at[1, 3], w_ref, sems.at[1]),
        start(turn_hbm.at[2], early_ref.at[0], sems.at[2]), start(w_hbm.at[1, 0], early_ref.at[1], sems.at[3]),
    ]
    cotangent = jnp.concatenate([ref[...] for ref in c_refs], axis=0)
    coming[0].wait()
    cotangent = dot(turn_ref[...], cotangent).astype(BF16)
    cot_ref[...] = cotangent
    coming[1].wait()
    da_ref[...] = dot_nt(cotangent, w_ref[...]).astype(BF16)
    finish(coming[2:])


def column_main(sizes, m_ref, cot_ref, da_ref, early_ref, g_ref, w_hbm, turn_hbm,
                dm_hbm, mid_hbm, n_hbm, att_hbm, dqkv_hbm,
                w_ref, turn_ref, dm_ref, mid_ref, n_ref, att_ref, dqkv_ref, q_ref, k_ref, v_ref, p_ref, sems):
    height, cols, width, together = sizes
    coming = [
        start(w_hbm.at[1, 1], w_ref.at[0], sems.at[0]), start(w_hbm.at[1, 2], w_ref.at[1], sems.at[1]),
        start(turn_hbm.at[3], turn_ref, sems.at[2]),
    ]
    middle = dot(early_ref[0], m_ref[...])
    mid_ref[...] = middle.astype(BF16)
    going = [start(mid_ref, mid_hbm, sems.at[3])]
    centred, inverse = statistics(middle)
    normed = (centred * inverse * g_ref[1:2]).astype(BF16)
    n_ref[...] = normed
    going.append(start(n_ref, n_hbm, sems.at[4]))
    q_ref[...] = dot(normed, early_ref[1]).astype(BF16)
    coming[0].wait()
    k_ref[...] = dot(normed, w_ref[0]).astype(BF16)
    coming[1].wait()
    v_ref[...] = dot(normed, w_ref[1]).astype(BF16)
    count = together * height
    groups = cols // together
    attention_forward(q_ref, k_ref, v_ref, att_ref, p_ref, groups, count, width, height)
    going.append(start(att_ref, att_hbm, sems.at[5]))
    attention_back(q_ref, k_ref, v_ref, p_ref, da_ref, dqkv_ref, groups, count, width)
    going.append(start(dqkv_ref, dqkv_hbm, sems.at[6]))
    d_normed = input_back(dqkv_ref, [early_ref.at[1], w_ref.at[0], w_ref.at[1]])
    middle = mid_ref[...].astype(F32)
    d_middle = cot_ref[...].astype(F32) + norm_back(middle, g_ref[1:2], d_normed)
    coming[2].wait()
    finish(going + send_turned(turn_ref, d_middle.astype(BF16), dm_ref, quarters(dm_hbm), sems.at[pl.ds(7, 4)]))


def column_last(parts, plane, cot_hbm, mid_hbm, n_hbm, att_hbm, dqkv_hbm, w_hbm, turn_hbm, *refs):
    out_hbms, refs = refs[:parts], refs[parts:]
    keep_hbms, send_hbms, refs = refs[:plane], refs[plane : 2 * plane], refs[2 * plane :]
    out_ref, keep_ref, send_ref, w_ref, turn_ref, flat_ref, dqkv_ref, sems, out_sems = refs
    coming = [
        start(turn_hbm.at[6], turn_ref.at[0], sems.at[0]), start(n_hbm, flat_ref.at[0], sems.at[1]),
        start(dqkv_hbm, dqkv_ref, sems.at[2]), start(att_hbm, flat_ref.at[1], sems.at[3]),
        start(cot_hbm, flat_ref.at[2], sems.at[4]), start(mid_hbm, flat_ref.at[3], sems.at[5]),
        start(w_hbm.at[1, 3], w_ref, sems.at[6]), start(turn_hbm.at[5], turn_ref.at[1], sems.at[7]),
    ]
    finish(coming[:3])
    normed = dot(flat_ref[0], turn_ref[0]).astype(BF16)
    for part in range(3):
        weight_grad(part, normed, third(dqkv_ref, part), keep_ref, send_ref)
    finish(coming[3:])
    attended = dot(flat_ref[1], turn_ref[0]).astype(BF16)
    weight_grad(3, attended, flat_ref[2], keep_ref, send_ref)
    going = send_grads(keep_ref, send_ref, keep_hbms, send_hbms, out_sems)
    output = (flat_ref[3].astype(F32) + dot(flat_ref[1], w_ref[...])).astype(BF16)
    finish(going + send_turned(turn_ref.at[1], output, out_ref, out_hbms, sems.at[pl.ds(8, parts)]))


def add_pairs(count, *refs):
    keep_hbms, got_refs, sum_refs, (keep_ref, sems) = (
        refs[:count], refs[count : 2 * count], refs[2 * count : 3 * count], refs[3 * count :]
    )
    coming = [start(hbm, keep_ref.at[at], sems.at[at]) for at, hbm in enumerate(keep_hbms)]
    for at, copy in enumerate(coming):
        copy.wait()
        sum_refs[at][...] = (keep_ref[at].astype(F32) + got_refs[at][...].astype(F32)).astype(BF16)


NEAR, FAR, ANY = pltpu.VMEM, pltpu.HBM, None


def call(kernel, ins, outs, scratch):
    def spec(where):
        return pl.BlockSpec(memory_space=pltpu.HBM if where is FAR else pltpu.VMEM)

    def place(item, where):
        return item if where is ANY else pltpu.with_memory_space_constraint(item, where)

    return pl.pallas_call(
        kernel,
        in_specs=[spec(where) for _, where in ins],
        out_specs=[spec(where) for _, where in outs],
        out_shape=[jax.ShapeDtypeStruct(shape, BF16) if where is ANY else where(shape, BF16) for shape, where in outs],
        scratch_shapes=scratch,
        compiler_params=pltpu.CompilerParams(vmem_limit_bytes=48 * 1024 * 1024),
        cost_estimate=pl.CostEstimate(flops=1 << 20, bytes_accessed=1 << 10, transcendentals=0),
    )(*[place(item, where) for item, where in ins])


def swap(item, axis, count, step):
    return lax.ppermute(item, axis, [(at, at ^ step) for at in range(count)])


def chip_sums(keeps, sends, col_parts):
    got = [swap(send, "col", col_parts, 1) for send in sends]
    count, shape = len(keeps), keeps[0].shape
    return call(
        functools.partial(add_pairs, count),
        [(item, FAR) for item in keeps] + [(item, ANY) for item in got], [(shape, ANY)] * count,
        [pltpu.VMEM((count, *shape), BF16), pltpu.SemaphoreType.DMA((count,))],
    )


def plane_pieces(sums, plane, core):
    return [item if step == 0 else swap(item, "col", plane * core, step * core) for step, item in enumerate(sums)]


def last_sums(pieces, row_parts):
    parts, size, channels = pieces[0].shape
    held = sum(piece.astype(F32) for piece in pieces).astype(BF16)
    held = held.reshape(parts, row_parts, size // row_parts, channels)
    result = held[:, 0].astype(F32)
    for step in range(1, row_parts):
        result = result + swap(held[:, step], "row", row_parts, step).astype(F32)
    return result


def body(row_parts, col_parts, field, cotangent, gains, weights):
    high, wide, channels = field.shape
    core = 2
    plane = col_parts // core
    rows = high // col_parts
    cols = wide // row_parts
    tokens = high * wide
    height = high * row_parts
    length = wide * col_parts
    width = channels // HEADS
    together = min(cols, max(1, 256 // height))
    devices = row_parts * col_parts
    my_row = lax.axis_index("row")

    flat, triple = (tokens, channels), (tokens, 3 * channels)
    probs = (rows * HEADS, length, length)
    packed = (4, channels // col_parts, channels)

    def scratch(*shape):
        return pltpu.VMEM(shape, BF16)

    def at(where, *items):
        return [(item, where) for item in items]

    square = scratch(*flat)
    copies = pltpu.SemaphoreType.DMA
    assert channels == tokens
    turns = [
        ((rows, col_parts, row_parts, cols), (2, 1, 0, 3), {}, 0),
        ((row_parts, col_parts, rows, cols), (2, 1, 0, 3), {}, 0),
        ((height, cols), (1, 0), {}, 0),
        ((cols, height), (1, 0), {}, 0),
        ((row_parts, high, cols), (2, 0, 1), {0: "row"}, 0),
        ((cols, row_parts, high), (1, 2, 0), {1: "row"}, 0),
        ((row_parts, plane, core, channels // devices), (2, 1, 0, 3), {0: "row", 1: "plane", 2: "core"}, 1),
    ]

    def all_to_all(item):
        item = item.reshape(devices, rows * cols, channels)
        return lax.all_to_all(item, ("row", "col"), 0, 0, tiled=True).reshape(tokens, channels)

    x = lax.all_to_all(field.reshape(col_parts, rows, wide, channels), "col", 0, 0, tiled=True)
    cots = []
    for step in range(row_parts):
        piece = lax.dynamic_slice_in_dim(cotangent, (my_row ^ step) * cols, cols, axis=1)
        piece = piece if step == 0 else swap(piece, "row", row_parts, step)
        cots.append(piece.reshape(high * cols, channels))
    turn, = call(
        functools.partial(set_up, turns), [], at(FAR, (len(turns), *flat)),
        [scratch(len(turns), *flat), copies((len(turns),))],
    )

    sizes = (rows, length, width)
    mid, normed, query, key, value, attended, prob = call(
        functools.partial(row_forward, sizes),
        at(ANY, x, gains) + at(FAR, weights, turn), at(FAR, *[flat] * 6, probs),
        [scratch(4, *flat)] + [square] * 7 + [scratch(*probs), copies((5,)), copies((6,)), copies((4,))],
    )
    mid, cots = lax.optimization_barrier((mid, cots))
    cot, d_att, early = call(
        functools.partial(column_first, row_parts),
        at(ANY, *cots) + at(FAR, weights, turn), at(NEAR, flat, flat, (2, *flat)), [square, square, copies((4,))],
    )
    mid = all_to_all(mid)

    count = together * height
    d_mid, *kept = call(
        functools.partial(column_main, (height, cols, width, together)),
        at(ANY, mid) + at(NEAR, cot, d_att, early) + at(ANY, gains) + at(FAR, weights, turn),
        at(FAR, flat, flat, flat, flat, triple),
        [scratch(2, *flat)] + [square] * 5 + [scratch(*triple)] + [square] * 3
        + [scratch(cols // together * HEADS, count, count), copies((11,))],
    )
    d_mid = all_to_all(d_mid)
    results = call(
        functools.partial(column_last, row_parts, plane),
        at(FAR, cot, *kept, weights, turn), at(FAR, *[(high * cols, channels)] * row_parts, *[packed] * (2 * plane)),
        [square, scratch(plane, *packed), scratch(plane, *packed), square, scratch(2, *flat), scratch(4, *flat),
         scratch(*triple), copies((8 + row_parts,)), copies((2 * plane,))],
    )
    outs, grads = results[:row_parts], results[row_parts:]
    sums_b = chip_sums(grads[:plane], grads[plane:], col_parts)
    pieces_b = plane_pieces(sums_b, plane, core)
    near, far = [outs[0], swap(outs[1], "row", row_parts, 1)], outs[2:]
    d_mid, near, far, _ = lax.optimization_barrier((d_mid, near, far, sums_b))
    results = call(
        functools.partial(row_back, (rows, length, width, plane)),
        at(ANY, d_mid) + at(FAR, weights, turn, normed, query, key, value, attended, prob),
        at(ANY, flat) + at(FAR, triple, *[packed] * (2 * plane)),
        [square, scratch(2, *flat)] + [square] * 5 + [scratch(*probs), square, scratch(*triple)]
        + [scratch(plane, *packed), scratch(plane, *packed), copies((11,)), copies((2 * plane,))],
    )
    (d_mid, dqkv, *grads), pieces_b, far = lax.optimization_barrier((results, pieces_b, far))
    sums_a = chip_sums(grads[:plane], grads[plane:], col_parts)
    pieces_a = plane_pieces(sums_a, plane, core)
    dqkv, pieces_b, far, _ = lax.optimization_barrier((dqkv, pieces_b, far, sums_a))
    field_grad, = call(
        field_back, at(ANY, x, d_mid, gains) + at(FAR, dqkv, weights), at(FAR, x.shape),
        [scratch(*triple), scratch(3, *flat), scratch(*x.shape), copies((3,))],
    )
    field_grad, pieces_a[1] = lax.optimization_barrier((field_grad, pieces_a[1]))
    field_grad = lax.all_to_all(field_grad, "col", 0, 0, tiled=True).reshape(high, wide, channels)
    grads_b = last_sums(pieces_b, row_parts)
    output = jnp.zeros((high, wide, channels), BF16)
    for step, piece in enumerate((*near, *far)):
        piece = (piece if step < 2 else swap(piece, "row", row_parts, step)).reshape(high, cols, channels)
        output = lax.dynamic_update_slice_in_dim(output, piece, (my_row ^ step) * cols, axis=1)
    grads_a = last_sums(pieces_a, row_parts)
    return output, field_grad, jnp.concatenate([grads_a, grads_b], axis=0)


def solution(mesh):
    return jax.shard_map(
        functools.partial(body, mesh.shape["row"], mesh.shape["col"]),
        mesh=mesh,
        in_specs=(P("row", "col", None), P("row", "col", None), P(), P()),
        out_specs=(P("row", "col", None), P("row", "col", None), P(None, ("row", "col"), None)),
        check_vma=False,
    )
```

```python
import functools
import math

import jax
import jax.numpy as jnp
from jax import lax
from jax.experimental import pallas as pl
from jax.experimental.pallas import tpu as pltpu
from jax.sharding import PartitionSpec as P

HEADS = 8
eps = 1e-05
F32 = jnp.float32
BF16 = jnp.bfloat16


def log2(n):
    assert n & (n - 1) == 0
    return n.bit_length() - 1


def dot(left, right):
    return jnp.dot(left, right, preferred_element_type=F32)


def dot_nt(left, right):
    return lax.dot_general(left, right, (((1,), (1,)), ((), ())), preferred_element_type=F32)


def dot_tn(left, right):
    return lax.dot_general(left, right, (((0,), (0,)), ((), ())), preferred_element_type=F32)


def one_hot(sizes, order, me=None, lead=0):
    total = math.prod(sizes)
    index = lax.broadcasted_iota(jnp.int32, (total, total), lead)
    found = {}
    for axis in reversed(order):
        found[axis] = index & (sizes[axis] - 1)
        index = index >> log2(sizes[axis])
    source, shift = None, 0
    for axis in reversed(range(len(sizes))):
        digit = found[axis] << shift
        source = digit if source is None else source | digit
        shift += log2(sizes[axis])
    if me:
        place, shift = 0, 0
        for axis in reversed(range(len(sizes))):
            if axis in me:
                place = place | (me[axis] << shift)
            shift += log2(sizes[axis])
        source = source ^ place
    hit = source == lax.broadcasted_iota(jnp.int32, (total, total), 1 - lead)
    return jnp.where(hit, 1.0, 0.0).astype(BF16)


def statistics(values):
    average = jnp.mean(values, axis=-1, keepdims=True)
    centred = values - average
    spread = jnp.mean(centred * centred, axis=-1, keepdims=True)
    return centred, lax.rsqrt(spread + eps)


def norm_back(values, gain, d_normed):
    centred, inverse = statistics(values)
    unit = centred * inverse
    scaled = d_normed * gain
    return inverse * (
        scaled
        - jnp.mean(scaled, axis=-1, keepdims=True)
        - unit * jnp.mean(scaled * unit, axis=-1, keepdims=True)
    )


def head_lanes(count, width):
    return lax.broadcasted_iota(jnp.int32, (count, 2 * width), 1) < width


def attention_forward(q_ref, k_ref, v_ref, att_ref, p_ref, groups, count, width, span):
    first = head_lanes(count, width)
    pairs = HEADS // 2
    scale = width ** (-0.5)

    def step(index, carry):
        group, pair = index // pairs, index % pairs
        rows = pl.ds(pl.multiple_of(group * count, count), count)
        lanes = pl.ds(pl.multiple_of(pair * 2 * width, 2 * width), 2 * width)
        query, key, value = q_ref[rows, lanes] * scale, k_ref[rows, lanes], v_ref[rows, lanes]
        zero = jnp.zeros_like(query)
        total = jnp.zeros((count, 2 * width), F32)
        for half in range(2):
            mine = first if half == 0 else jnp.logical_not(first)
            scores = dot_nt(key, jnp.where(mine, query, zero))
            if span < count:
                shift = log2(span)
                same = (lax.broadcasted_iota(jnp.int32, (count, count), 0) >> shift) == (
                    lax.broadcasted_iota(jnp.int32, (count, count), 1) >> shift
                )
                scores = jnp.where(same, scores, -jnp.inf)
            expo = jnp.exp(scores - jnp.max(scores, axis=0, keepdims=True))
            probs = (expo * (1.0 / jnp.sum(expo, axis=0, keepdims=True))).astype(BF16)
            p_ref[index * 2 + half] = probs
            total += dot_tn(probs, jnp.where(mine, value, zero))
        att_ref[rows, lanes] = total.astype(BF16)
        return carry

    lax.fori_loop(0, groups * pairs, step, 0, unroll=2)


def attention_back(q_ref, k_ref, v_ref, p_ref, da_ref, dqkv_ref, groups, count, width):
    first = head_lanes(count, width)
    pairs = HEADS // 2
    channels = HEADS * width
    scale = width ** (-0.5)

    def step(index, carry):
        group, pair = index // pairs, index % pairs
        rows = pl.ds(pl.multiple_of(group * count, count), count)
        lanes = pl.ds(pl.multiple_of(pair * 2 * width, 2 * width), 2 * width)
        query, key, value = q_ref[rows, lanes] * scale, k_ref[rows, lanes], v_ref[rows, lanes]
        d_out = da_ref[rows, lanes]
        zero = jnp.zeros_like(query)
        d_query = jnp.zeros((count, 2 * width), F32)
        d_key, d_value = d_query, d_query
        for half in range(2):
            mine = first if half == 0 else jnp.logical_not(first)
            probs = p_ref[index * 2 + half]
            d_mine = jnp.where(mine, d_out, zero)
            d_probs = dot_nt(value, d_mine)
            probs32 = probs.astype(F32)
            weighted = probs32 * d_probs
            total = jnp.sum(weighted, axis=0, keepdims=True)
            d_scores = (weighted - probs32 * total).astype(BF16)
            d_query += dot_tn(d_scores, jnp.where(mine, key, zero))
            d_key += dot(d_scores, jnp.where(mine, query, zero))
            d_value += dot(probs, d_mine)
        for part, item in enumerate((d_query * scale, d_key, d_value)):
            at = pl.ds(pl.multiple_of(part * channels + pair * 2 * width, 2 * width), 2 * width)
            dqkv_ref[rows, at] = item.astype(BF16)
        return carry

    lax.fori_loop(0, groups * pairs, step, 0, unroll=2)


def start(source, target, sem):
    copy = pltpu.make_async_copy(source, target, sem)
    copy.start()
    return copy


def finish(copies):
    for copy in copies:
        copy.wait()


def set_up(turns, turn_hbm, turn_ref, sems):
    my_row, my_col = lax.axis_index("row"), lax.axis_index("col")
    places = {"row": my_row, "plane": my_col >> 1, "core": my_col & 1}
    going = []
    for at, (sizes, order, me, lead) in enumerate(turns):
        turn_ref[at] = one_hot(sizes, order, {axis: places[name] for axis, name in me.items()}, lead)
        going.append(start(turn_ref.at[at], turn_hbm.at[at], sems.at[at]))
    finish(going)


def weight_grad(part, left, right, keep_ref, send_ref):
    plane, _, size, _ = keep_ref.shape
    whole = dot_tn(left, right).astype(BF16)
    for group in range(plane):
        send_ref[group, part] = whole[(plane + group) * size : (plane + group + 1) * size]
        keep_ref[group, part] = whole[group * size : (group + 1) * size]


def send_grads(keep_ref, send_ref, keep_hbms, send_hbms, sems):
    plane = keep_ref.shape[0]
    going = [start(send_ref.at[at], send_hbms[at], sems.at[at]) for at in range(plane)]
    return going + [start(keep_ref.at[at], keep_hbms[at], sems.at[plane + at]) for at in range(plane)]


def third(ref, part):
    channels = ref.shape[-1] // 3
    return ref[:, part * channels : (part + 1) * channels]


def send_turned(turn_ref, values, stage_ref, targets, sems):
    size = values.shape[0] // len(targets)
    going = []
    for at, target in enumerate(targets):
        piece = pl.ds(at * size, size)
        stage_ref[piece] = dot(turn_ref[piece], values).astype(BF16)
        going.append(start(stage_ref.at[piece], target, sems.at[at]))
    return going


def quarters(ref):
    size = ref.shape[0] // 4
    return [ref.at[pl.ds(at * size, size)] for at in range(4)]


def input_back(dqkv_ref, w_refs):
    total = dot_nt(third(dqkv_ref, 0), w_refs[0][...])
    total += dot_nt(third(dqkv_ref, 1), w_refs[1][...])
    total += dot_nt(third(dqkv_ref, 2), w_refs[2][...])
    return total.astype(BF16).astype(F32)


def rows_of(x_ref):
    _, rows, _, channels = x_ref.shape
    length = x_ref.shape[0] * x_ref.shape[2]
    pieces = [x_ref[:, i].reshape(length, channels) for i in range(rows)]
    return jnp.concatenate(pieces, axis=0).astype(F32)


def row_forward(sizes, x_ref, g_ref, w_hbm, turn_hbm, mid_hbm, n_hbm, q_hbm, k_hbm, v_hbm, att_hbm, p_hbm,
                w_ref, turn_ref, mid_ref, n_ref, q_ref, k_ref, v_ref, att_ref, p_ref, in_sems, out_sems, sems):
    rows, length, width = sizes
    coming = [start(w_hbm.at[0, part], w_ref.at[part], in_sems.at[part]) for part in range(4)]
    coming.append(start(turn_hbm.at[0], turn_ref, in_sems.at[4]))
    centred, inverse = statistics(rows_of(x_ref))
    normed = (centred * inverse * g_ref[0:1]).astype(BF16)
    n_ref[...] = normed
    going = [start(n_ref, n_hbm, out_sems.at[0])]
    for part, (ref, hbm) in enumerate(((q_ref, q_hbm), (k_ref, k_hbm), (v_ref, v_hbm))):
        coming[part].wait()
        ref[...] = dot(normed, w_ref[part]).astype(BF16)
        going.append(start(ref, hbm, out_sems.at[1 + part]))
    attention_forward(q_ref, k_ref, v_ref, att_ref, p_ref, rows, length, width, length)
    going.append(start(p_ref, p_hbm, out_sems.at[5]))
    going.append(start(att_ref, att_hbm, out_sems.at[4]))
    coming[3].wait()
    middle = (rows_of(x_ref) + dot(att_ref[...], w_ref[3])).astype(BF16)
    coming[4].wait()
    finish(going + send_turned(turn_ref, middle, mid_ref, quarters(mid_hbm), sems))


def row_back(sizes, d_ref, w_hbm, turn_hbm, n_hbm, q_hbm, k_hbm, v_hbm, att_hbm, p_hbm, *refs):
    rows, length, width, plane = sizes
    dm_ref, dqkv_hbm, keep_hbms, send_hbms = refs[0], refs[1], refs[2 : 2 + plane], refs[2 + plane : 2 + 2 * plane]
    w_ref, turn_ref, n_ref, q_ref, k_ref, v_ref, att_ref, p_ref, da_ref, dqkv_ref = refs[2 + 2 * plane : -4]
    keep_ref, send_ref, sems, out_sems = refs[-4:]
    half = p_ref.shape[0] // 2
    coming = [
        start(turn_hbm.at[1], turn_ref.at[0], sems.at[0]), start(w_hbm.at[0, 3], w_ref, sems.at[1]),
        start(v_hbm, v_ref, sems.at[2]), start(k_hbm, k_ref, sems.at[3]), start(q_hbm, q_ref, sems.at[4]),
        start(p_hbm.at[pl.ds(0, half)], p_ref.at[pl.ds(0, half)], sems.at[5]),
        start(p_hbm.at[pl.ds(half, half)], p_ref.at[pl.ds(half, half)], sems.at[6]),
        start(turn_hbm.at[6], turn_ref.at[1], sems.at[7]), start(att_hbm, att_ref, sems.at[8]),
        start(n_hbm, n_ref, sems.at[9]),
    ]
    coming[0].wait()
    d_middle = dot(turn_ref[0], d_ref[...]).astype(BF16)
    dm_ref[...] = d_middle
    coming[1].wait()
    da_ref[...] = dot_nt(d_middle, w_ref[...]).astype(BF16)
    finish(coming[2:7])
    attention_back(q_ref, k_ref, v_ref, p_ref, da_ref, dqkv_ref, rows, length, width)
    going = [start(dqkv_ref, dqkv_hbm, sems.at[10])]
    finish(coming[7:])
    normed = dot(n_ref[...], turn_ref[1]).astype(BF16)
    for part in range(3):
        weight_grad(part, normed, third(dqkv_ref, part), keep_ref, send_ref)
    attended = dot(att_ref[...], turn_ref[1]).astype(BF16)
    weight_grad(3, attended, dm_ref[...], keep_ref, send_ref)
    finish(going + send_grads(keep_ref, send_ref, keep_hbms, send_hbms, out_sems))


def field_back(x_ref, dm_ref, g_ref, dqkv_hbm, w_hbm, fg_hbm, dqkv_ref, w_ref, fg_ref, sems):
    coming = [start(dqkv_hbm, dqkv_ref, sems.at[0]), start(w_hbm.at[0, 0:3], w_ref, sems.at[1])]
    _, rows, _, channels = x_ref.shape
    length = x_ref.shape[0] * x_ref.shape[2]
    finish(coming)
    d_normed = input_back(dqkv_ref, [w_ref.at[part] for part in range(3)])
    result = dm_ref[...].astype(F32) + norm_back(rows_of(x_ref), g_ref[0:1], d_normed)
    result = result.astype(BF16)
    for i in range(rows):
        piece = result[i * length : (i + 1) * length]
        fg_ref[:, i] = piece.reshape(fg_ref.shape[0], fg_ref.shape[2], channels)
    start(fg_ref, fg_hbm, sems.at[2]).wait()


def column_first(parts, *refs):
    c_refs, (w_hbm, turn_hbm, cot_ref, da_ref, early_ref, w_ref, turn_ref, sems) = refs[:parts], refs[parts:]
    coming = [
        start(turn_hbm.at[4], turn_ref, sems.at[0]), start(w_hbm.at[1, 3], w_ref, sems.at[1]),
        start(turn_hbm.at[2], early_ref.at[0], sems.at[2]), start(w_hbm.at[1, 0], early_ref.at[1], sems.at[3]),
    ]
    cotangent = jnp.concatenate([ref[...] for ref in c_refs], axis=0)
    coming[0].wait()
    cotangent = dot(turn_ref[...], cotangent).astype(BF16)
    cot_ref[...] = cotangent
    coming[1].wait()
    da_ref[...] = dot_nt(cotangent, w_ref[...]).astype(BF16)
    finish(coming[2:])


def column_main(sizes, m_ref, cot_ref, da_ref, early_ref, g_ref, w_hbm, turn_hbm,
                dm_hbm, mid_hbm, n_hbm, att_hbm, dqkv_hbm,
                w_ref, turn_ref, dm_ref, mid_ref, n_ref, att_ref, dqkv_ref, q_ref, k_ref, v_ref, p_ref, sems):
    height, cols, width, together = sizes
    coming = [
        start(w_hbm.at[1, 1], w_ref.at[0], sems.at[0]), start(w_hbm.at[1, 2], w_ref.at[1], sems.at[1]),
        start(turn_hbm.at[3], turn_ref, sems.at[2]),
    ]
    middle = dot(early_ref[0], m_ref[...])
    mid_ref[...] = middle.astype(BF16)
    going = [start(mid_ref, mid_hbm, sems.at[3])]
    centred, inverse = statistics(middle)
    normed = (centred * inverse * g_ref[1:2]).astype(BF16)
    n_ref[...] = normed
    going.append(start(n_ref, n_hbm, sems.at[4]))
    q_ref[...] = dot(normed, early_ref[1]).astype(BF16)
    coming[0].wait()
    k_ref[...] = dot(normed, w_ref[0]).astype(BF16)
    coming[1].wait()
    v_ref[...] = dot(normed, w_ref[1]).astype(BF16)
    count = together * height
    groups = cols // together
    attention_forward(q_ref, k_ref, v_ref, att_ref, p_ref, groups, count, width, height)
    going.append(start(att_ref, att_hbm, sems.at[5]))
    attention_back(q_ref, k_ref, v_ref, p_ref, da_ref, dqkv_ref, groups, count, width)
    going.append(start(dqkv_ref, dqkv_hbm, sems.at[6]))
    d_normed = input_back(dqkv_ref, [early_ref.at[1], w_ref.at[0], w_ref.at[1]])
    middle = mid_ref[...].astype(F32)
    d_middle = cot_ref[...].astype(F32) + norm_back(middle, g_ref[1:2], d_normed)
    coming[2].wait()
    finish(going + send_turned(turn_ref, d_middle.astype(BF16), dm_ref, quarters(dm_hbm), sems.at[pl.ds(7, 4)]))


def column_last(parts, plane, cot_hbm, mid_hbm, n_hbm, att_hbm, dqkv_hbm, w_hbm, turn_hbm, *refs):
    out_hbms, refs = refs[:parts], refs[parts:]
    keep_hbms, send_hbms, refs = refs[:plane], refs[plane : 2 * plane], refs[2 * plane :]
    out_ref, keep_ref, send_ref, w_ref, turn_ref, flat_ref, dqkv_ref, sems, out_sems = refs
    coming = [
        start(turn_hbm.at[6], turn_ref.at[0], sems.at[0]), start(n_hbm, flat_ref.at[0], sems.at[1]),
        start(dqkv_hbm, dqkv_ref, sems.at[2]), start(att_hbm, flat_ref.at[1], sems.at[3]),
        start(cot_hbm, flat_ref.at[2], sems.at[4]), start(mid_hbm, flat_ref.at[3], sems.at[5]),
        start(w_hbm.at[1, 3], w_ref, sems.at[6]), start(turn_hbm.at[5], turn_ref.at[1], sems.at[7]),
    ]
    finish(coming[:3])
    normed = dot(flat_ref[0], turn_ref[0]).astype(BF16)
    for part in range(3):
        weight_grad(part, normed, third(dqkv_ref, part), keep_ref, send_ref)
    finish(coming[3:])
    attended = dot(flat_ref[1], turn_ref[0]).astype(BF16)
    weight_grad(3, attended, flat_ref[2], keep_ref, send_ref)
    going = send_grads(keep_ref, send_ref, keep_hbms, send_hbms, out_sems)
    output = (flat_ref[3].astype(F32) + dot(flat_ref[1], w_ref[...])).astype(BF16)
    finish(going + send_turned(turn_ref.at[1], output, out_ref, out_hbms, sems.at[pl.ds(8, parts)]))


def add_pairs(count, *refs):
    keep_hbms, got_refs, sum_refs, (keep_ref, sems) = (
        refs[:count], refs[count : 2 * count], refs[2 * count : 3 * count], refs[3 * count :]
    )
    coming = [start(hbm, keep_ref.at[at], sems.at[at]) for at, hbm in enumerate(keep_hbms)]
    for at, copy in enumerate(coming):
        copy.wait()
        sum_refs[at][...] = (keep_ref[at].astype(F32) + got_refs[at][...].astype(F32)).astype(BF16)


NEAR, FAR, ANY = pltpu.VMEM, pltpu.HBM, None


def call(kernel, ins, outs, scratch):
    def spec(where):
        return pl.BlockSpec(memory_space=pltpu.HBM if where is FAR else pltpu.VMEM)

    def place(item, where):
        return item if where is ANY else pltpu.with_memory_space_constraint(item, where)

    return pl.pallas_call(
        kernel,
        in_specs=[spec(where) for _, where in ins],
        out_specs=[spec(where) for _, where in outs],
        out_shape=[jax.ShapeDtypeStruct(shape, BF16) if where is ANY else where(shape, BF16) for shape, where in outs],
        scratch_shapes=scratch,
        compiler_params=pltpu.CompilerParams(vmem_limit_bytes=48 * 1024 * 1024),
        cost_estimate=pl.CostEstimate(flops=1 << 20, bytes_accessed=1 << 10, transcendentals=0),
    )(*[place(item, where) for item, where in ins])


def swap(item, axis, count, step):
    return lax.ppermute(item, axis, [(at, at ^ step) for at in range(count)])


def chip_sums(keeps, sends, col_parts):
    got = [swap(send, "col", col_parts, 1) for send in sends]
    count, shape = len(keeps), keeps[0].shape
    return call(
        functools.partial(add_pairs, count),
        [(item, FAR) for item in keeps] + [(item, ANY) for item in got], [(shape, ANY)] * count,
        [pltpu.VMEM((count, *shape), BF16), pltpu.SemaphoreType.DMA((count,))],
    )


def plane_pieces(sums, plane, core):
    return [item if step == 0 else swap(item, "col", plane * core, step * core) for step, item in enumerate(sums)]


def last_sums(pieces, row_parts):
    parts, size, channels = pieces[0].shape
    held = sum(piece.astype(F32) for piece in pieces).astype(BF16)
    held = held.reshape(parts, row_parts, size // row_parts, channels)
    result = held[:, 0].astype(F32)
    for step in range(1, row_parts):
        result = result + swap(held[:, step], "row", row_parts, step).astype(F32)
    return result


def body(row_parts, col_parts, field, cotangent, gains, weights):
    high, wide, channels = field.shape
    core = 2
    plane = col_parts // core
    rows = high // col_parts
    cols = wide // row_parts
    tokens = high * wide
    height = high * row_parts
    length = wide * col_parts
    width = channels // HEADS
    together = min(cols, max(1, 256 // height))
    devices = row_parts * col_parts
    my_row = lax.axis_index("row")

    flat, triple = (tokens, channels), (tokens, 3 * channels)
    probs = (rows * HEADS, length, length)
    packed = (4, channels // col_parts, channels)

    def scratch(*shape):
        return pltpu.VMEM(shape, BF16)

    def at(where, *items):
        return [(item, where) for item in items]

    square = scratch(*flat)
    copies = pltpu.SemaphoreType.DMA
    assert channels == tokens
    turns = [
        ((rows, col_parts, row_parts, cols), (2, 1, 0, 3), {}, 0),
        ((row_parts, col_parts, rows, cols), (2, 1, 0, 3), {}, 0),
        ((height, cols), (1, 0), {}, 0),
        ((cols, height), (1, 0), {}, 0),
        ((row_parts, high, cols), (2, 0, 1), {0: "row"}, 0),
        ((cols, row_parts, high), (1, 2, 0), {1: "row"}, 0),
        ((row_parts, plane, core, channels // devices), (2, 1, 0, 3), {0: "row", 1: "plane", 2: "core"}, 1),
    ]

    def all_to_all(item):
        item = item.reshape(devices, rows * cols, channels)
        return lax.all_to_all(item, ("row", "col"), 0, 0, tiled=True).reshape(tokens, channels)

    x = lax.all_to_all(field.reshape(col_parts, rows, wide, channels), "col", 0, 0, tiled=True)
    cots = []
    for step in range(row_parts):
        piece = lax.dynamic_slice_in_dim(cotangent, (my_row ^ step) * cols, cols, axis=1)
        piece = piece if step == 0 else swap(piece, "row", row_parts, step)
        cots.append(piece.reshape(high * cols, channels))
    turn, = call(
        functools.partial(set_up, turns), [], at(FAR, (len(turns), *flat)),
        [scratch(len(turns), *flat), copies((len(turns),))],
    )

    sizes = (rows, length, width)
    mid, normed, query, key, value, attended, prob = call(
        functools.partial(row_forward, sizes),
        at(ANY, x, gains) + at(FAR, weights, turn), at(FAR, *[flat] * 6, probs),
        [scratch(4, *flat)] + [square] * 7 + [scratch(*probs), copies((5,)), copies((6,)), copies((4,))],
    )
    mid, cots = lax.optimization_barrier((mid, cots))
    cot, d_att, early = call(
        functools.partial(column_first, row_parts),
        at(ANY, *cots) + at(FAR, weights, turn), at(NEAR, flat, flat, (2, *flat)), [square, square, copies((4,))],
    )
    mid = all_to_all(mid)

    count = together * height
    d_mid, *kept = call(
        functools.partial(column_main, (height, cols, width, together)),
        at(ANY, mid) + at(NEAR, cot, d_att, early) + at(ANY, gains) + at(FAR, weights, turn),
        at(FAR, flat, flat, flat, flat, triple),
        [scratch(2, *flat)] + [square] * 5 + [scratch(*triple)] + [square] * 3
        + [scratch(cols // together * HEADS, count, count), copies((11,))],
    )
    d_mid = all_to_all(d_mid)
    results = call(
        functools.partial(column_last, row_parts, plane),
        at(FAR, cot, *kept, weights, turn), at(FAR, *[(high * cols, channels)] * row_parts, *[packed] * (2 * plane)),
        [square, scratch(plane, *packed), scratch(plane, *packed), square, scratch(2, *flat), scratch(4, *flat),
         scratch(*triple), copies((8 + row_parts,)), copies((2 * plane,))],
    )
    outs, grads = results[:row_parts], results[row_parts:]
    sums_b = chip_sums(grads[:plane], grads[plane:], col_parts)
    pieces_b = plane_pieces(sums_b, plane, core)
    near, far = [outs[0], swap(outs[1], "row", row_parts, 1)], outs[2:]
    d_mid, far, _ = lax.optimization_barrier((d_mid, far, sums_b))
    results = call(
        functools.partial(row_back, (rows, length, width, plane)),
        at(ANY, d_mid) + at(FAR, weights, turn, normed, query, key, value, attended, prob),
        at(ANY, flat) + at(FAR, triple, *[packed] * (2 * plane)),
        [square, scratch(2, *flat)] + [square] * 5 + [scratch(*probs), square, scratch(*triple)]
        + [scratch(plane, *packed), scratch(plane, *packed), copies((11,)), copies((2 * plane,))],
    )
    (d_mid, dqkv, *grads), pieces_b, near = lax.optimization_barrier((results, pieces_b, near))
    sums_a = chip_sums(grads[:plane], grads[plane:], col_parts)
    pieces_a = plane_pieces(sums_a, plane, core)
    dqkv, _ = lax.optimization_barrier((dqkv, sums_a))
    field_grad, = call(
        field_back, at(ANY, x, d_mid, gains) + at(FAR, dqkv, weights), at(FAR, x.shape),
        [scratch(*triple), scratch(3, *flat), scratch(*x.shape), copies((3,))],
    )
    field_grad, pieces_a[1], pieces_b, far = lax.optimization_barrier((field_grad, pieces_a[1], pieces_b, far))
    grads_b = last_sums(pieces_b, row_parts)
    output = jnp.zeros((high, wide, channels), BF16)
    for step, piece in enumerate((*near, *far)):
        piece = (piece if step < 2 else swap(piece, "row", row_parts, step)).reshape(high, cols, channels)
        output = lax.dynamic_update_slice_in_dim(output, piece, (my_row ^ step) * cols, axis=1)
    field_grad = lax.all_to_all(field_grad, "col", 0, 0, tiled=True).reshape(high, wide, channels)
    field_grad, pieces_a = lax.optimization_barrier((field_grad, pieces_a))
    grads_a = last_sums(pieces_a, row_parts)
    return output, field_grad, jnp.concatenate([grads_a, grads_b], axis=0)


def solution(mesh):
    return jax.shard_map(
        functools.partial(body, mesh.shape["row"], mesh.shape["col"]),
        mesh=mesh,
        in_specs=(P("row", "col", None), P("row", "col", None), P(), P()),
        out_specs=(P("row", "col", None), P("row", "col", None), P(None, ("row", "col"), None)),
        check_vma=False,
    )
```

```python
import functools
import math

import jax
import jax.numpy as jnp
from jax import lax
from jax.experimental import pallas as pl
from jax.experimental.pallas import tpu as pltpu
from jax.sharding import PartitionSpec as P

HEADS = 8
eps = 1e-05
F32 = jnp.float32
BF16 = jnp.bfloat16


def log2(n):
    assert n & (n - 1) == 0
    return n.bit_length() - 1


def dot(left, right):
    return jnp.dot(left, right, preferred_element_type=F32)


def dot_nt(left, right):
    return lax.dot_general(left, right, (((1,), (1,)), ((), ())), preferred_element_type=F32)


def dot_tn(left, right):
    return lax.dot_general(left, right, (((0,), (0,)), ((), ())), preferred_element_type=F32)


def one_hot(sizes, order, me=None, lead=0):
    total = math.prod(sizes)
    index = lax.broadcasted_iota(jnp.int32, (total, total), lead)
    found = {}
    for axis in reversed(order):
        found[axis] = index & (sizes[axis] - 1)
        index = index >> log2(sizes[axis])
    source, shift = None, 0
    for axis in reversed(range(len(sizes))):
        digit = found[axis] << shift
        source = digit if source is None else source | digit
        shift += log2(sizes[axis])
    if me:
        place, shift = 0, 0
        for axis in reversed(range(len(sizes))):
            if axis in me:
                place = place | (me[axis] << shift)
            shift += log2(sizes[axis])
        source = source ^ place
    hit = source == lax.broadcasted_iota(jnp.int32, (total, total), 1 - lead)
    return jnp.where(hit, 1.0, 0.0).astype(BF16)


def statistics(values):
    average = jnp.mean(values, axis=-1, keepdims=True)
    centred = values - average
    spread = jnp.mean(centred * centred, axis=-1, keepdims=True)
    return centred, lax.rsqrt(spread + eps)


def norm_back(values, gain, d_normed):
    centred, inverse = statistics(values)
    unit = centred * inverse
    scaled = d_normed * gain
    return inverse * (
        scaled
        - jnp.mean(scaled, axis=-1, keepdims=True)
        - unit * jnp.mean(scaled * unit, axis=-1, keepdims=True)
    )


def head_lanes(count, width):
    return lax.broadcasted_iota(jnp.int32, (count, 2 * width), 1) < width


def attention_forward(q_ref, k_ref, v_ref, att_ref, p_ref, groups, count, width, span):
    first = head_lanes(count, width)
    pairs = HEADS // 2
    scale = width ** (-0.5)

    def step(index, carry):
        group, pair = index // pairs, index % pairs
        rows = pl.ds(pl.multiple_of(group * count, count), count)
        lanes = pl.ds(pl.multiple_of(pair * 2 * width, 2 * width), 2 * width)
        query, key, value = q_ref[rows, lanes] * scale, k_ref[rows, lanes], v_ref[rows, lanes]
        zero = jnp.zeros_like(query)
        total = jnp.zeros((count, 2 * width), F32)
        for half in range(2):
            mine = first if half == 0 else jnp.logical_not(first)
            scores = dot_nt(key, jnp.where(mine, query, zero))
            if span < count:
                shift = log2(span)
                same = (lax.broadcasted_iota(jnp.int32, (count, count), 0) >> shift) == (
                    lax.broadcasted_iota(jnp.int32, (count, count), 1) >> shift
                )
                scores = jnp.where(same, scores, -jnp.inf)
            expo = jnp.exp(scores - jnp.max(scores, axis=0, keepdims=True))
            probs = (expo * (1.0 / jnp.sum(expo, axis=0, keepdims=True))).astype(BF16)
            p_ref[index * 2 + half] = probs
            total += dot_tn(probs, jnp.where(mine, value, zero))
        att_ref[rows, lanes] = total.astype(BF16)
        return carry

    lax.fori_loop(0, groups * pairs, step, 0, unroll=2)


def attention_back(q_ref, k_ref, v_ref, p_ref, da_ref, dqkv_ref, groups, count, width):
    first = head_lanes(count, width)
    pairs = HEADS // 2
    channels = HEADS * width
    scale = width ** (-0.5)

    def step(index, carry):
        group, pair = index // pairs, index % pairs
        rows = pl.ds(pl.multiple_of(group * count, count), count)
        lanes = pl.ds(pl.multiple_of(pair * 2 * width, 2 * width), 2 * width)
        query, key, value = q_ref[rows, lanes] * scale, k_ref[rows, lanes], v_ref[rows, lanes]
        d_out = da_ref[rows, lanes]
        zero = jnp.zeros_like(query)
        d_query = jnp.zeros((count, 2 * width), F32)
        d_key, d_value = d_query, d_query
        for half in range(2):
            mine = first if half == 0 else jnp.logical_not(first)
            probs = p_ref[index * 2 + half]
            d_mine = jnp.where(mine, d_out, zero)
            d_probs = dot_nt(value, d_mine)
            probs32 = probs.astype(F32)
            weighted = probs32 * d_probs
            total = jnp.sum(weighted, axis=0, keepdims=True)
            d_scores = (weighted - probs32 * total).astype(BF16)
            d_query += dot_tn(d_scores, jnp.where(mine, key, zero))
            d_key += dot(d_scores, jnp.where(mine, query, zero))
            d_value += dot(probs, d_mine)
        for part, item in enumerate((d_query * scale, d_key, d_value)):
            at = pl.ds(pl.multiple_of(part * channels + pair * 2 * width, 2 * width), 2 * width)
            dqkv_ref[rows, at] = item.astype(BF16)
        return carry

    lax.fori_loop(0, groups * pairs, step, 0, unroll=2)


def start(source, target, sem):
    copy = pltpu.make_async_copy(source, target, sem)
    copy.start()
    return copy


def finish(copies):
    for copy in copies:
        copy.wait()


def set_up(turns, turn_hbm, turn_ref, sems):
    my_row, my_col = lax.axis_index("row"), lax.axis_index("col")
    places = {"row": my_row, "plane": my_col >> 1, "core": my_col & 1}
    going = []
    for at, (sizes, order, me, lead) in enumerate(turns):
        turn_ref[at] = one_hot(sizes, order, {axis: places[name] for axis, name in me.items()}, lead)
        going.append(start(turn_ref.at[at], turn_hbm.at[at], sems.at[at]))
    finish(going)


def weight_grad(part, left, right, keep_ref, send_ref):
    plane, _, size, _ = keep_ref.shape
    whole = dot_tn(left, right).astype(BF16)
    for group in range(plane):
        send_ref[group, part] = whole[(plane + group) * size : (plane + group + 1) * size]
        keep_ref[group, part] = whole[group * size : (group + 1) * size]


def send_grads(keep_ref, send_ref, keep_hbms, send_hbms, sems):
    plane = keep_ref.shape[0]
    going = [start(send_ref.at[at], send_hbms[at], sems.at[at]) for at in range(plane)]
    return going + [start(keep_ref.at[at], keep_hbms[at], sems.at[plane + at]) for at in range(plane)]


def third(ref, part):
    channels = ref.shape[-1] // 3
    return ref[:, part * channels : (part + 1) * channels]


def send_turned(turn_ref, values, stage_ref, targets, sems):
    size = values.shape[0] // len(targets)
    going = []
    for at, target in enumerate(targets):
        piece = pl.ds(at * size, size)
        stage_ref[piece] = dot(turn_ref[piece], values).astype(BF16)
        going.append(start(stage_ref.at[piece], target, sems.at[at]))
    return going


def quarters(ref):
    size = ref.shape[0] // 4
    return [ref.at[pl.ds(at * size, size)] for at in range(4)]


def input_back(dqkv_ref, w_refs):
    total = dot_nt(third(dqkv_ref, 0), w_refs[0][...])
    total += dot_nt(third(dqkv_ref, 1), w_refs[1][...])
    total += dot_nt(third(dqkv_ref, 2), w_refs[2][...])
    return total.astype(BF16).astype(F32)


def rows_of(x_ref):
    _, rows, _, channels = x_ref.shape
    length = x_ref.shape[0] * x_ref.shape[2]
    pieces = [x_ref[:, i].reshape(length, channels) for i in range(rows)]
    return jnp.concatenate(pieces, axis=0).astype(F32)


def row_forward(sizes, x_ref, g_ref, w_hbm, turn_hbm, mid_hbm, n_hbm, q_hbm, k_hbm, v_hbm, att_hbm, p_hbm,
                w_ref, turn_ref, mid_ref, n_ref, q_ref, k_ref, v_ref, att_ref, p_ref, in_sems, out_sems, sems):
    rows, length, width = sizes
    coming = [start(w_hbm.at[0, part], w_ref.at[part], in_sems.at[part]) for part in range(4)]
    coming.append(start(turn_hbm.at[0], turn_ref, in_sems.at[4]))
    centred, inverse = statistics(rows_of(x_ref))
    normed = (centred * inverse * g_ref[0:1]).astype(BF16)
    n_ref[...] = normed
    going = [start(n_ref, n_hbm, out_sems.at[0])]
    for part, (ref, hbm) in enumerate(((q_ref, q_hbm), (k_ref, k_hbm), (v_ref, v_hbm))):
        coming[part].wait()
        ref[...] = dot(normed, w_ref[part]).astype(BF16)
        going.append(start(ref, hbm, out_sems.at[1 + part]))
    attention_forward(q_ref, k_ref, v_ref, att_ref, p_ref, rows, length, width, length)
    going.append(start(p_ref, p_hbm, out_sems.at[5]))
    going.append(start(att_ref, att_hbm, out_sems.at[4]))
    coming[3].wait()
    middle = (rows_of(x_ref) + dot(att_ref[...], w_ref[3])).astype(BF16)
    coming[4].wait()
    finish(going + send_turned(turn_ref, middle, mid_ref, quarters(mid_hbm), sems))


def row_back(sizes, d_ref, w_hbm, turn_hbm, n_hbm, q_hbm, k_hbm, v_hbm, att_hbm, p_hbm, *refs):
    rows, length, width, plane = sizes
    dm_ref, dqkv_hbm, keep_hbms, send_hbms = refs[0], refs[1], refs[2 : 2 + plane], refs[2 + plane : 2 + 2 * plane]
    w_ref, turn_ref, n_ref, q_ref, k_ref, v_ref, att_ref, p_ref, da_ref, dqkv_ref = refs[2 + 2 * plane : -4]
    keep_ref, send_ref, sems, out_sems = refs[-4:]
    half = p_ref.shape[0] // 2
    coming = [
        start(turn_hbm.at[1], turn_ref.at[0], sems.at[0]), start(w_hbm.at[0, 3], w_ref, sems.at[1]),
        start(v_hbm, v_ref, sems.at[2]), start(k_hbm, k_ref, sems.at[3]), start(q_hbm, q_ref, sems.at[4]),
        start(p_hbm.at[pl.ds(0, half)], p_ref.at[pl.ds(0, half)], sems.at[5]),
        start(p_hbm.at[pl.ds(half, half)], p_ref.at[pl.ds(half, half)], sems.at[6]),
        start(turn_hbm.at[6], turn_ref.at[1], sems.at[7]), start(att_hbm, att_ref, sems.at[8]),
        start(n_hbm, n_ref, sems.at[9]),
    ]
    coming[0].wait()
    d_middle = dot(turn_ref[0], d_ref[...]).astype(BF16)
    dm_ref[...] = d_middle
    coming[1].wait()
    da_ref[...] = dot_nt(d_middle, w_ref[...]).astype(BF16)
    finish(coming[2:7])
    attention_back(q_ref, k_ref, v_ref, p_ref, da_ref, dqkv_ref, rows, length, width)
    going = [start(dqkv_ref, dqkv_hbm, sems.at[10])]
    finish(coming[7:])
    normed = dot(n_ref[...], turn_ref[1]).astype(BF16)
    for part in range(3):
        weight_grad(part, normed, third(dqkv_ref, part), keep_ref, send_ref)
    attended = dot(att_ref[...], turn_ref[1]).astype(BF16)
    weight_grad(3, attended, dm_ref[...], keep_ref, send_ref)
    finish(going + send_grads(keep_ref, send_ref, keep_hbms, send_hbms, out_sems))


def field_back(x_ref, dm_ref, g_ref, dqkv_hbm, w_hbm, fg_hbm, dqkv_ref, w_ref, fg_ref, sems):
    coming = [start(dqkv_hbm, dqkv_ref, sems.at[0]), start(w_hbm.at[0, 0:3], w_ref, sems.at[1])]
    _, rows, _, channels = x_ref.shape
    length = x_ref.shape[0] * x_ref.shape[2]
    finish(coming)
    d_normed = input_back(dqkv_ref, [w_ref.at[part] for part in range(3)])
    result = dm_ref[...].astype(F32) + norm_back(rows_of(x_ref), g_ref[0:1], d_normed)
    result = result.astype(BF16)
    for i in range(rows):
        piece = result[i * length : (i + 1) * length]
        fg_ref[:, i] = piece.reshape(fg_ref.shape[0], fg_ref.shape[2], channels)
    start(fg_ref, fg_hbm, sems.at[2]).wait()


def column_first(parts, *refs):
    c_refs, (w_hbm, turn_hbm, cot_ref, da_ref, early_ref, w_ref, turn_ref, sems) = refs[:parts], refs[parts:]
    coming = [
        start(turn_hbm.at[4], turn_ref, sems.at[0]), start(w_hbm.at[1, 3], w_ref, sems.at[1]),
        start(turn_hbm.at[2], early_ref.at[0], sems.at[2]), start(w_hbm.at[1, 0], early_ref.at[1], sems.at[3]),
    ]
    cotangent = jnp.concatenate([ref[...] for ref in c_refs], axis=0)
    coming[0].wait()
    cotangent = dot(turn_ref[...], cotangent).astype(BF16)
    cot_ref[...] = cotangent
    coming[1].wait()
    da_ref[...] = dot_nt(cotangent, w_ref[...]).astype(BF16)
    finish(coming[2:])


def column_main(sizes, m_ref, cot_ref, da_ref, early_ref, g_ref, w_hbm, turn_hbm,
                dm_hbm, mid_hbm, n_hbm, att_hbm, dqkv_hbm,
                w_ref, turn_ref, dm_ref, mid_ref, n_ref, att_ref, dqkv_ref, q_ref, k_ref, v_ref, p_ref, sems):
    height, cols, width, together = sizes
    coming = [
        start(w_hbm.at[1, 1], w_ref.at[0], sems.at[0]), start(w_hbm.at[1, 2], w_ref.at[1], sems.at[1]),
        start(turn_hbm.at[3], turn_ref, sems.at[2]),
    ]
    middle = dot(early_ref[0], m_ref[...])
    mid_ref[...] = middle.astype(BF16)
    going = [start(mid_ref, mid_hbm, sems.at[3])]
    centred, inverse = statistics(middle)
    normed = (centred * inverse * g_ref[1:2]).astype(BF16)
    n_ref[...] = normed
    going.append(start(n_ref, n_hbm, sems.at[4]))
    q_ref[...] = dot(normed, early_ref[1]).astype(BF16)
    coming[0].wait()
    k_ref[...] = dot(normed, w_ref[0]).astype(BF16)
    coming[1].wait()
    v_ref[...] = dot(normed, w_ref[1]).astype(BF16)
    count = together * height
    groups = cols // together
    attention_forward(q_ref, k_ref, v_ref, att_ref, p_ref, groups, count, width, height)
    going.append(start(att_ref, att_hbm, sems.at[5]))
    attention_back(q_ref, k_ref, v_ref, p_ref, da_ref, dqkv_ref, groups, count, width)
    going.append(start(dqkv_ref, dqkv_hbm, sems.at[6]))
    d_normed = input_back(dqkv_ref, [early_ref.at[1], w_ref.at[0], w_ref.at[1]])
    middle = mid_ref[...].astype(F32)
    d_middle = cot_ref[...].astype(F32) + norm_back(middle, g_ref[1:2], d_normed)
    coming[2].wait()
    finish(going + send_turned(turn_ref, d_middle.astype(BF16), dm_ref, quarters(dm_hbm), sems.at[pl.ds(7, 4)]))


def column_last(parts, plane, cot_hbm, mid_hbm, n_hbm, att_hbm, dqkv_hbm, w_hbm, turn_hbm, *refs):
    out_hbms, refs = refs[:parts], refs[parts:]
    keep_hbms, send_hbms, refs = refs[:plane], refs[plane : 2 * plane], refs[2 * plane :]
    out_ref, keep_ref, send_ref, w_ref, turn_ref, flat_ref, dqkv_ref, sems, out_sems = refs
    coming = [
        start(turn_hbm.at[7], turn_ref.at[0], sems.at[0]), start(n_hbm, flat_ref.at[0], sems.at[1]),
        start(dqkv_hbm, dqkv_ref, sems.at[2]), start(att_hbm, flat_ref.at[1], sems.at[3]),
        start(cot_hbm, flat_ref.at[2], sems.at[4]), start(mid_hbm, flat_ref.at[3], sems.at[5]),
        start(w_hbm.at[1, 3], w_ref, sems.at[6]), start(turn_hbm.at[5], turn_ref.at[1], sems.at[7]),
    ]
    finish(coming[:3])
    normed = dot(flat_ref[0], turn_ref[0]).astype(BF16)
    for part in range(3):
        weight_grad(part, normed, third(dqkv_ref, part), keep_ref, send_ref)
    finish(coming[3:])
    attended = dot(flat_ref[1], turn_ref[0]).astype(BF16)
    weight_grad(3, attended, flat_ref[2], keep_ref, send_ref)
    going = send_grads(keep_ref, send_ref, keep_hbms, send_hbms, out_sems)
    output = (flat_ref[3].astype(F32) + dot(flat_ref[1], w_ref[...])).astype(BF16)
    finish(going + send_turned(turn_ref.at[1], output, out_ref, out_hbms, sems.at[pl.ds(8, parts)]))


def add_pairs(count, *refs):
    keep_hbms, got_refs, sum_refs, (keep_ref, sems) = (
        refs[:count], refs[count : 2 * count], refs[2 * count : 3 * count], refs[3 * count :]
    )
    coming = [start(hbm, keep_ref.at[at], sems.at[at]) for at, hbm in enumerate(keep_hbms)]
    for at, copy in enumerate(coming):
        copy.wait()
        sum_refs[at][...] = (keep_ref[at].astype(F32) + got_refs[at][...].astype(F32)).astype(BF16)


NEAR, FAR, ANY = pltpu.VMEM, pltpu.HBM, None


def call(kernel, ins, outs, scratch):
    def spec(where):
        return pl.BlockSpec(memory_space=pltpu.HBM if where is FAR else pltpu.VMEM)

    def place(item, where):
        return item if where is ANY else pltpu.with_memory_space_constraint(item, where)

    return pl.pallas_call(
        kernel,
        in_specs=[spec(where) for _, where in ins],
        out_specs=[spec(where) for _, where in outs],
        out_shape=[jax.ShapeDtypeStruct(shape, BF16) if where is ANY else where(shape, BF16) for shape, where in outs],
        scratch_shapes=scratch,
        compiler_params=pltpu.CompilerParams(vmem_limit_bytes=48 * 1024 * 1024),
        cost_estimate=pl.CostEstimate(flops=1 << 20, bytes_accessed=1 << 10, transcendentals=0),
    )(*[place(item, where) for item, where in ins])


def swap(item, axis, count, step):
    return lax.ppermute(item, axis, [(at, at ^ step) for at in range(count)])


def chip_sums(keeps, sends, col_parts):
    got = [swap(send, "col", col_parts, 1) for send in sends]
    count, shape = len(keeps), keeps[0].shape
    return call(
        functools.partial(add_pairs, count),
        [(item, FAR) for item in keeps] + [(item, ANY) for item in got], [(shape, ANY)] * count,
        [pltpu.VMEM((count, *shape), BF16), pltpu.SemaphoreType.DMA((count,))],
    )


def plane_pieces(sums, plane, core):
    return [item if step == 0 else swap(item, "col", plane * core, step * core) for step, item in enumerate(sums)]


def last_sums_at_once(pieces, row_parts):
    parts, size, channels = pieces[0].shape
    held = sum(piece.astype(F32) for piece in pieces).astype(BF16)
    held = held.reshape(parts, row_parts, size // row_parts, channels).transpose(1, 0, 2, 3)
    got = lax.all_to_all(held, "row", 0, 0, tiled=True)
    return jnp.sum(got.astype(F32), axis=0)


def last_sums(pieces, row_parts):
    parts, size, channels = pieces[0].shape
    held = sum(piece.astype(F32) for piece in pieces).astype(BF16)
    held = held.reshape(parts, row_parts, size // row_parts, channels)
    result = held[:, 0].astype(F32)
    for step in range(1, row_parts):
        result = result + swap(held[:, step], "row", row_parts, step).astype(F32)
    return result


def body(row_parts, col_parts, field, cotangent, gains, weights):
    high, wide, channels = field.shape
    core = 2
    plane = col_parts // core
    rows = high // col_parts
    cols = wide // row_parts
    tokens = high * wide
    height = high * row_parts
    length = wide * col_parts
    width = channels // HEADS
    together = min(cols, max(1, 256 // height))
    devices = row_parts * col_parts
    my_row = lax.axis_index("row")

    flat, triple = (tokens, channels), (tokens, 3 * channels)
    probs = (rows * HEADS, length, length)
    packed = (4, channels // col_parts, channels)

    def scratch(*shape):
        return pltpu.VMEM(shape, BF16)

    def at(where, *items):
        return [(item, where) for item in items]

    square = scratch(*flat)
    copies = pltpu.SemaphoreType.DMA
    assert channels == tokens
    turns = [
        ((rows, col_parts, row_parts, cols), (2, 1, 0, 3), {}, 0),
        ((row_parts, col_parts, rows, cols), (2, 1, 0, 3), {}, 0),
        ((height, cols), (1, 0), {}, 0),
        ((cols, height), (1, 0), {}, 0),
        ((row_parts, high, cols), (2, 0, 1), {0: "row"}, 0),
        ((cols, row_parts, high), (1, 2, 0), {1: "row"}, 0),
        ((row_parts, plane, core, channels // devices), (2, 1, 0, 3), {0: "row", 1: "plane", 2: "core"}, 1),
        ((row_parts, plane, core, channels // devices), (2, 1, 0, 3), {1: "plane", 2: "core"}, 1),
    ]

    def all_to_all(item):
        item = item.reshape(devices, rows * cols, channels)
        return lax.all_to_all(item, ("row", "col"), 0, 0, tiled=True).reshape(tokens, channels)

    x = lax.all_to_all(field.reshape(col_parts, rows, wide, channels), "col", 0, 0, tiled=True)
    cots = []
    for step in range(row_parts):
        piece = lax.dynamic_slice_in_dim(cotangent, (my_row ^ step) * cols, cols, axis=1)
        piece = piece if step == 0 else swap(piece, "row", row_parts, step)
        cots.append(piece.reshape(high * cols, channels))
    turn, = call(
        functools.partial(set_up, turns), [], at(FAR, (len(turns), *flat)),
        [scratch(len(turns), *flat), copies((len(turns),))],
    )

    sizes = (rows, length, width)
    mid, normed, query, key, value, attended, prob = call(
        functools.partial(row_forward, sizes),
        at(ANY, x, gains) + at(FAR, weights, turn), at(FAR, *[flat] * 6, probs),
        [scratch(4, *flat)] + [square] * 7 + [scratch(*probs), copies((5,)), copies((6,)), copies((4,))],
    )
    mid, cots = lax.optimization_barrier((mid, cots))
    cot, d_att, early = call(
        functools.partial(column_first, row_parts),
        at(ANY, *cots) + at(FAR, weights, turn), at(NEAR, flat, flat, (2, *flat)), [square, square, copies((4,))],
    )
    mid = all_to_all(mid)

    count = together * height
    d_mid, *kept = call(
        functools.partial(column_main, (height, cols, width, together)),
        at(ANY, mid) + at(NEAR, cot, d_att, early) + at(ANY, gains) + at(FAR, weights, turn),
        at(FAR, flat, flat, flat, flat, triple),
        [scratch(2, *flat)] + [square] * 5 + [scratch(*triple)] + [square] * 3
        + [scratch(cols // together * HEADS, count, count), copies((11,))],
    )
    d_mid = all_to_all(d_mid)
    results = call(
        functools.partial(column_last, row_parts, plane),
        at(FAR, cot, *kept, weights, turn), at(FAR, *[(high * cols, channels)] * row_parts, *[packed] * (2 * plane)),
        [square, scratch(plane, *packed), scratch(plane, *packed), square, scratch(2, *flat), scratch(4, *flat),
         scratch(*triple), copies((8 + row_parts,)), copies((2 * plane,))],
    )
    outs, grads = results[:row_parts], results[row_parts:]
    sums_b = chip_sums(grads[:plane], grads[plane:], col_parts)
    pieces_b = plane_pieces(sums_b, plane, core)
    pieces_out = [outs[0], swap(outs[1], "row", row_parts, 1)]
    d_mid, rest, _ = lax.optimization_barrier((d_mid, outs[2:], sums_b))
    pieces_out += [swap(item, "row", row_parts, 2 + step) for step, item in enumerate(rest[:1])]
    results = call(
        functools.partial(row_back, (rows, length, width, plane)),
        at(ANY, d_mid) + at(FAR, weights, turn, normed, query, key, value, attended, prob),
        at(ANY, flat) + at(FAR, triple, *[packed] * (2 * plane)),
        [square, scratch(2, *flat)] + [square] * 5 + [scratch(*probs), square, scratch(*triple)]
        + [scratch(plane, *packed), scratch(plane, *packed), copies((11,)), copies((2 * plane,))],
    )
    (d_mid, dqkv, *grads), pieces_b, pieces_out, rest = lax.optimization_barrier(
        (results, pieces_b, pieces_out, rest[1:])
    )
    sums_a = chip_sums(grads[:plane], grads[plane:], col_parts)
    pieces_a = plane_pieces(sums_a, plane, core)
    dqkv, rest, _ = lax.optimization_barrier((dqkv, rest, sums_a))
    pieces_out += [swap(item, "row", row_parts, 3 + step) for step, item in enumerate(rest)]
    field_grad, = call(
        field_back, at(ANY, x, d_mid, gains) + at(FAR, dqkv, weights), at(FAR, x.shape),
        [scratch(*triple), scratch(3, *flat), scratch(*x.shape), copies((3,))],
    )
    field_grad, pieces_b = lax.optimization_barrier((field_grad, pieces_b))
    grads_b = last_sums_at_once(pieces_b, row_parts)
    field_grad, pieces_a = lax.optimization_barrier((field_grad, pieces_a))
    field_grad = lax.all_to_all(field_grad, "col", 0, 0, tiled=True).reshape(high, wide, channels)
    output = jnp.zeros((high, wide, channels), BF16)
    for step, piece in enumerate(pieces_out):
        piece = piece.reshape(high, cols, channels)
        output = lax.dynamic_update_slice_in_dim(output, piece, (my_row ^ step) * cols, axis=1)
    grads_a = last_sums(pieces_a, row_parts)
    return output, field_grad, jnp.concatenate([grads_a, grads_b], axis=0)


def solution(mesh):
    return jax.shard_map(
        functools.partial(body, mesh.shape["row"], mesh.shape["col"]),
        mesh=mesh,
        in_specs=(P("row", "col", None), P("row", "col", None), P(), P()),
        out_specs=(P("row", "col", None), P("row", "col", None), P(None, ("row", "col"), None)),
        check_vma=False,
    )
```

```python
import functools
import math

import jax
import jax.numpy as jnp
from jax import lax
from jax.experimental import pallas as pl
from jax.experimental.pallas import tpu as pltpu
from jax.sharding import PartitionSpec as P

HEADS = 8
eps = 1e-05
F32 = jnp.float32
BF16 = jnp.bfloat16


def log2(n):
    assert n & (n - 1) == 0
    return n.bit_length() - 1


def dot(left, right):
    return jnp.dot(left, right, preferred_element_type=F32)


def dot_nt(left, right):
    return lax.dot_general(left, right, (((1,), (1,)), ((), ())), preferred_element_type=F32)


def dot_tn(left, right):
    return lax.dot_general(left, right, (((0,), (0,)), ((), ())), preferred_element_type=F32)


def one_hot(sizes, order, me=None, lead=0):
    total = math.prod(sizes)
    index = lax.broadcasted_iota(jnp.int32, (total, total), lead)
    found = {}
    for axis in reversed(order):
        found[axis] = index & (sizes[axis] - 1)
        index = index >> log2(sizes[axis])
    source, shift = None, 0
    for axis in reversed(range(len(sizes))):
        digit = found[axis] << shift
        source = digit if source is None else source | digit
        shift += log2(sizes[axis])
    if me:
        place, shift = 0, 0
        for axis in reversed(range(len(sizes))):
            if axis in me:
                place = place | (me[axis] << shift)
            shift += log2(sizes[axis])
        source = source ^ place
    hit = source == lax.broadcasted_iota(jnp.int32, (total, total), 1 - lead)
    return jnp.where(hit, 1.0, 0.0).astype(BF16)


def statistics(values):
    average = jnp.mean(values, axis=-1, keepdims=True)
    centred = values - average
    spread = jnp.mean(centred * centred, axis=-1, keepdims=True)
    return centred, lax.rsqrt(spread + eps)


def norm_back(values, gain, d_normed):
    centred, inverse = statistics(values)
    unit = centred * inverse
    scaled = d_normed * gain
    return inverse * (
        scaled
        - jnp.mean(scaled, axis=-1, keepdims=True)
        - unit * jnp.mean(scaled * unit, axis=-1, keepdims=True)
    )


def head_lanes(count, width):
    return lax.broadcasted_iota(jnp.int32, (count, 2 * width), 1) < width


def attention_forward(q_ref, k_ref, v_ref, att_ref, p_ref, groups, count, width, span, unroll=2):
    first = head_lanes(count, width)
    pairs = HEADS // 2
    scale = width ** (-0.5)

    def step(index, carry):
        group, pair = index // pairs, index % pairs
        rows = pl.ds(pl.multiple_of(group * count, count), count)
        lanes = pl.ds(pl.multiple_of(pair * 2 * width, 2 * width), 2 * width)
        query, key, value = q_ref[rows, lanes] * scale, k_ref[rows, lanes], v_ref[rows, lanes]
        zero = jnp.zeros_like(query)
        total = jnp.zeros((count, 2 * width), F32)
        for half in range(2):
            mine = first if half == 0 else jnp.logical_not(first)
            scores = dot_nt(key, jnp.where(mine, query, zero))
            if span < count:
                shift = log2(span)
                same = (lax.broadcasted_iota(jnp.int32, (count, count), 0) >> shift) == (
                    lax.broadcasted_iota(jnp.int32, (count, count), 1) >> shift
                )
                scores = jnp.where(same, scores, -jnp.inf)
            expo = jnp.exp(scores - jnp.max(scores, axis=0, keepdims=True))
            probs = (expo * (1.0 / jnp.sum(expo, axis=0, keepdims=True))).astype(BF16)
            p_ref[index * 2 + half] = probs
            total += dot_tn(probs, jnp.where(mine, value, zero))
        att_ref[rows, lanes] = total.astype(BF16)
        return carry

    lax.fori_loop(0, groups * pairs, step, 0, unroll=unroll)


def attention_back(q_ref, k_ref, v_ref, p_ref, da_ref, dqkv_ref, groups, count, width, unroll=2):
    first = head_lanes(count, width)
    pairs = HEADS // 2
    channels = HEADS * width
    scale = width ** (-0.5)

    def step(index, carry):
        group, pair = index // pairs, index % pairs
        rows = pl.ds(pl.multiple_of(group * count, count), count)
        lanes = pl.ds(pl.multiple_of(pair * 2 * width, 2 * width), 2 * width)
        query, key, value = q_ref[rows, lanes] * scale, k_ref[rows, lanes], v_ref[rows, lanes]
        d_out = da_ref[rows, lanes]
        zero = jnp.zeros_like(query)
        d_query = jnp.zeros((count, 2 * width), F32)
        d_key, d_value = d_query, d_query
        for half in range(2):
            mine = first if half == 0 else jnp.logical_not(first)
            probs = p_ref[index * 2 + half]
            d_mine = jnp.where(mine, d_out, zero)
            d_probs = dot_nt(value, d_mine)
            probs32 = probs.astype(F32)
            weighted = probs32 * d_probs
            total = jnp.sum(weighted, axis=0, keepdims=True)
            d_scores = (weighted - probs32 * total).astype(BF16)
            d_query += dot_tn(d_scores, jnp.where(mine, key, zero))
            d_key += dot(d_scores, jnp.where(mine, query, zero))
            d_value += dot(probs, d_mine)
        for part, item in enumerate((d_query * scale, d_key, d_value)):
            at = pl.ds(pl.multiple_of(part * channels + pair * 2 * width, 2 * width), 2 * width)
            dqkv_ref[rows, at] = item.astype(BF16)
        return carry

    lax.fori_loop(0, groups * pairs, step, 0, unroll=unroll)


def start(source, target, sem):
    copy = pltpu.make_async_copy(source, target, sem)
    copy.start()
    return copy


def finish(copies):
    for copy in copies:
        copy.wait()


def set_up(turns, turn_hbm, turn_ref, sems):
    my_row, my_col = lax.axis_index("row"), lax.axis_index("col")
    places = {"row": my_row, "plane": my_col >> 1, "core": my_col & 1}
    going = []
    for at, (sizes, order, me, lead) in enumerate(turns):
        turn_ref[at] = one_hot(sizes, order, {axis: places[name] for axis, name in me.items()}, lead)
        going.append(start(turn_ref.at[at], turn_hbm.at[at], sems.at[at]))
    finish(going)


def weight_grad(part, left, right, keep_ref, send_ref):
    plane, _, size, _ = keep_ref.shape
    whole = dot_tn(left, right).astype(BF16)
    for group in range(plane):
        send_ref[group, part] = whole[(plane + group) * size : (plane + group + 1) * size]
        keep_ref[group, part] = whole[group * size : (group + 1) * size]


def send_grads(keep_ref, send_ref, keep_hbms, send_hbms, sems):
    plane = keep_ref.shape[0]
    going = [start(send_ref.at[at], send_hbms[at], sems.at[at]) for at in range(plane)]
    return going + [start(keep_ref.at[at], keep_hbms[at], sems.at[plane + at]) for at in range(plane)]


def third(ref, part):
    channels = ref.shape[-1] // 3
    return ref[:, part * channels : (part + 1) * channels]


def send_turned(turn_ref, values, stage_ref, targets, sems):
    size = values.shape[0] // len(targets)
    going = []
    for at, target in enumerate(targets):
        piece = pl.ds(at * size, size)
        stage_ref[piece] = dot(turn_ref[piece], values).astype(BF16)
        going.append(start(stage_ref.at[piece], target, sems.at[at]))
    return going


def quarters(ref):
    size = ref.shape[0] // 4
    return [ref.at[pl.ds(at * size, size)] for at in range(4)]


def input_back(dqkv_ref, w_refs):
    total = dot_nt(third(dqkv_ref, 0), w_refs[0][...])
    total += dot_nt(third(dqkv_ref, 1), w_refs[1][...])
    total += dot_nt(third(dqkv_ref, 2), w_refs[2][...])
    return total.astype(BF16).astype(F32)


def rows_of(x_ref):
    _, rows, _, channels = x_ref.shape
    length = x_ref.shape[0] * x_ref.shape[2]
    pieces = [x_ref[:, i].reshape(length, channels) for i in range(rows)]
    return jnp.concatenate(pieces, axis=0).astype(F32)


def row_forward(sizes, x_ref, g_ref, w_hbm, turn_hbm, mid_hbm, n_hbm, q_hbm, k_hbm, v_hbm, att_hbm, p_hbm,
                w_ref, turn_ref, mid_ref, n_ref, q_ref, k_ref, v_ref, att_ref, p_ref, in_sems, out_sems, sems):
    rows, length, width = sizes
    coming = [start(w_hbm.at[0, part], w_ref.at[part], in_sems.at[part]) for part in range(4)]
    coming.append(start(turn_hbm.at[0], turn_ref, in_sems.at[4]))
    centred, inverse = statistics(rows_of(x_ref))
    normed = (centred * inverse * g_ref[0:1]).astype(BF16)
    n_ref[...] = normed
    going = [start(n_ref, n_hbm, out_sems.at[0])]
    for part, (ref, hbm) in enumerate(((q_ref, q_hbm), (k_ref, k_hbm), (v_ref, v_hbm))):
        coming[part].wait()
        ref[...] = dot(normed, w_ref[part]).astype(BF16)
        going.append(start(ref, hbm, out_sems.at[1 + part]))
    attention_forward(q_ref, k_ref, v_ref, att_ref, p_ref, rows, length, width, length)
    going.append(start(p_ref, p_hbm, out_sems.at[5]))
    going.append(start(att_ref, att_hbm, out_sems.at[4]))
    coming[3].wait()
    middle = (rows_of(x_ref) + dot(att_ref[...], w_ref[3])).astype(BF16)
    coming[4].wait()
    finish(going + send_turned(turn_ref, middle, mid_ref, quarters(mid_hbm), sems))


def row_back(sizes, d_ref, w_hbm, turn_hbm, n_hbm, q_hbm, k_hbm, v_hbm, att_hbm, p_hbm, *refs):
    rows, length, width, plane = sizes
    dm_ref, dqkv_hbm, keep_hbms, send_hbms = refs[0], refs[1], refs[2 : 2 + plane], refs[2 + plane : 2 + 2 * plane]
    w_ref, turn_ref, n_ref, q_ref, k_ref, v_ref, att_ref, p_ref, da_ref, dqkv_ref = refs[2 + 2 * plane : -4]
    keep_ref, send_ref, sems, out_sems = refs[-4:]
    half = p_ref.shape[0] // 2
    coming = [
        start(turn_hbm.at[1], turn_ref.at[0], sems.at[0]), start(w_hbm.at[0, 3], w_ref, sems.at[1]),
        start(v_hbm, v_ref, sems.at[2]), start(k_hbm, k_ref, sems.at[3]), start(q_hbm, q_ref, sems.at[4]),
        start(p_hbm.at[pl.ds(0, half)], p_ref.at[pl.ds(0, half)], sems.at[5]),
        start(p_hbm.at[pl.ds(half, half)], p_ref.at[pl.ds(half, half)], sems.at[6]),
        start(turn_hbm.at[6], turn_ref.at[1], sems.at[7]), start(att_hbm, att_ref, sems.at[8]),
        start(n_hbm, n_ref, sems.at[9]),
    ]
    coming[0].wait()
    d_middle = dot(turn_ref[0], d_ref[...]).astype(BF16)
    dm_ref[...] = d_middle
    coming[1].wait()
    da_ref[...] = dot_nt(d_middle, w_ref[...]).astype(BF16)
    finish(coming[2:7])
    attention_back(q_ref, k_ref, v_ref, p_ref, da_ref, dqkv_ref, rows, length, width)
    going = [start(dqkv_ref, dqkv_hbm, sems.at[10])]
    finish(coming[7:])
    normed = dot(n_ref[...], turn_ref[1]).astype(BF16)
    for part in range(3):
        weight_grad(part, normed, third(dqkv_ref, part), keep_ref, send_ref)
    attended = dot(att_ref[...], turn_ref[1]).astype(BF16)
    weight_grad(3, attended, dm_ref[...], keep_ref, send_ref)
    finish(going + send_grads(keep_ref, send_ref, keep_hbms, send_hbms, out_sems))


def field_back(x_ref, dm_ref, g_ref, dqkv_hbm, w_hbm, fg_hbm, dqkv_ref, w_ref, fg_ref, sems):
    coming = [start(dqkv_hbm, dqkv_ref, sems.at[0]), start(w_hbm.at[0, 0:3], w_ref, sems.at[1])]
    _, rows, _, channels = x_ref.shape
    length = x_ref.shape[0] * x_ref.shape[2]
    finish(coming)
    d_normed = input_back(dqkv_ref, [w_ref.at[part] for part in range(3)])
    result = dm_ref[...].astype(F32) + norm_back(rows_of(x_ref), g_ref[0:1], d_normed)
    result = result.astype(BF16)
    for i in range(rows):
        piece = result[i * length : (i + 1) * length]
        fg_ref[:, i] = piece.reshape(fg_ref.shape[0], fg_ref.shape[2], channels)
    start(fg_ref, fg_hbm, sems.at[2]).wait()


def column_first(parts, *refs):
    c_refs, (w_hbm, turn_hbm, cot_ref, da_ref, early_ref, w_ref, turn_ref, sems) = refs[:parts], refs[parts:]
    coming = [
        start(turn_hbm.at[4], turn_ref, sems.at[0]), start(w_hbm.at[1, 3], w_ref, sems.at[1]),
        start(turn_hbm.at[2], early_ref.at[0], sems.at[2]), start(w_hbm.at[1, 0], early_ref.at[1], sems.at[3]),
    ]
    cotangent = jnp.concatenate([ref[...] for ref in c_refs], axis=0)
    coming[0].wait()
    cotangent = dot(turn_ref[...], cotangent).astype(BF16)
    cot_ref[...] = cotangent
    coming[1].wait()
    da_ref[...] = dot_nt(cotangent, w_ref[...]).astype(BF16)
    finish(coming[2:])


def column_main(sizes, m_ref, cot_ref, da_ref, early_ref, g_ref, w_hbm, turn_hbm,
                dm_hbm, mid_hbm, n_hbm, att_hbm, dqkv_hbm,
                w_ref, turn_ref, dm_ref, mid_ref, n_ref, att_ref, dqkv_ref, q_ref, k_ref, v_ref, p_ref, sems):
    height, cols, width, together = sizes
    coming = [
        start(w_hbm.at[1, 1], w_ref.at[0], sems.at[0]), start(w_hbm.at[1, 2], w_ref.at[1], sems.at[1]),
        start(turn_hbm.at[3], turn_ref, sems.at[2]),
    ]
    middle = dot(early_ref[0], m_ref[...])
    mid_ref[...] = middle.astype(BF16)
    going = [start(mid_ref, mid_hbm, sems.at[3])]
    centred, inverse = statistics(middle)
    normed = (centred * inverse * g_ref[1:2]).astype(BF16)
    n_ref[...] = normed
    going.append(start(n_ref, n_hbm, sems.at[4]))
    q_ref[...] = dot(normed, early_ref[1]).astype(BF16)
    coming[0].wait()
    k_ref[...] = dot(normed, w_ref[0]).astype(BF16)
    coming[1].wait()
    v_ref[...] = dot(normed, w_ref[1]).astype(BF16)
    count = together * height
    groups = cols // together
    attention_forward(q_ref, k_ref, v_ref, att_ref, p_ref, groups, count, width, height, 4)
    going.append(start(att_ref, att_hbm, sems.at[5]))
    attention_back(q_ref, k_ref, v_ref, p_ref, da_ref, dqkv_ref, groups, count, width, 4)
    going.append(start(dqkv_ref, dqkv_hbm, sems.at[6]))
    d_normed = input_back(dqkv_ref, [early_ref.at[1], w_ref.at[0], w_ref.at[1]])
    middle = mid_ref[...].astype(F32)
    d_middle = cot_ref[...].astype(F32) + norm_back(middle, g_ref[1:2], d_normed)
    coming[2].wait()
    finish(going + send_turned(turn_ref, d_middle.astype(BF16), dm_ref, quarters(dm_hbm), sems.at[pl.ds(7, 4)]))


def column_last(parts, plane, cot_hbm, mid_hbm, n_hbm, att_hbm, dqkv_hbm, w_hbm, turn_hbm, *refs):
    out_hbms, refs = refs[:parts], refs[parts:]
    keep_hbms, send_hbms, refs = refs[:plane], refs[plane : 2 * plane], refs[2 * plane :]
    out_ref, keep_ref, send_ref, w_ref, turn_ref, flat_ref, dqkv_ref, sems, out_sems = refs
    coming = [
        start(turn_hbm.at[6], turn_ref.at[0], sems.at[0]), start(n_hbm, flat_ref.at[0], sems.at[1]),
        start(dqkv_hbm, dqkv_ref, sems.at[2]), start(att_hbm, flat_ref.at[1], sems.at[3]),
        start(cot_hbm, flat_ref.at[2], sems.at[4]), start(mid_hbm, flat_ref.at[3], sems.at[5]),
        start(w_hbm.at[1, 3], w_ref, sems.at[6]), start(turn_hbm.at[5], turn_ref.at[1], sems.at[7]),
    ]
    finish(coming[:3])
    normed = dot(flat_ref[0], turn_ref[0]).astype(BF16)
    for part in range(3):
        weight_grad(part, normed, third(dqkv_ref, part), keep_ref, send_ref)
    finish(coming[3:])
    attended = dot(flat_ref[1], turn_ref[0]).astype(BF16)
    weight_grad(3, attended, flat_ref[2], keep_ref, send_ref)
    going = send_grads(keep_ref, send_ref, keep_hbms, send_hbms, out_sems)
    output = (flat_ref[3].astype(F32) + dot(flat_ref[1], w_ref[...])).astype(BF16)
    finish(going + send_turned(turn_ref.at[1], output, out_ref, out_hbms, sems.at[pl.ds(8, parts)]))


def add_pairs(count, *refs):
    keep_hbms, got_refs, sum_refs, (keep_ref, sems) = (
        refs[:count], refs[count : 2 * count], refs[2 * count : 3 * count], refs[3 * count :]
    )
    coming = [start(hbm, keep_ref.at[at], sems.at[at]) for at, hbm in enumerate(keep_hbms)]
    for at, copy in enumerate(coming):
        copy.wait()
        sum_refs[at][...] = (keep_ref[at].astype(F32) + got_refs[at][...].astype(F32)).astype(BF16)


NEAR, FAR, ANY = pltpu.VMEM, pltpu.HBM, None


def call(kernel, ins, outs, scratch):
    def spec(where):
        return pl.BlockSpec(memory_space=pltpu.HBM if where is FAR else pltpu.VMEM)

    def place(item, where):
        return item if where is ANY else pltpu.with_memory_space_constraint(item, where)

    return pl.pallas_call(
        kernel,
        in_specs=[spec(where) for _, where in ins],
        out_specs=[spec(where) for _, where in outs],
        out_shape=[jax.ShapeDtypeStruct(shape, BF16) if where is ANY else where(shape, BF16) for shape, where in outs],
        scratch_shapes=scratch,
        compiler_params=pltpu.CompilerParams(vmem_limit_bytes=48 * 1024 * 1024),
        cost_estimate=pl.CostEstimate(flops=1 << 20, bytes_accessed=1 << 10, transcendentals=0),
    )(*[place(item, where) for item, where in ins])


def swap(item, axis, count, step):
    return lax.ppermute(item, axis, [(at, at ^ step) for at in range(count)])


def chip_sums(keeps, sends, col_parts):
    got = [swap(send, "col", col_parts, 1) for send in sends]
    count, shape = len(keeps), keeps[0].shape
    return call(
        functools.partial(add_pairs, count),
        [(item, FAR) for item in keeps] + [(item, ANY) for item in got], [(shape, ANY)] * count,
        [pltpu.VMEM((count, *shape), BF16), pltpu.SemaphoreType.DMA((count,))],
    )


def plane_pieces(sums, plane, core):
    return [item if step == 0 else swap(item, "col", plane * core, step * core) for step, item in enumerate(sums)]


def last_sums(pieces, row_parts):
    parts, size, channels = pieces[0].shape
    held = sum(piece.astype(F32) for piece in pieces).astype(BF16)
    held = held.reshape(parts, row_parts, size // row_parts, channels)
    result = held[:, 0].astype(F32)
    for step in range(1, row_parts):
        result = result + swap(held[:, step], "row", row_parts, step).astype(F32)
    return result


def body(row_parts, col_parts, field, cotangent, gains, weights):
    high, wide, channels = field.shape
    core = 2
    plane = col_parts // core
    rows = high // col_parts
    cols = wide // row_parts
    tokens = high * wide
    height = high * row_parts
    length = wide * col_parts
    width = channels // HEADS
    together = min(cols, max(1, 128 // height))
    devices = row_parts * col_parts
    my_row = lax.axis_index("row")

    flat, triple = (tokens, channels), (tokens, 3 * channels)
    probs = (rows * HEADS, length, length)
    packed = (4, channels // col_parts, channels)

    def scratch(*shape):
        return pltpu.VMEM(shape, BF16)

    def at(where, *items):
        return [(item, where) for item in items]

    square = scratch(*flat)
    copies = pltpu.SemaphoreType.DMA
    assert channels == tokens
    turns = [
        ((rows, col_parts, row_parts, cols), (2, 1, 0, 3), {}, 0),
        ((row_parts, col_parts, rows, cols), (2, 1, 0, 3), {}, 0),
        ((height, cols), (1, 0), {}, 0),
        ((cols, height), (1, 0), {}, 0),
        ((row_parts, high, cols), (2, 0, 1), {0: "row"}, 0),
        ((cols, row_parts, high), (1, 2, 0), {1: "row"}, 0),
        ((row_parts, plane, core, channels // devices), (2, 1, 0, 3), {0: "row", 1: "plane", 2: "core"}, 1),
    ]

    def all_to_all(item):
        item = item.reshape(devices, rows * cols, channels)
        return lax.all_to_all(item, ("row", "col"), 0, 0, tiled=True).reshape(tokens, channels)

    x = lax.all_to_all(field.reshape(col_parts, rows, wide, channels), "col", 0, 0, tiled=True)
    cots = []
    for step in range(row_parts):
        piece = lax.dynamic_slice_in_dim(cotangent, (my_row ^ step) * cols, cols, axis=1)
        piece = piece if step == 0 else swap(piece, "row", row_parts, step)
        cots.append(piece.reshape(high * cols, channels))
    turn, = call(
        functools.partial(set_up, turns), [], at(FAR, (len(turns), *flat)),
        [scratch(len(turns), *flat), copies((len(turns),))],
    )

    sizes = (rows, length, width)
    mid, normed, query, key, value, attended, prob = call(
        functools.partial(row_forward, sizes),
        at(ANY, x, gains) + at(FAR, weights, turn), at(FAR, *[flat] * 6, probs),
        [scratch(4, *flat)] + [square] * 7 + [scratch(*probs), copies((5,)), copies((6,)), copies((4,))],
    )
    mid, cots = lax.optimization_barrier((mid, cots))
    cot, d_att, early = call(
        functools.partial(column_first, row_parts),
        at(ANY, *cots) + at(FAR, weights, turn), at(NEAR, flat, flat, (2, *flat)), [square, square, copies((4,))],
    )
    mid = all_to_all(mid)

    count = together * height
    d_mid, *kept = call(
        functools.partial(column_main, (height, cols, width, together)),
        at(ANY, mid) + at(NEAR, cot, d_att, early) + at(ANY, gains) + at(FAR, weights, turn),
        at(FAR, flat, flat, flat, flat, triple),
        [scratch(2, *flat)] + [square] * 5 + [scratch(*triple)] + [square] * 3
        + [scratch(cols // together * HEADS, count, count), copies((11,))],
    )
    d_mid = all_to_all(d_mid)
    results = call(
        functools.partial(column_last, row_parts, plane),
        at(FAR, cot, *kept, weights, turn), at(FAR, *[(high * cols, channels)] * row_parts, *[packed] * (2 * plane)),
        [square, scratch(plane, *packed), scratch(plane, *packed), square, scratch(2, *flat), scratch(4, *flat),
         scratch(*triple), copies((8 + row_parts,)), copies((2 * plane,))],
    )
    outs, grads = results[:row_parts], results[row_parts:]
    sums_b = chip_sums(grads[:plane], grads[plane:], col_parts)
    pieces_b = plane_pieces(sums_b, plane, core)
    pieces_out = [outs[0], swap(outs[1], "row", row_parts, 1)]
    d_mid, rest, _ = lax.optimization_barrier((d_mid, outs[2:], sums_b))
    pieces_out += [swap(item, "row", row_parts, 2 + step) for step, item in enumerate(rest[:1])]
    results = call(
        functools.partial(row_back, (rows, length, width, plane)),
        at(ANY, d_mid) + at(FAR, weights, turn, normed, query, key, value, attended, prob),
        at(ANY, flat) + at(FAR, triple, *[packed] * (2 * plane)),
        [square, scratch(2, *flat)] + [square] * 5 + [scratch(*probs), square, scratch(*triple)]
        + [scratch(plane, *packed), scratch(plane, *packed), copies((11,)), copies((2 * plane,))],
    )
    (d_mid, dqkv, *grads), pieces_b, pieces_out, rest = lax.optimization_barrier(
        (results, pieces_b, pieces_out, rest[1:])
    )
    sums_a = chip_sums(grads[:plane], grads[plane:], col_parts)
    pieces_a = plane_pieces(sums_a, plane, core)
    dqkv, _ = lax.optimization_barrier((dqkv, sums_a))
    field_grad, = call(
        field_back, at(ANY, x, d_mid, gains) + at(FAR, dqkv, weights), at(FAR, x.shape),
        [scratch(*triple), scratch(3, *flat), scratch(*x.shape), copies((3,))],
    )
    field_grad, pieces_b = lax.optimization_barrier((field_grad, pieces_b))
    grads_b = last_sums(pieces_b, row_parts)
    field_grad, pieces_a, rest = lax.optimization_barrier((field_grad, pieces_a, rest))
    field_grad = lax.all_to_all(field_grad, "col", 0, 0, tiled=True).reshape(high, wide, channels)
    pieces_out += [swap(item, "row", row_parts, 3 + step) for step, item in enumerate(rest)]
    output = jnp.zeros((high, wide, channels), BF16)
    for step, piece in enumerate(pieces_out):
        piece = piece.reshape(high, cols, channels)
        output = lax.dynamic_update_slice_in_dim(output, piece, (my_row ^ step) * cols, axis=1)
    grads_a = last_sums(pieces_a, row_parts)
    return output, field_grad, jnp.concatenate([grads_a, grads_b], axis=0)


def solution(mesh):
    return jax.shard_map(
        functools.partial(body, mesh.shape["row"], mesh.shape["col"]),
        mesh=mesh,
        in_specs=(P("row", "col", None), P("row", "col", None), P(), P()),
        out_specs=(P("row", "col", None), P("row", "col", None), P(None, ("row", "col"), None)),
        check_vma=False,
    )
```

```python
import functools
import math

import jax
import jax.numpy as jnp
from jax import lax
from jax.experimental import pallas as pl
from jax.experimental.pallas import tpu as pltpu
from jax.sharding import PartitionSpec as P

HEADS = 8
eps = 1e-05
F32 = jnp.float32
BF16 = jnp.bfloat16


def log2(n):
    assert n & (n - 1) == 0
    return n.bit_length() - 1


def dot(left, right):
    return jnp.dot(left, right, preferred_element_type=F32)


def dot_nt(left, right):
    return lax.dot_general(left, right, (((1,), (1,)), ((), ())), preferred_element_type=F32)


def dot_tn(left, right):
    return lax.dot_general(left, right, (((0,), (0,)), ((), ())), preferred_element_type=F32)


def one_hot(sizes, order, me=None, lead=0):
    total = math.prod(sizes)
    index = lax.broadcasted_iota(jnp.int32, (total, total), lead)
    found = {}
    for axis in reversed(order):
        found[axis] = index & (sizes[axis] - 1)
        index = index >> log2(sizes[axis])
    source, shift = None, 0
    for axis in reversed(range(len(sizes))):
        digit = found[axis] << shift
        source = digit if source is None else source | digit
        shift += log2(sizes[axis])
    if me:
        place, shift = 0, 0
        for axis in reversed(range(len(sizes))):
            if axis in me:
                place = place | (me[axis] << shift)
            shift += log2(sizes[axis])
        source = source ^ place
    hit = source == lax.broadcasted_iota(jnp.int32, (total, total), 1 - lead)
    return jnp.where(hit, 1.0, 0.0).astype(BF16)


def statistics(values):
    average = jnp.mean(values, axis=-1, keepdims=True)
    centred = values - average
    spread = jnp.mean(centred * centred, axis=-1, keepdims=True)
    return centred, lax.rsqrt(spread + eps)


def norm_back(values, gain, d_normed):
    centred, inverse = statistics(values)
    unit = centred * inverse
    scaled = d_normed * gain
    return inverse * (
        scaled
        - jnp.mean(scaled, axis=-1, keepdims=True)
        - unit * jnp.mean(scaled * unit, axis=-1, keepdims=True)
    )


def head_lanes(count, width):
    return lax.broadcasted_iota(jnp.int32, (count, 2 * width), 1) < width


def attention_forward(q_ref, k_ref, v_ref, att_ref, p_ref, groups, count, width, span, unroll=4):
    first = head_lanes(count, width)
    pairs = HEADS // 2
    scale = width ** (-0.5)

    def step(index, carry):
        group, pair = index // pairs, index % pairs
        rows = pl.ds(pl.multiple_of(group * count, count), count)
        lanes = pl.ds(pl.multiple_of(pair * 2 * width, 2 * width), 2 * width)
        query, key, value = q_ref[rows, lanes] * scale, k_ref[rows, lanes], v_ref[rows, lanes]
        zero = jnp.zeros_like(query)
        total = jnp.zeros((count, 2 * width), F32)
        for half in range(2):
            mine = first if half == 0 else jnp.logical_not(first)
            scores = dot_nt(key, jnp.where(mine, query, zero))
            if span < count:
                shift = log2(span)
                same = (lax.broadcasted_iota(jnp.int32, (count, count), 0) >> shift) == (
                    lax.broadcasted_iota(jnp.int32, (count, count), 1) >> shift
                )
                scores = jnp.where(same, scores, -jnp.inf)
            expo = jnp.exp(scores - jnp.max(scores, axis=0, keepdims=True))
            probs = (expo * (1.0 / jnp.sum(expo, axis=0, keepdims=True))).astype(BF16)
            p_ref[index * 2 + half] = probs
            total += dot_tn(probs, jnp.where(mine, value, zero))
        att_ref[rows, lanes] = total.astype(BF16)
        return carry

    lax.fori_loop(0, groups * pairs, step, 0, unroll=unroll)


def attention_back(q_ref, k_ref, v_ref, p_ref, da_ref, dqkv_ref, groups, count, width, unroll=4):
    first = head_lanes(count, width)
    pairs = HEADS // 2
    channels = HEADS * width
    scale = width ** (-0.5)

    def step(index, carry):
        group, pair = index // pairs, index % pairs
        rows = pl.ds(pl.multiple_of(group * count, count), count)
        lanes = pl.ds(pl.multiple_of(pair * 2 * width, 2 * width), 2 * width)
        query, key, value = q_ref[rows, lanes] * scale, k_ref[rows, lanes], v_ref[rows, lanes]
        d_out = da_ref[rows, lanes]
        zero = jnp.zeros_like(query)
        d_query = jnp.zeros((count, 2 * width), F32)
        d_key, d_value = d_query, d_query
        for half in range(2):
            mine = first if half == 0 else jnp.logical_not(first)
            probs = p_ref[index * 2 + half]
            d_mine = jnp.where(mine, d_out, zero)
            d_probs = dot_nt(value, d_mine)
            probs32 = probs.astype(F32)
            weighted = probs32 * d_probs
            total = jnp.sum(weighted, axis=0, keepdims=True)
            d_scores = (weighted - probs32 * total).astype(BF16)
            d_query += dot_tn(d_scores, jnp.where(mine, key, zero))
            d_key += dot(d_scores, jnp.where(mine, query, zero))
            d_value += dot(probs, d_mine)
        for part, item in enumerate((d_query * scale, d_key, d_value)):
            at = pl.ds(pl.multiple_of(part * channels + pair * 2 * width, 2 * width), 2 * width)
            dqkv_ref[rows, at] = item.astype(BF16)
        return carry

    lax.fori_loop(0, groups * pairs, step, 0, unroll=unroll)


def start(source, target, sem):
    copy = pltpu.make_async_copy(source, target, sem)
    copy.start()
    return copy


def finish(copies):
    for copy in copies:
        copy.wait()


def set_up(turns, turn_hbm, turn_ref, sems):
    my_row, my_col = lax.axis_index("row"), lax.axis_index("col")
    places = {"row": my_row, "plane": my_col >> 1, "core": my_col & 1}
    going = []
    for at, (sizes, order, me, lead) in enumerate(turns):
        turn_ref[at] = one_hot(sizes, order, {axis: places[name] for axis, name in me.items()}, lead)
        going.append(start(turn_ref.at[at], turn_hbm.at[at], sems.at[at]))
    finish(going)


def weight_grad(part, left, right, keep_ref, send_ref):
    plane, _, size, _ = keep_ref.shape
    whole = dot_tn(left, right).astype(BF16)
    for group in range(plane):
        send_ref[group, part] = whole[(plane + group) * size : (plane + group + 1) * size]
        keep_ref[group, part] = whole[group * size : (group + 1) * size]


def send_grads(keep_ref, send_ref, keep_hbms, send_hbms, sems):
    plane = keep_ref.shape[0]
    going = [start(send_ref.at[at], send_hbms[at], sems.at[at]) for at in range(plane)]
    return going + [start(keep_ref.at[at], keep_hbms[at], sems.at[plane + at]) for at in range(plane)]


def third(ref, part):
    channels = ref.shape[-1] // 3
    return ref[:, part * channels : (part + 1) * channels]


def send_turned(turn_ref, values, stage_ref, targets, sems):
    size = values.shape[0] // len(targets)
    going = []
    for at, target in enumerate(targets):
        piece = pl.ds(at * size, size)
        stage_ref[piece] = dot(turn_ref[piece], values).astype(BF16)
        going.append(start(stage_ref.at[piece], target, sems.at[at]))
    return going


def quarters(ref):
    size = ref.shape[0] // 4
    return [ref.at[pl.ds(at * size, size)] for at in range(4)]


def input_back(dqkv_ref, w_refs):
    total = dot_nt(third(dqkv_ref, 0), w_refs[0][...])
    total += dot_nt(third(dqkv_ref, 1), w_refs[1][...])
    total += dot_nt(third(dqkv_ref, 2), w_refs[2][...])
    return total.astype(BF16).astype(F32)


def rows_of(x_ref):
    _, rows, _, channels = x_ref.shape
    length = x_ref.shape[0] * x_ref.shape[2]
    pieces = [x_ref[:, i].reshape(length, channels) for i in range(rows)]
    return jnp.concatenate(pieces, axis=0).astype(F32)


def row_forward(sizes, x_ref, g_ref, w_hbm, turn_hbm, mid_hbm, n_hbm, q_hbm, k_hbm, v_hbm, att_hbm, p_hbm,
                w_ref, turn_ref, mid_ref, n_ref, q_ref, k_ref, v_ref, att_ref, p_ref, in_sems, out_sems, sems):
    rows, length, width = sizes
    coming = [start(w_hbm.at[0, part], w_ref.at[part], in_sems.at[part]) for part in range(4)]
    coming.append(start(turn_hbm.at[0], turn_ref, in_sems.at[4]))
    centred, inverse = statistics(rows_of(x_ref))
    normed = (centred * inverse * g_ref[0:1]).astype(BF16)
    n_ref[...] = normed
    going = [start(n_ref, n_hbm, out_sems.at[0])]
    for part, (ref, hbm) in enumerate(((q_ref, q_hbm), (k_ref, k_hbm), (v_ref, v_hbm))):
        coming[part].wait()
        ref[...] = dot(normed, w_ref[part]).astype(BF16)
        going.append(start(ref, hbm, out_sems.at[1 + part]))
    attention_forward(q_ref, k_ref, v_ref, att_ref, p_ref, rows, length, width, length)
    going.append(start(p_ref, p_hbm, out_sems.at[5]))
    going.append(start(att_ref, att_hbm, out_sems.at[4]))
    coming[3].wait()
    middle = (rows_of(x_ref) + dot(att_ref[...], w_ref[3])).astype(BF16)
    coming[4].wait()
    finish(going + send_turned(turn_ref, middle, mid_ref, quarters(mid_hbm), sems))


def row_back(sizes, d_ref, w_hbm, turn_hbm, n_hbm, q_hbm, k_hbm, v_hbm, att_hbm, p_hbm, *refs):
    rows, length, width, plane = sizes
    dm_ref, dqkv_hbm, keep_hbms, send_hbms = refs[0], refs[1], refs[2 : 2 + plane], refs[2 + plane : 2 + 2 * plane]
    w_ref, turn_ref, n_ref, q_ref, k_ref, v_ref, att_ref, p_ref, da_ref, dqkv_ref = refs[2 + 2 * plane : -4]
    keep_ref, send_ref, sems, out_sems = refs[-4:]
    half = p_ref.shape[0] // 2
    coming = [
        start(turn_hbm.at[1], turn_ref.at[0], sems.at[0]), start(w_hbm.at[0, 3], w_ref, sems.at[1]),
        start(v_hbm, v_ref, sems.at[2]), start(k_hbm, k_ref, sems.at[3]), start(q_hbm, q_ref, sems.at[4]),
        start(p_hbm.at[pl.ds(0, half)], p_ref.at[pl.ds(0, half)], sems.at[5]),
        start(p_hbm.at[pl.ds(half, half)], p_ref.at[pl.ds(half, half)], sems.at[6]),
        start(turn_hbm.at[6], turn_ref.at[1], sems.at[7]), start(att_hbm, att_ref, sems.at[8]),
        start(n_hbm, n_ref, sems.at[9]),
    ]
    coming[0].wait()
    d_middle = dot(turn_ref[0], d_ref[...]).astype(BF16)
    dm_ref[...] = d_middle
    coming[1].wait()
    da_ref[...] = dot_nt(d_middle, w_ref[...]).astype(BF16)
    finish(coming[2:7])
    attention_back(q_ref, k_ref, v_ref, p_ref, da_ref, dqkv_ref, rows, length, width)
    going = [start(dqkv_ref, dqkv_hbm, sems.at[10])]
    finish(coming[7:])
    normed = dot(n_ref[...], turn_ref[1]).astype(BF16)
    for part in range(3):
        weight_grad(part, normed, third(dqkv_ref, part), keep_ref, send_ref)
    attended = dot(att_ref[...], turn_ref[1]).astype(BF16)
    weight_grad(3, attended, dm_ref[...], keep_ref, send_ref)
    finish(going + send_grads(keep_ref, send_ref, keep_hbms, send_hbms, out_sems))


def field_back(x_ref, dm_ref, g_ref, dqkv_hbm, w_hbm, fg_hbm, dqkv_ref, w_ref, fg_ref, sems):
    coming = [start(dqkv_hbm, dqkv_ref, sems.at[0]), start(w_hbm.at[0, 0:3], w_ref, sems.at[1])]
    _, rows, _, channels = x_ref.shape
    length = x_ref.shape[0] * x_ref.shape[2]
    finish(coming)
    d_normed = input_back(dqkv_ref, [w_ref.at[part] for part in range(3)])
    result = dm_ref[...].astype(F32) + norm_back(rows_of(x_ref), g_ref[0:1], d_normed)
    result = result.astype(BF16)
    for i in range(rows):
        piece = result[i * length : (i + 1) * length]
        fg_ref[:, i] = piece.reshape(fg_ref.shape[0], fg_ref.shape[2], channels)
    start(fg_ref, fg_hbm, sems.at[2]).wait()


def store(x_ref, x_hbm, sem):
    start(x_ref, x_hbm, sem).wait()


def column_first(parts, *refs):
    c_refs, (w_hbm, turn_hbm, cot_ref, da_ref, early_ref, w_ref, turn_ref, sems) = refs[:parts], refs[parts:]
    coming = [
        start(turn_hbm.at[4], turn_ref, sems.at[0]), start(w_hbm.at[1, 3], w_ref, sems.at[1]),
        start(turn_hbm.at[2], early_ref.at[0], sems.at[2]), start(w_hbm.at[1, 0], early_ref.at[1], sems.at[3]),
    ]
    cotangent = jnp.concatenate([ref[...] for ref in c_refs], axis=0)
    coming[0].wait()
    cotangent = dot(turn_ref[...], cotangent).astype(BF16)
    cot_ref[...] = cotangent
    coming[1].wait()
    da_ref[...] = dot_nt(cotangent, w_ref[...]).astype(BF16)
    finish(coming[2:])


def column_main(sizes, m_ref, cot_ref, da_ref, early_ref, g_ref, w_hbm, turn_hbm,
                dm_hbm, mid_hbm, n_hbm, att_hbm, dqkv_hbm,
                w_ref, turn_ref, dm_ref, mid_ref, n_ref, att_ref, dqkv_ref, q_ref, k_ref, v_ref, p_ref, sems):
    height, cols, width, together = sizes
    coming = [
        start(w_hbm.at[1, 1], w_ref.at[0], sems.at[0]), start(w_hbm.at[1, 2], w_ref.at[1], sems.at[1]),
        start(turn_hbm.at[3], turn_ref, sems.at[2]),
    ]
    middle = dot(early_ref[0], m_ref[...])
    mid_ref[...] = middle.astype(BF16)
    going = [start(mid_ref, mid_hbm, sems.at[3])]
    centred, inverse = statistics(middle)
    normed = (centred * inverse * g_ref[1:2]).astype(BF16)
    n_ref[...] = normed
    going.append(start(n_ref, n_hbm, sems.at[4]))
    q_ref[...] = dot(normed, early_ref[1]).astype(BF16)
    coming[0].wait()
    k_ref[...] = dot(normed, w_ref[0]).astype(BF16)
    coming[1].wait()
    v_ref[...] = dot(normed, w_ref[1]).astype(BF16)
    count = together * height
    groups = cols // together
    attention_forward(q_ref, k_ref, v_ref, att_ref, p_ref, groups, count, width, height)
    going.append(start(att_ref, att_hbm, sems.at[5]))
    attention_back(q_ref, k_ref, v_ref, p_ref, da_ref, dqkv_ref, groups, count, width)
    going.append(start(dqkv_ref, dqkv_hbm, sems.at[6]))
    d_normed = input_back(dqkv_ref, [early_ref.at[1], w_ref.at[0], w_ref.at[1]])
    middle = mid_ref[...].astype(F32)
    d_middle = cot_ref[...].astype(F32) + norm_back(middle, g_ref[1:2], d_normed)
    coming[2].wait()
    finish(going + send_turned(turn_ref, d_middle.astype(BF16), dm_ref, quarters(dm_hbm), sems.at[pl.ds(7, 4)]))


def column_last(parts, plane, cot_hbm, mid_hbm, n_hbm, att_hbm, dqkv_hbm, w_hbm, turn_hbm, *refs):
    out_hbms, refs = refs[:parts], refs[parts:]
    keep_hbms, send_hbms, refs = refs[:plane], refs[plane : 2 * plane], refs[2 * plane :]
    out_ref, keep_ref, send_ref, w_ref, turn_ref, flat_ref, dqkv_ref, sems, out_sems = refs
    coming = [
        start(turn_hbm.at[6], turn_ref.at[0], sems.at[0]), start(n_hbm, flat_ref.at[0], sems.at[1]),
        start(dqkv_hbm, dqkv_ref, sems.at[2]), start(att_hbm, flat_ref.at[1], sems.at[3]),
        start(cot_hbm, flat_ref.at[2], sems.at[4]), start(mid_hbm, flat_ref.at[3], sems.at[5]),
        start(w_hbm.at[1, 3], w_ref, sems.at[6]), start(turn_hbm.at[5], turn_ref.at[1], sems.at[7]),
    ]
    finish(coming[:3])
    normed = dot(flat_ref[0], turn_ref[0]).astype(BF16)
    for part in range(3):
        weight_grad(part, normed, third(dqkv_ref, part), keep_ref, send_ref)
    finish(coming[3:])
    attended = dot(flat_ref[1], turn_ref[0]).astype(BF16)
    weight_grad(3, attended, flat_ref[2], keep_ref, send_ref)
    going = send_grads(keep_ref, send_ref, keep_hbms, send_hbms, out_sems)
    output = (flat_ref[3].astype(F32) + dot(flat_ref[1], w_ref[...])).astype(BF16)
    finish(going + send_turned(turn_ref.at[1], output, out_ref, out_hbms, sems.at[pl.ds(8, parts)]))


def add_pairs(count, *refs):
    keep_hbms, got_refs, sum_refs, (keep_ref, sems) = (
        refs[:count], refs[count : 2 * count], refs[2 * count : 3 * count], refs[3 * count :]
    )
    coming = [start(hbm, keep_ref.at[at], sems.at[at]) for at, hbm in enumerate(keep_hbms)]
    for at, copy in enumerate(coming):
        copy.wait()
        sum_refs[at][...] = (keep_ref[at].astype(F32) + got_refs[at][...].astype(F32)).astype(BF16)


NEAR, FAR, ANY = pltpu.VMEM, pltpu.HBM, None


def call(kernel, ins, outs, scratch, flops=1 << 20):
    def spec(where):
        return pl.BlockSpec(memory_space=pltpu.HBM if where is FAR else pltpu.VMEM)

    def place(item, where):
        return item if where is ANY else pltpu.with_memory_space_constraint(item, where)

    return pl.pallas_call(
        kernel,
        in_specs=[spec(where) for _, where in ins],
        out_specs=[spec(where) for _, where in outs],
        out_shape=[jax.ShapeDtypeStruct(shape, BF16) if where is ANY else where(shape, BF16) for shape, where in outs],
        scratch_shapes=scratch,
        compiler_params=pltpu.CompilerParams(vmem_limit_bytes=48 * 1024 * 1024),
        cost_estimate=pl.CostEstimate(flops=flops, bytes_accessed=1 << 10, transcendentals=0),
    )(*[place(item, where) for item, where in ins])


def swap(item, axis, count, step):
    return lax.ppermute(item, axis, [(at, at ^ step) for at in range(count)])


def chip_sums(keeps, sends, col_parts):
    got = [swap(send, "col", col_parts, 1) for send in sends]
    count, shape = len(keeps), keeps[0].shape
    return call(
        functools.partial(add_pairs, count),
        [(item, FAR) for item in keeps] + [(item, ANY) for item in got], [(shape, ANY)] * count,
        [pltpu.VMEM((count, *shape), BF16), pltpu.SemaphoreType.DMA((count,))],
    )


def plane_pieces(sums, plane, core):
    return [item if step == 0 else swap(item, "col", plane * core, step * core) for step, item in enumerate(sums)]


def last_sums(pieces, row_parts):
    parts, size, channels = pieces[0].shape
    held = sum(piece.astype(F32) for piece in pieces).astype(BF16)
    held = held.reshape(parts, row_parts, size // row_parts, channels)
    result = held[:, 0].astype(F32)
    for step in range(1, row_parts):
        result = result + swap(held[:, step], "row", row_parts, step).astype(F32)
    return result


def body(row_parts, col_parts, field, cotangent, gains, weights):
    high, wide, channels = field.shape
    core = 2
    plane = col_parts // core
    rows = high // col_parts
    cols = wide // row_parts
    tokens = high * wide
    height = high * row_parts
    length = wide * col_parts
    width = channels // HEADS
    together = min(cols, max(1, 256 // height))
    devices = row_parts * col_parts
    my_row = lax.axis_index("row")

    flat, triple = (tokens, channels), (tokens, 3 * channels)
    probs = (rows * HEADS, length, length)
    packed = (4, channels // col_parts, channels)

    def scratch(*shape):
        return pltpu.VMEM(shape, BF16)

    def at(where, *items):
        return [(item, where) for item in items]

    square = scratch(*flat)
    copies = pltpu.SemaphoreType.DMA
    assert channels == tokens
    turns = [
        ((rows, col_parts, row_parts, cols), (2, 1, 0, 3), {}, 0),
        ((row_parts, col_parts, rows, cols), (2, 1, 0, 3), {}, 0),
        ((height, cols), (1, 0), {}, 0),
        ((cols, height), (1, 0), {}, 0),
        ((row_parts, high, cols), (2, 0, 1), {0: "row"}, 0),
        ((cols, row_parts, high), (1, 2, 0), {1: "row"}, 0),
        ((row_parts, plane, core, channels // devices), (2, 1, 0, 3), {0: "row", 1: "plane", 2: "core"}, 1),
    ]

    def all_to_all(item):
        item = item.reshape(devices, rows * cols, channels)
        return lax.all_to_all(item, ("row", "col"), 0, 0, tiled=True).reshape(tokens, channels)

    x = lax.all_to_all(field.reshape(col_parts, rows, wide, channels), "col", 0, 0, tiled=True)
    cots = []
    for step in range(row_parts):
        piece = lax.dynamic_slice_in_dim(cotangent, (my_row ^ step) * cols, cols, axis=1)
        piece = piece if step == 0 else swap(piece, "row", row_parts, step)
        cots.append(piece.reshape(high * cols, channels))
    turn, = call(
        functools.partial(set_up, turns), [], at(FAR, (len(turns), *flat)),
        [scratch(len(turns), *flat), copies((len(turns),))],
    )

    sizes = (rows, length, width)
    mid, normed, query, key, value, attended, prob = call(
        functools.partial(row_forward, sizes),
        at(ANY, x, gains) + at(FAR, weights, turn), at(FAR, *[flat] * 6, probs),
        [scratch(4, *flat)] + [square] * 7 + [scratch(*probs), copies((5,)), copies((6,)), copies((4,))],
    )
    mid, cots = lax.optimization_barrier((mid, cots))
    cot, d_att, early = call(
        functools.partial(column_first, row_parts),
        at(ANY, *cots) + at(FAR, weights, turn), at(NEAR, flat, flat, (2, *flat)), [square, square, copies((4,))],
    )
    mid = all_to_all(mid)

    count = together * height
    d_mid, *kept = call(
        functools.partial(column_main, (height, cols, width, together)),
        at(ANY, mid) + at(NEAR, cot, d_att, early) + at(ANY, gains) + at(FAR, weights, turn),
        at(FAR, flat, flat, flat, flat, triple),
        [scratch(2, *flat)] + [square] * 5 + [scratch(*triple)] + [square] * 3
        + [scratch(cols // together * HEADS, count, count), copies((11,))],
    )
    d_mid = all_to_all(d_mid)
    results = call(
        functools.partial(column_last, row_parts, plane),
        at(FAR, cot, *kept, weights, turn), at(FAR, *[(high * cols, channels)] * row_parts, *[packed] * (2 * plane)),
        [square, scratch(plane, *packed), scratch(plane, *packed), square, scratch(2, *flat), scratch(4, *flat),
         scratch(*triple), copies((8 + row_parts,)), copies((2 * plane,))],
    )
    outs, grads = results[:row_parts], results[row_parts:]
    sums_b = chip_sums(grads[:plane], grads[plane:], col_parts)
    pieces_b = plane_pieces(sums_b, plane, core)
    pieces_out = [outs[0], swap(outs[1], "row", row_parts, 1)]
    d_mid, rest, _ = lax.optimization_barrier((d_mid, outs[2:], sums_b))
    results = call(
        functools.partial(row_back, (rows, length, width, plane)),
        at(ANY, d_mid) + at(FAR, weights, turn, normed, query, key, value, attended, prob),
        at(ANY, flat) + at(FAR, triple, *[packed] * (2 * plane)),
        [square, scratch(2, *flat)] + [square] * 5 + [scratch(*probs), square, scratch(*triple)]
        + [scratch(plane, *packed), scratch(plane, *packed), copies((11,)), copies((2 * plane,))],
    )
    (d_mid, dqkv, *grads), pieces_b, pieces_out, rest = lax.optimization_barrier(
        (results, pieces_b, pieces_out, rest)
    )
    second = [swap(item, "row", row_parts, 2) for item in rest[:1]]
    sums_a = chip_sums(grads[:plane], grads[plane:], col_parts)
    pieces_a = plane_pieces(sums_a, plane, core)
    dqkv, _, second = lax.optimization_barrier((dqkv, sums_a, second))
    field_grad, = call(
        field_back, at(ANY, x, d_mid, gains) + at(FAR, dqkv, weights), at(FAR, x.shape),
        [scratch(*triple), scratch(3, *flat), scratch(*x.shape), copies((3,))],
    )
    field_grad, pieces_b = lax.optimization_barrier((field_grad, pieces_b))
    grads_b = last_sums(pieces_b, row_parts)
    field_grad, pieces_a, rest = lax.optimization_barrier((field_grad, pieces_a, rest[1:]))
    field_grad = lax.all_to_all(field_grad, "col", 0, 0, tiled=True)
    field_grad, = call(store, at(ANY, field_grad), at(FAR, field_grad.shape), [copies], 1 << 34)
    field_grad = field_grad.reshape(high, wide, channels)
    pieces_out += second + [swap(item, "row", row_parts, 3 + step) for step, item in enumerate(rest)]
    output = jnp.zeros((high, wide, channels), BF16)
    for step, piece in enumerate(pieces_out):
        piece = piece.reshape(high, cols, channels)
        output = lax.dynamic_update_slice_in_dim(output, piece, (my_row ^ step) * cols, axis=1)
    grads_a = last_sums(pieces_a, row_parts)
    return output, field_grad, jnp.concatenate([grads_a, grads_b], axis=0)


def solution(mesh):
    return jax.shard_map(
        functools.partial(body, mesh.shape["row"], mesh.shape["col"]),
        mesh=mesh,
        in_specs=(P("row", "col", None), P("row", "col", None), P(), P()),
        out_specs=(P("row", "col", None), P("row", "col", None), P(None, ("row", "col"), None)),
        check_vma=False,
    )
```

```python
import functools
import math

import jax
import jax.numpy as jnp
from jax import lax
from jax.experimental import pallas as pl
from jax.experimental.pallas import tpu as pltpu
from jax.sharding import PartitionSpec as P

HEADS = 8
eps = 1e-05
F32 = jnp.float32
BF16 = jnp.bfloat16


def log2(n):
    assert n & (n - 1) == 0
    return n.bit_length() - 1


def dot(left, right):
    return jnp.dot(left, right, preferred_element_type=F32)


def dot_nt(left, right):
    return lax.dot_general(left, right, (((1,), (1,)), ((), ())), preferred_element_type=F32)


def dot_tn(left, right):
    return lax.dot_general(left, right, (((0,), (0,)), ((), ())), preferred_element_type=F32)


def one_hot(sizes, order, me=None, lead=0):
    total = math.prod(sizes)
    index = lax.broadcasted_iota(jnp.int32, (total, total), lead)
    found = {}
    for axis in reversed(order):
        found[axis] = index & (sizes[axis] - 1)
        index = index >> log2(sizes[axis])
    source, shift = None, 0
    for axis in reversed(range(len(sizes))):
        digit = found[axis] << shift
        source = digit if source is None else source | digit
        shift += log2(sizes[axis])
    if me:
        place, shift = 0, 0
        for axis in reversed(range(len(sizes))):
            if axis in me:
                place = place | (me[axis] << shift)
            shift += log2(sizes[axis])
        source = source ^ place
    hit = source == lax.broadcasted_iota(jnp.int32, (total, total), 1 - lead)
    return jnp.where(hit, 1.0, 0.0).astype(BF16)


def statistics(values):
    average = jnp.mean(values, axis=-1, keepdims=True)
    centred = values - average
    spread = jnp.mean(centred * centred, axis=-1, keepdims=True)
    return centred, lax.rsqrt(spread + eps)


def norm_back(values, gain, d_normed):
    centred, inverse = statistics(values)
    unit = centred * inverse
    scaled = d_normed * gain
    return inverse * (
        scaled
        - jnp.mean(scaled, axis=-1, keepdims=True)
        - unit * jnp.mean(scaled * unit, axis=-1, keepdims=True)
    )


def head_lanes(count, width):
    return lax.broadcasted_iota(jnp.int32, (count, 2 * width), 1) < width


def attention_forward(q_ref, k_ref, v_ref, att_ref, p_ref, groups, count, width, span, unroll=4):
    first = head_lanes(count, width)
    pairs = HEADS // 2
    scale = width ** (-0.5)

    def step(index, carry):
        group, pair = index // pairs, index % pairs
        rows = pl.ds(pl.multiple_of(group * count, count), count)
        lanes = pl.ds(pl.multiple_of(pair * 2 * width, 2 * width), 2 * width)
        query, key, value = q_ref[rows, lanes] * scale, k_ref[rows, lanes], v_ref[rows, lanes]
        zero = jnp.zeros_like(query)
        total = jnp.zeros((count, 2 * width), F32)
        for half in range(2):
            mine = first if half == 0 else jnp.logical_not(first)
            scores = dot_nt(key, jnp.where(mine, query, zero))
            if span < count:
                shift = log2(span)
                same = (lax.broadcasted_iota(jnp.int32, (count, count), 0) >> shift) == (
                    lax.broadcasted_iota(jnp.int32, (count, count), 1) >> shift
                )
                scores = jnp.where(same, scores, -jnp.inf)
            expo = jnp.exp(scores - jnp.max(scores, axis=0, keepdims=True))
            probs = (expo * (1.0 / jnp.sum(expo, axis=0, keepdims=True))).astype(BF16)
            p_ref[index * 2 + half] = probs
            total += dot_tn(probs, jnp.where(mine, value, zero))
        att_ref[rows, lanes] = total.astype(BF16)
        return carry

    lax.fori_loop(0, groups * pairs, step, 0, unroll=unroll)


def attention_back(q_ref, k_ref, v_ref, p_ref, da_ref, dqkv_ref, groups, count, width, unroll=4):
    first = head_lanes(count, width)
    pairs = HEADS // 2
    channels = HEADS * width
    scale = width ** (-0.5)

    def step(index, carry):
        group, pair = index // pairs, index % pairs
        rows = pl.ds(pl.multiple_of(group * count, count), count)
        lanes = pl.ds(pl.multiple_of(pair * 2 * width, 2 * width), 2 * width)
        query, key, value = q_ref[rows, lanes] * scale, k_ref[rows, lanes], v_ref[rows, lanes]
        d_out = da_ref[rows, lanes]
        zero = jnp.zeros_like(query)
        d_query = jnp.zeros((count, 2 * width), F32)
        d_key, d_value = d_query, d_query
        for half in range(2):
            mine = first if half == 0 else jnp.logical_not(first)
            probs = p_ref[index * 2 + half]
            d_mine = jnp.where(mine, d_out, zero)
            d_probs = dot_nt(value, d_mine)
            probs32 = probs.astype(F32)
            weighted = probs32 * d_probs
            total = jnp.sum(weighted, axis=0, keepdims=True)
            d_scores = (weighted - probs32 * total).astype(BF16)
            d_query += dot_tn(d_scores, jnp.where(mine, key, zero))
            d_key += dot(d_scores, jnp.where(mine, query, zero))
            d_value += dot(probs, d_mine)
        for part, item in enumerate((d_query * scale, d_key, d_value)):
            at = pl.ds(pl.multiple_of(part * channels + pair * 2 * width, 2 * width), 2 * width)
            dqkv_ref[rows, at] = item.astype(BF16)
        return carry

    lax.fori_loop(0, groups * pairs, step, 0, unroll=unroll)


def start(source, target, sem):
    copy = pltpu.make_async_copy(source, target, sem)
    copy.start()
    return copy


def finish(copies):
    for copy in copies:
        copy.wait()


def set_up(turns, turn_hbm, turn_ref, sems):
    my_row, my_col = lax.axis_index("row"), lax.axis_index("col")
    places = {"row": my_row, "plane": my_col >> 1, "core": my_col & 1}
    going = []
    for at, (sizes, order, me, lead) in enumerate(turns):
        turn_ref[at] = one_hot(sizes, order, {axis: places[name] for axis, name in me.items()}, lead)
        going.append(start(turn_ref.at[at], turn_hbm.at[at], sems.at[at]))
    finish(going)


def weight_grad(part, left, right, keep_ref, send_ref):
    plane, _, size, _ = keep_ref.shape
    whole = dot_tn(left, right).astype(BF16)
    for group in range(plane):
        send_ref[group, part] = whole[(plane + group) * size : (plane + group + 1) * size]
        keep_ref[group, part] = whole[group * size : (group + 1) * size]


def send_grads(keep_ref, send_ref, keep_hbms, send_hbms, sems):
    plane = keep_ref.shape[0]
    going = [start(send_ref.at[at], send_hbms[at], sems.at[at]) for at in range(plane)]
    return going + [start(keep_ref.at[at], keep_hbms[at], sems.at[plane + at]) for at in range(plane)]


def third(ref, part):
    channels = ref.shape[-1] // 3
    return ref[:, part * channels : (part + 1) * channels]


def send_turned(turn_ref, values, stage_ref, targets, sems):
    size = values.shape[0] // len(targets)
    going = []
    for at, target in enumerate(targets):
        piece = pl.ds(at * size, size)
        stage_ref[piece] = dot(turn_ref[piece], values).astype(BF16)
        going.append(start(stage_ref.at[piece], target, sems.at[at]))
    return going


def quarters(ref):
    size = ref.shape[0] // 4
    return [ref.at[pl.ds(at * size, size)] for at in range(4)]


def input_back(dqkv_ref, w_refs):
    total = dot_nt(third(dqkv_ref, 0), w_refs[0][...])
    total += dot_nt(third(dqkv_ref, 1), w_refs[1][...])
    total += dot_nt(third(dqkv_ref, 2), w_refs[2][...])
    return total.astype(BF16).astype(F32)


def rows_of(x_ref):
    _, rows, _, channels = x_ref.shape
    length = x_ref.shape[0] * x_ref.shape[2]
    pieces = [x_ref[:, i].reshape(length, channels) for i in range(rows)]
    return jnp.concatenate(pieces, axis=0).astype(F32)


def row_forward(sizes, x_ref, g_ref, w_hbm, turn_hbm, mid_hbm, n_hbm, q_hbm, k_hbm, v_hbm, att_hbm, p_hbm,
                w_ref, turn_ref, mid_ref, n_ref, q_ref, k_ref, v_ref, att_ref, p_ref, in_sems, out_sems, sems):
    rows, length, width = sizes
    coming = [start(w_hbm.at[0, part], w_ref.at[part], in_sems.at[part]) for part in range(4)]
    coming.append(start(turn_hbm.at[0], turn_ref, in_sems.at[4]))
    centred, inverse = statistics(rows_of(x_ref))
    normed = (centred * inverse * g_ref[0:1]).astype(BF16)
    n_ref[...] = normed
    going = [start(n_ref, n_hbm, out_sems.at[0])]
    for part, (ref, hbm) in enumerate(((q_ref, q_hbm), (k_ref, k_hbm), (v_ref, v_hbm))):
        coming[part].wait()
        ref[...] = dot(normed, w_ref[part]).astype(BF16)
        going.append(start(ref, hbm, out_sems.at[1 + part]))
    attention_forward(q_ref, k_ref, v_ref, att_ref, p_ref, rows, length, width, length)
    going.append(start(p_ref, p_hbm, out_sems.at[5]))
    going.append(start(att_ref, att_hbm, out_sems.at[4]))
    coming[3].wait()
    middle = (rows_of(x_ref) + dot(att_ref[...], w_ref[3])).astype(BF16)
    coming[4].wait()
    finish(going + send_turned(turn_ref, middle, mid_ref, quarters(mid_hbm), sems))


def row_back(sizes, d_ref, x_ref, g_ref, w_hbm, turn_hbm, n_hbm, q_hbm, k_hbm, v_hbm, att_hbm, p_hbm, *refs):
    rows, length, width, plane = sizes
    fg_hbm, keep_hbms, send_hbms = refs[0], refs[1 : 1 + plane], refs[1 + plane : 1 + 2 * plane]
    w_ref, turn_ref, dm_ref, n_ref, q_ref, k_ref, v_ref, att_ref, p_ref, da_ref, dqkv_ref = refs[1 + 2 * plane : -5]
    fg_ref, keep_ref, send_ref, sems, out_sems = refs[-5:]
    half = p_ref.shape[0] // 2
    coming = [
        start(turn_hbm.at[1], turn_ref.at[0], sems.at[0]), start(w_hbm.at[0, 3], w_ref.at[3], sems.at[1]),
        start(v_hbm, v_ref, sems.at[2]), start(k_hbm, k_ref, sems.at[3]), start(q_hbm, q_ref, sems.at[4]),
        start(p_hbm.at[pl.ds(0, half)], p_ref.at[pl.ds(0, half)], sems.at[5]),
        start(p_hbm.at[pl.ds(half, half)], p_ref.at[pl.ds(half, half)], sems.at[6]),
        start(w_hbm.at[0, 0:3], w_ref.at[0:3], sems.at[7]),
        start(turn_hbm.at[6], turn_ref.at[1], sems.at[8]), start(att_hbm, att_ref, sems.at[9]),
        start(n_hbm, n_ref, sems.at[10]),
    ]
    coming[0].wait()
    d_middle = dot(turn_ref[0], d_ref[...]).astype(BF16)
    dm_ref[...] = d_middle
    coming[1].wait()
    da_ref[...] = dot_nt(d_middle, w_ref[3]).astype(BF16)
    finish(coming[2:7])
    attention_back(q_ref, k_ref, v_ref, p_ref, da_ref, dqkv_ref, rows, length, width)
    coming[7].wait()
    d_normed = input_back(dqkv_ref, [w_ref.at[part] for part in range(3)])
    result = dm_ref[...].astype(F32) + norm_back(rows_of(x_ref), g_ref[0:1], d_normed)
    result = result.astype(BF16)
    for i in range(rows):
        piece = result[i * length : (i + 1) * length]
        fg_ref[:, i] = piece.reshape(fg_ref.shape[0], fg_ref.shape[2], fg_ref.shape[3])
    going = [start(fg_ref, fg_hbm, sems.at[11])]
    finish(coming[8:])
    normed = dot(n_ref[...], turn_ref[1]).astype(BF16)
    for part in range(3):
        weight_grad(part, normed, third(dqkv_ref, part), keep_ref, send_ref)
    attended = dot(att_ref[...], turn_ref[1]).astype(BF16)
    weight_grad(3, attended, dm_ref[...], keep_ref, send_ref)
    finish(going + send_grads(keep_ref, send_ref, keep_hbms, send_hbms, out_sems))


def store(x_ref, x_hbm, sem):
    start(x_ref, x_hbm, sem).wait()


def column_first(parts, *refs):
    c_refs, (w_hbm, turn_hbm, cot_ref, da_ref, early_ref, w_ref, turn_ref, sems) = refs[:parts], refs[parts:]
    coming = [
        start(turn_hbm.at[4], turn_ref, sems.at[0]), start(w_hbm.at[1, 3], w_ref, sems.at[1]),
        start(turn_hbm.at[2], early_ref.at[0], sems.at[2]), start(w_hbm.at[1, 0], early_ref.at[1], sems.at[3]),
    ]
    cotangent = jnp.concatenate([ref[...] for ref in c_refs], axis=0)
    coming[0].wait()
    cotangent = dot(turn_ref[...], cotangent).astype(BF16)
    cot_ref[...] = cotangent
    coming[1].wait()
    da_ref[...] = dot_nt(cotangent, w_ref[...]).astype(BF16)
    finish(coming[2:])


def column_main(sizes, m_ref, cot_ref, da_ref, early_ref, g_ref, w_hbm, turn_hbm,
                dm_hbm, mid_hbm, n_hbm, att_hbm, dqkv_hbm,
                w_ref, turn_ref, dm_ref, mid_ref, n_ref, att_ref, dqkv_ref, q_ref, k_ref, v_ref, p_ref, sems):
    height, cols, width, together = sizes
    coming = [
        start(w_hbm.at[1, 1], w_ref.at[0], sems.at[0]), start(w_hbm.at[1, 2], w_ref.at[1], sems.at[1]),
        start(turn_hbm.at[3], turn_ref, sems.at[2]),
    ]
    middle = dot(early_ref[0], m_ref[...])
    mid_ref[...] = middle.astype(BF16)
    going = [start(mid_ref, mid_hbm, sems.at[3])]
    centred, inverse = statistics(middle)
    normed = (centred * inverse * g_ref[1:2]).astype(BF16)
    n_ref[...] = normed
    going.append(start(n_ref, n_hbm, sems.at[4]))
    q_ref[...] = dot(normed, early_ref[1]).astype(BF16)
    coming[0].wait()
    k_ref[...] = dot(normed, w_ref[0]).astype(BF16)
    coming[1].wait()
    v_ref[...] = dot(normed, w_ref[1]).astype(BF16)
    count = together * height
    groups = cols // together
    attention_forward(q_ref, k_ref, v_ref, att_ref, p_ref, groups, count, width, height)
    going.append(start(att_ref, att_hbm, sems.at[5]))
    attention_back(q_ref, k_ref, v_ref, p_ref, da_ref, dqkv_ref, groups, count, width)
    going.append(start(dqkv_ref, dqkv_hbm, sems.at[6]))
    d_normed = input_back(dqkv_ref, [early_ref.at[1], w_ref.at[0], w_ref.at[1]])
    middle = mid_ref[...].astype(F32)
    d_middle = cot_ref[...].astype(F32) + norm_back(middle, g_ref[1:2], d_normed)
    coming[2].wait()
    finish(going + send_turned(turn_ref, d_middle.astype(BF16), dm_ref, quarters(dm_hbm), sems.at[pl.ds(7, 4)]))


def column_last(parts, plane, cot_hbm, mid_hbm, n_hbm, att_hbm, dqkv_hbm, w_hbm, turn_hbm, *refs):
    out_hbms, refs = refs[:parts], refs[parts:]
    keep_hbms, send_hbms, refs = refs[:plane], refs[plane : 2 * plane], refs[2 * plane :]
    out_ref, keep_ref, send_ref, w_ref, turn_ref, flat_ref, dqkv_ref, sems, out_sems = refs
    coming = [
        start(turn_hbm.at[6], turn_ref.at[0], sems.at[0]), start(n_hbm, flat_ref.at[0], sems.at[1]),
        start(dqkv_hbm, dqkv_ref, sems.at[2]), start(att_hbm, flat_ref.at[1], sems.at[3]),
        start(cot_hbm, flat_ref.at[2], sems.at[4]), start(mid_hbm, flat_ref.at[3], sems.at[5]),
        start(w_hbm.at[1, 3], w_ref, sems.at[6]), start(turn_hbm.at[5], turn_ref.at[1], sems.at[7]),
    ]
    finish(coming[:3])
    normed = dot(flat_ref[0], turn_ref[0]).astype(BF16)
    for part in range(3):
        weight_grad(part, normed, third(dqkv_ref, part), keep_ref, send_ref)
    finish(coming[3:])
    attended = dot(flat_ref[1], turn_ref[0]).astype(BF16)
    weight_grad(3, attended, flat_ref[2], keep_ref, send_ref)
    going = send_grads(keep_ref, send_ref, keep_hbms, send_hbms, out_sems)
    output = (flat_ref[3].astype(F32) + dot(flat_ref[1], w_ref[...])).astype(BF16)
    finish(going + send_turned(turn_ref.at[1], output, out_ref, out_hbms, sems.at[pl.ds(8, parts)]))


def add_pairs(count, *refs):
    keep_hbms, got_refs, sum_refs, (keep_ref, sems) = (
        refs[:count], refs[count : 2 * count], refs[2 * count : 3 * count], refs[3 * count :]
    )
    coming = [start(hbm, keep_ref.at[at], sems.at[at]) for at, hbm in enumerate(keep_hbms)]
    for at, copy in enumerate(coming):
        copy.wait()
        sum_refs[at][...] = (keep_ref[at].astype(F32) + got_refs[at][...].astype(F32)).astype(BF16)


NEAR, FAR, ANY = pltpu.VMEM, pltpu.HBM, None


def call(kernel, ins, outs, scratch):
    def spec(where):
        return pl.BlockSpec(memory_space=pltpu.HBM if where is FAR else pltpu.VMEM)

    def place(item, where):
        return item if where is ANY else pltpu.with_memory_space_constraint(item, where)

    return pl.pallas_call(
        kernel,
        in_specs=[spec(where) for _, where in ins],
        out_specs=[spec(where) for _, where in outs],
        out_shape=[jax.ShapeDtypeStruct(shape, BF16) if where is ANY else where(shape, BF16) for shape, where in outs],
        scratch_shapes=scratch,
        compiler_params=pltpu.CompilerParams(vmem_limit_bytes=48 * 1024 * 1024),
        cost_estimate=pl.CostEstimate(flops=1 << 20, bytes_accessed=1 << 10, transcendentals=0),
    )(*[place(item, where) for item, where in ins])


def swap(item, axis, count, step):
    return lax.ppermute(item, axis, [(at, at ^ step) for at in range(count)])


def chip_sums(keeps, sends, col_parts):
    got = [swap(send, "col", col_parts, 1) for send in sends]
    count, shape = len(keeps), keeps[0].shape
    return call(
        functools.partial(add_pairs, count),
        [(item, FAR) for item in keeps] + [(item, ANY) for item in got], [(shape, ANY)] * count,
        [pltpu.VMEM((count, *shape), BF16), pltpu.SemaphoreType.DMA((count,))],
    )


def plane_pieces(sums, plane, core):
    return [item if step == 0 else swap(item, "col", plane * core, step * core) for step, item in enumerate(sums)]


def last_sums(pieces, row_parts):
    parts, size, channels = pieces[0].shape
    held = sum(piece.astype(F32) for piece in pieces).astype(BF16)
    held = held.reshape(parts, row_parts, size // row_parts, channels)
    result = held[:, 0].astype(F32)
    for step in range(1, row_parts):
        result = result + swap(held[:, step], "row", row_parts, step).astype(F32)
    return result


def body(row_parts, col_parts, field, cotangent, gains, weights):
    high, wide, channels = field.shape
    core = 2
    plane = col_parts // core
    rows = high // col_parts
    cols = wide // row_parts
    tokens = high * wide
    height = high * row_parts
    length = wide * col_parts
    width = channels // HEADS
    together = min(cols, max(1, 256 // height))
    devices = row_parts * col_parts
    my_row = lax.axis_index("row")

    flat, triple = (tokens, channels), (tokens, 3 * channels)
    probs = (rows * HEADS, length, length)
    packed = (4, channels // col_parts, channels)

    def scratch(*shape):
        return pltpu.VMEM(shape, BF16)

    def at(where, *items):
        return [(item, where) for item in items]

    square = scratch(*flat)
    copies = pltpu.SemaphoreType.DMA
    assert channels == tokens
    turns = [
        ((rows, col_parts, row_parts, cols), (2, 1, 0, 3), {}, 0),
        ((row_parts, col_parts, rows, cols), (2, 1, 0, 3), {}, 0),
        ((height, cols), (1, 0), {}, 0),
        ((cols, height), (1, 0), {}, 0),
        ((row_parts, high, cols), (2, 0, 1), {0: "row"}, 0),
        ((cols, row_parts, high), (1, 2, 0), {1: "row"}, 0),
        ((row_parts, plane, core, channels // devices), (2, 1, 0, 3), {0: "row", 1: "plane", 2: "core"}, 1),
    ]

    def all_to_all(item):
        item = item.reshape(devices, rows * cols, channels)
        return lax.all_to_all(item, ("row", "col"), 0, 0, tiled=True).reshape(tokens, channels)

    x = lax.all_to_all(field.reshape(col_parts, rows, wide, channels), "col", 0, 0, tiled=True)
    cots = []
    for step in range(row_parts):
        piece = lax.dynamic_slice_in_dim(cotangent, (my_row ^ step) * cols, cols, axis=1)
        piece = piece if step == 0 else swap(piece, "row", row_parts, step)
        cots.append(piece.reshape(high * cols, channels))
    turn, = call(
        functools.partial(set_up, turns), [], at(FAR, (len(turns), *flat)),
        [scratch(len(turns), *flat), copies((len(turns),))],
    )

    sizes = (rows, length, width)
    mid, normed, query, key, value, attended, prob = call(
        functools.partial(row_forward, sizes),
        at(ANY, x, gains) + at(FAR, weights, turn), at(FAR, *[flat] * 6, probs),
        [scratch(4, *flat)] + [square] * 7 + [scratch(*probs), copies((5,)), copies((6,)), copies((4,))],
    )
    mid, cots = lax.optimization_barrier((mid, cots))
    cot, d_att, early = call(
        functools.partial(column_first, row_parts),
        at(ANY, *cots) + at(FAR, weights, turn), at(NEAR, flat, flat, (2, *flat)), [square, square, copies((4,))],
    )
    mid = all_to_all(mid)

    count = together * height
    d_mid, *kept = call(
        functools.partial(column_main, (height, cols, width, together)),
        at(ANY, mid) + at(NEAR, cot, d_att, early) + at(ANY, gains) + at(FAR, weights, turn),
        at(FAR, flat, flat, flat, flat, triple),
        [scratch(2, *flat)] + [square] * 5 + [scratch(*triple)] + [square] * 3
        + [scratch(cols // together * HEADS, count, count), copies((11,))],
    )
    d_mid = all_to_all(d_mid)
    results = call(
        functools.partial(column_last, row_parts, plane),
        at(FAR, cot, *kept, weights, turn), at(FAR, *[(high * cols, channels)] * row_parts, *[packed] * (2 * plane)),
        [square, scratch(plane, *packed), scratch(plane, *packed), square, scratch(2, *flat), scratch(4, *flat),
         scratch(*triple), copies((8 + row_parts,)), copies((2 * plane,))],
    )
    outs, grads = results[:row_parts], results[row_parts:]
    sums_b = chip_sums(grads[:plane], grads[plane:], col_parts)
    pieces_b = plane_pieces(sums_b, plane, core)
    pieces_out = [outs[0], swap(outs[1], "row", row_parts, 1)]
    d_mid, rest, _ = lax.optimization_barrier((d_mid, outs[2:], sums_b))
    results = call(
        functools.partial(row_back, (rows, length, width, plane)),
        at(ANY, d_mid, x, gains) + at(FAR, weights, turn, normed, query, key, value, attended, prob),
        at(FAR, x.shape, *[packed] * (2 * plane)),
        [scratch(4, *flat), scratch(2, *flat)] + [square] * 6 + [scratch(*probs), square, scratch(*triple)]
        + [scratch(*x.shape), scratch(plane, *packed), scratch(plane, *packed), copies((12,)), copies((2 * plane,))],
    )
    (field_grad, *grads), pieces_b, pieces_out, rest = lax.optimization_barrier((results, pieces_b, pieces_out, rest))
    field_grad = lax.all_to_all(field_grad, "col", 0, 0, tiled=True)
    pieces_out += [swap(item, "row", row_parts, 2) for item in rest[:1]]
    pieces_a = plane_pieces(chip_sums(grads[:plane], grads[plane:], col_parts), plane, core)
    field_grad, pieces_b, rest = lax.optimization_barrier((field_grad, pieces_b, rest[1:]))
    grads_b = last_sums(pieces_b, row_parts)
    pieces_out += [swap(item, "row", row_parts, 3 + step) for step, item in enumerate(rest)]
    field_grad, = call(store, at(ANY, field_grad), at(FAR, field_grad.shape), [copies])
    field_grad = field_grad.reshape(high, wide, channels)
    output = jnp.zeros((high, wide, channels), BF16)
    for step, piece in enumerate(pieces_out):
        piece = piece.reshape(high, cols, channels)
        output = lax.dynamic_update_slice_in_dim(output, piece, (my_row ^ step) * cols, axis=1)
    grads_a = last_sums(pieces_a, row_parts)
    return output, field_grad, jnp.concatenate([grads_a, grads_b], axis=0)


def solution(mesh):
    return jax.shard_map(
        functools.partial(body, mesh.shape["row"], mesh.shape["col"]),
        mesh=mesh,
        in_specs=(P("row", "col", None), P("row", "col", None), P(), P()),
        out_specs=(P("row", "col", None), P("row", "col", None), P(None, ("row", "col"), None)),
        check_vma=False,
    )
```

```python
import functools
import math

import jax
import jax.numpy as jnp
from jax import lax
from jax.experimental import pallas as pl
from jax.experimental.pallas import tpu as pltpu
from jax.sharding import PartitionSpec as P

HEADS = 8
eps = 1e-05
F32 = jnp.float32
BF16 = jnp.bfloat16


def log2(n):
    assert n & (n - 1) == 0
    return n.bit_length() - 1


def dot(left, right):
    return jnp.dot(left, right, preferred_element_type=F32)


def dot_nt(left, right):
    return lax.dot_general(left, right, (((1,), (1,)), ((), ())), preferred_element_type=F32)


def dot_tn(left, right):
    return lax.dot_general(left, right, (((0,), (0,)), ((), ())), preferred_element_type=F32)


def one_hot(sizes, order, me=None, lead=0):
    total = math.prod(sizes)
    index = lax.broadcasted_iota(jnp.int32, (total, total), lead)
    found = {}
    for axis in reversed(order):
        found[axis] = index & (sizes[axis] - 1)
        index = index >> log2(sizes[axis])
    source, shift = None, 0
    for axis in reversed(range(len(sizes))):
        digit = found[axis] << shift
        source = digit if source is None else source | digit
        shift += log2(sizes[axis])
    if me:
        place, shift = 0, 0
        for axis in reversed(range(len(sizes))):
            if axis in me:
                place = place | (me[axis] << shift)
            shift += log2(sizes[axis])
        source = source ^ place
    hit = source == lax.broadcasted_iota(jnp.int32, (total, total), 1 - lead)
    return jnp.where(hit, 1.0, 0.0).astype(BF16)


def statistics(values):
    average = jnp.mean(values, axis=-1, keepdims=True)
    centred = values - average
    spread = jnp.mean(centred * centred, axis=-1, keepdims=True)
    return centred, lax.rsqrt(spread + eps)


def norm_back(values, gain, d_normed):
    centred, inverse = statistics(values)
    unit = centred * inverse
    scaled = d_normed * gain
    return inverse * (
        scaled
        - jnp.mean(scaled, axis=-1, keepdims=True)
        - unit * jnp.mean(scaled * unit, axis=-1, keepdims=True)
    )


def head_lanes(count, width):
    return lax.broadcasted_iota(jnp.int32, (count, 2 * width), 1) < width


def attention_forward(q_ref, k_ref, v_ref, att_ref, p_ref, groups, count, width, span, unroll=4):
    first = head_lanes(count, width)
    pairs = HEADS // 2
    scale = width ** (-0.5)

    def step(index, carry):
        group, pair = index // pairs, index % pairs
        rows = pl.ds(pl.multiple_of(group * count, count), count)
        lanes = pl.ds(pl.multiple_of(pair * 2 * width, 2 * width), 2 * width)
        query, key, value = q_ref[rows, lanes] * scale, k_ref[rows, lanes], v_ref[rows, lanes]
        zero = jnp.zeros_like(query)
        total = jnp.zeros((count, 2 * width), F32)
        for half in range(2):
            mine = first if half == 0 else jnp.logical_not(first)
            scores = dot_nt(key, jnp.where(mine, query, zero))
            if span < count:
                shift = log2(span)
                same = (lax.broadcasted_iota(jnp.int32, (count, count), 0) >> shift) == (
                    lax.broadcasted_iota(jnp.int32, (count, count), 1) >> shift
                )
                scores = jnp.where(same, scores, -jnp.inf)
            expo = jnp.exp(scores - jnp.max(scores, axis=0, keepdims=True))
            probs = (expo * (1.0 / jnp.sum(expo, axis=0, keepdims=True))).astype(BF16)
            p_ref[index * 2 + half] = probs
            total += dot_tn(probs, jnp.where(mine, value, zero))
        att_ref[rows, lanes] = total.astype(BF16)
        return carry

    lax.fori_loop(0, groups * pairs, step, 0, unroll=unroll)


def attention_back(q_ref, k_ref, v_ref, p_ref, da_ref, dqkv_ref, groups, count, width, unroll=4):
    first = head_lanes(count, width)
    pairs = HEADS // 2
    channels = HEADS * width
    scale = width ** (-0.5)

    def step(index, carry):
        group, pair = index // pairs, index % pairs
        rows = pl.ds(pl.multiple_of(group * count, count), count)
        lanes = pl.ds(pl.multiple_of(pair * 2 * width, 2 * width), 2 * width)
        query, key, value = q_ref[rows, lanes] * scale, k_ref[rows, lanes], v_ref[rows, lanes]
        d_out = da_ref[rows, lanes]
        zero = jnp.zeros_like(query)
        d_query = jnp.zeros((count, 2 * width), F32)
        d_key, d_value = d_query, d_query
        for half in range(2):
            mine = first if half == 0 else jnp.logical_not(first)
            probs = p_ref[index * 2 + half]
            d_mine = jnp.where(mine, d_out, zero)
            d_probs = dot_nt(value, d_mine)
            probs32 = probs.astype(F32)
            weighted = probs32 * d_probs
            total = jnp.sum(weighted, axis=0, keepdims=True)
            d_scores = (weighted - probs32 * total).astype(BF16)
            d_query += dot_tn(d_scores, jnp.where(mine, key, zero))
            d_key += dot(d_scores, jnp.where(mine, query, zero))
            d_value += dot(probs, d_mine)
        for part, item in enumerate((d_query * scale, d_key, d_value)):
            at = pl.ds(pl.multiple_of(part * channels + pair * 2 * width, 2 * width), 2 * width)
            dqkv_ref[rows, at] = item.astype(BF16)
        return carry

    lax.fori_loop(0, groups * pairs, step, 0, unroll=unroll)


def start(source, target, sem):
    copy = pltpu.make_async_copy(source, target, sem)
    copy.start()
    return copy


def finish(copies):
    for copy in copies:
        copy.wait()


def set_up(turns, turn_hbm, turn_ref, sems):
    my_row, my_col = lax.axis_index("row"), lax.axis_index("col")
    places = {"row": my_row, "plane": my_col >> 1, "core": my_col & 1}
    going = []
    for at, (sizes, order, me, lead) in enumerate(turns):
        turn_ref[at] = one_hot(sizes, order, {axis: places[name] for axis, name in me.items()}, lead)
        going.append(start(turn_ref.at[at], turn_hbm.at[at], sems.at[at]))
    finish(going)


def weight_grad(part, left, right, keep_ref, send_ref):
    plane, _, size, _ = keep_ref.shape
    whole = dot_tn(left, right).astype(BF16)
    for group in range(plane):
        send_ref[group, part] = whole[(plane + group) * size : (plane + group + 1) * size]
        keep_ref[group, part] = whole[group * size : (group + 1) * size]


def send_grads(keep_ref, send_ref, keep_hbms, send_hbms, sems):
    plane = keep_ref.shape[0]
    going = [start(send_ref.at[at], send_hbms[at], sems.at[at]) for at in range(plane)]
    return going + [start(keep_ref.at[at], keep_hbms[at], sems.at[plane + at]) for at in range(plane)]


def third(ref, part):
    channels = ref.shape[-1] // 3
    return ref[:, part * channels : (part + 1) * channels]


def send_turned(turn_ref, values, stage_ref, targets, sems):
    size = values.shape[0] // len(targets)
    going = []
    for at, target in enumerate(targets):
        piece = pl.ds(at * size, size)
        stage_ref[piece] = dot(turn_ref[piece], values).astype(BF16)
        going.append(start(stage_ref.at[piece], target, sems.at[at]))
    return going


def quarters(ref):
    size = ref.shape[0] // 4
    return [ref.at[pl.ds(at * size, size)] for at in range(4)]


def input_back(dqkv_ref, w_refs):
    total = dot_nt(third(dqkv_ref, 0), w_refs[0][...])
    total += dot_nt(third(dqkv_ref, 1), w_refs[1][...])
    total += dot_nt(third(dqkv_ref, 2), w_refs[2][...])
    return total.astype(BF16).astype(F32)


def rows_of(x_ref):
    _, rows, _, channels = x_ref.shape
    length = x_ref.shape[0] * x_ref.shape[2]
    pieces = [x_ref[:, i].reshape(length, channels) for i in range(rows)]
    return jnp.concatenate(pieces, axis=0).astype(F32)


def row_forward(sizes, x_ref, g_ref, w_hbm, turn_hbm, mid_hbm, n_hbm, q_hbm, k_hbm, v_hbm, att_hbm, p_hbm,
                w_ref, turn_ref, mid_ref, n_ref, q_ref, k_ref, v_ref, att_ref, p_ref, in_sems, out_sems, sems):
    rows, length, width = sizes
    coming = [start(w_hbm.at[0, part], w_ref.at[part], in_sems.at[part]) for part in range(4)]
    coming.append(start(turn_hbm.at[0], turn_ref, in_sems.at[4]))
    centred, inverse = statistics(rows_of(x_ref))
    normed = (centred * inverse * g_ref[0:1]).astype(BF16)
    n_ref[...] = normed
    going = [start(n_ref, n_hbm, out_sems.at[0])]
    for part, (ref, hbm) in enumerate(((q_ref, q_hbm), (k_ref, k_hbm), (v_ref, v_hbm))):
        coming[part].wait()
        ref[...] = dot(normed, w_ref[part]).astype(BF16)
        going.append(start(ref, hbm, out_sems.at[1 + part]))
    attention_forward(q_ref, k_ref, v_ref, att_ref, p_ref, rows, length, width, length)
    going.append(start(p_ref, p_hbm, out_sems.at[5]))
    going.append(start(att_ref, att_hbm, out_sems.at[4]))
    coming[3].wait()
    middle = (rows_of(x_ref) + dot(att_ref[...], w_ref[3])).astype(BF16)
    coming[4].wait()
    finish(going + send_turned(turn_ref, middle, mid_ref, quarters(mid_hbm), sems))


def row_back(sizes, d_ref, x_ref, g_ref, w_hbm, turn_hbm, n_hbm, q_hbm, k_hbm, v_hbm, att_hbm, p_hbm, *refs):
    rows, length, width, plane = sizes
    fg_hbm, keep_hbms, send_hbms = refs[0], refs[1 : 1 + plane], refs[1 + plane : 1 + 2 * plane]
    w_ref, turn_ref, dm_ref, n_ref, q_ref, k_ref, v_ref, att_ref, p_ref, da_ref, dqkv_ref = refs[1 + 2 * plane : -5]
    fg_ref, keep_ref, send_ref, sems, out_sems = refs[-5:]
    half = p_ref.shape[0] // 2
    coming = [
        start(turn_hbm.at[1], turn_ref.at[0], sems.at[0]), start(w_hbm.at[0, 3], w_ref.at[3], sems.at[1]),
        start(v_hbm, v_ref, sems.at[2]), start(k_hbm, k_ref, sems.at[3]), start(q_hbm, q_ref, sems.at[4]),
        start(p_hbm.at[pl.ds(0, half)], p_ref.at[pl.ds(0, half)], sems.at[5]),
        start(p_hbm.at[pl.ds(half, half)], p_ref.at[pl.ds(half, half)], sems.at[6]),
        start(w_hbm.at[0, 0:3], w_ref.at[0:3], sems.at[7]),
        start(turn_hbm.at[6], turn_ref.at[1], sems.at[8]), start(att_hbm, att_ref, sems.at[9]),
        start(n_hbm, n_ref, sems.at[10]),
    ]
    coming[0].wait()
    d_middle = dot(turn_ref[0], d_ref[...]).astype(BF16)
    dm_ref[...] = d_middle
    coming[1].wait()
    da_ref[...] = dot_nt(d_middle, w_ref[3]).astype(BF16)
    finish(coming[2:7])
    attention_back(q_ref, k_ref, v_ref, p_ref, da_ref, dqkv_ref, rows, length, width)
    coming[7].wait()
    d_normed = input_back(dqkv_ref, [w_ref.at[part] for part in range(3)])
    result = dm_ref[...].astype(F32) + norm_back(rows_of(x_ref), g_ref[0:1], d_normed)
    result = result.astype(BF16)
    for i in range(rows):
        piece = result[i * length : (i + 1) * length]
        fg_ref[:, i] = piece.reshape(fg_ref.shape[0], fg_ref.shape[2], fg_ref.shape[3])
    going = [start(fg_ref, fg_hbm, sems.at[11])]
    finish(coming[8:])
    normed = dot(n_ref[...], turn_ref[1]).astype(BF16)
    for part in range(3):
        weight_grad(part, normed, third(dqkv_ref, part), keep_ref, send_ref)
    attended = dot(att_ref[...], turn_ref[1]).astype(BF16)
    weight_grad(3, attended, dm_ref[...], keep_ref, send_ref)
    finish(going + send_grads(keep_ref, send_ref, keep_hbms, send_hbms, out_sems))


def store(x_ref, x_hbm, sem):
    start(x_ref, x_hbm, sem).wait()


def column_first(parts, *refs):
    c_refs, (w_hbm, turn_hbm, cot_ref, da_ref, early_ref, w_ref, turn_ref, sems) = refs[:parts], refs[parts:]
    coming = [
        start(turn_hbm.at[4], turn_ref, sems.at[0]), start(w_hbm.at[1, 3], w_ref, sems.at[1]),
        start(turn_hbm.at[2], early_ref.at[0], sems.at[2]), start(w_hbm.at[1, 0], early_ref.at[1], sems.at[3]),
    ]
    cotangent = jnp.concatenate([ref[...] for ref in c_refs], axis=0)
    coming[0].wait()
    cotangent = dot(turn_ref[...], cotangent).astype(BF16)
    cot_ref[...] = cotangent
    coming[1].wait()
    da_ref[...] = dot_nt(cotangent, w_ref[...]).astype(BF16)
    finish(coming[2:])


def column_main(sizes, m_ref, cot_ref, da_ref, early_ref, g_ref, w_hbm, turn_hbm,
                dm_hbm, mid_hbm, n_hbm, att_hbm, dqkv_hbm,
                w_ref, turn_ref, dm_ref, mid_ref, n_ref, att_ref, dqkv_ref, q_ref, k_ref, v_ref, p_ref, sems):
    height, cols, width, together = sizes
    coming = [
        start(w_hbm.at[1, 1], w_ref.at[0], sems.at[0]), start(w_hbm.at[1, 2], w_ref.at[1], sems.at[1]),
        start(turn_hbm.at[3], turn_ref, sems.at[2]),
    ]
    middle = dot(early_ref[0], m_ref[...])
    mid_ref[...] = middle.astype(BF16)
    going = [start(mid_ref, mid_hbm, sems.at[3])]
    centred, inverse = statistics(middle)
    normed = (centred * inverse * g_ref[1:2]).astype(BF16)
    n_ref[...] = normed
    going.append(start(n_ref, n_hbm, sems.at[4]))
    q_ref[...] = dot(normed, early_ref[1]).astype(BF16)
    coming[0].wait()
    k_ref[...] = dot(normed, w_ref[0]).astype(BF16)
    coming[1].wait()
    v_ref[...] = dot(normed, w_ref[1]).astype(BF16)
    count = together * height
    groups = cols // together
    attention_forward(q_ref, k_ref, v_ref, att_ref, p_ref, groups, count, width, height)
    going.append(start(att_ref, att_hbm, sems.at[5]))
    attention_back(q_ref, k_ref, v_ref, p_ref, da_ref, dqkv_ref, groups, count, width)
    going.append(start(dqkv_ref, dqkv_hbm, sems.at[6]))
    d_normed = input_back(dqkv_ref, [early_ref.at[1], w_ref.at[0], w_ref.at[1]])
    middle = mid_ref[...].astype(F32)
    d_middle = cot_ref[...].astype(F32) + norm_back(middle, g_ref[1:2], d_normed)
    coming[2].wait()
    finish(going + send_turned(turn_ref, d_middle.astype(BF16), dm_ref, quarters(dm_hbm), sems.at[pl.ds(7, 4)]))


def column_last(parts, plane, cot_hbm, mid_hbm, n_hbm, att_hbm, dqkv_hbm, w_hbm, turn_hbm, *refs):
    out_hbms, refs = refs[:parts], refs[parts:]
    keep_hbms, send_hbms, refs = refs[:plane], refs[plane : 2 * plane], refs[2 * plane :]
    out_ref, keep_ref, send_ref, w_ref, turn_ref, flat_ref, dqkv_ref, sems, out_sems = refs
    coming = [
        start(turn_hbm.at[6], turn_ref.at[0], sems.at[0]), start(n_hbm, flat_ref.at[0], sems.at[1]),
        start(dqkv_hbm, dqkv_ref, sems.at[2]), start(att_hbm, flat_ref.at[1], sems.at[3]),
        start(cot_hbm, flat_ref.at[2], sems.at[4]), start(mid_hbm, flat_ref.at[3], sems.at[5]),
        start(w_hbm.at[1, 3], w_ref, sems.at[6]), start(turn_hbm.at[5], turn_ref.at[1], sems.at[7]),
    ]
    finish(coming[:3])
    normed = dot(flat_ref[0], turn_ref[0]).astype(BF16)
    for part in range(3):
        weight_grad(part, normed, third(dqkv_ref, part), keep_ref, send_ref)
    finish(coming[3:])
    attended = dot(flat_ref[1], turn_ref[0]).astype(BF16)
    weight_grad(3, attended, flat_ref[2], keep_ref, send_ref)
    going = send_grads(keep_ref, send_ref, keep_hbms, send_hbms, out_sems)
    output = (flat_ref[3].astype(F32) + dot(flat_ref[1], w_ref[...])).astype(BF16)
    finish(going + send_turned(turn_ref.at[1], output, out_ref, out_hbms, sems.at[pl.ds(8, parts)]))


def add_pairs(count, *refs):
    keep_hbms, got_refs, sum_refs, (keep_ref, sems) = (
        refs[:count], refs[count : 2 * count], refs[2 * count : 3 * count], refs[3 * count :]
    )
    coming = [start(hbm, keep_ref.at[at], sems.at[at]) for at, hbm in enumerate(keep_hbms)]
    for at, copy in enumerate(coming):
        copy.wait()
        sum_refs[at][...] = (keep_ref[at].astype(F32) + got_refs[at][...].astype(F32)).astype(BF16)


NEAR, FAR, ANY = pltpu.VMEM, pltpu.HBM, None


def call(kernel, ins, outs, scratch):
    def spec(where):
        return pl.BlockSpec(memory_space=pltpu.HBM if where is FAR else pltpu.VMEM)

    def place(item, where):
        return item if where is ANY else pltpu.with_memory_space_constraint(item, where)

    return pl.pallas_call(
        kernel,
        in_specs=[spec(where) for _, where in ins],
        out_specs=[spec(where) for _, where in outs],
        out_shape=[jax.ShapeDtypeStruct(shape, BF16) if where is ANY else where(shape, BF16) for shape, where in outs],
        scratch_shapes=scratch,
        compiler_params=pltpu.CompilerParams(vmem_limit_bytes=48 * 1024 * 1024),
        cost_estimate=pl.CostEstimate(flops=1 << 20, bytes_accessed=1 << 10, transcendentals=0),
    )(*[place(item, where) for item, where in ins])


def swap(item, axis, count, step):
    return lax.ppermute(item, axis, [(at, at ^ step) for at in range(count)])


def chip_sums(keeps, sends, col_parts):
    got = [swap(send, "col", col_parts, 1) for send in sends]
    count, shape = len(keeps), keeps[0].shape
    return call(
        functools.partial(add_pairs, count),
        [(item, FAR) for item in keeps] + [(item, ANY) for item in got], [(shape, ANY)] * count,
        [pltpu.VMEM((count, *shape), BF16), pltpu.SemaphoreType.DMA((count,))],
    )


def plane_pieces(sums, plane, core):
    return [item if step == 0 else swap(item, "col", plane * core, step * core) for step, item in enumerate(sums)]


def last_sums(pieces, row_parts):
    parts, size, channels = pieces[0].shape
    held = sum(piece.astype(F32) for piece in pieces).astype(BF16)
    held = held.reshape(parts, row_parts, size // row_parts, channels)
    result = held[:, 0].astype(F32)
    for step in range(1, row_parts):
        result = result + swap(held[:, step], "row", row_parts, step).astype(F32)
    return result


def body(row_parts, col_parts, field, cotangent, gains, weights):
    high, wide, channels = field.shape
    core = 2
    plane = col_parts // core
    rows = high // col_parts
    cols = wide // row_parts
    tokens = high * wide
    height = high * row_parts
    length = wide * col_parts
    width = channels // HEADS
    together = min(cols, max(1, 256 // height))
    devices = row_parts * col_parts
    my_row = lax.axis_index("row")

    flat, triple = (tokens, channels), (tokens, 3 * channels)
    probs = (rows * HEADS, length, length)
    packed = (4, channels // col_parts, channels)

    def scratch(*shape):
        return pltpu.VMEM(shape, BF16)

    def at(where, *items):
        return [(item, where) for item in items]

    square = scratch(*flat)
    copies = pltpu.SemaphoreType.DMA
    assert channels == tokens
    turns = [
        ((rows, col_parts, row_parts, cols), (2, 1, 0, 3), {}, 0),
        ((row_parts, col_parts, rows, cols), (2, 1, 0, 3), {}, 0),
        ((height, cols), (1, 0), {}, 0),
        ((cols, height), (1, 0), {}, 0),
        ((row_parts, high, cols), (2, 0, 1), {0: "row"}, 0),
        ((cols, row_parts, high), (1, 2, 0), {1: "row"}, 0),
        ((row_parts, plane, core, channels // devices), (2, 1, 0, 3), {0: "row", 1: "plane", 2: "core"}, 1),
    ]

    def all_to_all(item):
        item = item.reshape(devices, rows * cols, channels)
        return lax.all_to_all(item, ("row", "col"), 0, 0, tiled=True).reshape(tokens, channels)

    x = lax.all_to_all(field.reshape(col_parts, rows, wide, channels), "col", 0, 0, tiled=True)
    cots = []
    for step in range(row_parts):
        piece = lax.dynamic_slice_in_dim(cotangent, (my_row ^ step) * cols, cols, axis=1)
        piece = piece if step == 0 else swap(piece, "row", row_parts, step)
        cots.append(piece.reshape(high * cols, channels))
    turn, = call(
        functools.partial(set_up, turns), [], at(FAR, (len(turns), *flat)),
        [scratch(len(turns), *flat), copies((len(turns),))],
    )

    sizes = (rows, length, width)
    mid, normed, query, key, value, attended, prob = call(
        functools.partial(row_forward, sizes),
        at(ANY, x, gains) + at(FAR, weights, turn), at(FAR, *[flat] * 6, probs),
        [scratch(4, *flat)] + [square] * 7 + [scratch(*probs), copies((5,)), copies((6,)), copies((4,))],
    )
    mid, cots = lax.optimization_barrier((mid, cots))
    cot, d_att, early = call(
        functools.partial(column_first, row_parts),
        at(ANY, *cots) + at(FAR, weights, turn), at(NEAR, flat, flat, (2, *flat)), [square, square, copies((4,))],
    )
    mid = all_to_all(mid)

    count = together * height
    d_mid, *kept = call(
        functools.partial(column_main, (height, cols, width, together)),
        at(ANY, mid) + at(NEAR, cot, d_att, early) + at(ANY, gains) + at(FAR, weights, turn),
        at(FAR, flat, flat, flat, flat, triple),
        [scratch(2, *flat)] + [square] * 5 + [scratch(*triple)] + [square] * 3
        + [scratch(cols // together * HEADS, count, count), copies((11,))],
    )
    d_mid = all_to_all(d_mid)
    results = call(
        functools.partial(column_last, row_parts, plane),
        at(FAR, cot, *kept, weights, turn), at(FAR, *[(high * cols, channels)] * row_parts, *[packed] * (2 * plane)),
        [square, scratch(plane, *packed), scratch(plane, *packed), square, scratch(2, *flat), scratch(4, *flat),
         scratch(*triple), copies((8 + row_parts,)), copies((2 * plane,))],
    )
    outs, grads = results[:row_parts], results[row_parts:]
    sums_b = chip_sums(grads[:plane], grads[plane:], col_parts)
    pieces_b = plane_pieces(sums_b, plane, core)
    pieces_out = [outs[0], swap(outs[1], "row", row_parts, 1)]
    d_mid, rest, _ = lax.optimization_barrier((d_mid, outs[2:], sums_b))
    results = call(
        functools.partial(row_back, (rows, length, width, plane)),
        at(ANY, d_mid, x, gains) + at(FAR, weights, turn, normed, query, key, value, attended, prob),
        at(FAR, x.shape, *[packed] * (2 * plane)),
        [scratch(4, *flat), scratch(2, *flat)] + [square] * 6 + [scratch(*probs), square, scratch(*triple)]
        + [scratch(*x.shape), scratch(plane, *packed), scratch(plane, *packed), copies((12,)), copies((2 * plane,))],
    )
    (field_grad, *grads), pieces_b, pieces_out, rest = lax.optimization_barrier((results, pieces_b, pieces_out, rest))
    field_grad = lax.all_to_all(field_grad, "col", 0, 0, tiled=True)
    sums_a = chip_sums(grads[:plane], grads[plane:], col_parts)
    pieces_a = plane_pieces(sums_a, plane, core)
    second, _ = lax.optimization_barrier((rest[:1], sums_a))
    second = [swap(item, "row", row_parts, 2) for item in second]
    field_grad, pieces_b, rest = lax.optimization_barrier((field_grad, pieces_b, rest[1:]))
    grads_b = last_sums(pieces_b, row_parts)
    pieces_a, second, pieces_out = lax.optimization_barrier((pieces_a, second, pieces_out))
    pieces_out += second + [swap(item, "row", row_parts, 3 + step) for step, item in enumerate(rest)]
    field_grad, = call(store, at(ANY, field_grad), at(FAR, field_grad.shape), [copies])
    field_grad = field_grad.reshape(high, wide, channels)
    output = jnp.zeros((high, wide, channels), BF16)
    for step, piece in enumerate(pieces_out):
        piece = piece.reshape(high, cols, channels)
        output = lax.dynamic_update_slice_in_dim(output, piece, (my_row ^ step) * cols, axis=1)
    grads_a = last_sums(pieces_a, row_parts)
    return output, field_grad, jnp.concatenate([grads_a, grads_b], axis=0)


def solution(mesh):
    return jax.shard_map(
        functools.partial(body, mesh.shape["row"], mesh.shape["col"]),
        mesh=mesh,
        in_specs=(P("row", "col", None), P("row", "col", None), P(), P()),
        out_specs=(P("row", "col", None), P("row", "col", None), P(None, ("row", "col"), None)),
        check_vma=False,
    )
```

```python
import functools
import math

import jax
import jax.numpy as jnp
from jax import lax
from jax.experimental import pallas as pl
from jax.experimental.pallas import tpu as pltpu
from jax.sharding import PartitionSpec as P

HEADS = 8
eps = 1e-05
F32 = jnp.float32
BF16 = jnp.bfloat16


def log2(n):
    assert n & (n - 1) == 0
    return n.bit_length() - 1


def dot(left, right):
    return jnp.dot(left, right, preferred_element_type=F32)


def dot_nt(left, right):
    return lax.dot_general(left, right, (((1,), (1,)), ((), ())), preferred_element_type=F32)


def dot_tn(left, right):
    return lax.dot_general(left, right, (((0,), (0,)), ((), ())), preferred_element_type=F32)


def one_hot(sizes, order, me=None, lead=0):
    total = math.prod(sizes)
    index = lax.broadcasted_iota(jnp.int32, (total, total), lead)
    found = {}
    for axis in reversed(order):
        found[axis] = index & (sizes[axis] - 1)
        index = index >> log2(sizes[axis])
    source, shift = None, 0
    for axis in reversed(range(len(sizes))):
        digit = found[axis] << shift
        source = digit if source is None else source | digit
        shift += log2(sizes[axis])
    if me:
        place, shift = 0, 0
        for axis in reversed(range(len(sizes))):
            if axis in me:
                place = place | (me[axis] << shift)
            shift += log2(sizes[axis])
        source = source ^ place
    hit = source == lax.broadcasted_iota(jnp.int32, (total, total), 1 - lead)
    return jnp.where(hit, 1.0, 0.0).astype(BF16)


def statistics(values):
    average = jnp.mean(values, axis=-1, keepdims=True)
    centred = values - average
    spread = jnp.mean(centred * centred, axis=-1, keepdims=True)
    return centred, lax.rsqrt(spread + eps)


def norm_back(values, gain, d_normed):
    centred, inverse = statistics(values)
    unit = centred * inverse
    scaled = d_normed * gain
    return inverse * (
        scaled
        - jnp.mean(scaled, axis=-1, keepdims=True)
        - unit * jnp.mean(scaled * unit, axis=-1, keepdims=True)
    )


def head_lanes(count, width):
    return lax.broadcasted_iota(jnp.int32, (count, 2 * width), 1) < width


def attention_forward(q_ref, k_ref, v_ref, att_ref, p_ref, groups, count, width, span, unroll=4):
    first = head_lanes(count, width)
    pairs = HEADS // 2
    scale = width ** (-0.5)

    def step(index, carry):
        group, pair = index // pairs, index % pairs
        rows = pl.ds(pl.multiple_of(group * count, count), count)
        lanes = pl.ds(pl.multiple_of(pair * 2 * width, 2 * width), 2 * width)
        query, key, value = q_ref[rows, lanes] * scale, k_ref[rows, lanes], v_ref[rows, lanes]
        zero = jnp.zeros_like(query)
        total = jnp.zeros((count, 2 * width), F32)
        for half in range(2):
            mine = first if half == 0 else jnp.logical_not(first)
            scores = dot_nt(key, jnp.where(mine, query, zero))
            if span < count:
                shift = log2(span)
                same = (lax.broadcasted_iota(jnp.int32, (count, count), 0) >> shift) == (
                    lax.broadcasted_iota(jnp.int32, (count, count), 1) >> shift
                )
                scores = jnp.where(same, scores, -jnp.inf)
            expo = jnp.exp(scores - jnp.max(scores, axis=0, keepdims=True))
            probs = (expo * (1.0 / jnp.sum(expo, axis=0, keepdims=True))).astype(BF16)
            p_ref[index * 2 + half] = probs
            total += dot_tn(probs, jnp.where(mine, value, zero))
        att_ref[rows, lanes] = total.astype(BF16)
        return carry

    lax.fori_loop(0, groups * pairs, step, 0, unroll=unroll)


def attention_back(q_ref, k_ref, v_ref, p_ref, da_ref, dqkv_ref, groups, count, width, unroll=4):
    first = head_lanes(count, width)
    pairs = HEADS // 2
    channels = HEADS * width
    scale = width ** (-0.5)

    def step(index, carry):
        group, pair = index // pairs, index % pairs
        rows = pl.ds(pl.multiple_of(group * count, count), count)
        lanes = pl.ds(pl.multiple_of(pair * 2 * width, 2 * width), 2 * width)
        query, key, value = q_ref[rows, lanes] * scale, k_ref[rows, lanes], v_ref[rows, lanes]
        d_out = da_ref[rows, lanes]
        zero = jnp.zeros_like(query)
        d_query = jnp.zeros((count, 2 * width), F32)
        d_key, d_value = d_query, d_query
        for half in range(2):
            mine = first if half == 0 else jnp.logical_not(first)
            probs = p_ref[index * 2 + half]
            d_mine = jnp.where(mine, d_out, zero)
            d_probs = dot_nt(value, d_mine)
            probs32 = probs.astype(F32)
            weighted = probs32 * d_probs
            total = jnp.sum(weighted, axis=0, keepdims=True)
            d_scores = (weighted - probs32 * total).astype(BF16)
            d_query += dot_tn(d_scores, jnp.where(mine, key, zero))
            d_key += dot(d_scores, jnp.where(mine, query, zero))
            d_value += dot(probs, d_mine)
        for part, item in enumerate((d_query * scale, d_key, d_value)):
            at = pl.ds(pl.multiple_of(part * channels + pair * 2 * width, 2 * width), 2 * width)
            dqkv_ref[rows, at] = item.astype(BF16)
        return carry

    lax.fori_loop(0, groups * pairs, step, 0, unroll=unroll)


def start(source, target, sem):
    copy = pltpu.make_async_copy(source, target, sem)
    copy.start()
    return copy


def finish(copies):
    for copy in copies:
        copy.wait()


def set_up(turns, turn_hbm, turn_ref, sems):
    my_row, my_col = lax.axis_index("row"), lax.axis_index("col")
    places = {"row": my_row, "plane": my_col >> 1, "core": my_col & 1}
    going = []
    for at, (sizes, order, me, lead) in enumerate(turns):
        turn_ref[at] = one_hot(sizes, order, {axis: places[name] for axis, name in me.items()}, lead)
        going.append(start(turn_ref.at[at], turn_hbm.at[at], sems.at[at]))
    finish(going)


def weight_grad(part, left, right, keep_ref, send_ref):
    plane, _, size, _ = keep_ref.shape
    whole = dot_tn(left, right).astype(BF16)
    for group in range(plane):
        send_ref[group, part] = whole[(plane + group) * size : (plane + group + 1) * size]
        keep_ref[group, part] = whole[group * size : (group + 1) * size]


def send_grads(keep_ref, send_ref, keep_hbms, send_hbms, sems):
    plane = keep_ref.shape[0]
    going = [start(send_ref.at[at], send_hbms[at], sems.at[at]) for at in range(plane)]
    return going + [start(keep_ref.at[at], keep_hbms[at], sems.at[plane + at]) for at in range(plane)]


def third(ref, part):
    channels = ref.shape[-1] // 3
    return ref[:, part * channels : (part + 1) * channels]


def send_turned(turn_ref, values, stage_ref, targets, sems):
    size = values.shape[0] // len(targets)
    going = []
    for at, target in enumerate(targets):
        piece = pl.ds(at * size, size)
        stage_ref[piece] = dot(turn_ref[piece], values).astype(BF16)
        going.append(start(stage_ref.at[piece], target, sems.at[at]))
    return going


def quarters(ref):
    size = ref.shape[0] // 4
    return [ref.at[pl.ds(at * size, size)] for at in range(4)]


def input_back(dqkv_ref, w_refs):
    total = dot_nt(third(dqkv_ref, 0), w_refs[0][...])
    total += dot_nt(third(dqkv_ref, 1), w_refs[1][...])
    total += dot_nt(third(dqkv_ref, 2), w_refs[2][...])
    return total.astype(BF16).astype(F32)


def rows_of(x_ref):
    _, rows, _, channels = x_ref.shape
    length = x_ref.shape[0] * x_ref.shape[2]
    pieces = [x_ref[:, i].reshape(length, channels) for i in range(rows)]
    return jnp.concatenate(pieces, axis=0).astype(F32)


def row_forward(sizes, x_ref, g_ref, w_hbm, turn_hbm, mid_hbm, n_hbm, q_hbm, k_hbm, v_hbm, att_hbm, p_hbm,
                w_ref, turn_ref, mid_ref, n_ref, q_ref, k_ref, v_ref, att_ref, p_ref, in_sems, out_sems, sems):
    rows, length, width = sizes
    coming = [start(w_hbm.at[0, part], w_ref.at[part], in_sems.at[part]) for part in range(4)]
    coming.append(start(turn_hbm.at[0], turn_ref, in_sems.at[4]))
    centred, inverse = statistics(rows_of(x_ref))
    normed = (centred * inverse * g_ref[0:1]).astype(BF16)
    n_ref[...] = normed
    going = [start(n_ref, n_hbm, out_sems.at[0])]
    for part, (ref, hbm) in enumerate(((q_ref, q_hbm), (k_ref, k_hbm), (v_ref, v_hbm))):
        coming[part].wait()
        ref[...] = dot(normed, w_ref[part]).astype(BF16)
        going.append(start(ref, hbm, out_sems.at[1 + part]))
    attention_forward(q_ref, k_ref, v_ref, att_ref, p_ref, rows, length, width, length)
    going.append(start(p_ref, p_hbm, out_sems.at[5]))
    going.append(start(att_ref, att_hbm, out_sems.at[4]))
    coming[3].wait()
    middle = (rows_of(x_ref) + dot(att_ref[...], w_ref[3])).astype(BF16)
    coming[4].wait()
    finish(going + send_turned(turn_ref, middle, mid_ref, quarters(mid_hbm), sems))


def row_back(sizes, d_ref, x_ref, g_ref, w_hbm, turn_hbm, n_hbm, q_hbm, k_hbm, v_hbm, att_hbm, p_hbm, *refs):
    rows, length, width, plane = sizes
    fg_hbm, keep_hbms, send_hbms = refs[0], refs[1 : 1 + plane], refs[1 + plane : 1 + 2 * plane]
    w_ref, turn_ref, dm_ref, n_ref, q_ref, k_ref, v_ref, att_ref, p_ref, da_ref, dqkv_ref = refs[1 + 2 * plane : -5]
    fg_ref, keep_ref, send_ref, sems, out_sems = refs[-5:]
    half = p_ref.shape[0] // 2
    coming = [
        start(turn_hbm.at[1], turn_ref.at[0], sems.at[0]), start(w_hbm.at[0, 3], w_ref.at[3], sems.at[1]),
        start(v_hbm, v_ref, sems.at[2]), start(k_hbm, k_ref, sems.at[3]), start(q_hbm, q_ref, sems.at[4]),
        start(p_hbm.at[pl.ds(0, half)], p_ref.at[pl.ds(0, half)], sems.at[5]),
        start(p_hbm.at[pl.ds(half, half)], p_ref.at[pl.ds(half, half)], sems.at[6]),
        start(w_hbm.at[0, 0:3], w_ref.at[0:3], sems.at[7]),
        start(turn_hbm.at[6], turn_ref.at[1], sems.at[8]), start(att_hbm, att_ref, sems.at[9]),
        start(n_hbm, n_ref, sems.at[10]),
    ]
    coming[0].wait()
    d_middle = dot(turn_ref[0], d_ref[...]).astype(BF16)
    dm_ref[...] = d_middle
    coming[1].wait()
    da_ref[...] = dot_nt(d_middle, w_ref[3]).astype(BF16)
    finish(coming[2:7])
    attention_back(q_ref, k_ref, v_ref, p_ref, da_ref, dqkv_ref, rows, length, width)
    coming[7].wait()
    d_normed = input_back(dqkv_ref, [w_ref.at[part] for part in range(3)])
    result = dm_ref[...].astype(F32) + norm_back(rows_of(x_ref), g_ref[0:1], d_normed)
    result = result.astype(BF16)
    for i in range(rows):
        piece = result[i * length : (i + 1) * length]
        fg_ref[:, i] = piece.reshape(fg_ref.shape[0], fg_ref.shape[2], fg_ref.shape[3])
    going = [start(fg_ref, fg_hbm, sems.at[11])]
    finish(coming[8:])
    normed = dot(n_ref[...], turn_ref[1]).astype(BF16)
    for part in range(3):
        weight_grad(part, normed, third(dqkv_ref, part), keep_ref, send_ref)
    attended = dot(att_ref[...], turn_ref[1]).astype(BF16)
    weight_grad(3, attended, dm_ref[...], keep_ref, send_ref)
    finish(going + send_grads(keep_ref, send_ref, keep_hbms, send_hbms, out_sems))


def store(x_ref, x_hbm, sem):
    start(x_ref, x_hbm, sem).wait()


def column_first(parts, *refs):
    c_refs, (w_hbm, turn_hbm, cot_ref, da_ref, early_ref, w_ref, turn_ref, sems) = refs[:parts], refs[parts:]
    coming = [
        start(turn_hbm.at[4], turn_ref, sems.at[0]), start(w_hbm.at[1, 3], w_ref, sems.at[1]),
        start(turn_hbm.at[2], early_ref.at[0], sems.at[2]), start(w_hbm.at[1, 0], early_ref.at[1], sems.at[3]),
    ]
    cotangent = jnp.concatenate([ref[...] for ref in c_refs], axis=0)
    coming[0].wait()
    cotangent = dot(turn_ref[...], cotangent).astype(BF16)
    cot_ref[...] = cotangent
    coming[1].wait()
    da_ref[...] = dot_nt(cotangent, w_ref[...]).astype(BF16)
    finish(coming[2:])


def column_main(sizes, m_ref, cot_ref, da_ref, early_ref, g_ref, w_hbm, turn_hbm,
                dm_hbm, mid_hbm, n_hbm, att_hbm, dqkv_hbm,
                w_ref, turn_ref, dm_ref, mid_ref, n_ref, att_ref, dqkv_ref, q_ref, k_ref, v_ref, p_ref, sems):
    height, cols, width, together = sizes
    coming = [
        start(w_hbm.at[1, 1], w_ref.at[0], sems.at[0]), start(w_hbm.at[1, 2], w_ref.at[1], sems.at[1]),
        start(turn_hbm.at[3], turn_ref, sems.at[2]),
    ]
    middle = dot(early_ref[0], m_ref[...])
    mid_ref[...] = middle.astype(BF16)
    going = [start(mid_ref, mid_hbm, sems.at[3])]
    centred, inverse = statistics(middle)
    normed = (centred * inverse * g_ref[1:2]).astype(BF16)
    n_ref[...] = normed
    going.append(start(n_ref, n_hbm, sems.at[4]))
    q_ref[...] = dot(normed, early_ref[1]).astype(BF16)
    coming[0].wait()
    k_ref[...] = dot(normed, w_ref[0]).astype(BF16)
    coming[1].wait()
    v_ref[...] = dot(normed, w_ref[1]).astype(BF16)
    count = together * height
    groups = cols // together
    attention_forward(q_ref, k_ref, v_ref, att_ref, p_ref, groups, count, width, height)
    going.append(start(att_ref, att_hbm, sems.at[5]))
    attention_back(q_ref, k_ref, v_ref, p_ref, da_ref, dqkv_ref, groups, count, width)
    going.append(start(dqkv_ref, dqkv_hbm, sems.at[6]))
    d_normed = input_back(dqkv_ref, [early_ref.at[1], w_ref.at[0], w_ref.at[1]])
    middle = mid_ref[...].astype(F32)
    d_middle = cot_ref[...].astype(F32) + norm_back(middle, g_ref[1:2], d_normed)
    coming[2].wait()
    finish(going + send_turned(turn_ref, d_middle.astype(BF16), dm_ref, quarters(dm_hbm), sems.at[pl.ds(7, 4)]))


def column_last(parts, plane, cot_hbm, mid_hbm, n_hbm, att_hbm, dqkv_hbm, w_hbm, turn_hbm, *refs):
    out_hbms, refs = refs[:parts], refs[parts:]
    keep_hbms, send_hbms, refs = refs[:plane], refs[plane : 2 * plane], refs[2 * plane :]
    out_ref, keep_ref, send_ref, w_ref, turn_ref, flat_ref, dqkv_ref, sems, out_sems = refs
    coming = [
        start(turn_hbm.at[6], turn_ref.at[0], sems.at[0]), start(n_hbm, flat_ref.at[0], sems.at[1]),
        start(dqkv_hbm, dqkv_ref, sems.at[2]), start(att_hbm, flat_ref.at[1], sems.at[3]),
        start(cot_hbm, flat_ref.at[2], sems.at[4]), start(mid_hbm, flat_ref.at[3], sems.at[5]),
        start(w_hbm.at[1, 3], w_ref, sems.at[6]), start(turn_hbm.at[5], turn_ref.at[1], sems.at[7]),
    ]
    finish(coming[:3])
    normed = dot(flat_ref[0], turn_ref[0]).astype(BF16)
    for part in range(3):
        weight_grad(part, normed, third(dqkv_ref, part), keep_ref, send_ref)
    finish(coming[3:])
    attended = dot(flat_ref[1], turn_ref[0]).astype(BF16)
    weight_grad(3, attended, flat_ref[2], keep_ref, send_ref)
    going = send_grads(keep_ref, send_ref, keep_hbms, send_hbms, out_sems)
    output = (flat_ref[3].astype(F32) + dot(flat_ref[1], w_ref[...])).astype(BF16)
    finish(going + send_turned(turn_ref.at[1], output, out_ref, out_hbms, sems.at[pl.ds(8, parts)]))


def add_pairs(count, *refs):
    keep_hbms, got_refs, sum_refs, (keep_ref, sems) = (
        refs[:count], refs[count : 2 * count], refs[2 * count : 3 * count], refs[3 * count :]
    )
    coming = [start(hbm, keep_ref.at[at], sems.at[at]) for at, hbm in enumerate(keep_hbms)]
    for at, copy in enumerate(coming):
        copy.wait()
        sum_refs[at][...] = (keep_ref[at].astype(F32) + got_refs[at][...].astype(F32)).astype(BF16)


NEAR, FAR, ANY = pltpu.VMEM, pltpu.HBM, None


def call(kernel, ins, outs, scratch):
    def spec(where):
        return pl.BlockSpec(memory_space=pltpu.HBM if where is FAR else pltpu.VMEM)

    def place(item, where):
        return item if where is ANY else pltpu.with_memory_space_constraint(item, where)

    return pl.pallas_call(
        kernel,
        in_specs=[spec(where) for _, where in ins],
        out_specs=[spec(where) for _, where in outs],
        out_shape=[jax.ShapeDtypeStruct(shape, BF16) if where is ANY else where(shape, BF16) for shape, where in outs],
        scratch_shapes=scratch,
        compiler_params=pltpu.CompilerParams(vmem_limit_bytes=48 * 1024 * 1024),
        cost_estimate=pl.CostEstimate(flops=1 << 20, bytes_accessed=1 << 10, transcendentals=0),
    )(*[place(item, where) for item, where in ins])


def swap(item, axis, count, step):
    return lax.ppermute(item, axis, [(at, at ^ step) for at in range(count)])


def chip_sums(keeps, sends, col_parts):
    got = [swap(send, "col", col_parts, 1) for send in sends]
    count, shape = len(keeps), keeps[0].shape
    return call(
        functools.partial(add_pairs, count),
        [(item, FAR) for item in keeps] + [(item, ANY) for item in got], [(shape, ANY)] * count,
        [pltpu.VMEM((count, *shape), BF16), pltpu.SemaphoreType.DMA((count,))],
    )


def plane_pieces(sums, plane, core):
    return [item if step == 0 else swap(item, "col", plane * core, step * core) for step, item in enumerate(sums)]


def last_sums(pieces, row_parts):
    parts, size, channels = pieces[0].shape
    held = sum(piece.astype(F32) for piece in pieces).astype(BF16)
    held = held.reshape(parts, row_parts, size // row_parts, channels)
    result = held[:, 0].astype(F32)
    for step in range(1, row_parts):
        result = result + swap(held[:, step], "row", row_parts, step).astype(F32)
    return result


def body(row_parts, col_parts, field, cotangent, gains, weights):
    high, wide, channels = field.shape
    core = 2
    plane = col_parts // core
    rows = high // col_parts
    cols = wide // row_parts
    tokens = high * wide
    height = high * row_parts
    length = wide * col_parts
    width = channels // HEADS
    together = min(cols, max(1, 256 // height))
    devices = row_parts * col_parts
    my_row = lax.axis_index("row")

    flat, triple = (tokens, channels), (tokens, 3 * channels)
    probs = (rows * HEADS, length, length)
    packed = (4, channels // col_parts, channels)

    def scratch(*shape):
        return pltpu.VMEM(shape, BF16)

    def at(where, *items):
        return [(item, where) for item in items]

    square = scratch(*flat)
    copies = pltpu.SemaphoreType.DMA
    assert channels == tokens
    turns = [
        ((rows, col_parts, row_parts, cols), (2, 1, 0, 3), {}, 0),
        ((row_parts, col_parts, rows, cols), (2, 1, 0, 3), {}, 0),
        ((height, cols), (1, 0), {}, 0),
        ((cols, height), (1, 0), {}, 0),
        ((row_parts, high, cols), (2, 0, 1), {0: "row"}, 0),
        ((cols, row_parts, high), (1, 2, 0), {1: "row"}, 0),
        ((row_parts, plane, core, channels // devices), (2, 1, 0, 3), {0: "row", 1: "plane", 2: "core"}, 1),
    ]

    def all_to_all(item):
        item = item.reshape(devices, rows * cols, channels)
        return lax.all_to_all(item, ("row", "col"), 0, 0, tiled=True).reshape(tokens, channels)

    x = lax.all_to_all(field.reshape(col_parts, rows, wide, channels), "col", 0, 0, tiled=True)
    cots = []
    for step in range(row_parts):
        piece = lax.dynamic_slice_in_dim(cotangent, (my_row ^ step) * cols, cols, axis=1)
        piece = piece if step == 0 else swap(piece, "row", row_parts, step)
        cots.append(piece.reshape(high * cols, channels))
    turn, = call(
        functools.partial(set_up, turns), [], at(FAR, (len(turns), *flat)),
        [scratch(len(turns), *flat), copies((len(turns),))],
    )

    sizes = (rows, length, width)
    mid, normed, query, key, value, attended, prob = call(
        functools.partial(row_forward, sizes),
        at(ANY, x, gains) + at(FAR, weights, turn), at(FAR, *[flat] * 6, probs),
        [scratch(4, *flat)] + [square] * 7 + [scratch(*probs), copies((5,)), copies((6,)), copies((4,))],
    )
    mid, cots = lax.optimization_barrier((mid, cots))
    cot, d_att, early = call(
        functools.partial(column_first, row_parts),
        at(ANY, *cots) + at(FAR, weights, turn), at(NEAR, flat, flat, (2, *flat)), [square, square, copies((4,))],
    )
    mid = all_to_all(mid)

    count = together * height
    d_mid, *kept = call(
        functools.partial(column_main, (height, cols, width, together)),
        at(ANY, mid) + at(NEAR, cot, d_att, early) + at(ANY, gains) + at(FAR, weights, turn),
        at(FAR, flat, flat, flat, flat, triple),
        [scratch(2, *flat)] + [square] * 5 + [scratch(*triple)] + [square] * 3
        + [scratch(cols // together * HEADS, count, count), copies((11,))],
    )
    d_mid = all_to_all(d_mid)
    results = call(
        functools.partial(column_last, row_parts, plane),
        at(FAR, cot, *kept, weights, turn), at(FAR, *[(high * cols, channels)] * row_parts, *[packed] * (2 * plane)),
        [square, scratch(plane, *packed), scratch(plane, *packed), square, scratch(2, *flat), scratch(4, *flat),
         scratch(*triple), copies((8 + row_parts,)), copies((2 * plane,))],
    )
    outs, grads = results[:row_parts], results[row_parts:]
    sums_b = chip_sums(grads[:plane], grads[plane:], col_parts)
    pieces_b = plane_pieces(sums_b, plane, core)
    pieces_out = [outs[0], swap(outs[1], "row", row_parts, 1)]
    d_mid, rest, _ = lax.optimization_barrier((d_mid, outs[2:], sums_b))
    results = call(
        functools.partial(row_back, (rows, length, width, plane)),
        at(ANY, d_mid, x, gains) + at(FAR, weights, turn, normed, query, key, value, attended, prob),
        at(FAR, x.shape, *[packed] * (2 * plane)),
        [scratch(4, *flat), scratch(2, *flat)] + [square] * 6 + [scratch(*probs), square, scratch(*triple)]
        + [scratch(*x.shape), scratch(plane, *packed), scratch(plane, *packed), copies((12,)), copies((2 * plane,))],
    )
    (field_grad, *grads), pieces_b, pieces_out, rest = lax.optimization_barrier((results, pieces_b, pieces_out, rest))
    field_grad = lax.all_to_all(field_grad, "col", 0, 0, tiled=True)
    sums_a = chip_sums(grads[:plane], grads[plane:], col_parts)
    pieces_a = plane_pieces(sums_a, plane, core)
    second, _ = lax.optimization_barrier((rest[:1], sums_a))
    second = [swap(item, "row", row_parts, 2) for item in second]
    field_grad, pieces_b, rest, second = lax.optimization_barrier((field_grad, pieces_b, rest[1:], second))
    pieces_out += second
    grads_b = last_sums(pieces_b, row_parts)
    pieces_out += [swap(item, "row", row_parts, 3 + step) for step, item in enumerate(rest)]
    field_grad, = call(store, at(ANY, field_grad), at(FAR, field_grad.shape), [copies])
    field_grad = field_grad.reshape(high, wide, channels)
    output = jnp.zeros((high, wide, channels), BF16)
    for step, piece in enumerate(pieces_out):
        piece = piece.reshape(high, cols, channels)
        output = lax.dynamic_update_slice_in_dim(output, piece, (my_row ^ step) * cols, axis=1)
    grads_a = last_sums(pieces_a, row_parts)
    return output, field_grad, jnp.concatenate([grads_a, grads_b], axis=0)


def solution(mesh):
    return jax.shard_map(
        functools.partial(body, mesh.shape["row"], mesh.shape["col"]),
        mesh=mesh,
        in_specs=(P("row", "col", None), P("row", "col", None), P(), P()),
        out_specs=(P("row", "col", None), P("row", "col", None), P(None, ("row", "col"), None)),
        check_vma=False,
    )
```
